32 devices in a mesh: dp: 8 (over z, x), mp: 4 (over y, core).
Axes of the slice: x: 2, y: 2, z: 4, core: 2. Of those that a mesh axis runs over, the one named last changes fastest.
Arguments:
- tokens: bfloat16 [32768, 768], P(('dp', 'mp')), may hold values from -6 to 6
- lengths: int32 [128], P('dp'), may hold values from 65 to 512, as said below
- cotangent: bfloat16 [32768, 768], P(('dp', 'mp')), may hold values from -6 to 6
- w_qkv: float32 [768, 12, 192], P('dp', 'mp'), may hold values from -0.109375 to 0.109375
- w_o: float32 [768, 768], P(('dp', 'mp')), may hold values from -0.875 to 0.875
- w_in: float32 [768, 3072], P(None, ('dp', 'mp')), may hold values from -0.21875 to 0.21875
- w_out: float32 [3072, 768], P(('dp', 'mp')), may hold values from -0.109375 to 0.109375
- gain_attn: float32 [768], replicated, may hold values from 0.5 to 1.5
- gain_ffn: float32 [768], replicated, may hold values from 0.5 to 1.5
- pos_table: float32 [32, 12], replicated, may hold values from -4 to 4
- phm_rules: float32 [4, 4, 4], replicated, may hold values from -4 to 4
- down_left: float32 [4, 192], replicated, may hold values from -1.2 to 1.2
- down_right: float32 [4, 12], replicated, may hold values from -1.2 to 1.2
- up_left: float32 [4, 12], replicated, may hold values from -1.2 to 1.2
- up_right: float32 [4, 192], replicated, may hold values from -1.2 to 1.2
Outputs:
- out: bfloat16 [32768, 768], P(('dp', 'mp'))
- grad_tokens: bfloat16 [32768, 768], P(('dp', 'mp'))
- grad_w_qkv: float32 [768, 12, 192], P('dp', 'mp')
- grad_w_o: float32 [768, 768], P(('dp', 'mp'))
- grad_w_in: float32 [768, 3072], P(None, ('dp', 'mp'))
- grad_w_out: float32 [3072, 768], P(('dp', 'mp'))
- grad_gain_attn: float32 [768], replicated
- grad_gain_ffn: float32 [768], replicated
- grad_pos_table: float32 [32, 12], replicated
- grad_phm_rules: float32 [4, 4, 4], replicated
- grad_down_left: float32 [4, 192], replicated
- grad_down_right: float32 [4, 12], replicated
- grad_up_left: float32 [4, 12], replicated
- grad_up_right: float32 [4, 192], replicated
The draws below stay inside these ranges and needn't reach their ends.
Inputs may be any that keep to these rules, and one draw needn't show every extreme that they name: `lengths`: entry g * 16 + j is the length of sequence j of group g; its slot length is 512 for j below 4, 256 for j below 8, else 128; each length is more than half of its slot length and at most the slot length, and in every group one of the first 4 sequences fills its slot.
All inputs are finite; a program needn't handle non-finite values.
Results may differ from the reference program's by a relative error of at most 0.024.
The reference program's roundings to bfloat16 on the way count: a program that leaves them out, or rounds other values in their place, can miss the bound.
Values may be sent and summed in bfloat16 or wider, within the bound.
A program may use at most 192 MiB of HBM per device.

```python
import jax
import jax.numpy as jnp
import numpy as np
from jax import lax

D = 768
H = 12
DH = 64
FF = 3072
NB = 32
MAXDIST = 128
ADAPT = 48
KRON = 4
LEN_LONG = 512
LEN_MID = 256
LEN_SHORT = 128
SEG = 128
NSET = 4
SEQ_G = 16
GROUP_TOK = 4096
TOKENS = 32768
N_DP = 8
N_MP = 4


def draw_lengths(key, part):
    key = jax.random.fold_in(key, 7)
    slot_cap = jnp.concatenate([jnp.full((NSET,), LEN_LONG, jnp.int32), jnp.full((NSET,), LEN_MID, jnp.int32), jnp.full((2 * NSET,), LEN_SHORT, jnp.int32)])
    slot_cap = jnp.tile(slot_cap[None, :], (N_DP, 1))
    raw_bits = jax.random.randint(jax.random.fold_in(key, 1), (N_DP, SEQ_G), 0, 1 << 20, dtype=jnp.int32)
    half_cap = slot_cap // 2
    drawn = half_cap + 1 + raw_bits % (slot_cap - half_cap)
    chosen = jax.random.randint(jax.random.fold_in(key, 2), (N_DP, 1), 0, NSET, dtype=jnp.int32)
    column = jnp.arange(SEQ_G, dtype=jnp.int32)[None, :]
    drawn = jnp.where(column == chosen, LEN_LONG, drawn)
    return drawn.reshape(N_DP * SEQ_G).astype(jnp.int32)


def level_of(rng, shape, cuts, smallest, top_value):
    def one(position, shards_of):
        heights = jax.random.uniform(jax.random.fold_in(jax.random.fold_in(rng, 6), position), (shards_of,), jnp.float32, smallest / len(cuts), top_value / len(cuts))
        return jnp.repeat(jnp.exp(heights), shape[position] // shards_of).reshape((-1,) + (1,) * (len(shape) - position - 1))

    level = one(*cuts[0])
    for cut in cuts[1:]:
        level = level * one(*cut)
    return level


def noise(stream_key, extent, scale, limit, shards=(), kind=jnp.bfloat16):
    values = jax.random.normal(stream_key, extent, jnp.float32) * scale
    if len(shards) > 0:
        values = level_of(stream_key, extent, shards, -0.22, 0.18) * values
    return jnp.clip(values, min=-limit, max=limit).astype(kind)


def setup_inputs(seed: int = 0) -> dict:
    seeds = jax.random.split(jax.random.key(seed), 16)
    return {
        "tokens": noise(seeds[0], (TOKENS, D), 1.0, 6.0, ((0, 32),)),
        "lengths": draw_lengths(jax.random.fold_in(seeds[15], 71), 0),
        "cotangent": noise(seeds[2], (TOKENS, D), 1.0, 6.0, ((0, 32),)),
        "w_qkv": noise(seeds[3], (D, H, 3 * DH), (4 * D) ** -0.5, 0.109375, ((0, 8), (1, 4)), jnp.float32),
        "w_o": noise(seeds[4], (D, D), (D // 16) ** -0.5, 0.875, ((0, 32),), jnp.float32),
        "w_in": noise(seeds[5], (D, FF), D ** -0.5, 0.21875, ((1, 32),), jnp.float32),
        "w_out": noise(seeds[6], (FF, D), FF ** -0.5, 0.109375, ((0, 32),), jnp.float32),
        "gain_attn": jnp.clip(1.0 + 0.1 * jax.random.normal(seeds[7], (D,), jnp.float32), 0.5, 1.5),
        "gain_ffn": jnp.clip(1.0 + 0.1 * jax.random.normal(seeds[8], (D,), jnp.float32), 0.5, 1.5),
        "pos_table": noise(seeds[9], (NB, H), 1.0, 4.0, (), jnp.float32),
        "phm_rules": noise(seeds[10], (KRON, KRON, KRON), 1.0, 4.0, (), jnp.float32),
        "down_left": noise(seeds[11], (KRON, D // KRON), 0.2, 1.2, (), jnp.float32),
        "down_right": noise(seeds[12], (KRON, ADAPT // KRON), 0.2, 1.2, (), jnp.float32),
        "up_left": noise(seeds[13], (KRON, ADAPT // KRON), 0.2, 1.2, (), jnp.float32),
        "up_right": noise(seeds[14], (KRON, D // KRON), 0.2, 1.2, (), jnp.float32),
    }


@jax.custom_vjp
def low(v):
    return lax.optimization_barrier(v.astype(jnp.bfloat16)).astype(jnp.float32)

@jax.custom_vjp
def low_back(v):
    return v

def low_keep(v):
    return (low(v), None)

def low_pass(kept, grad):
    return (grad,)

def back_keep(v):
    return (v, None)

def back_low(kept, grad):
    return (low(grad),)
low.defvjp(low_keep, low_pass)
low_back.defvjp(back_keep, back_low)
NORM_EPS = 1e-06
MASK_FILL = -1000000000.0
FULL_PRECISION = lax.Precision.HIGHEST

def rel_buckets(length):
    offsets = np.arange(-(length - 1), length)
    half_count = NB // 2
    exact_count = half_count // 2
    upward = (offsets > 0).astype(np.int64) * half_count
    distance = np.abs(offsets)
    scaled = np.log(np.maximum(distance, 1) / exact_count) / np.log(MAXDIST / exact_count) * (half_count - exact_count)
    far_bucket = np.minimum(exact_count + np.floor(np.maximum(scaled, 0.0)).astype(np.int64), half_count - 1)
    return upward + np.where(distance < exact_count, distance, far_bucket)

def bucket_grid(length):
    table_index = rel_buckets(length)
    spread = np.arange(length)[None, :] - np.arange(length)[:, None] + length - 1
    return table_index[spread]

def bucket_shapes():
    return ((LEN_LONG, NSET), (LEN_MID, NSET), (LEN_SHORT, 2 * NSET))

def valid_rows(lengths):
    pieces = []
    offset = 0
    for length, seq_count in bucket_shapes():
        places = jnp.arange(length, dtype=jnp.int32)
        chosen = lengths[offset:offset + seq_count].astype(jnp.int32)
        pieces.append((places[None, :] < chosen[:, None]).reshape(length * seq_count))
        offset = offset + seq_count
    return jnp.concatenate(pieces)

def product(left_side, right_side):
    return jnp.dot(left_side, right_side, precision=FULL_PRECISION)

def normed(values, gain):
    return values * lax.rsqrt(lax.optimization_barrier(jnp.mean(values * values, axis=-1, keepdims=True)) + NORM_EPS) * gain

def gelu_exact(values):
    return jax.nn.gelu(values, approximate=False)

def adapter_weights(phm_rules, down_left, down_right, up_left, up_right):
    w_down = jnp.einsum('iab,ip,iq->apbq', phm_rules, down_left, down_right, precision=FULL_PRECISION).reshape(D, ADAPT)
    w_up = jnp.einsum('iab,ip,iq->apbq', phm_rules, up_left, up_right, precision=FULL_PRECISION).reshape(ADAPT, D)
    return (w_down, w_up)

def attend_bucket(packed, live_mask, pos_table, length):
    queries = packed[:, :, :, 0]
    key_part = packed[:, :, :, 1]
    values = packed[:, :, :, 2]
    scores = jnp.einsum('slhd,smhd->shlm', queries, key_part, precision=FULL_PRECISION)
    score_bias = jnp.transpose(pos_table[bucket_grid(length)], (2, 0, 1))
    scores = low_back(scores + score_bias[None])
    scores = jnp.where(live_mask[:, None, None, :], scores, MASK_FILL)
    attn_probs = low(jax.nn.softmax(scores, axis=-1))
    return jnp.einsum('shlm,smhd->slhd', attn_probs, values, precision=FULL_PRECISION)

def group_forward(tokens_group, params, live_mask):
    w_qkv, w_o, w_in, w_out, gain_attn, gain_ffn, pos_table, phm_rules, down_left, down_right, up_left, up_right = params
    normed_attn = low(normed(tokens_group, gain_attn))
    packed = product(normed_attn, low(w_qkv).reshape(D, H * 3 * DH))
    packed = low(low_back(packed)).reshape(GROUP_TOK, H, 3, DH)
    contexts = []
    offset = 0
    for length, seq_count in bucket_shapes():
        row_span = length * seq_count
        bucket_rows = packed[offset:offset + row_span].reshape(seq_count, length, H, 3, DH)
        bucket_live = live_mask[offset:offset + row_span].reshape(seq_count, length)
        contexts.append(attend_bucket(bucket_rows, bucket_live, pos_table, length).reshape(row_span, H * DH))
        offset = offset + row_span
    context = low(low_back(jnp.concatenate(contexts, axis=0)))
    midway = tokens_group + low_back(product(context, low(w_o)))
    normed_ffn = low(normed(midway, gain_ffn))
    ffn_pre = low_back(product(normed_ffn, low(w_in)))
    ffn_act = low(gelu_exact(ffn_pre))
    ffn_out = low_back(product(ffn_act, low(w_out)))
    w_down, w_up = adapter_weights(phm_rules, down_left, down_right, up_left, up_right)
    squeezed = low_back(product(low(ffn_out), low(w_down)))
    lifted = low(gelu_exact(squeezed))
    return midway + ffn_out + low_back(product(lifted, low(w_up)))

def reference(tokens, lengths, cotangent, w_qkv, w_o, w_in, w_out, gain_attn, gain_ffn, pos_table, phm_rules, down_left, down_right, up_left, up_right):
    params = (w_qkv, w_o, w_in, w_out, gain_attn, gain_ffn, pos_table, phm_rules, down_left, down_right, up_left, up_right)
    seg_count = GROUP_TOK // (N_MP * SEG)

    def to_stream(array):
        return array.reshape(N_MP, seg_count, SEG, D).transpose(1, 0, 2, 3).reshape(GROUP_TOK, D)

    def to_rows(array):
        return array.reshape(seg_count, N_MP, SEG, D).transpose(1, 0, 2, 3).reshape(GROUP_TOK, D)

    def one_group(totals, group_item):
        tokens_group, cotangent_group, lengths_group = group_item
        live_mask = valid_rows(lengths_group)
        result, pullback = jax.vjp(lambda tokens_in, params_in: group_forward(tokens_in, params_in, live_mask), to_stream(tokens_group), params)
        grad_input, grad_params = pullback(to_stream(cotangent_group) * live_mask[:, None].astype(jnp.float32))
        totals = tuple((summed + added for summed, added in zip(totals, grad_params)))
        return (totals, (to_rows(result), to_rows(grad_input)))
    stacked = (tokens.astype(jnp.float32).reshape(N_DP, GROUP_TOK, D), cotangent.astype(jnp.float32).reshape(N_DP, GROUP_TOK, D), lengths.reshape(N_DP, SEQ_G))
    totals, (result_rows, grad_rows) = lax.scan(one_group, tuple((jnp.zeros_like(weight_item) for weight_item in params)), stacked)
    return (result_rows.reshape(TOKENS, D).astype(jnp.bfloat16), grad_rows.reshape(TOKENS, D).astype(jnp.bfloat16), totals[0], totals[1], totals[2], totals[3], totals[4], totals[5], totals[6], totals[7], totals[8], totals[9], totals[10], totals[11])
```

```python
import functools

import jax
import jax.experimental.pallas as pl
import jax.experimental.pallas.tpu as pltpu
import jax.numpy as jnp
import numpy as np
from jax import lax
from jax.sharding import PartitionSpec as P

D = 768
DH = 64
NB = 32
MAXDIST = 128
ADAPT = 48
LEN_LONG = 512
LEN_MID = 256
LEN_SHORT = 128
SEG = 128


NORM_EPS = 1e-06
FULL_PRECISION = lax.Precision.HIGHEST


def rel_buckets(length):
    offsets = np.arange(-(length - 1), length)
    half_count = NB // 2
    exact_count = half_count // 2
    upward = (offsets > 0).astype(np.int64) * half_count
    distance = np.abs(offsets)
    scaled = (
        np.log(np.maximum(distance, 1) / exact_count)
        / np.log(MAXDIST / exact_count)
        * (half_count - exact_count)
    )
    far_bucket = np.minimum(
        exact_count + np.floor(np.maximum(scaled, 0.0)).astype(np.int64), half_count - 1
    )
    return upward + np.where(distance < exact_count, distance, far_bucket)


def normed(values, gain):
    return values * lax.rsqrt(jnp.mean(values * values, axis=-1, keepdims=True) + NORM_EPS) * gain


def gelu_exact(values):
    return jax.nn.gelu(values, approximate=False)


def adapter_weights(phm_rules, down_left, down_right, up_left, up_right):
    w_down = jnp.einsum(
        "iab,ip,iq->apbq", phm_rules, down_left, down_right, precision=FULL_PRECISION
    ).reshape(D, ADAPT)
    w_up = jnp.einsum(
        "iab,ip,iq->apbq", phm_rules, up_left, up_right, precision=FULL_PRECISION
    ).reshape(ADAPT, D)
    return (w_down, w_up)


MESH = pl.DeviceIdType.MESH


class Place:
    def __init__(self, depth):
        d, m = lax.axis_index("dp"), lax.axis_index("mp")
        self.depth = depth
        self.d, self.m = d, m
        self.z, self.x, self.y, self.c = d // 2, d % 2, m // 2, m % 2
        dx, dy, c = 1 - 2 * self.x, 2 - 4 * self.y, self.c
        self.sib = (d, m + 1 - 2 * c)
        self.right, self.left = (d + 2, m), (d - 2, m)
        self.mp_peer = ((d, m + 1 - 2 * c), (d, m + dy), (d, 3 - m))
        self.xn, self.yn = (d + dx, m), (d, m + dy)
        self.a_nbr = (d + (1 - c) * dx, m + c * dy)
        self.b_nbr = (d + c * dx, m + (1 - c) * dy)
        self.a = self.x + c * (self.y - self.x)
        self.b = self.y + c * (self.x - self.y)

    def by_core(self, run):
        for core in (0, 1):
            pl.when(self.c == core)(functools.partial(run, core))

    def flip(self, bit):
        step = 1 << bit
        return (self.d + step * (1 - 2 * ((self.d // step) % 2)), self.m)

    def barrier(self, bits):
        sem = pltpu.get_barrier_semaphore()

        def greet(dev):
            pl.semaphore_signal(sem, 1, device_id=dev, device_id_type=MESH)

        pals = [*self.mp_peer, self.xn] + [self.flip(bit) for bit in range(2, bits)]
        for dev in pals:
            greet(dev)
        pl.when(self.z > 0)(lambda: greet(self.left))
        pl.when(self.z < self.depth - 1)(lambda: greet(self.right))
        ends = jnp.minimum(self.z, 1) + jnp.minimum(self.depth - 1 - self.z, 1)
        pl.semaphore_wait(sem, len(pals) + ends)


def remote(src, dst, send, recv, dev):
    return pltpu.make_async_remote_copy(
        src_ref=src, dst_ref=dst, send_sem=send, recv_sem=recv, device_id=dev, device_id_type=MESH
    )


def slot_of(buf, by_head, p):
    return buf.at[p.y, p.c, p.z, p.x] if by_head else buf.at[p.z, p.x, p.y, p.c]


def pair_of(buf, by_head, core, b, z):
    if by_head:
        return buf.at[b, 0, z] if core == 0 else buf.at[:, 1, z, b]
    return buf.at[z, :, b, 0] if core == 0 else buf.at[z, b, :, 1]


class Gather:
    def __init__(self, p, by_head, shard, buf, send, recv, own):
        self.p, self.by_head, self.shard, self.buf = p, by_head, shard, buf
        self.send, self.recv, self.own = send, recv, own
        n = p.depth
        self.first = remote(shard, slot_of(buf, by_head, p), send.at[5 * n], recv.at[4 * n], p.a_nbr)
        self.keep = pltpu.make_async_copy(shard, slot_of(buf, by_head, p), own)

    @staticmethod
    def sems(n):
        return [
            pltpu.SemaphoreType.DMA((5 * n + 1,)),
            pltpu.SemaphoreType.DMA((4 * n + 1,)),
            pltpu.SemaphoreType.DMA,
        ]

    def _copy(self, core, b, z, kind):
        p, n = self.p, self.p.depth
        ref = pair_of(self.buf, self.by_head, core, b, z)
        if kind == "right":
            return remote(ref, ref, self.send.at[z], self.recv.at[z], p.right)
        if kind == "left":
            return remote(ref, ref, self.send.at[n + z], self.recv.at[z], p.left)
        return remote(ref, ref, self.send.at[2 * n + z], self.recv.at[n + z], p.b_nbr)

    def _sib(self, core, b, z):
        n = self.p.depth
        ref = pair_of(self.buf, self.by_head, core, b, z)
        return remote(ref, ref, self.send.at[3 * n + b * n + z], self.recv.at[2 * n + b * n + z], self.p.sib)

    def start(self):
        self.keep.start()
        self.first.start()

    def _spread(self, core, z, right, left):
        p = self.p
        if right:
            pl.when(p.z < p.depth - 1)(lambda: self._copy(core, p.b, z, "right").start())
        if left:
            pl.when(p.z > 0)(lambda: self._copy(core, p.b, z, "left").start())
        self._copy(core, p.b, z, "b").start()
        self._sib(core, p.b, z).start()

    def along(self, k):
        p = self.p
        if isinstance(k, int) and k == 0:
            self.keep.wait()
            self.first.wait_recv()
            p.by_core(lambda core: self._spread(core, p.z, True, True))
            return

        def from_left(core):
            self._copy(core, p.b, p.z - k, "right").wait_recv()
            self._spread(core, p.z - k, True, False)

        def from_right(core):
            self._copy(core, p.b, p.z + k, "left").wait_recv()
            self._spread(core, p.z + k, False, True)

        pl.when(p.z - k >= 0)(lambda: p.by_core(from_left))
        pl.when(p.z + k < p.depth)(lambda: p.by_core(from_right))

    def across(self, k):
        p = self.p

        def one(z, core):
            self._copy(core, 1 - p.b, z, "b").wait_recv()
            self._sib(core, 1 - p.b, z).start()

        pl.when(p.z - k >= 0)(lambda: p.by_core(lambda core: one(p.z - k, core)))
        if not (isinstance(k, int) and k == 0):
            pl.when(p.z + k < p.depth)(lambda: p.by_core(lambda core: one(p.z + k, core)))

    def finish(self):
        p, n = self.p, self.p.depth

        def each(z, carry):
            def one(core):
                for b in (0, 1):
                    self._sib(1 - core, b, z).wait_recv()

            p.by_core(one)
            return carry

        lax.fori_loop(0, n, each, 0)

    def drain(self):
        p, n = self.p, self.p.depth
        self.first.wait_send()

        def each(z, carry):
            def one(core):
                pl.when(jnp.logical_and(p.z < n - 1, z <= p.z))(
                    lambda: self._copy(core, p.b, z, "right").wait_send()
                )
                pl.when(jnp.logical_and(p.z > 0, z >= p.z))(
                    lambda: self._copy(core, p.b, z, "left").wait_send()
                )
                self._copy(core, p.b, z, "b").wait_send()
                for b in (0, 1):
                    self._sib(core, b, z).wait_send()

            p.by_core(one)
            return carry

        lax.fori_loop(0, n, each, 0)


class Exchange:
    def __init__(self, p, src, dst, send, recv, own):
        m = p.m
        c, other = m % 2, 1 - m % 2
        self.local = [
            pltpu.make_async_copy(src.at[m], dst.at[m], own.at[0]),
            pltpu.make_async_copy(src.at[4 + c], dst.at[4 + c], own.at[1]),
            pltpu.make_async_copy(src.at[pl.ds(6, 2)], dst.at[pl.ds(6, 2)], own.at[2]),
        ]
        self.out = [
            remote(src.at[dev[1]], dst.at[m], send.at[j], recv.at[j], dev)
            for j, dev in enumerate(p.mp_peer)
        ] + [remote(src.at[4 + other], dst.at[4 + c], send.at[3], recv.at[3], p.sib)]

    @staticmethod
    def sems():
        return [
            pltpu.SemaphoreType.DMA((4,)),
            pltpu.SemaphoreType.DMA((4,)),
            pltpu.SemaphoreType.DMA((3,)),
        ]

    def start(self):
        for copy in self.out + self.local:
            copy.start()

    def finish(self):
        for copy in self.local:
            copy.wait()
        for copy in self.out:
            copy.wait_recv()

    def drain(self):
        for copy in self.out:
            copy.wait_send()


def add_rows(dst, src, rows):
    step = 32 if rows % 32 == 0 else 16

    def one(i, carry):
        at = pl.ds(pl.multiple_of(i * step, step), step)
        total = dst[at, :].astype(jnp.float32) + src[at, :].astype(jnp.float32)
        dst[at, :] = total.astype(dst.dtype)
        return carry

    lax.fori_loop(0, rows // step, one, 0)


class Scatter:
    def __init__(self, p, by_head, part, total, half, quarter, arrive, last, send, recv):
        self.p, self.by_head, self.part, self.total = p, by_head, part, total
        self.half, self.quarter, self.arrive, self.last = half, quarter, arrive, last
        self.send, self.recv = send, recv
        self.rows = part.shape[-2]

    @staticmethod
    def scratch(n, rows, cols, dtype=jnp.bfloat16):
        return [
            pltpu.VMEM((n, 2, 2, rows, cols), dtype),
            pltpu.VMEM((n, 2, rows, cols), dtype),
            pltpu.VMEM((n + 1, 2, rows, cols), dtype),
            pltpu.VMEM((rows, cols), dtype),
            pltpu.SemaphoreType.DMA((3 * n + 1,)),
            pltpu.SemaphoreType.DMA((3 * n + 2,)),
        ]

    def order(self, k):
        n = self.p.depth
        base = k // 2 if k % 2 == 0 else n - 1 - k // 2
        near = 1 - jnp.minimum(self.p.z // max(n // 2, 1), 1)
        return base + near * (n - 1 - 2 * base)

    def _region(self, core, z):
        return self.part.at[:, core, z] if self.by_head else self.part.at[z, :, :, core]

    def _half_pair(self, core, b, z):
        over_first = (core == 0) != self.by_head
        return self.half.at[z, :, b] if over_first else self.half.at[z, b]

    def _sib(self, core, z):
        return remote(
            self._region(1 - core, z), self.half.at[z], self.send.at[z], self.recv.at[z], self.p.sib
        )

    def _b(self, core, z):
        n, p = self.p.depth, self.p
        return remote(
            self._half_pair(core, 1 - p.b, z), self.quarter.at[z], self.send.at[n + z], self.recv.at[n + z], p.b_nbr
        )

    def _right(self, z):
        n, p = self.p.depth, self.p
        return remote(
            self.quarter.at[z], self.arrive.at[z], self.send.at[2 * n + z], self.recv.at[2 * n + z], p.right
        )

    def _left(self, z, goal):
        n, p = self.p.depth, self.p
        return remote(
            self.quarter.at[z], self.arrive.at[goal], self.send.at[2 * n + z], self.recv.at[2 * n + goal], p.left
        )

    def _a(self):
        n, p = self.p.depth, self.p
        return remote(
            self.quarter.at[p.z, 1 - p.a], self.last, self.send.at[3 * n], self.recv.at[3 * n + 1], p.a_nbr
        )

    def start(self, k):
        z = self.order(k)
        self.p.by_core(lambda core: self._sib(core, z).start())

    def to_half(self, k):
        z = self.order(k)

        def one(core):
            self._sib(core, z).wait_recv()
            region = self._region(core, z)
            for i in (0, 1):
                for j in (0, 1):
                    add_rows(self.half.at[z, i, j], region.at[i, j], self.rows)
            self._b(core, z).start()

        self.p.by_core(one)

    def to_quarter(self, k):
        z = self.order(k)

        def one(core):
            self._b(core, z).wait_recv()
            for i in (0, 1):
                add_rows(self.quarter.at[z, i], self._half_pair(core, self.p.b, z).at[i], self.rows)

        self.p.by_core(one)

    def _take(self, z, slot):
        for i in (0, 1):
            add_rows(self.quarter.at[z, i], self.arrive.at[slot, i], self.rows)

    def pass_on(self, k):
        p, n = self.p, self.p.depth
        z = self.order(k)

        def rightward():
            def take():
                self._right(z).wait_recv()
                self._take(z, z)

            pl.when(p.z > 0)(take)
            self._right(z).start()

        def leftward():
            def take():
                self._left(z, z).wait_recv()
                self._take(z, z)

            pl.when(p.z < n - 1)(take)
            pl.when(z == p.z - 1)(lambda: self._left(z, n).start())
            pl.when(z < p.z - 1)(lambda: self._left(z, z).start())

        pl.when(z > p.z)(rightward)
        pl.when(z < p.z)(leftward)

    def collect(self):
        p, n = self.p, self.p.depth

        def from_left():
            self._right(p.z).wait_recv()
            self._take(p.z, p.z)

        def from_right():
            self._left(p.z, n).wait_recv()
            self._take(p.z, n)

        pl.when(p.z > 0)(from_left)
        pl.when(p.z < n - 1)(from_right)
        self._a().start()

    def finish(self):
        p = self.p
        self._a().wait_recv()
        self.total[...] = self.quarter[p.z, p.a].astype(jnp.float32) + self.last[...].astype(jnp.float32)

    def drain(self):
        p, n = self.p, self.p.depth
        self._a().wait_send()

        def each(z, carry):
            def one(core):
                self._sib(core, z).wait_send()
                self._b(core, z).wait_send()

            p.by_core(one)
            pl.when(z != p.z)(lambda: self._right(z).wait_send())
            return carry

        lax.fori_loop(0, n, each, 0)

    def steps(self):
        n = self.p.depth
        todo = [lambda: [self.start(k) for k in range(n)]]
        todo += [functools.partial(self.to_half, k) for k in range(n)]
        for k in range(n):
            todo.append(functools.partial(lambda k: (self.to_quarter(k), self.pass_on(k)), k))
        return todo + [self.collect, self.finish]


class Sum:
    def __init__(self, p, bits, value, slots, send, recv):
        self.p, self.bits, self.value, self.slots = p, bits, value, slots
        self.send, self.recv = send, recv

    @staticmethod
    def scratch(bits, rows):
        return [
            pltpu.VMEM((2 * (bits + 2), rows, 128), jnp.float32),
            pltpu.SemaphoreType.DMA((bits + 2,)),
            pltpu.SemaphoreType.DMA((bits + 2,)),
        ]

    def _copy(self, s):
        p = self.p
        dev = (p.sib, p.yn, *[p.flip(bit) for bit in range(self.bits)])[s]
        return remote(self.slots.at[2 * s], self.slots.at[2 * s + 1], self.send.at[s], self.recv.at[s], dev)

    def steps(self):
        def begin():
            self.slots[0] = self.value[...]
            self._copy(0).start()

        def one(s):
            self._copy(s).wait_recv()
            total = self.slots[2 * s] + self.slots[2 * s + 1]
            if s == self.bits + 1:
                self.value[...] = total
            else:
                self.slots[2 * s + 2] = total
                self._copy(s + 1).start()

        return [begin] + [functools.partial(one, s) for s in range(self.bits + 2)]

    def drain(self):
        for s in range(self.bits + 2):
            self._copy(s).wait_send()


def in_waves(lists, lag):
    for t in range(max(len(todo) + lag * r for r, todo in enumerate(lists))):
        for r, todo in enumerate(lists):
            if 0 <= t - lag * r < len(todo):
                todo[t - lag * r]()


def gather_kernel(p_depth, tok, cot, wq, wo, wi, wu, tok_s, cot_s, gq, go, gi, gu, *sems):
    p = Place(p_depth)
    n = p_depth
    arrays = []
    for i, (by_head, shard, buf) in enumerate(
        ((True, wq, gq), (False, wo, go), (False, wi, gi), (False, wu, gu))
    ):
        arrays.append(Gather(p, by_head, shard, buf, *sems[3 * i : 3 * i + 3]))
    rows = [Exchange(p, tok, tok_s, *sems[12:15]), Exchange(p, cot, cot_s, *sems[15:18])]
    p.barrier(0)
    for g in arrays:
        g.start()
    rows[0].start()
    if n <= 8:
        for k in range(n):
            for g in arrays:
                g.along(k)
            if k > 0:
                for g in arrays:
                    g.across(k - 1)
            if k == 1:
                rows[1].start()
        for g in arrays:
            g.across(n - 1)
    else:
        for g in arrays:
            g.along(0)
            lax.fori_loop(1, n, lambda k, carry: (g.along(k), carry)[1], 0)
        rows[1].start()
        for g in arrays:
            g.across(0)
            lax.fori_loop(1, n, lambda k, carry: (g.across(k), carry)[1], 0)
    for g in arrays + rows:
        g.finish()
    for g in arrays + rows:
        g.drain()


def gather_all(depth, tok, cot, shards):
    hbm = pl.BlockSpec(memory_space=pl.ANY)
    outs = [jax.ShapeDtypeStruct(tok.shape, tok.dtype)] * 2
    for i, s in enumerate(shards):
        lead = (2, 2, depth, 2) if i == 0 else (depth, 2, 2, 2)
        outs.append(jax.ShapeDtypeStruct(lead + s.shape, s.dtype))
    sems = Gather.sems(depth) * 4 + Exchange.sems() * 2
    return pl.pallas_call(
        functools.partial(gather_kernel, depth),
        out_shape=outs,
        in_specs=[hbm] * 6,
        out_specs=[hbm] * 6,
        scratch_shapes=sems,
        compiler_params=pltpu.CompilerParams(collective_id=0, has_side_effects=True),
        name="gather",
    )(tok, cot, *shards)


def scatter_kernel(depth, bits, pq, po, pi, pu, small, out_s, gtok_s, oq, oo, oi, ou, small_o, out, gtok, *scr):
    p = Place(depth)
    arrays = []
    for i, (by_head, part, total) in enumerate(
        ((False, pu, ou), (False, pi, oi), (False, po, oo), (True, pq, oq))
    ):
        arrays.append(Scatter(p, by_head, part, total, *scr[6 * i : 6 * i + 6]))
    rows = [Exchange(p, out_s, out, *scr[24:27]), Exchange(p, gtok_s, gtok, *scr[27:30])]
    small_o[...] = small[...]
    sums = Sum(p, bits, small_o, *scr[30:33])
    p.barrier(bits)
    for r in rows:
        r.start()
    in_waves([sums.steps()] + [g.steps() for g in arrays], min(depth, 4))
    for r in rows:
        r.finish()
    for g in arrays + rows + [sums]:
        g.drain()


def scatter_all(depth, bits, parts, small, out_s, gtok_s):
    hbm = pl.BlockSpec(memory_space=pl.ANY)
    vmem = pl.BlockSpec(memory_space=pltpu.VMEM)
    outs = [jax.ShapeDtypeStruct(s.shape[4:], jnp.float32) for s in parts]
    outs += [jax.ShapeDtypeStruct(small.shape, jnp.float32)]
    outs += [jax.ShapeDtypeStruct(out_s.shape, out_s.dtype)] * 2
    scr = []
    for s in (parts[3], parts[2], parts[1], parts[0]):
        scr += Scatter.scratch(depth, *s.shape[4:])
    scr += Exchange.sems() * 2 + Sum.scratch(bits, small.shape[0])
    return pl.pallas_call(
        functools.partial(scatter_kernel, depth, bits),
        out_shape=outs,
        in_specs=[vmem] * 5 + [hbm] * 2,
        out_specs=[vmem] * 5 + [hbm] * 2,
        scratch_shapes=scr,
        compiler_params=pltpu.CompilerParams(
            collective_id=1, has_side_effects=True, vmem_limit_bytes=60 * 2**20
        ),
        name="scatter",
    )(*parts, small, out_s, gtok_s)

SPANS = ((0, LEN_LONG), (LEN_LONG, LEN_MID), (LEN_LONG + LEN_MID, LEN_SHORT), (LEN_LONG + LEN_MID + LEN_SHORT, LEN_SHORT))
TILE = 128
QKV_PAD = 640
CTX_PAD = 256
MASK_LOW = -1e9
NN = (((1,), (0,)), ((), ()))
NT = (((1,), (1,)), ((), ()))


def dot(a, b, dims=NN):
    return lax.dot_general(a, b, dims, preferred_element_type=jnp.float32)


def offset_row(pos_table):
    buckets = rel_buckets(257)
    offset = np.clip(256 - np.arange(512), -256, 256) + 256
    onehot = (buckets[offset][:, None] == np.arange(NB)[None, :]).astype(np.float32)
    return jnp.einsum("rb,bh->hr", jnp.asarray(onehot), pos_table, precision=FULL_PRECISION)


def table_onehot():
    buckets = rel_buckets(257)
    offset = np.clip(256 - np.arange(512), -256, 256) + 256
    index = np.concatenate([buckets[offset], np.full(128, NB // 2 - 1), np.full(128, NB - 1)])
    return (index[:, None] == np.arange(NB)[None, :]).astype(np.float32)


def bias_tiles(row):
    spread = pltpu.roll(jnp.broadcast_to(row, (TILE, 512)), 0, 1, stride=1, stride_axis=0)
    far = [jnp.broadcast_to(row[:, at : at + 1], (TILE, TILE)) for at in (511, 0)]
    near = [spread[:, 256 - 128 * delta : 384 - 128 * delta] for delta in (-1, 0, 1)]
    return [far[0], *near, far[1]]


def diagonal_sums(tiles):
    grid = jnp.concatenate([jnp.zeros((TILE, TILE), jnp.float32), tiles[2], tiles[1], tiles[0]], axis=1)
    rows = TILE
    while rows > 8:
        rows //= 2
        grid = grid[:rows] + pltpu.roll(grid[rows:], 512 - rows, 1)
    total = grid[0:1]
    for r in range(1, 8):
        total = total + pltpu.roll(grid[r : r + 1], 512 - r, 1)
    return total


def swap_halves(tile):
    return jnp.concatenate([tile[:, DH:], tile[:, :DH]], axis=1)


def lanes_below(shape, at=DH):
    return lax.broadcasted_iota(jnp.int32, shape, len(shape) - 1) < at


def key_side(qk, mask):
    swapped = swap_halves(qk)
    return jnp.where(lanes_below(qk.shape), swapped, mask), swapped


def query_side(qk):
    lane = lax.broadcasted_iota(jnp.int32, qk.shape, 1)
    return jnp.where(lane < DH, qk, jnp.where(lane == DH, 1.0, 0.0).astype(qk.dtype))


def probabilities(keys, queries, tiles, q0, length, width):
    scores = dot(keys, queries, NT)
    blocks = []
    for kb in range(length // TILE):
        deltas = [max(-2, min(2, kb - (q0 + qi))) + 2 for qi in range(width // TILE)]
        bias = tiles[deltas[0]] if len(deltas) == 1 else jnp.concatenate([tiles[d] for d in deltas], axis=1)
        blocks.append(scores[kb * TILE : (kb + 1) * TILE] + bias)
    top = blocks[0]
    for block in blocks[1:]:
        top = jnp.maximum(top, block)
    top = jnp.max(top, axis=0, keepdims=True)
    blocks = [jnp.exp(block - top) for block in blocks]
    total = blocks[0]
    for block in blocks[1:]:
        total = total + block
    inverse = 1.0 / jnp.sum(total, axis=0, keepdims=True)
    return [block * inverse for block in blocks]


def join(blocks, axis=0):
    return blocks[0] if len(blocks) == 1 else jnp.concatenate(blocks, axis=axis)


def attend_group(packed, mask_ref, rows, context):
    tiles = [bias_tiles(rows[h : h + 1, :]) for h in range(3)]
    for offset, length in SPANS:
        span = pl.ds(offset, length)
        mask = mask_ref[span, :]
        keys = [key_side(packed[span, h * TILE : (h + 1) * TILE], mask)[0] for h in range(3)]
        values = [packed[span, (3 + t) * TILE : (4 + t) * TILE].T for t in range(2)]
        width = min(length, 256)
        for q0 in range(0, length, width):
            here = pl.ds(offset + q0, width)
            outs = []
            for h in range(3):
                queries = query_side(packed[here, h * TILE : (h + 1) * TILE])
                probs = probabilities(keys[h], queries, tiles[h], q0 // TILE, length, width)
                probs = join([block.astype(jnp.bfloat16) for block in probs])
                full = dot(values[h // 2], probs)
                outs.append(full[(h % 2) * DH : (h % 2 + 1) * DH])
            context[here, :TILE] = jnp.concatenate(outs[:2], axis=0).T.astype(jnp.bfloat16)
            last = jnp.concatenate([outs[2], jnp.zeros_like(outs[2])], axis=0)
            context[here, TILE:] = last.T.astype(jnp.bfloat16)


def attend_group_back(packed, mask_ref, rows, grad_context, grad_packed, sums):
    far_shape = (TILE, TILE)
    tiles = [bias_tiles(rows[h : h + 1, :]) for h in range(3)]
    near = [[None] * 3 for _ in range(3)]
    far = [[jnp.zeros(far_shape, jnp.float32)] * 2 for _ in range(3)]
    for offset, length in SPANS:
        span = pl.ds(offset, length)
        mask = mask_ref[span, :]
        width = min(length, 256)
        grad_values = [None, None]
        for h in range(3):
            at = pl.ds(h * TILE, TILE)
            qk = packed[span, at]
            low = lanes_below(qk.shape)
            keys, swapped = key_side(qk, mask)
            upper_queries = jnp.where(low, jnp.zeros_like(qk), swapped)
            plain_keys = jnp.where(low, swapped, jnp.zeros_like(qk)).T
            values = packed[span, (3 + h // 2) * TILE : (4 + h // 2) * TILE]
            grad_keys = None
            grad_queries = []
            for q0 in range(0, length, width):
                here = pl.ds(offset + q0, width)
                probs = probabilities(keys, query_side(packed[here, at]), tiles[h], q0 // TILE, length, width)
                g_tile = grad_context[here, (h // 2) * TILE : (h // 2 + 1) * TILE]
                own = lanes_below(g_tile.shape) == (h % 2 == 0)
                g_tile = jnp.where(own, g_tile, jnp.zeros_like(g_tile))
                g_probs = dot(values, g_tile, NT)
                g_blocks = [g_probs[kb * TILE : (kb + 1) * TILE] for kb in range(length // TILE)]
                total = probs[0] * g_blocks[0]
                for kb in range(1, length // TILE):
                    total = total + probs[kb] * g_blocks[kb]
                centre = jnp.sum(total, axis=0, keepdims=True)
                low_probs = join([block.astype(jnp.bfloat16) for block in probs])
                g_scores = [(a * (g - centre)).astype(jnp.bfloat16) for a, g in zip(probs, g_blocks)]
                for kb, block in enumerate(g_scores):
                    wide = block.astype(jnp.float32)
                    for qi in range(width // TILE):
                        piece = wide[:, qi * TILE : (qi + 1) * TILE]
                        delta = kb - (q0 // TILE + qi)
                        if abs(delta) <= 1:
                            held = near[h][delta + 1]
                            near[h][delta + 1] = piece if held is None else held + piece
                        else:
                            side = 0 if delta < 0 else 1
                            far[h][side] = far[h][side] + piece
                g_scores = join(g_scores)
                g_v = dot(low_probs, g_tile)
                grad_values[h // 2] = g_v if grad_values[h // 2] is None else grad_values[h // 2] + g_v
                g_k = dot(g_scores, upper_queries[q0 : q0 + width])
                grad_keys = g_k if grad_keys is None else grad_keys + g_k
                grad_queries.append(dot(plain_keys, g_scores).T)
            grad_packed[span, at] = (join(grad_queries) + grad_keys).astype(jnp.bfloat16)
        for t in range(2):
            grad_packed[span, (3 + t) * TILE : (4 + t) * TILE] = grad_values[t].astype(jnp.bfloat16)
    for h in range(3):
        sums[h : h + 1, :512] = diagonal_sums(near[h])
        for side in range(2):
            sums[h : h + 1, 512 + side * TILE : 640 + side * TILE] = jnp.sum(far[h][side], axis=0, keepdims=True)


def attention_kernel(x_ref, gain, w_ref, mask, rows, normed_out, packed, context):
    @pl.when(pl.program_id(0) == 0)
    def _():
        x = x_ref[...].astype(jnp.float32)
        scale = lax.rsqrt(jnp.mean(x * x, axis=-1, keepdims=True) + NORM_EPS)
        normed_out[...] = (x * scale * gain[...]).astype(jnp.bfloat16)

    packed[0] = dot(normed_out[...], w_ref[0]).astype(jnp.bfloat16)
    attend_group(packed.at[0], mask, rows[0], context.at[0])


def attention(x, gain, w, mask, rows):
    n = x.shape[0]
    bf = jnp.bfloat16
    return pl.pallas_call(
        attention_kernel,
        grid=(4,),
        out_shape=[
            jax.ShapeDtypeStruct((n, D), bf),
            jax.ShapeDtypeStruct((4, n, QKV_PAD), bf),
            jax.ShapeDtypeStruct((4, n, CTX_PAD), bf),
        ],
        in_specs=[
            pl.BlockSpec((n, D), lambda i: (0, 0)),
            pl.BlockSpec((1, D), lambda i: (0, 0)),
            pl.BlockSpec((1, D, QKV_PAD), lambda i: (i, 0, 0)),
            pl.BlockSpec((n, TILE), lambda i: (0, 0)),
            pl.BlockSpec((1, 3, 512), lambda i: (i, 0, 0)),
        ],
        out_specs=[
            pl.BlockSpec((n, D), lambda i: (0, 0)),
            pl.BlockSpec((1, n, QKV_PAD), lambda i: (i, 0, 0)),
            pl.BlockSpec((1, n, CTX_PAD), lambda i: (i, 0, 0)),
        ],
        compiler_params=pltpu.CompilerParams(vmem_limit_bytes=56 * 2**20),
        name="attention",
    )(x, gain, w, mask, rows)


def attention_back_kernel(packed, grad_context, mask, rows, grad_packed, sums):
    attend_group_back(packed.at[0], mask, rows[0], grad_context.at[0], grad_packed.at[0], sums.at[0])


def attention_back(packed, grad_context, mask, rows):
    n = packed.shape[1]
    return pl.pallas_call(
        attention_back_kernel,
        grid=(4,),
        out_shape=[
            jax.ShapeDtypeStruct((4, n, QKV_PAD), jnp.bfloat16),
            jax.ShapeDtypeStruct((4, 3, 768), jnp.float32),
        ],
        in_specs=[
            pl.BlockSpec((1, n, QKV_PAD), lambda i: (i, 0, 0)),
            pl.BlockSpec((1, n, CTX_PAD), lambda i: (i, 0, 0)),
            pl.BlockSpec((n, TILE), lambda i: (0, 0)),
            pl.BlockSpec((1, 3, 512), lambda i: (i, 0, 0)),
        ],
        out_specs=[
            pl.BlockSpec((1, n, QKV_PAD), lambda i: (i, 0, 0)),
            pl.BlockSpec((1, 3, 768), lambda i: (i, 0, 0)),
        ],
        compiler_params=pltpu.CompilerParams(vmem_limit_bytes=56 * 2**20),
        name="attention_back",
    )(packed, grad_context, mask, rows)


def head_columns(w):
    qk = w[:, :, : 2 * DH].reshape(w.shape[0], 6 * DH)
    v = w[:, :, 2 * DH :].reshape(w.shape[0], 3 * DH)
    return jnp.pad(jnp.concatenate([qk, v], axis=1), ((0, 0), (0, QKV_PAD - 9 * DH)))


def from_head_columns(g):
    qk = g[:, : 6 * DH].reshape(g.shape[0], 3, 2 * DH)
    v = g[:, 6 * DH : 9 * DH].reshape(g.shape[0], 3, DH)
    return jnp.concatenate([qk, v], axis=2)


def key_mask(live):
    lane = jnp.arange(TILE)[None, :]
    return jnp.where((lane == DH) & ~live[:, None], MASK_LOW, 0.0).astype(jnp.bfloat16)


def round_up(n, m):
    return -(-n // m) * m


def pad_rows(a, rows):
    return jnp.pad(a, ((0, rows - a.shape[0]), (0, 0)))


HEADS = 12


def local(
    tokens,
    lengths,
    cotangent,
    w_qkv,
    w_o,
    w_in,
    w_out,
    gain_attn,
    gain_ffn,
    pos_table,
    phm_rules,
    down_left,
    down_right,
    up_left,
    up_right,
):
    dp_count, mp_count = lax.axis_size("dp"), lax.axis_size("mp")
    depth = dp_count // 2
    bits = dp_count.bit_length() - 1
    devices = dp_count * mp_count
    member = lax.axis_index("mp")
    tok_rows = tokens.shape[0]
    seg_count = tok_rows // SEG
    o_rows, in_rows, q_rows = w_o.shape[0], w_in.shape[1], w_qkv.shape[0]
    bf = jnp.bfloat16
    wq = pad_rows(head_columns(w_qkv.astype(bf)), round_up(q_rows, 16))
    wo = pad_rows(w_o.astype(bf), round_up(o_rows, 16))
    wi = pad_rows(w_in.astype(bf).T, round_up(in_rows, 16))
    wu = pad_rows(w_out.astype(bf), round_up(in_rows, 16))
    tok_s, cot_s, gq, go, gi, gu = gather_all(
        depth, tokens.reshape(seg_count, SEG, D), cotangent.reshape(seg_count, SEG, D), (wq, wo, wi, wu)
    )

    def plain(g, rows):
        return g.reshape(devices, g.shape[-2], D)[:, :rows].reshape(devices * rows, D)

    dense_o, dense_in_t, dense_out = plain(go, o_rows), plain(gi, in_rows), plain(gu, in_rows)
    qkv_full = gq.reshape(mp_count, dp_count, wq.shape[0], QKV_PAD)[:, :, :q_rows].reshape(mp_count, D, QKV_PAD)
    tokens_s = tok_s.reshape(tok_rows, D)
    own_lengths = jnp.stack([
        lengths[member], lengths[4 + member // 2 + 2 * (member % 2)], lengths[8 + member], lengths[12 + member]
    ])
    shapes = ((LEN_LONG, 1), (LEN_MID, 1), (LEN_SHORT, 2))
    pieces = []
    first = 0
    for length, seqs in shapes:
        spots = jnp.arange(length, dtype=jnp.int32)
        pieces.append((spots[None, :] < own_lengths[first : first + seqs, None]).reshape(-1))
        first += seqs
    live = jnp.concatenate(pieces)
    x_float = tokens_s.astype(jnp.float32)
    mask = key_mask(live)
    rows = offset_row(pos_table).reshape(mp_count, 3, 512)
    normed_attn, packed, context = attention(tokens_s, gain_attn[None], qkv_full, mask, rows)
    context_rows = context[:, :, : 3 * DH].transpose(1, 0, 2).reshape(tok_rows, D)
    midway = x_float + jnp.dot(context_rows, dense_o, preferred_element_type=jnp.float32)
    normed_ffn = normed(midway, gain_ffn).astype(bf)
    ffn_pre = jnp.dot(normed_ffn, dense_in_t.T, preferred_element_type=jnp.float32)
    ffn_act = gelu_exact(ffn_pre).astype(bf)
    ffn_out = jnp.dot(ffn_act, dense_out, preferred_element_type=jnp.float32)
    ffn_low = ffn_out.astype(bf)
    w_down, w_up = adapter_weights(phm_rules, down_left, down_right, up_left, up_right)
    down_low = w_down.astype(bf)
    up_low = w_up.astype(bf)
    squeezed = jnp.dot(ffn_low, down_low, preferred_element_type=jnp.float32)
    lifted = gelu_exact(squeezed).astype(bf)
    result = (midway + ffn_out + jnp.dot(lifted, up_low, preferred_element_type=jnp.float32)).astype(bf)
    grad_out = cot_s.reshape(tok_rows, D).astype(jnp.float32) * live[:, None].astype(jnp.float32)
    grad_out_low = grad_out.astype(bf)
    grad_w_up = jnp.dot(lifted.T, grad_out_low, preferred_element_type=jnp.float32)
    _, gelu_back_sq = jax.vjp(gelu_exact, squeezed)
    grad_sq = gelu_back_sq(jnp.dot(grad_out_low, up_low.T, preferred_element_type=jnp.float32))[0].astype(bf)
    grad_w_down = jnp.dot(ffn_low.T, grad_sq, preferred_element_type=jnp.float32)
    grad_ffn = (grad_out + jnp.dot(grad_sq, down_low.T, preferred_element_type=jnp.float32)).astype(bf)
    grad_w_out = jnp.dot(ffn_act.T, grad_ffn, preferred_element_type=jnp.float32).astype(bf)
    _, gelu_back_pre = jax.vjp(gelu_exact, ffn_pre)
    grad_pre = gelu_back_pre(jnp.dot(grad_ffn, dense_out.T, preferred_element_type=jnp.float32))[0].astype(bf)
    grad_w_in = jnp.dot(grad_pre.T, normed_ffn, preferred_element_type=jnp.float32).astype(bf)
    _, norm_back_ffn = jax.vjp(normed, midway, gain_ffn)
    grad_mid_part, grad_gain_ffn = norm_back_ffn(jnp.dot(grad_pre, dense_in_t, preferred_element_type=jnp.float32))
    grad_mid = grad_out + grad_mid_part
    grad_mid_low = grad_mid.astype(bf)
    grad_w_o = jnp.dot(context_rows.T, grad_mid_low, preferred_element_type=jnp.float32).astype(bf)
    grad_context = jnp.dot(grad_mid_low, dense_o.T, preferred_element_type=jnp.float32).astype(bf)
    grad_context = grad_context.reshape(tok_rows, mp_count, 3 * DH).transpose(1, 0, 2)
    grad_context = jnp.pad(grad_context, ((0, 0), (0, 0), (0, CTX_PAD - 3 * DH)))
    packed_grads, sums = attention_back(packed, grad_context, mask, rows)
    table_grad = jnp.einsum("hr,rb->bh", sums.reshape(HEADS, 768), table_onehot(), precision=FULL_PRECISION)
    grad_w_qkv = jnp.einsum("td,mtc->mdc", normed_attn, packed_grads, preferred_element_type=jnp.float32).astype(bf)
    grad_n1 = jnp.einsum("mtc,mdc->td", packed_grads, qkv_full, preferred_element_type=jnp.float32)
    _, norm_back_attn = jax.vjp(normed, x_float, gain_attn)
    grad_x_part, grad_gain_attn = norm_back_attn(grad_n1)
    grad_tokens = (grad_mid + grad_x_part).astype(bf)
    _, adapter_back = jax.vjp(adapter_weights, phm_rules, down_left, down_right, up_left, up_right)
    small_list = (grad_gain_attn, grad_gain_ffn, table_grad) + adapter_back((grad_w_down, grad_w_up))
    flat = jnp.concatenate([s.reshape(-1) for s in small_list])
    small_rows = round_up(-(-flat.size // 128), 8)
    small = jnp.pad(flat, (0, small_rows * 128 - flat.size)).reshape(small_rows, 128)

    def slots(g, rows):
        padded = jnp.pad(g.reshape(devices, rows, D), ((0, 0), (0, round_up(rows, 16) - rows), (0, 0)))
        return padded.reshape(depth, 2, 2, 2, padded.shape[1], D)

    part_q = grad_w_qkv.reshape(mp_count, dp_count, q_rows, QKV_PAD)
    part_q = jnp.pad(part_q, ((0, 0), (0, 0), (0, wq.shape[0] - q_rows), (0, 0)))
    part_q = part_q.reshape(2, 2, depth, 2, wq.shape[0], QKV_PAD)
    oq, oo, oi, ou, summed, out, gtok = scatter_all(
        depth,
        bits,
        (part_q, slots(grad_w_o, o_rows), slots(grad_w_in, in_rows), slots(grad_w_out, in_rows)),
        small,
        result.reshape(seg_count, SEG, D),
        grad_tokens.reshape(seg_count, SEG, D),
    )
    smalls = []
    flat = summed.reshape(-1)
    first = 0
    for s in small_list:
        smalls.append(flat[first : first + s.size].reshape(s.shape))
        first += s.size
    return (
        out.reshape(tok_rows, D),
        gtok.reshape(tok_rows, D),
        from_head_columns(oq[:q_rows]),
        oo[:o_rows],
        oi[:in_rows].T,
        ou[:in_rows],
        *smalls,
    )


def solution(mesh):
    return jax.shard_map(
        local,
        mesh=mesh,
        in_specs=(
            P(("dp", "mp"), None),
            P("dp"),
            P(("dp", "mp"), None),
            P("dp", "mp", None),
            P(("dp", "mp"), None),
            P(None, ("dp", "mp")),
            P(("dp", "mp"), None),
            P(),
            P(),
            P(),
            P(),
            P(),
            P(),
            P(),
            P(),
        ),
        out_specs=(
            P(("dp", "mp"), None),
            P(("dp", "mp"), None),
            P("dp", "mp", None),
            P(("dp", "mp"), None),
            P(None, ("dp", "mp")),
            P(("dp", "mp"), None),
            P(),
            P(),
            P(),
            P(),
            P(),
            P(),
            P(),
            P(),
        ),
        check_vma=False,
    )
```

```python
import functools
import itertools

import jax
import jax.experimental.pallas as pl
import jax.experimental.pallas.tpu as pltpu
import jax.numpy as jnp
import numpy as np
from jax import lax
from jax.sharding import PartitionSpec as P

D = 768
DH = 64
NB = 32
MAXDIST = 128
ADAPT = 48
LEN_LONG = 512
LEN_MID = 256
LEN_SHORT = 128
SEG = 128


NORM_EPS = 1e-06
FULL_PRECISION = lax.Precision.HIGHEST


def rel_buckets(length):
    offsets = np.arange(-(length - 1), length)
    half_count = NB // 2
    exact_count = half_count // 2
    upward = (offsets > 0).astype(np.int64) * half_count
    distance = np.abs(offsets)
    scaled = (
        np.log(np.maximum(distance, 1) / exact_count)
        / np.log(MAXDIST / exact_count)
        * (half_count - exact_count)
    )
    far_bucket = np.minimum(
        exact_count + np.floor(np.maximum(scaled, 0.0)).astype(np.int64), half_count - 1
    )
    return upward + np.where(distance < exact_count, distance, far_bucket)


def normed(values, gain):
    return values * lax.rsqrt(jnp.mean(values * values, axis=-1, keepdims=True) + NORM_EPS) * gain


def gelu_exact(values):
    return jax.nn.gelu(values, approximate=False)


def adapter_weights(phm_rules, down_left, down_right, up_left, up_right):
    w_down = jnp.einsum(
        "iab,ip,iq->apbq", phm_rules, down_left, down_right, precision=FULL_PRECISION
    ).reshape(D, ADAPT)
    w_up = jnp.einsum(
        "iab,ip,iq->apbq", phm_rules, up_left, up_right, precision=FULL_PRECISION
    ).reshape(ADAPT, D)
    return (w_down, w_up)


MESH = pl.DeviceIdType.MESH


class Place:
    def __init__(self, depth):
        d, m = lax.axis_index("dp"), lax.axis_index("mp")
        self.depth = depth
        self.d, self.m = d, m
        self.z, self.x, self.y, self.c = d // 2, d % 2, m // 2, m % 2
        dx, dy, c = 1 - 2 * self.x, 2 - 4 * self.y, self.c
        self.sib = (d, m + 1 - 2 * c)
        self.right, self.left = (d + 2, m), (d - 2, m)
        self.mp_peer = ((d, m + 1 - 2 * c), (d, m + dy), (d, 3 - m))
        self.xn, self.yn = (d + dx, m), (d, m + dy)
        self.a_nbr = (d + (1 - c) * dx, m + c * dy)
        self.b_nbr = (d + c * dx, m + (1 - c) * dy)
        self.a = self.x + c * (self.y - self.x)
        self.b = self.y + c * (self.x - self.y)

    def by_core(self, run):
        for core in (0, 1):
            pl.when(self.c == core)(functools.partial(run, core))

    def flip(self, bit):
        step = 1 << bit
        return (self.d + step * (1 - 2 * ((self.d // step) % 2)), self.m)

    def barrier(self, bits):
        sem = pltpu.get_barrier_semaphore()

        def greet(dev):
            pl.semaphore_signal(sem, 1, device_id=dev, device_id_type=MESH)

        pals = [*self.mp_peer, self.xn] + [self.flip(bit) for bit in range(2, bits)]
        for dev in pals:
            greet(dev)
        pl.when(self.z > 0)(lambda: greet(self.left))
        pl.when(self.z < self.depth - 1)(lambda: greet(self.right))
        ends = jnp.minimum(self.z, 1) + jnp.minimum(self.depth - 1 - self.z, 1)
        pl.semaphore_wait(sem, len(pals) + ends)


def remote(src, dst, send, recv, dev):
    return pltpu.make_async_remote_copy(
        src_ref=src, dst_ref=dst, send_sem=send, recv_sem=recv, device_id=dev, device_id_type=MESH
    )


def slot_of(buf, by_head, p):
    return buf.at[p.y, p.c, p.z, p.x] if by_head else buf.at[p.z, p.x, p.y, p.c]


def pair_of(buf, by_head, core, b, z):
    if by_head:
        return buf.at[b, 0, z] if core == 0 else buf.at[:, 1, z, b]
    return buf.at[z, :, b, 0] if core == 0 else buf.at[z, b, :, 1]


class Gather:
    def __init__(self, p, by_head, shard, buf, send, recv, own):
        self.p, self.by_head, self.shard, self.buf = p, by_head, shard, buf
        self.send, self.recv, self.own = send, recv, own
        n = p.depth
        self.first = remote(shard, slot_of(buf, by_head, p), send.at[5 * n], recv.at[4 * n], p.a_nbr)
        self.keep = pltpu.make_async_copy(shard, slot_of(buf, by_head, p), own)

    @staticmethod
    def sems(n):
        return [
            pltpu.SemaphoreType.DMA((5 * n + 1,)),
            pltpu.SemaphoreType.DMA((4 * n + 1,)),
            pltpu.SemaphoreType.DMA,
        ]

    def _copy(self, core, b, z, kind):
        p, n = self.p, self.p.depth
        ref = pair_of(self.buf, self.by_head, core, b, z)
        if kind == "right":
            return remote(ref, ref, self.send.at[z], self.recv.at[z], p.right)
        if kind == "left":
            return remote(ref, ref, self.send.at[n + z], self.recv.at[z], p.left)
        return remote(ref, ref, self.send.at[2 * n + z], self.recv.at[n + z], p.b_nbr)

    def _sib(self, core, b, z):
        n = self.p.depth
        ref = pair_of(self.buf, self.by_head, core, b, z)
        return remote(ref, ref, self.send.at[3 * n + b * n + z], self.recv.at[2 * n + b * n + z], self.p.sib)

    def start(self):
        self.keep.start()
        self.first.start()

    def _spread(self, core, z, right, left):
        p = self.p
        if right:
            pl.when(p.z < p.depth - 1)(lambda: self._copy(core, p.b, z, "right").start())
        if left:
            pl.when(p.z > 0)(lambda: self._copy(core, p.b, z, "left").start())
        self._copy(core, p.b, z, "b").start()
        self._sib(core, p.b, z).start()

    def along(self, k):
        p = self.p
        if isinstance(k, int) and k == 0:
            self.keep.wait()
            self.first.wait_recv()
            p.by_core(lambda core: self._spread(core, p.z, True, True))
            return

        def from_left(core):
            self._copy(core, p.b, p.z - k, "right").wait_recv()
            self._spread(core, p.z - k, True, False)

        def from_right(core):
            self._copy(core, p.b, p.z + k, "left").wait_recv()
            self._spread(core, p.z + k, False, True)

        pl.when(p.z - k >= 0)(lambda: p.by_core(from_left))
        pl.when(p.z + k < p.depth)(lambda: p.by_core(from_right))

    def across(self, k):
        p = self.p

        def one(z, core):
            self._copy(core, 1 - p.b, z, "b").wait_recv()
            self._sib(core, 1 - p.b, z).start()

        pl.when(p.z - k >= 0)(lambda: p.by_core(lambda core: one(p.z - k, core)))
        if not (isinstance(k, int) and k == 0):
            pl.when(p.z + k < p.depth)(lambda: p.by_core(lambda core: one(p.z + k, core)))

    def finish(self):
        p, n = self.p, self.p.depth

        def each(z, carry):
            def one(core):
                for b in (0, 1):
                    self._sib(1 - core, b, z).wait_recv()

            p.by_core(one)
            return carry

        lax.fori_loop(0, n, each, 0)

    def drain(self):
        p, n = self.p, self.p.depth
        self.first.wait_send()

        def each(z, carry):
            def one(core):
                pl.when(jnp.logical_and(p.z < n - 1, z <= p.z))(
                    lambda: self._copy(core, p.b, z, "right").wait_send()
                )
                pl.when(jnp.logical_and(p.z > 0, z >= p.z))(
                    lambda: self._copy(core, p.b, z, "left").wait_send()
                )
                self._copy(core, p.b, z, "b").wait_send()
                for b in (0, 1):
                    self._sib(core, b, z).wait_send()

            p.by_core(one)
            return carry

        lax.fori_loop(0, n, each, 0)


class Exchange:
    def __init__(self, p, src, dst, send, recv, own):
        m = p.m
        c, other = m % 2, 1 - m % 2
        self.local = [
            pltpu.make_async_copy(src.at[m], dst.at[m], own.at[0]),
            pltpu.make_async_copy(src.at[4 + c], dst.at[4 + c], own.at[1]),
            pltpu.make_async_copy(src.at[pl.ds(6, 2)], dst.at[pl.ds(6, 2)], own.at[2]),
        ]
        self.out = [
            remote(src.at[dev[1]], dst.at[m], send.at[j], recv.at[j], dev)
            for j, dev in enumerate(p.mp_peer)
        ] + [remote(src.at[4 + other], dst.at[4 + c], send.at[3], recv.at[3], p.sib)]

    @staticmethod
    def sems():
        return [
            pltpu.SemaphoreType.DMA((4,)),
            pltpu.SemaphoreType.DMA((4,)),
            pltpu.SemaphoreType.DMA((3,)),
        ]

    def start(self):
        for copy in self.out + self.local:
            copy.start()

    def finish(self):
        for copy in self.local:
            copy.wait()
        for copy in self.out:
            copy.wait_recv()

    def drain(self):
        for copy in self.out:
            copy.wait_send()


def add_rows(dst, src, rows):
    step = 32 if rows % 32 == 0 else 16

    def one(i, carry):
        at = pl.ds(pl.multiple_of(i * step, step), step)
        total = dst[at, :].astype(jnp.float32) + src[at, :].astype(jnp.float32)
        dst[at, :] = total.astype(dst.dtype)
        return carry

    lax.fori_loop(0, rows // step, one, 0)


class Scatter:
    def __init__(self, p, by_head, part, total, half, quarter, arrive, last, send, recv, mine=None, mine_sem=None):
        self.p, self.by_head, self.part, self.total = p, by_head, part, total
        self.mine, self.mine_sem = mine, mine_sem
        self.half, self.quarter, self.arrive, self.last = half, quarter, arrive, last
        self.send, self.recv = send, recv
        self.rows = part.shape[-2]

    @staticmethod
    def scratch(n, rows, cols, dtype=jnp.bfloat16):
        return [
            pltpu.VMEM((n, 2, 2, rows, cols), dtype),
            pltpu.VMEM((n, 2, rows, cols), dtype),
            pltpu.VMEM((n + 1, 2, rows, cols), dtype),
            pltpu.VMEM((rows, cols), dtype),
            pltpu.SemaphoreType.DMA((3 * n + 1,)),
            pltpu.SemaphoreType.DMA((3 * n + 2,)),
        ]

    def order(self, k):
        n = self.p.depth
        base = k // 2 if k % 2 == 0 else n - 1 - k // 2
        near = 1 - jnp.minimum(self.p.z // max(n // 2, 1), 1)
        return base + near * (n - 1 - 2 * base)

    def _region(self, core, z):
        return self.part.at[:, core, z] if self.by_head else self.part.at[z, :, :, core]

    def _half_pair(self, core, b, z):
        over_first = (core == 0) != self.by_head
        return self.half.at[z, :, b] if over_first else self.half.at[z, b]

    def _sib(self, core, z):
        return remote(
            self._region(1 - core, z), self.half.at[z], self.send.at[z], self.recv.at[z], self.p.sib
        )

    def _b(self, core, z):
        n, p = self.p.depth, self.p
        return remote(
            self._half_pair(core, 1 - p.b, z), self.quarter.at[z], self.send.at[n + z], self.recv.at[n + z], p.b_nbr
        )

    def _right(self, z):
        n, p = self.p.depth, self.p
        return remote(
            self.quarter.at[z], self.arrive.at[z], self.send.at[2 * n + z], self.recv.at[2 * n + z], p.right
        )

    def _left(self, z, goal):
        n, p = self.p.depth, self.p
        return remote(
            self.quarter.at[z], self.arrive.at[goal], self.send.at[2 * n + z], self.recv.at[2 * n + goal], p.left
        )

    def _a(self):
        n, p = self.p.depth, self.p
        return remote(
            self.quarter.at[p.z, 1 - p.a], self.last, self.send.at[3 * n], self.recv.at[3 * n + 1], p.a_nbr
        )

    def _keep(self, core, z):
        return pltpu.make_async_copy(self._region(core, z), self.mine.at[z], self.mine_sem.at[z])

    def start(self, k):
        z = self.order(k)

        def one(core):
            self._sib(core, z).start()
            if self.mine is not None:
                self._keep(core, z).start()

        self.p.by_core(one)

    def to_half(self, k):
        z = self.order(k)

        def one(core):
            self._sib(core, z).wait_recv()
            region = self._region(core, z)
            if self.mine is not None:
                self._keep(core, z).wait()
                region = self.mine.at[z]
            for i in (0, 1):
                for j in (0, 1):
                    add_rows(self.half.at[z, i, j], region.at[i, j], self.rows)
            self._b(core, z).start()

        self.p.by_core(one)

    def to_quarter(self, k):
        z = self.order(k)

        def one(core):
            self._b(core, z).wait_recv()
            for i in (0, 1):
                add_rows(self.quarter.at[z, i], self._half_pair(core, self.p.b, z).at[i], self.rows)

        self.p.by_core(one)

    def _take(self, z, slot):
        for i in (0, 1):
            add_rows(self.quarter.at[z, i], self.arrive.at[slot, i], self.rows)

    def _send_left(self, z):
        p, n = self.p, self.p.depth
        pl.when(z == p.z - 1)(lambda: self._left(z, n).start())
        pl.when(z < p.z - 1)(lambda: self._left(z, z).start())

    def origin(self, k):
        p, n = self.p, self.p.depth
        z = self.order(k)
        pl.when(jnp.logical_and(p.z == 0, z > p.z))(lambda: self._right(z).start())
        pl.when(jnp.logical_and(p.z == n - 1, z < p.z))(lambda: self._send_left(z))

    def forward(self, k):
        p, n = self.p, self.p.depth
        z = self.order(k)

        def rightward():
            self._right(z).wait_recv()
            self._take(z, z)
            self._right(z).start()

        def leftward():
            self._left(z, z).wait_recv()
            self._take(z, z)
            self._send_left(z)

        pl.when(jnp.logical_and(p.z > 0, z > p.z))(rightward)
        pl.when(jnp.logical_and(p.z < n - 1, z < p.z))(leftward)

    def collect(self):
        p, n = self.p, self.p.depth

        def from_left():
            self._right(p.z).wait_recv()
            self._take(p.z, p.z)

        def from_right():
            self._left(p.z, n).wait_recv()
            self._take(p.z, n)

        pl.when(p.z > 0)(from_left)
        pl.when(p.z < n - 1)(from_right)
        self._a().start()

    def finish(self):
        p = self.p
        self._a().wait_recv()
        self.total[...] = self.quarter[p.z, p.a].astype(jnp.float32) + self.last[...].astype(jnp.float32)

    def drain(self):
        p, n = self.p, self.p.depth
        self._a().wait_send()

        def each(z, carry):
            def one(core):
                self._sib(core, z).wait_send()
                self._b(core, z).wait_send()

            p.by_core(one)
            pl.when(z != p.z)(lambda: self._right(z).wait_send())
            return carry

        lax.fori_loop(0, n, each, 0)

    def steps(self):
        n = self.p.depth
        todo = [lambda: [self.start(k) for k in range(n)]]
        todo += [functools.partial(self.to_half, k) for k in range(n)]
        for k in range(n):
            todo.append(functools.partial(lambda k: (self.to_quarter(k), self.origin(k), self.forward(k)), k))
        return todo


class Sum:
    def __init__(self, p, bits, value, slots, send, recv):
        self.p, self.bits, self.value, self.slots = p, bits, value, slots
        self.send, self.recv = send, recv

    @staticmethod
    def scratch(bits, rows):
        return [
            pltpu.VMEM((2 * (bits + 2), rows, 128), jnp.float32),
            pltpu.SemaphoreType.DMA((bits + 2,)),
            pltpu.SemaphoreType.DMA((bits + 2,)),
        ]

    def _copy(self, s):
        p = self.p
        dev = (p.sib, p.yn, *[p.flip(bit) for bit in range(self.bits)])[s]
        return remote(self.slots.at[2 * s], self.slots.at[2 * s + 1], self.send.at[s], self.recv.at[s], dev)

    def steps(self):
        def begin():
            self.slots[0] = self.value[...]
            self._copy(0).start()

        def one(s):
            self._copy(s).wait_recv()
            total = self.slots[2 * s] + self.slots[2 * s + 1]
            if s == self.bits + 1:
                self.value[...] = total
            else:
                self.slots[2 * s + 2] = total
                self._copy(s + 1).start()

        return [begin] + [functools.partial(one, s) for s in range(self.bits + 2)]

    def drain(self):
        for s in range(self.bits + 2):
            self._copy(s).wait_send()


def in_waves(lists, lag):
    for t in range(max(len(todo) + lag * r for r, todo in enumerate(lists))):
        for r, todo in enumerate(lists):
            if 0 <= t - lag * r < len(todo):
                todo[t - lag * r]()


def gather_kernel(p_depth, tok, cot, wq, wo, wi, wu, tok_s, cot_s, gq, go, gi, gu, *sems):
    p = Place(p_depth)
    n = p_depth
    arrays = []
    for i, (by_head, shard, buf) in enumerate(
        ((True, wq, gq), (False, wo, go), (False, wi, gi), (False, wu, gu))
    ):
        arrays.append(Gather(p, by_head, shard, buf, *sems[3 * i : 3 * i + 3]))
    rows = [Exchange(p, tok, tok_s, *sems[12:15]), Exchange(p, cot, cot_s, *sems[15:18])]
    p.barrier(0)
    for g in arrays:
        g.start()
    rows[0].start()
    if n <= 8:
        for k in range(n):
            for g in arrays:
                g.along(k)
            if k > 0:
                for g in arrays:
                    g.across(k - 1)
            if k == 1:
                rows[1].start()
        for g in arrays:
            g.across(n - 1)
    else:
        for g in arrays:
            g.along(0)
            lax.fori_loop(1, n, lambda k, carry: (g.along(k), carry)[1], 0)
        rows[1].start()
        for g in arrays:
            g.across(0)
            lax.fori_loop(1, n, lambda k, carry: (g.across(k), carry)[1], 0)
    for g in arrays + rows:
        g.finish()
    for g in arrays + rows:
        g.drain()


def gather_all(depth, tok, cot, shards):
    hbm = pl.BlockSpec(memory_space=pl.ANY)
    outs = [jax.ShapeDtypeStruct(tok.shape, tok.dtype)] * 2
    for i, s in enumerate(shards):
        lead = (2, 2, depth, 2) if i == 0 else (depth, 2, 2, 2)
        outs.append(jax.ShapeDtypeStruct(lead + s.shape, s.dtype))
    sems = Gather.sems(depth) * 4 + Exchange.sems() * 2
    return pl.pallas_call(
        functools.partial(gather_kernel, depth),
        out_shape=outs,
        in_specs=[hbm] * 6,
        out_specs=[hbm] * 6,
        scratch_shapes=sems,
        compiler_params=pltpu.CompilerParams(collective_id=0, has_side_effects=True),
        name="gather",
    )(tok, cot, *shards)


def scatter_kernel(depth, bits, pq, po, pi, pu, small, out_s, gtok_s, oq, oo, oi, ou, small_o, out, gtok, *scr):
    p = Place(depth)
    arrays = []
    for i, (by_head, part, total) in enumerate(
        ((False, pu, ou), (False, pi, oi), (False, po, oo), (True, pq, oq))
    ):
        arrays.append(Scatter(p, by_head, part, total, *scr[6 * i : 6 * i + 6]))
    rows = [Exchange(p, out_s, out, *scr[24:27]), Exchange(p, gtok_s, gtok, *scr[27:30])]
    small_o[...] = small[...]
    sums = Sum(p, bits, small_o, *scr[30:33])
    p.barrier(bits)
    rows[0].start()
    in_waves([g.steps() for g in arrays], min(depth, 4))
    rows[1].start()
    close(arrays, sums)
    for r in rows:
        r.finish()
    for g in arrays + rows + [sums]:
        g.drain()


def close(arrays, sums):
    closing = [g.collect for g in arrays] + [g.finish for g in arrays]
    for step in itertools.chain(*itertools.zip_longest(sums.steps(), closing)):
        if step is not None:
            step()


def scatter_all(depth, bits, parts, small, out_s, gtok_s):
    hbm = pl.BlockSpec(memory_space=pl.ANY)
    vmem = pl.BlockSpec(memory_space=pltpu.VMEM)
    outs = [jax.ShapeDtypeStruct(s.shape[4:], jnp.float32) for s in parts]
    outs += [jax.ShapeDtypeStruct(small.shape, jnp.float32)]
    outs += [jax.ShapeDtypeStruct(out_s.shape, out_s.dtype)] * 2
    scr = []
    for s in (parts[3], parts[2], parts[1], parts[0]):
        scr += Scatter.scratch(depth, *s.shape[4:])
    scr += Exchange.sems() * 2 + Sum.scratch(bits, small.shape[0])
    return pl.pallas_call(
        functools.partial(scatter_kernel, depth, bits),
        out_shape=outs,
        in_specs=[vmem] * 5 + [hbm] * 2,
        out_specs=[vmem] * 5 + [hbm] * 2,
        scratch_shapes=scr,
        compiler_params=pltpu.CompilerParams(
            collective_id=1, has_side_effects=True, vmem_limit_bytes=60 * 2**20
        ),
        name="scatter",
    )(*parts, small, out_s, gtok_s)

SPANS = ((0, LEN_LONG), (LEN_LONG, LEN_MID), (LEN_LONG + LEN_MID, LEN_SHORT), (LEN_LONG + LEN_MID + LEN_SHORT, LEN_SHORT))
TILE = 128
QKV_PAD = 640
CTX_PAD = 256
MASK_LOW = -1e9
NN = (((1,), (0,)), ((), ()))
NT = (((1,), (1,)), ((), ()))


def dot(a, b, dims=NN):
    return lax.dot_general(a, b, dims, preferred_element_type=jnp.float32)


def offset_row(pos_table):
    buckets = rel_buckets(257)
    offset = np.clip(256 - np.arange(512), -256, 256) + 256
    onehot = (buckets[offset][:, None] == np.arange(NB)[None, :]).astype(np.float32)
    return jnp.einsum("rb,bh->hr", jnp.asarray(onehot), pos_table, precision=FULL_PRECISION)


def table_onehot():
    buckets = rel_buckets(257)
    offset = np.clip(256 - np.arange(512), -256, 256) + 256
    index = np.concatenate([buckets[offset], np.full(128, NB // 2 - 1), np.full(128, NB - 1)])
    return (index[:, None] == np.arange(NB)[None, :]).astype(np.float32)


def bias_tiles(row):
    spread = pltpu.roll(jnp.broadcast_to(row, (TILE, 512)), 0, 1, stride=1, stride_axis=0)
    far = [jnp.broadcast_to(row[:, at : at + 1], (TILE, TILE)) for at in (511, 0)]
    near = [spread[:, 256 - 128 * delta : 384 - 128 * delta] for delta in (-1, 0, 1)]
    return [far[0], *near, far[1]]


def diagonal_sums(tiles):
    grid = jnp.concatenate([jnp.zeros((TILE, TILE), jnp.float32), tiles[2], tiles[1], tiles[0]], axis=1)
    rows = TILE
    while rows > 8:
        rows //= 2
        grid = grid[:rows] + pltpu.roll(grid[rows:], 512 - rows, 1)
    total = grid[0:1]
    for r in range(1, 8):
        total = total + pltpu.roll(grid[r : r + 1], 512 - r, 1)
    return total


def swap_halves(tile):
    return jnp.concatenate([tile[:, DH:], tile[:, :DH]], axis=1)


def lanes_below(shape, at=DH):
    return lax.broadcasted_iota(jnp.int32, shape, len(shape) - 1) < at


def key_side(qk, mask):
    swapped = swap_halves(qk)
    return jnp.where(lanes_below(qk.shape), swapped, mask), swapped


def query_side(qk):
    lane = lax.broadcasted_iota(jnp.int32, qk.shape, 1)
    return jnp.where(lane < DH, qk, jnp.where(lane == DH, 1.0, 0.0).astype(qk.dtype))


def probabilities(keys, queries, tiles, q0, length, width):
    scores = dot(keys, queries, NT)
    blocks = []
    for kb in range(length // TILE):
        deltas = [max(-2, min(2, kb - (q0 + qi))) + 2 for qi in range(width // TILE)]
        bias = tiles[deltas[0]] if len(deltas) == 1 else jnp.concatenate([tiles[d] for d in deltas], axis=1)
        blocks.append(scores[kb * TILE : (kb + 1) * TILE] + bias)
    top = blocks[0]
    for block in blocks[1:]:
        top = jnp.maximum(top, block)
    top = jnp.max(top, axis=0, keepdims=True)
    blocks = [jnp.exp(block - top) for block in blocks]
    total = blocks[0]
    for block in blocks[1:]:
        total = total + block
    inverse = 1.0 / jnp.sum(total, axis=0, keepdims=True)
    return [block * inverse for block in blocks]


def join(blocks, axis=0):
    return blocks[0] if len(blocks) == 1 else jnp.concatenate(blocks, axis=axis)


def value_lanes(group):
    stride = group * CTX_PAD // (3 * DH)
    lane = np.arange(CTX_PAD)
    column = lane // stride * group + lane % stride
    return np.where(lane % stride < group, column // DH, -1), column


def head_runs(group):
    heads, _ = value_lanes(group)
    runs = []
    for lane in range(CTX_PAD):
        head = int(heads[lane])
        head = runs[-1][2] if head < 0 else head
        if runs and runs[-1][2] == head:
            runs[-1][1] = lane + 1
        else:
            runs.append([lane, lane + 1, head])
    return runs


def head_lanes(shape, group, head):
    lane = lax.broadcasted_iota(jnp.int32, shape, len(shape) - 1)
    inside = None
    for lo, hi, h in head_runs(group):
        if h == head:
            run = jnp.logical_and(lane >= lo, lane < hi)
            inside = run if inside is None else jnp.logical_or(inside, run)
    return inside


def no_tick(j):
    pass


def attend_group(packed, mask_ref, rows, context, group, tick=no_tick):
    tiles = [bias_tiles(rows[h : h + 1, :]) for h in range(3)]
    for number, (offset, length) in enumerate(SPANS):
        span = pl.ds(offset, length)
        mask = mask_ref[span, :]
        keys = [key_side(packed[span, h * TILE : (h + 1) * TILE], mask)[0] for h in range(3)]
        values = packed[span, 3 * TILE :].T
        width = min(length, 256)
        for q0 in range(0, length, width):
            here = pl.ds(offset + q0, width)
            outs = []
            for h in range(3):
                queries = query_side(packed[here, h * TILE : (h + 1) * TILE])
                probs = probabilities(keys[h], queries, tiles[h], q0 // TILE, length, width)
                probs = join([block.astype(jnp.bfloat16) for block in probs])
                outs.append(dot(values, probs))
            whole = jnp.concatenate([outs[h][lo:hi] for lo, hi, h in head_runs(group)], axis=0)
            context[here, :] = whole.T.astype(jnp.bfloat16)
        tick(number)


def attend_group_back(packed, mask_ref, rows, grad_context, grad_packed, sums, group, tick=no_tick):
    far_shape = (TILE, TILE)
    tiles = [bias_tiles(rows[h : h + 1, :]) for h in range(3)]
    near = [[None] * 3 for _ in range(3)]
    far = [[jnp.zeros(far_shape, jnp.float32)] * 2 for _ in range(3)]
    for number, (offset, length) in enumerate(SPANS):
        span = pl.ds(offset, length)
        mask = mask_ref[span, :]
        width = min(length, 256)
        values = packed[span, 3 * TILE :]
        value_sums = {}
        for h in range(3):
            at = pl.ds(h * TILE, TILE)
            qk = packed[span, at]
            low = lanes_below(qk.shape)
            keys, swapped = key_side(qk, mask)
            upper_queries = jnp.where(low, jnp.zeros_like(qk), swapped)
            plain_keys = jnp.where(low, swapped, jnp.zeros_like(qk)).T
            grad_keys = None
            grad_queries = []
            for q0 in range(0, length, width):
                here = pl.ds(offset + q0, width)
                probs = probabilities(keys, query_side(packed[here, at]), tiles[h], q0 // TILE, length, width)
                g_tile = grad_context[here, :]
                g_tile = jnp.where(head_lanes(g_tile.shape, group, h), g_tile, jnp.zeros_like(g_tile))
                g_probs = dot(values, g_tile, NT)
                g_blocks = [g_probs[kb * TILE : (kb + 1) * TILE] for kb in range(length // TILE)]
                total = probs[0] * g_blocks[0]
                for kb in range(1, length // TILE):
                    total = total + probs[kb] * g_blocks[kb]
                centre = jnp.sum(total, axis=0, keepdims=True)
                low_probs = join([block.astype(jnp.bfloat16) for block in probs])
                g_scores = [(a * (g - centre)).astype(jnp.bfloat16) for a, g in zip(probs, g_blocks)]
                for kb, block in enumerate(g_scores):
                    wide = block.astype(jnp.float32)
                    for qi in range(width // TILE):
                        piece = wide[:, qi * TILE : (qi + 1) * TILE]
                        delta = kb - (q0 // TILE + qi)
                        if abs(delta) <= 1:
                            held = near[h][delta + 1]
                            near[h][delta + 1] = piece if held is None else held + piece
                        else:
                            side = 0 if delta < 0 else 1
                            far[h][side] = far[h][side] + piece
                g_scores = join(g_scores)
                g_v = dot(low_probs, g_tile)
                if q0 not in value_sums:
                    value_sums[q0] = g_v
                else:
                    value_sums[q0] = value_sums[q0] + g_v
                g_k = dot(g_scores, upper_queries[q0 : q0 + width])
                grad_keys = g_k if grad_keys is None else grad_keys + g_k
                grad_queries.append(dot(plain_keys, g_scores).T)
            grad_packed[span, at] = (join(grad_queries) + grad_keys).astype(jnp.bfloat16)
            tick(3 * number + h)
        grad_packed[span, 3 * TILE :] = functools.reduce(jnp.add, value_sums.values()).astype(jnp.bfloat16)
    for h in range(3):
        sums[h : h + 1, :512] = diagonal_sums(near[h])
        for side in range(2):
            sums[h : h + 1, 512 + side * TILE : 640 + side * TILE] = jnp.sum(far[h][side], axis=0, keepdims=True)


def attention_kernel(group, x_ref, gain, w_ref, mask, rows, normed_out, packed, context):
    @pl.when(pl.program_id(0) == 0)
    def _():
        x = x_ref[...].astype(jnp.float32)
        scale = lax.rsqrt(jnp.mean(x * x, axis=-1, keepdims=True) + NORM_EPS)
        normed_out[...] = (x * scale * gain[...]).astype(jnp.bfloat16)

    packed[0] = dot(normed_out[...], w_ref[0]).astype(jnp.bfloat16)
    attend_group(packed.at[0], mask, rows[0], context.at[0], group)


def attention(x, gain, w, mask, rows, group):
    n = x.shape[0]
    bf = jnp.bfloat16
    return pl.pallas_call(
        functools.partial(attention_kernel, group),
        grid=(4,),
        out_shape=[
            jax.ShapeDtypeStruct((n, D), bf),
            jax.ShapeDtypeStruct((4, n, QKV_PAD), bf),
            jax.ShapeDtypeStruct((4, n, CTX_PAD), bf),
        ],
        in_specs=[
            pl.BlockSpec((n, D), lambda i: (0, 0)),
            pl.BlockSpec((1, D), lambda i: (0, 0)),
            pl.BlockSpec((1, D, QKV_PAD), lambda i: (i, 0, 0)),
            pl.BlockSpec((n, TILE), lambda i: (0, 0)),
            pl.BlockSpec((1, 3, 512), lambda i: (i, 0, 0)),
        ],
        out_specs=[
            pl.BlockSpec((n, D), lambda i: (0, 0)),
            pl.BlockSpec((1, n, QKV_PAD), lambda i: (i, 0, 0)),
            pl.BlockSpec((1, n, CTX_PAD), lambda i: (i, 0, 0)),
        ],
        compiler_params=pltpu.CompilerParams(vmem_limit_bytes=56 * 2**20),
        name="attention",
    )(x, gain, w, mask, rows)


def attention_back_kernel(group, packed, grad_context, mask, rows, grad_packed, sums):
    attend_group_back(packed.at[0], mask, rows[0], grad_context.at[0], grad_packed.at[0], sums.at[0], group)


def attention_back(packed, grad_context, mask, rows, group):
    n = packed.shape[1]
    return pl.pallas_call(
        functools.partial(attention_back_kernel, group),
        grid=(4,),
        out_shape=[
            jax.ShapeDtypeStruct((4, n, QKV_PAD), jnp.bfloat16),
            jax.ShapeDtypeStruct((4, 3, 768), jnp.float32),
        ],
        in_specs=[
            pl.BlockSpec((1, n, QKV_PAD), lambda i: (i, 0, 0)),
            pl.BlockSpec((1, n, CTX_PAD), lambda i: (i, 0, 0)),
            pl.BlockSpec((n, TILE), lambda i: (0, 0)),
            pl.BlockSpec((1, 3, 512), lambda i: (i, 0, 0)),
        ],
        out_specs=[
            pl.BlockSpec((1, n, QKV_PAD), lambda i: (i, 0, 0)),
            pl.BlockSpec((1, 3, 768), lambda i: (i, 0, 0)),
        ],
        compiler_params=pltpu.CompilerParams(vmem_limit_bytes=56 * 2**20),
        name="attention_back",
    )(packed, grad_context, mask, rows)


def head_columns(w, group):
    n = w.shape[0]
    qk = w[:, :, : 2 * DH].reshape(n, 6 * DH)
    v = w[:, :, 2 * DH :].reshape(n, 3 * DH // group, group)
    v = jnp.pad(v, ((0, 0), (0, 0), (0, group // 3))).reshape(n, CTX_PAD)
    return jnp.concatenate([qk, v], axis=1)


def from_head_columns(g, group):
    n = g.shape[0]
    qk = g[:, : 6 * DH].reshape(n, 3, 2 * DH)
    v = g[:, 6 * DH :].reshape(n, 3 * DH // group, group * 4 // 3)[:, :, :group].reshape(n, 3, DH)
    return jnp.concatenate([qk, v], axis=2)


def key_mask(live):
    lane = jnp.arange(TILE)[None, :]
    return jnp.where((lane == DH) & ~live[:, None], MASK_LOW, 0.0).astype(jnp.bfloat16)


TN = (((0,), (0,)), ((), ()))
FCH = 512
RCH = 256
ADAPT_PAD = 128


def gelu_both(v):
    phi = 0.5 + 0.5 * lax.erf(v * np.float32(np.sqrt(0.5)))
    return v * phi, phi + v * (jnp.exp(-0.5 * v * v) * np.float32(1.0 / np.sqrt(2.0 * np.pi)))


def rows_of(i, size=RCH):
    return pl.ds(pl.multiple_of(i * size, size), size)


def each_of(count, body):
    lax.fori_loop(0, count, lambda i, carry: (body(i), carry)[1], 0)


def middle_kernel(
    x_hbm, ctx_hbm, wo_hbm, wi_hbm, wu_hbm, cot_hbm, gain, down, up, live,
    res_hbm, gmid_hbm, gctx_hbm, go_hbm, gi_hbm, gu_hbm, g_gain, g_down, g_up,
    x, ctx, wo, wi, wu, cot, mid, n2, act, dg, acc, gffn, glow, stage, sems,
):
    n = x.shape[0]
    ff = wi.shape[0]
    bf = jnp.bfloat16
    loads = [
        pltpu.make_async_copy(src, dst, sems.at[i])
        for i, (src, dst) in enumerate(
            ((x_hbm, x), (ctx_hbm, ctx), (wo_hbm, wo), (wi_hbm, wi), (wu_hbm, wu), (cot_hbm, cot))
        )
    ]
    for load in loads:
        load.start()
    for load in loads[:3]:
        load.wait()

    def first(i):
        r = rows_of(i)
        total = x[r, :].astype(jnp.float32)
        for m in range(4):
            total = total + dot(ctx[m, r, :], wo[m])
        mid[r, :] = total
        scale = lax.rsqrt(jnp.mean(total * total, axis=-1, keepdims=True) + NORM_EPS)
        n2[r, :] = (total * scale * gain[...]).astype(bf)

    each_of(n // RCH, first)
    loads[3].wait()
    loads[4].wait()
    acc[...] = jnp.zeros_like(acc)

    def forward(j):
        f = rows_of(j, FCH)
        for half in range(2):
            r = pl.ds(half * (n // 2), n // 2)
            value, slope = gelu_both(dot(n2[r, :], wi[f, :], NT))
            value = value.astype(bf)
            act[r, f] = value
            dg[r, f] = slope.astype(bf)
            acc[r, :] += dot(value, wu[f, :])

    each_of(ff // FCH, forward)
    loads[5].wait()
    g_down[...] = jnp.zeros_like(g_down)
    g_up[...] = jnp.zeros_like(g_up)
    g_gain[...] = jnp.zeros_like(g_gain)

    def adapter(i):
        r = rows_of(i)
        ffn = acc[r, :]
        low = ffn.astype(bf)
        value, slope = gelu_both(dot(low, down[...]))
        value = value.astype(bf)
        x[r, :] = (mid[r, :] + ffn + dot(value, up[...], NT)).astype(bf)
        g_out = cot[r, :].astype(jnp.float32) * live[r, :]
        g_low = g_out.astype(bf)
        cot[r, :] = g_low
        g_sq = (dot(g_low, up[...]) * slope).astype(bf)
        g_up[...] += dot(g_low, value, TN)
        g_down[...] += dot(low, g_sq, TN)
        gffn[r, :] = (g_out + dot(g_sq, down[...], NT)).astype(bf)

    each_of(n // RCH, adapter)
    out_copy = pltpu.make_async_copy(x, res_hbm, sems.at[0])
    out_copy.start()
    acc[...] = jnp.zeros_like(acc)

    def stores(j, slot):
        f = rows_of(j, FCH)
        return [
            pltpu.make_async_copy(stage.at[k, slot], dst.at[f], sems.at[6 + 2 * k + slot])
            for k, dst in enumerate((gu_hbm, gi_hbm))
        ]

    def backward(j):
        f = rows_of(j, FCH)
        slot = lax.rem(j, 2)

        def settle():
            for store in stores(j - 2, slot):
                store.wait()

        pl.when(j >= 2)(settle)
        for half in range(2):
            r = pl.ds(half * (n // 2), n // 2)
            g = (dot(gffn[r, :], wu[f, :], NT) * dg[r, f].astype(jnp.float32)).astype(bf)
            dg[r, f] = g
            acc[r, :] += dot(g, wi[f, :])
        stage[0, slot] = dot(act[:, f], gffn[...], TN).astype(bf)
        stage[1, slot] = dot(dg[:, f], n2[...], TN).astype(bf)
        for store in stores(j, slot):
            store.start()

    count = ff // FCH
    each_of(count, backward)

    def last(i):
        r = rows_of(i)
        total = mid[r, :]
        g_n2 = acc[r, :]
        scale = lax.rsqrt(jnp.mean(total * total, axis=-1, keepdims=True) + NORM_EPS)
        g_gain[...] += jnp.sum(total * scale * g_n2, axis=0, keepdims=True)
        scaled = gain[...] * g_n2
        centre = jnp.mean(total * scaled, axis=-1, keepdims=True)
        g_mid = cot[r, :].astype(jnp.float32) + scale * scaled - total * (scale * scale * scale * centre)
        mid[r, :] = g_mid
        low = g_mid.astype(bf)
        glow[r, :] = low

    each_of(n // RCH, last)
    mid_copy = pltpu.make_async_copy(mid, gmid_hbm, sems.at[1])
    mid_copy.start()
    for j in range(max(count - 2, 0), count):
        for store in stores(j, j % 2):
            store.wait()
    for m in range(4):
        stage[0, m // 2, (m % 2) * 256 : (m % 2 + 1) * 256] = dot(ctx[m], glow[...], TN).astype(bf)
    go_copies = [pltpu.make_async_copy(stage.at[0, k], go_hbm.at[pl.ds(512 * k, 512)], sems.at[6 + k]) for k in range(2)]
    for copy in go_copies:
        copy.start()
    for m in range(4):
        ctx[m] = dot(glow[...], wo[m], NT).astype(bf)
    ctx_copy = pltpu.make_async_copy(ctx, gctx_hbm, sems.at[2])
    ctx_copy.start()
    for copy in (out_copy, mid_copy, *go_copies, ctx_copy):
        copy.wait()


def middle(x, ctx, wo, wi, wu, cot, gain, down, up, live):
    n, ff = x.shape[0], wi.shape[0]
    bf, f32 = jnp.bfloat16, jnp.float32
    hbm = pl.BlockSpec(memory_space=pl.ANY)
    vmem = pl.BlockSpec(memory_space=pltpu.VMEM)
    shape = jax.ShapeDtypeStruct
    return pl.pallas_call(
        middle_kernel,
        out_shape=[
            shape((n, D), bf),
            shape((n, D), f32),
            shape((4, n, CTX_PAD), bf),
            shape((4 * CTX_PAD, D), bf),
            shape((ff, D), bf),
            shape((ff, D), bf),
            shape((1, D), f32),
            shape((D, ADAPT_PAD), f32),
            shape((D, ADAPT_PAD), f32),
        ],
        in_specs=[hbm] * 6 + [vmem] * 4,
        out_specs=[hbm] * 6 + [vmem] * 3,
        scratch_shapes=[
            pltpu.VMEM((n, D), bf),
            pltpu.VMEM((4, n, CTX_PAD), bf),
            pltpu.VMEM((4, CTX_PAD, D), bf),
            pltpu.VMEM((ff, D), bf),
            pltpu.VMEM((ff, D), bf),
            pltpu.VMEM((n, D), bf),
            pltpu.VMEM((n, D), f32),
            pltpu.VMEM((n, D), bf),
            pltpu.VMEM((n, ff), bf),
            pltpu.VMEM((n, ff), bf),
            pltpu.VMEM((n, D), f32),
            pltpu.VMEM((n, D), bf),
            pltpu.VMEM((n, D), bf),
            pltpu.VMEM((2, 2, FCH, D), bf),
            pltpu.SemaphoreType.DMA((10,)),
        ],
        compiler_params=pltpu.CompilerParams(vmem_limit_bytes=63 * 2**20),
        name="middle",
    )(x, ctx, wo, wi, wu, cot, gain, down, up, live)


class Slots:
    def __init__(self, places, timed):
        self.at = {}
        times = sorted(places.items(), key=lambda item: item[1])
        for when, step in sorted(timed, key=lambda item: item[0]):
            place = next((name for name, t in times if t >= when), None)
            self.at.setdefault(place, []).append(step)

    def run(self, place):
        for step in self.at.pop(place, ()):
            step()

    def tick(self, i, j):
        for place in sorted(name for name in self.at if name is not None and name[1] == j):
            pl.when(i == place[0])(functools.partial(self.run, place))


def front_kernel(
    depth, group, tok, cot, wq, wo, wi, wu, gain, mask, rows,
    tok_s, cot_s, gq_hbm, go, gi, gu, normed_hbm, packed_hbm, ctx_hbm,
    x, gq, nrm, packed, ctx, local, *sems,
):
    p = Place(depth)
    n = depth
    bf = jnp.bfloat16
    arrays = [
        Gather(p, by_head, shard, buf, *sems[3 * i : 3 * i + 3])
        for i, (by_head, shard, buf) in enumerate(
            ((True, wq, gq), (False, wo, go), (False, wi, gi), (False, wu, gu))
        )
    ]
    q, rest = arrays[0], arrays[1:]
    first, second = Exchange(p, tok, x, *sems[12:15]), Exchange(p, cot, cot_s, *sems[15:18])
    p.barrier(0)
    for g in arrays:
        g.start()
    first.start()
    for g in arrays:
        g.along(0)
    for k in range(1, n):
        for g in arrays:
            g.along(k)
        for g in arrays if k < n - 1 else [q]:
            g.across(k - 1)
        if k == 1:
            first.finish()
            keep_x = pltpu.make_async_copy(x, tok_s, local.at[0])
            keep_x.start()
            second.start()

            def norm(i):
                v = x[i].astype(jnp.float32)
                scale = lax.rsqrt(jnp.mean(v * v, axis=-1, keepdims=True) + NORM_EPS)
                nrm[rows_of(i, SEG), :] = (v * scale * gain[...]).astype(bf)

            each_of(x.shape[0], norm)
            keep_n = pltpu.make_async_copy(nrm, normed_hbm, local.at[1])
            keep_n.start()
    q.across(n - 1)
    q.finish()
    keep_q = pltpu.make_async_copy(gq, gq_hbm, local.at[2])
    keep_q.start()
    places = {(m, j): 5.0 * m + t for m in range(4) for j, t in enumerate((2.5, 4.0, 4.5, 5.0))}
    timed = []
    for i, g in enumerate(rest):
        timed.append((2.0 * i + 1.0, functools.partial(g.across, n - 2)))
        timed.append((2.0 * i + 7.0, functools.partial(g.across, n - 1)))
    slots = Slots(places, timed)

    def keeps(m):
        return [
            pltpu.make_async_copy(packed.at[m], packed_hbm.at[m], local.at[3 + m]),
            pltpu.make_async_copy(ctx.at[m], ctx_hbm.at[m], local.at[7 + m]),
        ]

    def heads(m):
        w = gq[m // 2, m % 2].reshape(D, QKV_PAD)
        packed[m] = dot(nrm[...], w).astype(bf)
        attend_group(packed.at[m], mask, rows[m], ctx.at[m], group, functools.partial(slots.tick, m))
        for copy in keeps(m):
            copy.start()

    each_of(4, heads)
    slots.run(None)
    for g in rest:
        g.finish()
    second.finish()
    for copy in [keep_x, keep_n, keep_q] + [c for m in range(4) for c in keeps(m)]:
        copy.wait()
    for g in arrays + [first, second]:
        g.drain()


def front(depth, group, tok, cot, shards, gain, mask, rows):
    hbm = pl.BlockSpec(memory_space=pl.ANY)
    vmem = pl.BlockSpec(memory_space=pltpu.VMEM)
    bf = jnp.bfloat16
    n = tok.shape[0] * SEG
    outs = [jax.ShapeDtypeStruct(tok.shape, tok.dtype)] * 2
    for i, s in enumerate(shards):
        lead = (2, 2, depth, 2) if i == 0 else (depth, 2, 2, 2)
        outs.append(jax.ShapeDtypeStruct(lead + s.shape, s.dtype))
    outs += [jax.ShapeDtypeStruct(shape, bf) for shape in ((n, D), (4, n, QKV_PAD), (4, n, CTX_PAD))]
    return pl.pallas_call(
        functools.partial(front_kernel, depth, group),
        out_shape=outs,
        in_specs=[hbm] * 6 + [vmem] * 3,
        out_specs=[hbm] * 9,
        scratch_shapes=[
            pltpu.VMEM(tok.shape, bf),
            pltpu.VMEM(outs[2].shape, bf),
            pltpu.VMEM((n, D), bf),
            pltpu.VMEM((4, n, QKV_PAD), bf),
            pltpu.VMEM((4, n, CTX_PAD), bf),
            pltpu.SemaphoreType.DMA((11,)),
        ]
        + Gather.sems(depth) * 4
        + Exchange.sems() * 2,
        compiler_params=pltpu.CompilerParams(
            collective_id=2, has_side_effects=True, vmem_limit_bytes=56 * 2**20
        ),
        name="front",
    )(tok, cot, *shards, gain, mask, rows)


ROW_GAIN, ROW_TABLE, ROW_OTHER = 0, 8, 24


def back_kernel(
    depth, bits, group,
    packed_hbm, gctx_hbm, gq_hbm, nrm_hbm, x_hbm, gmid_hbm, pu, pi, po, out_s, gain, mask, rows, onehot, other,
    oq, oo, oi, ou, small, out, gtok,
    packed, gctx, gq, nrm, x, gmid, acc, sums_s, part_q, gtok_s, local, mine_u, mine_i, mine_o, sem_u, sem_i, sem_o, *scr,
):
    p = Place(depth)
    n = depth
    bf = jnp.bfloat16
    u = Scatter(p, False, pu, ou, *scr[0:6], mine_u, sem_u)
    i_ = Scatter(p, False, pi, oi, *scr[6:12], mine_i, sem_i)
    o = Scatter(p, False, po, oo, *scr[12:18], mine_o, sem_o)
    q = Scatter(p, True, part_q, oq, *scr[18:24])
    arrays = [u, i_, o, q]
    row_out, row_g = Exchange(p, out_s, out, *scr[24:27]), Exchange(p, gtok_s, gtok, *scr[27:30])
    total = Sum(p, bits, small, *scr[30:33])
    heads_in = [
        [
            pltpu.make_async_copy(packed_hbm.at[m], packed.at[m], local.at[m]),
            pltpu.make_async_copy(gctx_hbm.at[m], gctx.at[m], local.at[4 + m]),
        ]
        for m in range(4)
    ]
    others_in = [
        pltpu.make_async_copy(src, dst, local.at[8 + k])
        for k, (src, dst) in enumerate(((nrm_hbm, nrm), (gq_hbm, gq), (x_hbm, x), (gmid_hbm, gmid)))
    ]
    for copy in heads_in[0]:
        copy.start()
    p.barrier(bits)
    for g in (u, i_):
        for k in range(n):
            g.start(k)
    for copy in others_in:
        copy.start()
    for copies in heads_in[1:]:
        for copy in copies:
            copy.start()
    row_out.start()
    for k in range(n):
        o.start(k)
    small[...] = jnp.zeros_like(small)
    small[ROW_OTHER:, :] = other[...]
    acc[...] = jnp.zeros_like(acc)
    for copies in heads_in:
        for copy in copies:
            copy.wait()
    for copy in others_in:
        copy.wait()

    span = 10.0
    places = {(m, j): span * m + 0.63 * (j + 1) for m in range(4) for j in range(12)}
    places |= {(m, 12): span * (m + 1) for m in range(4)}
    timed = []
    for g, half, quarter, ahead in ((u, 0.6, 6.0, 14.0), (i_, 5.0, 18.0, 30.0), (o, 11.0, 27.0, 39.0)):
        for k in range(n):
            timed.append((half + 1.3 * k, functools.partial(g.to_half, k)))
            timed.append((quarter + 3.0 * k, functools.partial(lambda g, k: (g.to_quarter(k), g.origin(k)), g, k)))
            timed.append((ahead + 4.0 * k, functools.partial(g.forward, k)))
    slots = Slots(places, timed)

    def heads(m):
        tick = functools.partial(slots.tick, m)
        attend_group_back(packed.at[m], mask, rows[m], gctx.at[m], packed.at[m], sums_s.at[m], group, tick)
        g = packed[m]
        for y in range(2):
            for c in range(2):
                pl.when(m == 2 * y + c)(functools.partial(weight_part, y, c))
        acc[...] += dot(g, gq[m // 2, m % 2].reshape(D, QKV_PAD), NT)
        tick(12)

    def weight_part(y, c):
        g = dot(nrm[...], packed[2 * y + c], TN).astype(bf)
        part_q[y, c] = g.reshape(part_q.shape[2:])

    each_of(4, heads)
    for k in range(n):
        q.start(k)
    slots.run(None)
    small[ROW_TABLE : ROW_TABLE + 16, :] = jnp.zeros((16, 128), jnp.float32)
    for m in range(4):
        small[ROW_TABLE + 3 * m : ROW_TABLE + 3 * m + 3, :] = lax.dot_general(
            sums_s[m], onehot[...], NN, precision=FULL_PRECISION, preferred_element_type=jnp.float32
        )

    def last(s, g_gain):
        r = rows_of(s, SEG)
        v = x[s].astype(jnp.float32)
        g_n1 = acc[r, :]
        scale = lax.rsqrt(jnp.mean(v * v, axis=-1, keepdims=True) + NORM_EPS)
        scaled = gain[...] * g_n1
        centre = jnp.mean(v * scaled, axis=-1, keepdims=True)
        gtok_s[s] = (gmid[r, :] + scale * scaled - v * (scale * scale * scale * centre)).astype(bf)
        return g_gain + jnp.sum(v * scale * g_n1, axis=0, keepdims=True)

    g_gain = lax.fori_loop(0, x.shape[0], last, jnp.zeros((1, D), jnp.float32))
    for k in range(D // 128):
        small[ROW_GAIN + k : ROW_GAIN + k + 1, :] = g_gain[:, 128 * k : 128 * (k + 1)]
    for k in range(n):
        q.to_half(k)
    row_g.start()
    for k in range(n):
        q.to_quarter(k)
        q.origin(k)
    for k in range(n):
        q.forward(k)
    close(arrays, total)
    for r in (row_out, row_g):
        r.finish()
    for g in arrays + [row_out, row_g, total]:
        g.drain()


def back(depth, bits, group, packed, gctx, gq, nrm, x, gmid, parts, out_s, gain, mask, rows, onehot, other):
    hbm = pl.BlockSpec(memory_space=pl.ANY)
    vmem = pl.BlockSpec(memory_space=pltpu.VMEM)
    bf, f32 = jnp.bfloat16, jnp.float32
    pq_shape = gq.shape
    shape = jax.ShapeDtypeStruct
    small_rows = ROW_OTHER + other.shape[0]
    outs = [shape(pq_shape[4:], f32)] + [shape(s.shape[4:], f32) for s in (parts[2], parts[1], parts[0])]
    outs += [shape((small_rows, 128), f32), shape(out_s.shape, bf), shape(x.shape, bf)]
    dma = pltpu.SemaphoreType.DMA
    scratch = [
        pltpu.VMEM(packed.shape, bf),
        pltpu.VMEM(gctx.shape, bf),
        pltpu.VMEM(gq.shape, bf),
        pltpu.VMEM(nrm.shape, bf),
        pltpu.VMEM(x.shape, bf),
        pltpu.VMEM(gmid.shape, f32),
        pltpu.VMEM(gmid.shape, f32),
        pltpu.VMEM((4, 3, 768), f32),
        pltpu.VMEM(pq_shape, bf),
        pltpu.VMEM(x.shape, bf),
        dma((12,)),
    ]
    scratch += [pltpu.VMEM((depth, 2, 2) + s.shape[4:], bf) for s in parts]
    scratch += [dma((depth,))] * 3
    for s in (*(s.shape for s in parts), pq_shape):
        scratch += Scatter.scratch(depth, *s[4:])
    scratch += Exchange.sems() * 2 + Sum.scratch(bits, small_rows)
    return pl.pallas_call(
        functools.partial(back_kernel, depth, bits, group),
        out_shape=outs,
        in_specs=[hbm] * 10 + [vmem] * 5,
        out_specs=[vmem] * 5 + [hbm] * 2,
        scratch_shapes=scratch,
        compiler_params=pltpu.CompilerParams(
            collective_id=3, has_side_effects=True, vmem_limit_bytes=63 * 2**20
        ),
        name="back",
    )(packed, gctx, gq, nrm, x, gmid, *parts, out_s, gain, mask, rows, onehot, other)


def round_up(n, m):
    return -(-n // m) * m


def pad_rows(a, rows):
    return jnp.pad(a, ((0, rows - a.shape[0]), (0, 0)))


HEADS = 12


def local(
    tokens,
    lengths,
    cotangent,
    w_qkv,
    w_o,
    w_in,
    w_out,
    gain_attn,
    gain_ffn,
    pos_table,
    phm_rules,
    down_left,
    down_right,
    up_left,
    up_right,
):
    dp_count, mp_count = lax.axis_size("dp"), lax.axis_size("mp")
    depth = dp_count // 2
    bits = dp_count.bit_length() - 1
    devices = dp_count * mp_count
    member = lax.axis_index("mp")
    tok_rows = tokens.shape[0]
    seg_count = tok_rows // SEG
    o_rows, in_rows, q_rows = w_o.shape[0], w_in.shape[1], w_qkv.shape[0]
    bf = jnp.bfloat16
    group = o_rows if o_rows % 24 == 0 and round_up(o_rows, 16) * 3 == o_rows * 4 else 3 * DH
    wq = pad_rows(head_columns(w_qkv.astype(bf), group), round_up(q_rows, 16))
    wo = pad_rows(w_o.astype(bf), round_up(o_rows, 16))
    wi = pad_rows(w_in.astype(bf).T, round_up(in_rows, 16))
    wu = pad_rows(w_out.astype(bf), round_up(in_rows, 16))
    own_lengths = jnp.stack([
        lengths[member], lengths[4 + member // 2 + 2 * (member % 2)], lengths[8 + member], lengths[12 + member]
    ])
    shapes = ((LEN_LONG, 1), (LEN_MID, 1), (LEN_SHORT, 2))
    pieces = []
    first = 0
    for length, seqs in shapes:
        spots = jnp.arange(length, dtype=jnp.int32)
        pieces.append((spots[None, :] < own_lengths[first : first + seqs, None]).reshape(-1))
        first += seqs
    live = jnp.concatenate(pieces)
    mask = key_mask(live)
    rows = offset_row(pos_table).reshape(mp_count, 3, 512)
    tok_in, cot_in = tokens.reshape(seg_count, SEG, D), cotangent.reshape(seg_count, SEG, D)
    merged = depth <= 8 and wq.shape[0] == q_rows
    if merged:
        tok_s, cot_s, gq, go, gi, gu, normed_attn, packed, context = front(
            depth, group, tok_in, cot_in, (wq, wo, wi, wu), gain_attn[None], mask, rows
        )
    else:
        tok_s, cot_s, gq, go, gi, gu = gather_all(depth, tok_in, cot_in, (wq, wo, wi, wu))
    tokens_s = tok_s.reshape(tok_rows, D)

    def plain(g, rows):
        return g.reshape(devices, g.shape[-2], D)[:, :rows].reshape(devices * rows, D)

    def slots(g, rows):
        padded = jnp.pad(g.reshape(devices, rows, D), ((0, 0), (0, round_up(rows, 16) - rows), (0, 0)))
        return padded.reshape(depth, 2, 2, 2, padded.shape[1], D)

    dense_in, dense_out = plain(gi, in_rows), plain(gu, in_rows)
    if group == o_rows:
        dense_o = go.reshape(mp_count, CTX_PAD, D)
    else:
        dense_o = plain(go, o_rows).reshape(mp_count, 3 * DH, D)
        dense_o = jnp.pad(dense_o, ((0, 0), (0, CTX_PAD - 3 * DH), (0, 0)))
    qkv_full = gq.reshape(mp_count, dp_count, wq.shape[0], QKV_PAD)[:, :, :q_rows].reshape(mp_count, D, QKV_PAD)
    if not merged:
        normed_attn, packed, context = attention(tokens_s, gain_attn[None], qkv_full, mask, rows, group)
    w_down, w_up = adapter_weights(phm_rules, down_left, down_right, up_left, up_right)
    wide = ((0, 0), (0, ADAPT_PAD - ADAPT))
    result, grad_mid, grad_context, grad_w_o, grad_w_in, grad_w_out, grad_gain_ffn, grad_w_down, grad_w_up = middle(
        tokens_s,
        context,
        dense_o,
        dense_in,
        dense_out,
        cot_s.reshape(tok_rows, D),
        gain_ffn[None],
        jnp.pad(w_down.astype(bf), wide),
        jnp.pad(w_up.T.astype(bf), wide),
        live[:, None].astype(jnp.float32),
    )
    grad_w_down, grad_w_up = grad_w_down[:, :ADAPT], grad_w_up[:, :ADAPT].T
    if group == o_rows:
        part_o = grad_w_o.reshape(depth, 2, 2, 2, round_up(o_rows, 16), D)
    else:
        part_o = slots(grad_w_o.reshape(mp_count, CTX_PAD, D)[:, : 3 * DH].reshape(D, D), o_rows)
    _, adapter_back = jax.vjp(adapter_weights, phm_rules, down_left, down_right, up_left, up_right)
    small_list = (grad_gain_ffn[0],) + adapter_back((grad_w_down, grad_w_up))
    flat = jnp.concatenate([s.reshape(-1) for s in small_list])
    other_rows = round_up(-(-flat.size // 128), 8)
    other = jnp.pad(flat, (0, other_rows * 128 - flat.size)).reshape(other_rows, 128)
    part_in, part_out = slots(grad_w_in, in_rows), slots(grad_w_out, in_rows)
    result = result.reshape(seg_count, SEG, D)
    onehot = jnp.asarray(np.pad(table_onehot(), ((0, 0), (0, 128 - NB))))
    if merged:
        oq, oo, oi, ou, summed, out, gtok = back(
            depth, bits, group, packed, grad_context, gq, normed_attn, tok_s, grad_mid,
            (part_out, part_in, part_o), result, gain_attn[None], mask, rows, onehot, other,
        )
    else:
        packed_grads, sums = attention_back(packed, grad_context, mask, rows, group)
        table_grad = jnp.dot(sums.reshape(HEADS, 768), onehot, precision=FULL_PRECISION)
        grad_w_qkv = jnp.einsum("td,mtc->mdc", normed_attn, packed_grads, preferred_element_type=jnp.float32).astype(bf)
        grad_n1 = jnp.einsum("mtc,mdc->td", packed_grads, qkv_full, preferred_element_type=jnp.float32)
        _, norm_back_attn = jax.vjp(normed, tokens_s.astype(jnp.float32), gain_attn)
        grad_x_part, grad_gain_attn = norm_back_attn(grad_n1)
        grad_tokens = (grad_mid + grad_x_part).astype(bf)
        small = jnp.concatenate([
            jnp.pad(grad_gain_attn.reshape(D // 128, 128), ((0, ROW_TABLE - D // 128), (0, 0))),
            jnp.pad(table_grad, ((0, ROW_OTHER - ROW_TABLE - HEADS), (0, 0))),
            other,
        ])
        part_q = grad_w_qkv.reshape(mp_count, dp_count, q_rows, QKV_PAD)
        part_q = jnp.pad(part_q, ((0, 0), (0, 0), (0, wq.shape[0] - q_rows), (0, 0)))
        part_q = part_q.reshape(2, 2, depth, 2, wq.shape[0], QKV_PAD)
        oq, oo, oi, ou, summed, out, gtok = scatter_all(
            depth, bits, (part_q, part_o, part_in, part_out), small, result, grad_tokens.reshape(seg_count, SEG, D)
        )
    smalls = [
        summed[ROW_GAIN : ROW_GAIN + D // 128].reshape(D),
        summed[ROW_TABLE : ROW_TABLE + HEADS, :NB].T,
    ]
    flat = summed[ROW_OTHER:].reshape(-1)
    first = 0
    for s in small_list:
        smalls.append(flat[first : first + s.size].reshape(s.shape))
        first += s.size
    smalls = [smalls[0], smalls[2], smalls[1], *smalls[3:]]
    return (
        out.reshape(tok_rows, D),
        gtok.reshape(tok_rows, D),
        from_head_columns(oq[:q_rows], group),
        oo[:o_rows],
        oi[:in_rows].T,
        ou[:in_rows],
        *smalls,
    )


def solution(mesh):
    return jax.shard_map(
        local,
        mesh=mesh,
        in_specs=(
            P(("dp", "mp"), None),
            P("dp"),
            P(("dp", "mp"), None),
            P("dp", "mp", None),
            P(("dp", "mp"), None),
            P(None, ("dp", "mp")),
            P(("dp", "mp"), None),
            P(),
            P(),
            P(),
            P(),
            P(),
            P(),
            P(),
            P(),
        ),
        out_specs=(
            P(("dp", "mp"), None),
            P(("dp", "mp"), None),
            P("dp", "mp", None),
            P(("dp", "mp"), None),
            P(None, ("dp", "mp")),
            P(("dp", "mp"), None),
            P(),
            P(),
            P(),
            P(),
            P(),
            P(),
            P(),
            P(),
        ),
        check_vma=False,
    )
```

```python
import functools
import itertools

import jax
import jax.experimental.pallas as pl
import jax.experimental.pallas.tpu as pltpu
import jax.numpy as jnp
import numpy as np
from jax import lax
from jax.sharding import PartitionSpec as P

D = 768
DH = 64
NB = 32
MAXDIST = 128
ADAPT = 48
KRON = 4
LEN_LONG = 512
LEN_MID = 256
LEN_SHORT = 128
SEG = 128


NORM_EPS = 1e-06
FULL_PRECISION = lax.Precision.HIGHEST


def rel_buckets(length):
    offsets = np.arange(-(length - 1), length)
    half_count = NB // 2
    exact_count = half_count // 2
    upward = (offsets > 0).astype(np.int64) * half_count
    distance = np.abs(offsets)
    scaled = (
        np.log(np.maximum(distance, 1) / exact_count)
        / np.log(MAXDIST / exact_count)
        * (half_count - exact_count)
    )
    far_bucket = np.minimum(
        exact_count + np.floor(np.maximum(scaled, 0.0)).astype(np.int64), half_count - 1
    )
    return upward + np.where(distance < exact_count, distance, far_bucket)


def normed(values, gain):
    return values * lax.rsqrt(jnp.mean(values * values, axis=-1, keepdims=True) + NORM_EPS) * gain


MESH = pl.DeviceIdType.MESH


class Place:
    def __init__(self, depth):
        d, m = lax.axis_index("dp"), lax.axis_index("mp")
        self.depth = depth
        self.d, self.m = d, m
        self.z, self.x, self.y, self.c = d // 2, d % 2, m // 2, m % 2
        dx, dy, c = 1 - 2 * self.x, 2 - 4 * self.y, self.c
        self.sib = (d, m + 1 - 2 * c)
        self.right, self.left = (d + 2, m), (d - 2, m)
        self.mp_peer = ((d, m + 1 - 2 * c), (d, m + dy), (d, 3 - m))
        self.xn, self.yn = (d + dx, m), (d, m + dy)
        self.a_nbr = (d + (1 - c) * dx, m + c * dy)
        self.b_nbr = (d + c * dx, m + (1 - c) * dy)
        self.a = self.x + c * (self.y - self.x)
        self.b = self.y + c * (self.x - self.y)

    def by_core(self, run):
        for core in (0, 1):
            pl.when(self.c == core)(functools.partial(run, core))

    def nearest(self, e):
        n, z = self.depth, self.z
        ahead = 1 - 2 * (z // ((n + 1) // 2))
        short = jnp.minimum(z, n - 1 - z)
        around = (1 - 2 * (e % 2)) * ((e + 1) // 2)
        return z + ahead * jnp.where(e <= 2 * short, around, e - short)

    def flip(self, bit):
        step = 1 << bit
        return (self.d + step * (1 - 2 * ((self.d // step) % 2)), self.m)

    def barrier(self, bits):
        sem = pltpu.get_barrier_semaphore()

        def greet(dev):
            pl.semaphore_signal(sem, 1, device_id=dev, device_id_type=MESH)

        pals = [*self.mp_peer, self.xn] + [self.flip(bit) for bit in range(2, bits)]
        for dev in pals:
            greet(dev)
        pl.when(self.z > 0)(lambda: greet(self.left))
        pl.when(self.z < self.depth - 1)(lambda: greet(self.right))
        ends = jnp.minimum(self.z, 1) + jnp.minimum(self.depth - 1 - self.z, 1)
        pl.semaphore_wait(sem, len(pals) + ends)


def remote(src, dst, send, recv, dev):
    return pltpu.make_async_remote_copy(
        src_ref=src, dst_ref=dst, send_sem=send, recv_sem=recv, device_id=dev, device_id_type=MESH
    )


def slot_of(buf, by_head, p):
    return buf.at[p.y, p.c, p.z, p.x] if by_head else buf.at[p.z, p.x, p.y, p.c]


def pair_of(buf, by_head, core, b, z):
    if by_head:
        return buf.at[b, 0, z] if core == 0 else buf.at[:, 1, z, b]
    return buf.at[z, :, b, 0] if core == 0 else buf.at[z, b, :, 1]


class Gather:
    def __init__(self, p, by_head, shard, buf, send, recv, own):
        self.p, self.by_head, self.shard, self.buf = p, by_head, shard, buf
        self.send, self.recv, self.own = send, recv, own
        n = p.depth
        self.first = remote(shard, slot_of(buf, by_head, p), send.at[5 * n], recv.at[4 * n], p.a_nbr)
        self.keep = pltpu.make_async_copy(shard, slot_of(buf, by_head, p), own)

    @staticmethod
    def sems(n):
        return [
            pltpu.SemaphoreType.DMA((5 * n + 1,)),
            pltpu.SemaphoreType.DMA((4 * n + 1,)),
            pltpu.SemaphoreType.DMA,
        ]

    def _copy(self, core, b, z, kind):
        p, n = self.p, self.p.depth
        ref = pair_of(self.buf, self.by_head, core, b, z)
        if kind == "right":
            return remote(ref, ref, self.send.at[z], self.recv.at[z], p.right)
        if kind == "left":
            return remote(ref, ref, self.send.at[n + z], self.recv.at[z], p.left)
        return remote(ref, ref, self.send.at[2 * n + z], self.recv.at[n + z], p.b_nbr)

    def _sib(self, core, b, z):
        n = self.p.depth
        ref = pair_of(self.buf, self.by_head, core, b, z)
        return remote(ref, ref, self.send.at[3 * n + b * n + z], self.recv.at[2 * n + b * n + z], self.p.sib)

    def start(self):
        self.keep.start()
        self.first.start()

    def _spread(self, core, z, right, left):
        p = self.p
        if right:
            pl.when(p.z < p.depth - 1)(lambda: self._copy(core, p.b, z, "right").start())
        if left:
            pl.when(p.z > 0)(lambda: self._copy(core, p.b, z, "left").start())
        self._copy(core, p.b, z, "b").start()
        self._sib(core, p.b, z).start()

    def along(self, k):
        p = self.p
        if isinstance(k, int) and k == 0:
            self.keep.wait()
            self.first.wait_recv()
            p.by_core(lambda core: self._spread(core, p.z, True, True))
            return

        def from_left(core):
            self._copy(core, p.b, p.z - k, "right").wait_recv()
            self._spread(core, p.z - k, True, False)

        def from_right(core):
            self._copy(core, p.b, p.z + k, "left").wait_recv()
            self._spread(core, p.z + k, False, True)

        pl.when(p.z - k >= 0)(lambda: p.by_core(from_left))
        pl.when(p.z + k < p.depth)(lambda: p.by_core(from_right))

    def across(self, k):
        p = self.p

        def one(z, core):
            self._copy(core, 1 - p.b, z, "b").wait_recv()
            self._sib(core, 1 - p.b, z).start()

        pl.when(p.z - k >= 0)(lambda: p.by_core(lambda core: one(p.z - k, core)))
        if not (isinstance(k, int) and k == 0):
            pl.when(p.z + k < p.depth)(lambda: p.by_core(lambda core: one(p.z + k, core)))

    def finish_at(self, z):
        def one(core):
            for b in (0, 1):
                self._sib(1 - core, b, z).wait_recv()

        self.p.by_core(one)

    def finish(self):
        each_of(self.p.depth, self.finish_at)

    def drain(self):
        p, n = self.p, self.p.depth
        self.first.wait_send()

        def each(z, carry):
            def one(core):
                pl.when(jnp.logical_and(p.z < n - 1, z <= p.z))(
                    lambda: self._copy(core, p.b, z, "right").wait_send()
                )
                pl.when(jnp.logical_and(p.z > 0, z >= p.z))(
                    lambda: self._copy(core, p.b, z, "left").wait_send()
                )
                self._copy(core, p.b, z, "b").wait_send()
                for b in (0, 1):
                    self._sib(core, b, z).wait_send()

            p.by_core(one)
            return carry

        lax.fori_loop(0, n, each, 0)


class Exchange:
    def __init__(self, p, src, dst, send, recv, own):
        m = p.m
        c, other = m % 2, 1 - m % 2
        self.local = [
            pltpu.make_async_copy(src.at[m], dst.at[m], own.at[0]),
            pltpu.make_async_copy(src.at[4 + c], dst.at[4 + c], own.at[1]),
            pltpu.make_async_copy(src.at[pl.ds(6, 2)], dst.at[pl.ds(6, 2)], own.at[2]),
        ]
        self.out = [
            remote(src.at[dev[1]], dst.at[m], send.at[j], recv.at[j], dev)
            for j, dev in enumerate(p.mp_peer)
        ] + [remote(src.at[4 + other], dst.at[4 + c], send.at[3], recv.at[3], p.sib)]

    @staticmethod
    def sems():
        return [
            pltpu.SemaphoreType.DMA((4,)),
            pltpu.SemaphoreType.DMA((4,)),
            pltpu.SemaphoreType.DMA((3,)),
        ]

    def start(self):
        for copy in self.out + self.local:
            copy.start()

    def finish(self):
        for copy in self.local:
            copy.wait()
        for copy in self.out:
            copy.wait_recv()

    def drain(self):
        for copy in self.out:
            copy.wait_send()


def add_rows(dst, src, rows):
    step = 32 if rows % 32 == 0 else 16

    def one(i, carry):
        at = pl.ds(pl.multiple_of(i * step, step), step)
        total = dst[at, :].astype(jnp.float32) + src[at, :].astype(jnp.float32)
        dst[at, :] = total.astype(dst.dtype)
        return carry

    lax.fori_loop(0, rows // step, one, 0)


class Scatter:
    def __init__(self, p, by_head, part, total, half, quarter, arrive, last, send, recv, mine=None, mine_sem=None):
        self.p, self.by_head, self.part, self.total = p, by_head, part, total
        self.mine, self.mine_sem = mine, mine_sem
        self.half, self.quarter, self.arrive, self.last = half, quarter, arrive, last
        self.send, self.recv = send, recv
        self.rows = part.shape[-2]

    @staticmethod
    def scratch(n, rows, cols, dtype=jnp.bfloat16):
        return [
            pltpu.VMEM((n, 2, 2, rows, cols), dtype),
            pltpu.VMEM((n, 2, rows, cols), dtype),
            pltpu.VMEM((n + 1, 2, rows, cols), dtype),
            pltpu.VMEM((rows, cols), dtype),
            pltpu.SemaphoreType.DMA((3 * n + 1,)),
            pltpu.SemaphoreType.DMA((3 * n + 2,)),
        ]

    def order(self, k):
        n = self.p.depth
        base = k // 2 if k % 2 == 0 else n - 1 - k // 2
        near = 1 - jnp.minimum(self.p.z // max(n // 2, 1), 1)
        return base + near * (n - 1 - 2 * base)

    def _region(self, core, z):
        return self.part.at[:, core, z] if self.by_head else self.part.at[z, :, :, core]

    def _half_pair(self, core, b, z):
        over_first = (core == 0) != self.by_head
        return self.half.at[z, :, b] if over_first else self.half.at[z, b]

    def _sib(self, core, z):
        return remote(
            self._region(1 - core, z), self.half.at[z], self.send.at[z], self.recv.at[z], self.p.sib
        )

    def _b(self, core, z):
        n, p = self.p.depth, self.p
        return remote(
            self._half_pair(core, 1 - p.b, z), self.quarter.at[z], self.send.at[n + z], self.recv.at[n + z], p.b_nbr
        )

    def _right(self, z):
        n, p = self.p.depth, self.p
        return remote(
            self.quarter.at[z], self.arrive.at[z], self.send.at[2 * n + z], self.recv.at[2 * n + z], p.right
        )

    def _left(self, z, goal):
        n, p = self.p.depth, self.p
        return remote(
            self.quarter.at[z], self.arrive.at[goal], self.send.at[2 * n + z], self.recv.at[2 * n + goal], p.left
        )

    def _a(self):
        n, p = self.p.depth, self.p
        return remote(
            self.quarter.at[p.z, 1 - p.a], self.last, self.send.at[3 * n], self.recv.at[3 * n + 1], p.a_nbr
        )

    def _keep(self, core, z):
        return pltpu.make_async_copy(self._region(core, z), self.mine.at[z], self.mine_sem.at[z])

    def start(self, k):
        z = self.order(k)

        def one(core):
            self._sib(core, z).start()
            if self.mine is not None:
                self._keep(core, z).start()

        self.p.by_core(one)

    def to_half(self, k):
        z = self.order(k)

        def one(core):
            self._sib(core, z).wait_recv()
            region = self._region(core, z)
            if self.mine is not None:
                self._keep(core, z).wait()
                region = self.mine.at[z]
            for i in (0, 1):
                for j in (0, 1):
                    add_rows(self.half.at[z, i, j], region.at[i, j], self.rows)
            self._b(core, z).start()

        self.p.by_core(one)

    def to_quarter(self, k):
        z = self.order(k)

        def one(core):
            self._b(core, z).wait_recv()
            for i in (0, 1):
                add_rows(self.quarter.at[z, i], self._half_pair(core, self.p.b, z).at[i], self.rows)

        self.p.by_core(one)

    def _take(self, z, slot):
        for i in (0, 1):
            add_rows(self.quarter.at[z, i], self.arrive.at[slot, i], self.rows)

    def _send_left(self, z):
        p, n = self.p, self.p.depth
        pl.when(z == p.z - 1)(lambda: self._left(z, n).start())
        pl.when(z < p.z - 1)(lambda: self._left(z, z).start())

    def origin(self, k):
        p, n = self.p, self.p.depth
        z = self.order(k)
        pl.when(jnp.logical_and(p.z == 0, z > p.z))(lambda: self._right(z).start())
        pl.when(jnp.logical_and(p.z == n - 1, z < p.z))(lambda: self._send_left(z))

    def forward(self, k):
        p, n = self.p, self.p.depth
        z = self.order(k)

        def rightward():
            self._right(z).wait_recv()
            self._take(z, z)
            self._right(z).start()

        def leftward():
            self._left(z, z).wait_recv()
            self._take(z, z)
            self._send_left(z)

        pl.when(jnp.logical_and(p.z > 0, z > p.z))(rightward)
        pl.when(jnp.logical_and(p.z < n - 1, z < p.z))(leftward)

    def collect(self):
        p, n = self.p, self.p.depth

        def from_left():
            self._right(p.z).wait_recv()
            self._take(p.z, p.z)

        def from_right():
            self._left(p.z, n).wait_recv()
            self._take(p.z, n)

        pl.when(p.z > 0)(from_left)
        pl.when(p.z < n - 1)(from_right)
        self._a().start()

    def finish(self):
        p = self.p
        self._a().wait_recv()
        self.total[...] = self.quarter[p.z, p.a].astype(jnp.float32) + self.last[...].astype(jnp.float32)

    def drain(self):
        p, n = self.p, self.p.depth
        self._a().wait_send()

        def each(z, carry):
            def one(core):
                self._sib(core, z).wait_send()
                self._b(core, z).wait_send()

            p.by_core(one)
            pl.when(z != p.z)(lambda: self._right(z).wait_send())
            return carry

        lax.fori_loop(0, n, each, 0)

    def steps(self):
        n = self.p.depth
        todo = [lambda: [self.start(k) for k in range(n)]]
        todo += [functools.partial(self.to_half, k) for k in range(n)]
        for k in range(n):
            todo.append(functools.partial(lambda k: (self.to_quarter(k), self.origin(k), self.forward(k)), k))
        return todo


class Sum:
    def __init__(self, p, bits, value, slots, send, recv):
        self.p, self.bits, self.value, self.slots = p, bits, value, slots
        self.send, self.recv = send, recv

    @staticmethod
    def scratch(bits, rows):
        return [
            pltpu.VMEM((2 * (bits + 2), rows, 128), jnp.float32),
            pltpu.SemaphoreType.DMA((bits + 2,)),
            pltpu.SemaphoreType.DMA((bits + 2,)),
        ]

    def _copy(self, s):
        p = self.p
        dev = (p.sib, p.yn, *[p.flip(bit) for bit in range(self.bits)])[s]
        return remote(self.slots.at[2 * s], self.slots.at[2 * s + 1], self.send.at[s], self.recv.at[s], dev)

    def steps(self):
        def begin():
            self.slots[0] = self.value[...]
            self._copy(0).start()

        def one(s):
            self._copy(s).wait_recv()
            total = self.slots[2 * s] + self.slots[2 * s + 1]
            if s == self.bits + 1:
                self.value[...] = total
            else:
                self.slots[2 * s + 2] = total
                self._copy(s + 1).start()

        return [begin] + [functools.partial(one, s) for s in range(self.bits + 2)]

    def drain(self):
        for s in range(self.bits + 2):
            self._copy(s).wait_send()


def in_waves(lists, lag):
    for t in range(max(len(todo) + lag * r for r, todo in enumerate(lists))):
        for r, todo in enumerate(lists):
            if 0 <= t - lag * r < len(todo):
                todo[t - lag * r]()


def gather_kernel(p_depth, tok, cot, wq, wo, wi, wu, tok_s, cot_s, gq, go, gi, gu, *sems):
    p = Place(p_depth)
    n = p_depth
    arrays = []
    for i, (by_head, shard, buf) in enumerate(
        ((True, wq, gq), (False, wo, go), (False, wi, gi), (False, wu, gu))
    ):
        arrays.append(Gather(p, by_head, shard, buf, *sems[3 * i : 3 * i + 3]))
    rows = [Exchange(p, tok, tok_s, *sems[12:15]), Exchange(p, cot, cot_s, *sems[15:18])]
    p.barrier(0)
    for g in arrays:
        g.start()
    rows[0].start()
    if n <= 8:
        for k in range(n):
            for g in arrays:
                g.along(k)
            if k > 0:
                for g in arrays:
                    g.across(k - 1)
            if k == 1:
                rows[1].start()
        for g in arrays:
            g.across(n - 1)
    else:
        for g in arrays:
            g.along(0)
            lax.fori_loop(1, n, lambda k, carry: (g.along(k), carry)[1], 0)
        rows[1].start()
        for g in arrays:
            g.across(0)
            lax.fori_loop(1, n, lambda k, carry: (g.across(k), carry)[1], 0)
    for g in arrays + rows:
        g.finish()
    for g in arrays + rows:
        g.drain()


def gather_all(depth, tok, cot, shards):
    hbm = pl.BlockSpec(memory_space=pl.ANY)
    outs = [jax.ShapeDtypeStruct(tok.shape, tok.dtype)] * 2
    for i, s in enumerate(shards):
        lead = (2, 2, depth, 2) if i == 0 else (depth, 2, 2, 2)
        outs.append(jax.ShapeDtypeStruct(lead + s.shape, s.dtype))
    sems = Gather.sems(depth) * 4 + Exchange.sems() * 2
    return pl.pallas_call(
        functools.partial(gather_kernel, depth),
        out_shape=outs,
        in_specs=[hbm] * 6,
        out_specs=[hbm] * 6,
        scratch_shapes=sems,
        compiler_params=pltpu.CompilerParams(collective_id=0, has_side_effects=True),
        name="gather",
    )(tok, cot, *shards)


def scatter_kernel(depth, bits, pq, po, pi, pu, small, out_s, gtok_s, oq, oo, oi, ou, small_o, out, gtok, *scr):
    p = Place(depth)
    arrays = []
    for i, (by_head, part, total) in enumerate(
        ((False, pu, ou), (False, pi, oi), (False, po, oo), (True, pq, oq))
    ):
        arrays.append(Scatter(p, by_head, part, total, *scr[6 * i : 6 * i + 6]))
    rows = [Exchange(p, out_s, out, *scr[24:27]), Exchange(p, gtok_s, gtok, *scr[27:30])]
    small_o[...] = small[...]
    sums = Sum(p, bits, small_o, *scr[30:33])
    p.barrier(bits)
    rows[0].start()
    in_waves([g.steps() for g in arrays], min(depth, 4))
    rows[1].start()
    close(arrays, sums)
    for r in rows:
        r.finish()
    for g in arrays + rows + [sums]:
        g.drain()


def close(arrays, sums):
    closing = [g.collect for g in arrays] + [g.finish for g in arrays]
    for step in itertools.chain(*itertools.zip_longest(sums.steps(), closing)):
        if step is not None:
            step()


def scatter_all(depth, bits, parts, small, out_s, gtok_s):
    hbm = pl.BlockSpec(memory_space=pl.ANY)
    vmem = pl.BlockSpec(memory_space=pltpu.VMEM)
    outs = [jax.ShapeDtypeStruct(s.shape[4:], jnp.float32) for s in parts]
    outs += [jax.ShapeDtypeStruct(small.shape, jnp.float32)]
    outs += [jax.ShapeDtypeStruct(out_s.shape, out_s.dtype)] * 2
    scr = []
    for s in (parts[3], parts[2], parts[1], parts[0]):
        scr += Scatter.scratch(depth, *s.shape[4:])
    scr += Exchange.sems() * 2 + Sum.scratch(bits, small.shape[0])
    return pl.pallas_call(
        functools.partial(scatter_kernel, depth, bits),
        out_shape=outs,
        in_specs=[vmem] * 5 + [hbm] * 2,
        out_specs=[vmem] * 5 + [hbm] * 2,
        scratch_shapes=scr,
        compiler_params=pltpu.CompilerParams(
            collective_id=1, has_side_effects=True, vmem_limit_bytes=60 * 2**20
        ),
        name="scatter",
    )(*parts, small, out_s, gtok_s)

SPANS = ((0, LEN_LONG), (LEN_LONG, LEN_MID), (LEN_LONG + LEN_MID, LEN_SHORT), (LEN_LONG + LEN_MID + LEN_SHORT, LEN_SHORT))
TILE = 128
QKV_PAD = 640
CTX_PAD = 256
ADAPT_PAD = 128
MASK_LOW = -1e9
NN = (((1,), (0,)), ((), ()))
NT = (((1,), (1,)), ((), ()))
TN = (((0,), (0,)), ((), ()))


def dot(a, b, dims=NN):
    return lax.dot_general(a, b, dims, preferred_element_type=jnp.float32)


def table_onehot():
    buckets = rel_buckets(257)
    offset = np.clip(256 - np.arange(512), -256, 256) + 256
    index = np.concatenate([buckets[offset], np.full(128, NB // 2 - 1), np.full(128, NB - 1)])
    return (index[:, None] == np.arange(NB)[None, :]).astype(np.float32)


def bias_tiles(row):
    spread = pltpu.roll(jnp.broadcast_to(row, (TILE, 512)), 0, 1, stride=1, stride_axis=0)
    far = [jnp.broadcast_to(row[:, at : at + 1], (TILE, TILE)) for at in (511, 0)]
    near = [spread[:, 256 - 128 * delta : 384 - 128 * delta] for delta in (-1, 0, 1)]
    return [far[0], *near, far[1]]


def diagonal_sums(tiles):
    grid = jnp.concatenate([jnp.zeros((TILE, TILE), jnp.float32), tiles[2], tiles[1], tiles[0]], axis=1)
    rows = TILE
    while rows > 8:
        rows //= 2
        grid = grid[:rows] + pltpu.roll(grid[rows:], 512 - rows, 1)
    total = grid[0:1]
    for r in range(1, 8):
        total = total + pltpu.roll(grid[r : r + 1], 512 - r, 1)
    return total


def swap_halves(tile):
    return jnp.concatenate([tile[:, DH:], tile[:, :DH]], axis=1)


def lanes_below(shape, at=DH):
    return lax.broadcasted_iota(jnp.int32, shape, len(shape) - 1) < at


def key_side(qk, mask):
    swapped = swap_halves(qk)
    return jnp.where(lanes_below(qk.shape), swapped, mask), swapped


def query_side(qk):
    lane = lax.broadcasted_iota(jnp.int32, qk.shape, 1)
    return jnp.where(lane < DH, qk, jnp.where(lane == DH, 1.0, 0.0).astype(qk.dtype))


def probabilities(keys, queries, tiles, q0, length, width):
    scores = dot(keys, queries, NT)
    blocks = []
    for kb in range(length // TILE):
        deltas = [max(-2, min(2, kb - (q0 + qi))) + 2 for qi in range(width // TILE)]
        bias = tiles[deltas[0]] if len(deltas) == 1 else jnp.concatenate([tiles[d] for d in deltas], axis=1)
        blocks.append(scores[kb * TILE : (kb + 1) * TILE] + bias)
    top = blocks[0]
    for block in blocks[1:]:
        top = jnp.maximum(top, block)
    top = jnp.max(top, axis=0, keepdims=True)
    blocks = [jnp.exp(block - top) for block in blocks]
    total = blocks[0]
    for block in blocks[1:]:
        total = total + block
    inverse = 1.0 / jnp.sum(total, axis=0, keepdims=True)
    return [block * inverse for block in blocks]


def join(blocks, axis=0):
    return blocks[0] if len(blocks) == 1 else jnp.concatenate(blocks, axis=axis)


def value_lanes(group):
    stride = group * CTX_PAD // (3 * DH)
    lane = np.arange(CTX_PAD)
    column = lane // stride * group + lane % stride
    return np.where(lane % stride < group, column // DH, -1), column


def head_runs(group):
    heads, _ = value_lanes(group)
    runs = []
    for lane in range(CTX_PAD):
        head = int(heads[lane])
        head = runs[-1][2] if head < 0 else head
        if runs and runs[-1][2] == head:
            runs[-1][1] = lane + 1
        else:
            runs.append([lane, lane + 1, head])
    return runs


def head_lanes(shape, group, head):
    lane = lax.broadcasted_iota(jnp.int32, shape, len(shape) - 1)
    inside = None
    for lo, hi, h in head_runs(group):
        if h == head:
            run = jnp.logical_and(lane >= lo, lane < hi)
            inside = run if inside is None else jnp.logical_or(inside, run)
    return inside


def no_tick(j):
    pass


def attend_group(packed, mask_ref, rows, context, group, tick=no_tick):
    tiles = [bias_tiles(rows[h : h + 1, :]) for h in range(3)]
    for number, (offset, length) in enumerate(SPANS):
        span = pl.ds(offset, length)
        mask = mask_ref[span, :]
        keys = [key_side(packed[span, h * TILE : (h + 1) * TILE], mask)[0] for h in range(3)]
        values = packed[span, 3 * TILE :].T
        width = min(length, 256)
        for q0 in range(0, length, width):
            here = pl.ds(offset + q0, width)
            outs = []
            for h in range(3):
                queries = query_side(packed[here, h * TILE : (h + 1) * TILE])
                probs = probabilities(keys[h], queries, tiles[h], q0 // TILE, length, width)
                probs = join([block.astype(jnp.bfloat16) for block in probs])
                outs.append(dot(values, probs))
            whole = jnp.concatenate([outs[h][lo:hi] for lo, hi, h in head_runs(group)], axis=0)
            context[here, :] = whole.T.astype(jnp.bfloat16)
            tick((number, q0))


def attend_group_back(packed, mask_ref, rows, grad_context, grad_packed, sums, group, tick=no_tick):
    far_shape = (TILE, TILE)
    tiles = [bias_tiles(rows[h : h + 1, :]) for h in range(3)]
    near = [[None] * 3 for _ in range(3)]
    far = [[jnp.zeros(far_shape, jnp.float32)] * 2 for _ in range(3)]
    for number, (offset, length) in enumerate(SPANS):
        span = pl.ds(offset, length)
        mask = mask_ref[span, :]
        width = min(length, 256)
        values = packed[span, 3 * TILE :]
        value_sums = {}
        for h in range(3):
            at = pl.ds(h * TILE, TILE)
            qk = packed[span, at]
            low = lanes_below(qk.shape)
            keys, swapped = key_side(qk, mask)
            upper_queries = jnp.where(low, jnp.zeros_like(qk), swapped)
            plain_keys = jnp.where(low, swapped, jnp.zeros_like(qk)).T
            grad_keys = None
            grad_queries = []
            for q0 in range(0, length, width):
                here = pl.ds(offset + q0, width)
                probs = probabilities(keys, query_side(packed[here, at]), tiles[h], q0 // TILE, length, width)
                g_tile = grad_context[here, :]
                g_tile = jnp.where(head_lanes(g_tile.shape, group, h), g_tile, jnp.zeros_like(g_tile))
                g_probs = dot(values, g_tile, NT)
                g_blocks = [g_probs[kb * TILE : (kb + 1) * TILE] for kb in range(length // TILE)]
                total = probs[0] * g_blocks[0]
                for kb in range(1, length // TILE):
                    total = total + probs[kb] * g_blocks[kb]
                centre = jnp.sum(total, axis=0, keepdims=True)
                low_probs = join([block.astype(jnp.bfloat16) for block in probs])
                g_scores = [(a * (g - centre)).astype(jnp.bfloat16) for a, g in zip(probs, g_blocks)]
                for kb, block in enumerate(g_scores):
                    wide = block.astype(jnp.float32)
                    for qi in range(width // TILE):
                        piece = wide[:, qi * TILE : (qi + 1) * TILE]
                        delta = kb - (q0 // TILE + qi)
                        if abs(delta) <= 1:
                            held = near[h][delta + 1]
                            near[h][delta + 1] = piece if held is None else held + piece
                        else:
                            side = 0 if delta < 0 else 1
                            far[h][side] = far[h][side] + piece
                g_scores = join(g_scores)
                g_v = dot(low_probs, g_tile)
                if q0 not in value_sums:
                    value_sums[q0] = g_v
                else:
                    value_sums[q0] = value_sums[q0] + g_v
                g_k = dot(g_scores, upper_queries[q0 : q0 + width])
                grad_keys = g_k if grad_keys is None else grad_keys + g_k
                grad_queries.append(dot(plain_keys, g_scores).T)
            grad_packed[span, at] = (join(grad_queries) + grad_keys).astype(jnp.bfloat16)
            tick(3 * number + h)
        grad_packed[span, 3 * TILE :] = functools.reduce(jnp.add, value_sums.values()).astype(jnp.bfloat16)
    for h in range(3):
        sums[h : h + 1, :512] = diagonal_sums(near[h])
        for side in range(2):
            sums[h : h + 1, 512 + side * TILE : 640 + side * TILE] = jnp.sum(far[h][side], axis=0, keepdims=True)


def attention_kernel(group, x_ref, gain, w_ref, mask, rows, normed_out, packed, context):
    @pl.when(pl.program_id(0) == 0)
    def _():
        x = x_ref[...].astype(jnp.float32)
        scale = lax.rsqrt(jnp.mean(x * x, axis=-1, keepdims=True) + NORM_EPS)
        normed_out[...] = (x * scale * gain[...]).astype(jnp.bfloat16)

    packed[0] = dot(normed_out[...], w_ref[0]).astype(jnp.bfloat16)
    attend_group(packed.at[0], mask, rows[0], context.at[0], group)


def attention(x, gain, w, mask, rows, group):
    n = x.shape[0]
    bf = jnp.bfloat16
    return pl.pallas_call(
        functools.partial(attention_kernel, group),
        grid=(4,),
        out_shape=[
            jax.ShapeDtypeStruct((n, D), bf),
            jax.ShapeDtypeStruct((4, n, QKV_PAD), bf),
            jax.ShapeDtypeStruct((4, n, CTX_PAD), bf),
        ],
        in_specs=[
            pl.BlockSpec((n, D), lambda i: (0, 0)),
            pl.BlockSpec((1, D), lambda i: (0, 0)),
            pl.BlockSpec((1, D, QKV_PAD), lambda i: (i, 0, 0)),
            pl.BlockSpec((n, TILE), lambda i: (0, 0)),
            pl.BlockSpec((1, 3, 512), lambda i: (i, 0, 0)),
        ],
        out_specs=[
            pl.BlockSpec((n, D), lambda i: (0, 0)),
            pl.BlockSpec((1, n, QKV_PAD), lambda i: (i, 0, 0)),
            pl.BlockSpec((1, n, CTX_PAD), lambda i: (i, 0, 0)),
        ],
        compiler_params=pltpu.CompilerParams(vmem_limit_bytes=56 * 2**20),
        name="attention",
    )(x, gain, w, mask, rows)


def attention_back_kernel(group, packed, grad_context, mask, rows, grad_packed, sums):
    attend_group_back(packed.at[0], mask, rows[0], grad_context.at[0], grad_packed.at[0], sums.at[0], group)


def attention_back(packed, grad_context, mask, rows, group):
    n = packed.shape[1]
    return pl.pallas_call(
        functools.partial(attention_back_kernel, group),
        grid=(4,),
        out_shape=[
            jax.ShapeDtypeStruct((4, n, QKV_PAD), jnp.bfloat16),
            jax.ShapeDtypeStruct((4, 3, 768), jnp.float32),
        ],
        in_specs=[
            pl.BlockSpec((1, n, QKV_PAD), lambda i: (i, 0, 0)),
            pl.BlockSpec((1, n, CTX_PAD), lambda i: (i, 0, 0)),
            pl.BlockSpec((n, TILE), lambda i: (0, 0)),
            pl.BlockSpec((1, 3, 512), lambda i: (i, 0, 0)),
        ],
        out_specs=[
            pl.BlockSpec((1, n, QKV_PAD), lambda i: (i, 0, 0)),
            pl.BlockSpec((1, 3, 768), lambda i: (i, 0, 0)),
        ],
        compiler_params=pltpu.CompilerParams(vmem_limit_bytes=56 * 2**20),
        name="attention_back",
    )(packed, grad_context, mask, rows)


def head_columns(w, group):
    n = w.shape[0]
    qk = w[:, :, : 2 * DH].reshape(n, 6 * DH)
    v = w[:, :, 2 * DH :].reshape(n, 3 * DH // group, group)
    v = jnp.pad(v, ((0, 0), (0, 0), (0, group // 3))).reshape(n, CTX_PAD)
    return jnp.concatenate([qk, v], axis=1)


def key_mask(live):
    lane = jnp.arange(TILE)[None, :]
    return jnp.where((lane == DH) & ~live[:, None], MASK_LOW, 0.0).astype(jnp.bfloat16)


def precise(a, b, dims=NN):
    return lax.dot_general(a, b, dims, precision=FULL_PRECISION, preferred_element_type=jnp.float32)


def offset_onehot():
    buckets = rel_buckets(257)
    offset = np.clip(256 - np.arange(512), -256, 256) + 256
    return (np.arange(NB)[:, None] == buckets[offset][None, :]).astype(np.float32)


def column_choice(group):
    choice = np.zeros((9 * DH, QKV_PAD), np.float32)
    for h in range(3):
        for k in range(2 * DH):
            choice[3 * DH * h + k, TILE * h + k] = 1
    heads, column = value_lanes(group)
    for lane in range(CTX_PAD):
        if heads[lane] >= 0:
            choice[3 * DH * heads[lane] + 2 * DH + column[lane] % DH, 3 * TILE + lane] = 1
    return choice


def own_length(lengths, member, number):
    at = (member, 4 + member // 2 + 2 * (member % 2), 8 + member, 12 + member)[number]
    return lengths[at]


def fill_mask(mask, lengths, member):
    for number, (offset, length) in enumerate(SPANS):
        row = lax.broadcasted_iota(jnp.int32, (length, TILE), 0)
        lane = lax.broadcasted_iota(jnp.int32, (length, TILE), 1)
        dead = jnp.logical_and(row >= own_length(lengths, member, number), lane == DH)
        mask[offset : offset + length, :] = jnp.where(dead, MASK_LOW, 0.0).astype(jnp.bfloat16)


def fill_rows(rows, pos_table, onehot):
    table = precise(pos_table[...], onehot[...])
    for m in range(4):
        rows[m] = table[3 * m : 3 * m + 3, :]


KA = ADAPT // KRON


def adapter_constants():
    i, b = np.arange(16) // 4, np.arange(16) % 4
    same = (np.arange(4)[:, None] == i[None, :]).astype(np.float32)
    pick = np.zeros((4, 4, 16), np.float32)
    pick[i, b, np.arange(16)] = 1
    fold = np.zeros((ADAPT_PAD, KA), np.float32)
    fold[np.arange(ADAPT), np.arange(ADAPT) % KA] = 1
    agree = np.zeros((ADAPT_PAD, 16), np.float32)
    agree[:ADAPT] = np.arange(ADAPT)[:, None] // KA == b[None, :]
    return same, pick, fold, agree


class Factor:
    def __init__(self, rules, tall, short, consts):
        self.same, _, self.fold, self.agree = consts
        spread = precise(tall, self.same, TN)
        self.tall = jnp.concatenate([spread] * KRON, axis=0)
        rows = spread.shape[0]
        self.rules = jnp.concatenate(
            [jnp.broadcast_to(rules[a : a + 1, :], (rows, 16)) for a in range(KRON)], axis=0
        )
        self.short = precise(self.fold, precise(short, self.same, TN)) * self.agree

    def whole(self):
        return precise(self.rules * self.tall, self.short, NT)

    def back(self, grad):
        wide = precise(grad, self.short)
        rows = wide.shape[0] // KRON
        tall = wide * self.rules
        tall = sum(tall[a * rows : (a + 1) * rows] for a in range(KRON))
        rules = wide * self.tall
        rules = [jnp.sum(rules[a * rows : (a + 1) * rows], axis=0, keepdims=True) for a in range(KRON)]
        short = precise(self.rules * self.tall, grad, TN) * self.agree.T
        short = precise(precise(self.same, short), self.fold)
        return jnp.concatenate(rules, axis=0), precise(self.same, tall, NT), short


def rule_tables(rules, pick):
    return [sum(precise(rules[i], pick[i], dims) for i in range(KRON)) for dims in (NN, TN)]


ROW_GAIN, ROW_TABLE, ROW_OTHER = 0, 8, 24
ROW_FFN, ROW_DL, ROW_UR, ROW_DR, ROW_UL, ROW_RULES, ROW_END = 0, 8, 16, 24, 28, 32, 48


def put_row(ref, at, row):
    for k in range(row.shape[1] // 128):
        ref[at + k : at + k + 1, :] = row[:, 128 * k : 128 * (k + 1)]


FCH = 768
RCH = 256


def gelu_both(v):
    phi = 0.5 + 0.5 * lax.erf(v * np.float32(np.sqrt(0.5)))
    return v * phi, phi + v * (jnp.exp(-0.5 * v * v) * np.float32(1.0 / np.sqrt(2.0 * np.pi)))


def rows_of(i, size=RCH):
    return pl.ds(pl.multiple_of(i * size, size), size)


def each_of(count, body):
    lax.fori_loop(0, count, lambda i, carry: (body(i), carry)[1], 0)


class Layer:
    def __init__(self, **refs):
        self.__dict__.update(refs)
        self.n = self.n2.shape[0]

    def midway(self, i):
        r = rows_of(i)
        total = self.x_rows(i)
        for m in range(4):
            total = total + dot(self.ctx[m, r, :], self.wo(m))
        self.mid[r, :] = total
        scale = lax.rsqrt(jnp.mean(total * total, axis=-1, keepdims=True) + NORM_EPS)
        self.n2[r, :] = (total * scale * self.gain[...]).astype(jnp.bfloat16)

    def forward(self, j):
        f = rows_of(j, self.chunk)
        for half in range(2):
            r = pl.ds(half * (self.n // 2), self.n // 2)
            value, slope = gelu_both(dot(self.n2[r, :], self.wi(j), NT))
            value = value.astype(jnp.bfloat16)
            self.act[r, f] = value
            self.dg[r, f] = slope.astype(jnp.bfloat16)
            self.acc[r, :] += dot(value, self.wu(j))

    def factors(self):
        consts = [c[...] for c in self.consts]
        by_a, by_b = rule_tables(self.rules, consts[1])
        d_left, d_right, u_left, u_right = self.sides
        return (
            Factor(by_a, d_left[...], d_right[...], consts),
            Factor(by_b, u_right[...], u_left[...], consts),
        )

    def prepare(self, member):
        down, up = self.factors()
        self.down[...] = down.whole().astype(jnp.bfloat16)
        self.up[...] = up.whole().astype(jnp.bfloat16)
        for number, (offset, length) in enumerate(SPANS):
            row = lax.broadcasted_iota(jnp.int32, (length, 1), 0)
            alive = row < own_length(self.lengths, member, number)
            self.live[offset : offset + length, :] = jnp.where(alive, 1.0, 0.0)

    def adapter(self, i):
        bf = jnp.bfloat16
        r = rows_of(i)
        ffn = self.acc[r, :]
        low = ffn.astype(bf)
        value, slope = gelu_both(dot(low, self.down[...]))
        value = value.astype(bf)
        self.res[r, :] = (self.mid[r, :] + ffn + dot(value, self.up[...], NT)).astype(bf)
        g_out = self.cot_rows(i) * self.live[r, :]
        g_low = g_out.astype(bf)
        self.gout[r, :] = g_low
        g_sq = (dot(g_low, self.up[...]) * slope).astype(bf)
        self.g_up[...] += dot(g_low, value, TN)
        self.g_down[...] += dot(low, g_sq, TN)
        self.gffn[r, :] = (g_out + dot(g_sq, self.down[...], NT)).astype(bf)

    def backward(self, j):
        bf = jnp.bfloat16
        f = rows_of(j, self.chunk)
        for half in range(2):
            r = pl.ds(half * (self.n // 2), self.n // 2)
            g = (dot(self.gffn[r, :], self.wu(j), NT) * self.dg[r, f].astype(jnp.float32)).astype(bf)
            self.dg[r, f] = g
            self.acc[r, :] += dot(g, self.wi(j))
        self.act[: self.chunk, f] = dot(self.act[:, f], self.gffn[...], TN).astype(bf)
        self.dg[: self.chunk, f] = dot(self.dg[:, f], self.n2[...], TN).astype(bf)
        for store in self.stores(j):
            store.start()

    def stores(self, j):
        f = rows_of(j, self.chunk)
        return [
            pltpu.make_async_copy(src.at[pl.ds(0, self.chunk), f], dst.at[f], self.sem.at[k, j])
            for k, (src, dst) in enumerate(((self.act, self.gu_hbm), (self.dg, self.gi_hbm)))
        ]

    def last(self, i):
        r = rows_of(i)
        total = self.mid[r, :]
        g_n2 = self.acc[r, :]
        scale = lax.rsqrt(jnp.mean(total * total, axis=-1, keepdims=True) + NORM_EPS)
        self.g_gain[...] += jnp.sum(total * scale * g_n2, axis=0, keepdims=True)
        scaled = self.gain[...] * g_n2
        centre = jnp.mean(total * scaled, axis=-1, keepdims=True)
        g_mid = self.gout[r, :].astype(jnp.float32) + scale * scaled - total * (scale * scale * scale * centre)
        self.mid[r, :] = g_mid
        self.glow[r, :] = g_mid.astype(jnp.bfloat16)

    def rest(self, out_sems):
        n, bf = self.n, jnp.bfloat16
        self.g_down[...] = jnp.zeros_like(self.g_down)
        self.g_up[...] = jnp.zeros_like(self.g_up)
        self.g_gain[...] = jnp.zeros_like(self.g_gain)
        each_of(n // RCH, self.adapter)
        copies = [pltpu.make_async_copy(self.res, self.res_hbm, out_sems.at[0])]
        copies[0].start()
        self.acc[...] = jnp.zeros_like(self.acc)
        each_of(self.count, self.backward)
        each_of(n // RCH, self.last)
        copies.append(pltpu.make_async_copy(self.mid, self.gmid_hbm, out_sems.at[1]))
        copies[1].start()
        for m in range(4):
            rows = slice(CTX_PAD * m, CTX_PAD * (m + 1))
            self.gffn[rows, :] = dot(self.ctx[m], self.glow[...], TN).astype(bf)
            self.ctx[m] = dot(self.glow[...], self.wo(m), NT).astype(bf)
        copies.append(pltpu.make_async_copy(self.gffn, self.go_hbm, out_sems.at[2]))
        copies.append(pltpu.make_async_copy(self.ctx, self.gctx_hbm, out_sems.at[3]))
        for copy in copies[2:]:
            copy.start()
        self.small_grads()
        each_of(self.count, lambda j: [store.wait() for store in self.stores(j)])
        for copy in copies:
            copy.wait()

    def small_grads(self):
        other, pick = self.other, self.consts[1]
        down, up = self.factors()
        g_a, g_dl, g_dr = down.back(self.g_down[...])
        g_b, g_ur, g_ul = up.back(self.g_up[...])
        other[...] = jnp.zeros_like(other)
        put_row(other, ROW_FFN, self.g_gain[...])
        for at, tall in ((ROW_DL, g_dl), (ROW_UR, g_ur)):
            other[at : at + 4, :] = tall[:, :128]
            other[at + 4 : at + 8, : tall.shape[1] - 128] = tall[:, 128:]
        for at, short in ((ROW_DR, g_dr), (ROW_UL, g_ul)):
            other[at : at + 4, :KA] = short
        for i in range(KRON):
            at = ROW_RULES + 4 * i
            other[at : at + 4, :KRON] = precise(g_a, pick[i], NT) + precise(pick[i], g_b, NT)


def middle_kernel(
    x_hbm, ctx_hbm, wo_hbm, wi_hbm, wu_hbm, cot_hbm, gain, lengths, rules, d_left, d_right, u_left, u_right,
    same, pick, fold, agree,
    res_hbm, gmid_hbm, gctx_hbm, go_hbm, gi_hbm, gu_hbm, other,
    down, up, g_down, g_up, g_gain, live, x, ctx, wo, wi, wu, cot, mid, n2, act, dg, acc, gffn, glow, sem, sems, out_sems,
):
    loads = [
        pltpu.make_async_copy(src, dst, sems.at[i])
        for i, (src, dst) in enumerate(
            ((x_hbm, x), (ctx_hbm, ctx), (wo_hbm, wo), (wi_hbm, wi), (wu_hbm, wu), (cot_hbm, cot))
        )
    ]
    for load in loads:
        load.start()
    layer = Layer(
        x_rows=lambda i: x[rows_of(i), :].astype(jnp.float32), cot_rows=lambda i: cot[rows_of(i), :].astype(jnp.float32),
        wo=lambda m: wo[m], wi=lambda j: wi[rows_of(j, FCH), :], wu=lambda j: wu[rows_of(j, FCH), :],
        chunk=FCH, count=wi.shape[0] // FCH, ctx=ctx, gain=gain, lengths=lengths, rules=rules,
        sides=(d_left, d_right, u_left, u_right), consts=(same, pick, fold, agree), down=down, up=up, g_down=g_down,
        g_up=g_up, g_gain=g_gain, live=live, mid=mid, n2=n2, act=act, dg=dg, acc=acc, gffn=gffn, glow=glow, res=x,
        gout=cot, other=other, sem=sem, res_hbm=res_hbm, gmid_hbm=gmid_hbm, gctx_hbm=gctx_hbm, go_hbm=go_hbm,
        gi_hbm=gi_hbm, gu_hbm=gu_hbm,
    )
    layer.prepare(lax.axis_index("mp"))
    for load in loads:
        load.wait()
    each_of(layer.n // RCH, layer.midway)
    acc[...] = jnp.zeros_like(acc)
    each_of(layer.count, layer.forward)
    layer.rest(out_sems)


def middle(x, ctx, wo, wi, wu, cot, gain, lengths, factors):
    n, ff = x.shape[0], wi.shape[0]
    bf, f32 = jnp.bfloat16, jnp.float32
    hbm = pl.BlockSpec(memory_space=pl.ANY)
    vmem = pl.BlockSpec(memory_space=pltpu.VMEM)
    shape = jax.ShapeDtypeStruct
    return pl.pallas_call(
        middle_kernel,
        out_shape=[
            shape((n, D), bf),
            shape((n, D), f32),
            shape((4, n, CTX_PAD), bf),
            shape((4 * CTX_PAD, D), bf),
            shape((ff, D), bf),
            shape((ff, D), bf),
            shape((ROW_END, 128), f32),
        ],
        in_specs=[hbm] * 6 + [vmem] + [pl.BlockSpec(memory_space=pltpu.SMEM)] + [vmem] * 9,
        out_specs=[hbm] * 6 + [vmem],
        scratch_shapes=[
            pltpu.VMEM((D, ADAPT_PAD), bf),
            pltpu.VMEM((D, ADAPT_PAD), bf),
            pltpu.VMEM((D, ADAPT_PAD), f32),
            pltpu.VMEM((D, ADAPT_PAD), f32),
            pltpu.VMEM((1, D), f32),
            pltpu.VMEM((n, 1), f32),
            pltpu.VMEM((n, D), bf),
            pltpu.VMEM((4, n, CTX_PAD), bf),
            pltpu.VMEM((4, CTX_PAD, D), bf),
            pltpu.VMEM((ff, D), bf),
            pltpu.VMEM((ff, D), bf),
            pltpu.VMEM((n, D), bf),
            pltpu.VMEM((n, D), f32),
            pltpu.VMEM((n, D), bf),
            pltpu.VMEM((n, ff), bf),
            pltpu.VMEM((n, ff), bf),
            pltpu.VMEM((n, D), f32),
            pltpu.VMEM((n, D), bf),
            pltpu.VMEM((n, D), bf),
            pltpu.SemaphoreType.DMA((2, ff // FCH)),
            pltpu.SemaphoreType.DMA((6,)),
            pltpu.SemaphoreType.DMA((4,)),
        ],
        compiler_params=pltpu.CompilerParams(vmem_limit_bytes=63 * 2**20),
        name="middle",
    )(x, ctx, wo, wi, wu, cot, gain, lengths, *factors, *map(jnp.asarray, adapter_constants()))


class Slots:
    def __init__(self, places, timed):
        self.at = {}
        times = sorted(places.items(), key=lambda item: item[1])
        for when, step in sorted(timed, key=lambda item: item[0]):
            place = next((name for name, t in times if t >= when), None)
            self.at.setdefault(place, []).append(step)

    def run(self, place):
        for step in self.at.pop(place, ()):
            step()

    def tick(self, i, j):
        for place in sorted(name for name in self.at if name is not None and name[1] == j):
            pl.when(i == place[0])(functools.partial(self.run, place))


FRONT = (
    "s:o s:q s:i a:o0",
    "ex0 a:q0 a:i0 a:q1",
    "n c:o0 c:q0 a:o1",
    "a:q2 s:u c:q1 c:q2",
    "a:o2 a:q3 c:q3 a:i1",
    "a:u0 c:o1 f:q c:i0",
    "c:o2 A A A",
    "a:o3 ex1 A A",
    "A a:u1 A A",
    "c:o3 c:i1 A A",
    "A a:i2 A A",
    "A A a:u2 c:u0",
    "A f:o O a:i3",
    "c:u1 F0 a:u3 c:i2",
    "c:u2 F1 c:i3 c:u3",
    "F2 F3",
)


def front_order():
    plan, now = {"first": []}, "first"
    pieces = 0
    for step in " ".join(FRONT).split():
        if step == "A":
            now, pieces = ("A", pieces), pieces + 1
        elif step[0] in "OF":
            plan["before", step] = plan.pop("open", [])
            now = "open"
        else:
            plan.setdefault(now, []).append(step)
    return plan


def front_kernel(
    depth, group, tok, cot, w_qkv, w_o, w_in, w_out, choice, gain, gain_ffn, lengths, pos_table, onehot,
    rules, d_left, d_right, u_left, u_right, same, pick, fold, agree,
    tok_s, gq_hbm, normed_hbm, packed_hbm, res_hbm, gmid_hbm, gctx_hbm, go_hbm, gi_hbm, gu_hbm, other,
    wq, wo, wi, wu, mask, rows, x, y, gq, go, gi, gu, nrm, packed, ctx,
    down, up, g_down, g_up, g_gain, live, mid, n2, act, dg, acc, gffn, res, glow, sem, out_sems, local, *sems,
):
    p = Place(depth)
    bf = jnp.bfloat16
    per_head = [dot(w_qkv[h].astype(bf), choice[3 * DH * h : 3 * DH * (h + 1), :]) for h in range(3)]
    wq[...] = sum(per_head).astype(bf)
    wo[...] = jnp.zeros_like(wo)
    wo[: w_o.shape[0], :] = w_o[...].astype(bf)
    wi[...] = w_in[...].astype(bf)
    wu[...] = w_out[...].astype(bf)
    arrays = {
        name: Gather(p, name == "q", shard, buf, *sems[3 * i : 3 * i + 3])
        for i, (name, shard, buf) in enumerate((("q", wq, gq), ("o", wo, go), ("i", wi, gi), ("u", wu, gu)))
    }
    first, second = Exchange(p, tok, x, *sems[12:15]), Exchange(p, cot, y, *sems[15:18])
    keep_x = pltpu.make_async_copy(x, tok_s, local.at[0])
    keep_n = pltpu.make_async_copy(nrm, normed_hbm, local.at[1])
    keep_q = pltpu.make_async_copy(gq, gq_hbm, local.at[2])
    quarter = RCH // SEG

    def float_rows(ref):
        return lambda i: ref[pl.ds(quarter * i, quarter)].reshape(RCH, D).astype(jnp.float32)

    layer = Layer(
        x_rows=float_rows(x), cot_rows=float_rows(y),
        wo=lambda m: go[m].reshape(CTX_PAD, D), wi=lambda j: gi[j].reshape(-1, D), wu=lambda j: gu[j].reshape(-1, D),
        chunk=8 * wi.shape[0], count=depth, ctx=ctx, gain=gain_ffn, lengths=lengths, rules=rules,
        sides=(d_left, d_right, u_left, u_right), consts=(same, pick, fold, agree), down=down, up=up, g_down=g_down,
        g_up=g_up, g_gain=g_gain, live=live, mid=mid, n2=n2, act=act, dg=dg, acc=acc, gffn=gffn, glow=glow, res=res,
        gout=nrm, other=other, sem=sem, res_hbm=res_hbm, gmid_hbm=gmid_hbm, gctx_hbm=gctx_hbm, go_hbm=go_hbm,
        gi_hbm=gi_hbm, gu_hbm=gu_hbm,
    )

    def norm(i):
        v = x[i].astype(jnp.float32)
        scale = lax.rsqrt(jnp.mean(v * v, axis=-1, keepdims=True) + NORM_EPS)
        nrm[rows_of(i, SEG), :] = (v * scale * gain[...]).astype(bf)

    def norms():
        first.finish()
        keep_x.start()
        each_of(x.shape[0], norm)
        keep_n.start()
        fill_mask(mask, lengths, p.m)
        fill_rows(rows, pos_table, onehot)
        layer.prepare(p.m)
        acc[...] = jnp.zeros_like(acc)

    def step(name):
        kind, rest = name[0], name[2:]
        if name == "n":
            norms()
        elif name in ("ex0", "ex1"):
            (first, second)[int(name[2])].start()
        elif kind == "s":
            arrays[rest].start()
        elif kind == "f":
            arrays[rest].finish()
        elif kind == "a":
            arrays[rest[0]].along(int(rest[1:]))
        elif kind == "c":
            arrays[rest[0]].across(int(rest[1:]))

    def steps(names):
        for name in names:
            step(name)

    plan = front_order()
    p.barrier(0)
    steps(plan["first"])
    keep_q.start()

    def piece(m, place):
        number, q0 = place
        at = {(0, 0): 0, (0, 256): 1, (1, 0): 2, (3, 0): 3}.get(place)
        if at is not None:
            for loop in range(4):
                names = plan.get(("A", 4 * loop + at))
                if names:
                    pl.when(m == loop)(functools.partial(steps, names))

    def keep(m):
        return pltpu.make_async_copy(packed.at[m], packed_hbm.at[m], local.at[3 + m])

    def heads(m):
        w = gq[m // 2, m % 2].reshape(D, QKV_PAD)
        packed[m] = dot(nrm[...], w).astype(bf)
        keep(m).start()
        attend_group(packed.at[m], mask, rows[m], ctx.at[m], group, functools.partial(piece, m))

    each_of(4, heads)
    steps(plan[("before", "O")])
    each_of(layer.n // RCH, layer.midway)

    def chunk(e):
        for k in range(depth):
            pl.when(e == k)(functools.partial(steps, plan[("before", f"F{k}")]))
        z = p.nearest(e)
        for name in "iu":
            arrays[name].finish_at(z)
        layer.forward(z)

    each_of(depth, chunk)
    second.finish()
    for copy in [keep_x, keep_n, keep_q] + [keep(m) for m in range(4)]:
        copy.wait()
    layer.rest(out_sems)
    for g in (*arrays.values(), first, second):
        g.drain()


def front(depth, group, tok, cot, shards, rows_of_shards, gains, lengths, pos_table, factors):
    hbm = pl.BlockSpec(memory_space=pl.ANY)
    vmem = pl.BlockSpec(memory_space=pltpu.VMEM)
    bf, f32 = jnp.bfloat16, jnp.float32
    shape = jax.ShapeDtypeStruct
    n = tok.shape[0] * SEG
    kept = [(rows, QKV_PAD if i == 0 else D) for i, rows in enumerate(rows_of_shards)]
    whole = [((2, 2, depth, 2) if i == 0 else (depth, 2, 2, 2)) + s for i, s in enumerate(kept)]
    ff = 8 * depth * kept[2][0]
    return pl.pallas_call(
        functools.partial(front_kernel, depth, group),
        out_shape=[
            shape(tok.shape, bf),
            shape(whole[0], bf),
            shape((n, D), bf),
            shape((4, n, QKV_PAD), bf),
            shape((n, D), bf),
            shape((n, D), f32),
            shape((4, n, CTX_PAD), bf),
            shape((4 * CTX_PAD, D), bf),
            shape((ff, D), bf),
            shape((ff, D), bf),
            shape((ROW_END, 128), f32),
        ],
        in_specs=[hbm] * 2 + [vmem] * 7 + [pl.BlockSpec(memory_space=pltpu.SMEM)] + [vmem] * 11,
        out_specs=[hbm] * 10 + [vmem],
        scratch_shapes=[pltpu.VMEM(s, bf) for s in kept]
        + [
            pltpu.VMEM((n, TILE), bf),
            pltpu.VMEM((4, 3, 512), f32),
            pltpu.VMEM(tok.shape, bf),
            pltpu.VMEM(tok.shape, bf),
            *[pltpu.VMEM(s, bf) for s in whole],
            pltpu.VMEM((n, D), bf),
            pltpu.VMEM((4, n, QKV_PAD), bf),
            pltpu.VMEM((4, n, CTX_PAD), bf),
            pltpu.VMEM((D, ADAPT_PAD), bf),
            pltpu.VMEM((D, ADAPT_PAD), bf),
            pltpu.VMEM((D, ADAPT_PAD), f32),
            pltpu.VMEM((D, ADAPT_PAD), f32),
            pltpu.VMEM((1, D), f32),
            pltpu.VMEM((n, 1), f32),
            pltpu.VMEM((n, D), f32),
            pltpu.VMEM((n, D), bf),
            pltpu.VMEM((n, ff), bf),
            pltpu.VMEM((n, ff), bf),
            pltpu.VMEM((n, D), f32),
            pltpu.VMEM((n, D), bf),
            pltpu.VMEM((n, D), bf),
            pltpu.VMEM((n, D), bf),
            pltpu.SemaphoreType.DMA((2, depth)),
            pltpu.SemaphoreType.DMA((4,)),
            pltpu.SemaphoreType.DMA((7,)),
        ]
        + Gather.sems(depth) * 4
        + Exchange.sems() * 2,
        compiler_params=pltpu.CompilerParams(
            collective_id=2, has_side_effects=True, vmem_limit_bytes=63 * 2**20
        ),
        name="front",
    )(
        tok, cot, *shards, jnp.asarray(column_choice(group), bf), *gains, lengths, pos_table,
        jnp.asarray(offset_onehot()), *factors, *map(jnp.asarray, adapter_constants()),
    )


def back_kernel(
    depth, bits, group,
    packed_hbm, gctx_hbm, gq_hbm, nrm_hbm, x_hbm, gmid_hbm, pu, pi, po, out_s, gain, lengths, pos_table, spread, onehot, other,
    oq, oo, oi, ou, small, out, gtok,
    mask, rows, packed, gctx, gq, nrm, x, gmid, acc, sums_s, part_q, gtok_s, res, local, mine_u, mine_i, mine_o, sem_u, sem_i, sem_o, *scr,
):
    p = Place(depth)
    n = depth
    bf = jnp.bfloat16
    u = Scatter(p, False, pu, ou, *scr[0:6], mine_u, sem_u)
    i_ = Scatter(p, False, pi, oi, *scr[6:12], mine_i, sem_i)
    o = Scatter(p, False, po, oo, *scr[12:18], mine_o, sem_o)
    q = Scatter(p, True, part_q, oq, *scr[18:24])
    arrays = [u, i_, o, q]
    row_out, row_g = Exchange(p, res, out, *scr[24:27]), Exchange(p, gtok_s, gtok, *scr[27:30])
    total = Sum(p, bits, small, *scr[30:33])
    heads_in = [
        [
            pltpu.make_async_copy(packed_hbm.at[m], packed.at[m], local.at[m]),
            pltpu.make_async_copy(gctx_hbm.at[m], gctx.at[m], local.at[4 + m]),
        ]
        for m in range(4)
    ]
    others_in = [
        pltpu.make_async_copy(src, dst, local.at[8 + k])
        for k, (src, dst) in enumerate(((nrm_hbm, nrm), (gq_hbm, gq), (x_hbm, x), (gmid_hbm, gmid), (out_s, res)))
    ]
    for copy in heads_in[0]:
        copy.start()
    p.barrier(bits)
    for g in (u, i_):
        for k in range(n):
            g.start(k)
    for copy in others_in:
        copy.start()
    for copies in heads_in[1:]:
        for copy in copies:
            copy.start()
    for k in range(n):
        o.start(k)
    small[...] = jnp.zeros_like(small)
    small[ROW_OTHER:, :] = other[...]
    acc[...] = jnp.zeros_like(acc)
    fill_mask(mask, lengths, p.m)
    fill_rows(rows, pos_table, spread)
    for copies in heads_in:
        for copy in copies:
            copy.wait()
    for copy in others_in:
        copy.wait()
    row_out.start()

    span = 10.0
    places = {(m, j): span * m + 0.63 * (j + 1) for m in range(4) for j in range(12)}
    places |= {(m, 12): span * (m + 1) for m in range(4)}
    timed = []
    for g, half, quarter, ahead in ((u, 0.6, 6.0, 14.0), (i_, 5.0, 18.0, 30.0), (o, 11.0, 27.0, 39.0)):
        for k in range(n):
            timed.append((half + 1.3 * k, functools.partial(g.to_half, k)))
            timed.append((quarter + 3.0 * k, functools.partial(lambda g, k: (g.to_quarter(k), g.origin(k)), g, k)))
            timed.append((ahead + 4.0 * k, functools.partial(g.forward, k)))
    slots = Slots(places, timed)

    def heads(m):
        tick = functools.partial(slots.tick, m)
        attend_group_back(packed.at[m], mask, rows[m], gctx.at[m], packed.at[m], sums_s.at[m], group, tick)
        g = packed[m]
        for y in range(2):
            for c in range(2):
                pl.when(m == 2 * y + c)(functools.partial(weight_part, y, c))
        acc[...] += dot(g, gq[m // 2, m % 2].reshape(D, QKV_PAD), NT)
        tick(12)

    def weight_part(y, c):
        g = dot(nrm[...], packed[2 * y + c], TN).astype(bf)
        part_q[y, c] = g.reshape(part_q.shape[2:])

    each_of(4, heads)
    for k in range(n):
        q.start(k)
    slots.run(None)
    small[ROW_TABLE : ROW_TABLE + 16, :] = jnp.zeros((16, 128), jnp.float32)
    for m in range(4):
        small[ROW_TABLE + 3 * m : ROW_TABLE + 3 * m + 3, :] = lax.dot_general(
            sums_s[m], onehot[...], NN, precision=FULL_PRECISION, preferred_element_type=jnp.float32
        )

    def last(s, g_gain):
        r = rows_of(s, SEG)
        v = x[s].astype(jnp.float32)
        g_n1 = acc[r, :]
        scale = lax.rsqrt(jnp.mean(v * v, axis=-1, keepdims=True) + NORM_EPS)
        scaled = gain[...] * g_n1
        centre = jnp.mean(v * scaled, axis=-1, keepdims=True)
        gtok_s[s] = (gmid[r, :] + scale * scaled - v * (scale * scale * scale * centre)).astype(bf)
        return g_gain + jnp.sum(v * scale * g_n1, axis=0, keepdims=True)

    g_gain = lax.fori_loop(0, x.shape[0], last, jnp.zeros((1, D), jnp.float32))
    put_row(small, ROW_GAIN, g_gain)
    for k in range(n):
        q.to_half(k)
    row_g.start()
    for k in range(n):
        q.to_quarter(k)
        q.origin(k)
    for k in range(n):
        q.forward(k)
    close(arrays, total)
    for r in (row_out, row_g):
        r.finish()
    for g in arrays + [row_out, row_g, total]:
        g.drain()


def back(depth, bits, group, packed, gctx, gq, nrm, x, gmid, parts, out_s, gain, lengths, pos_table, onehot, other):
    hbm = pl.BlockSpec(memory_space=pl.ANY)
    vmem = pl.BlockSpec(memory_space=pltpu.VMEM)
    bf, f32 = jnp.bfloat16, jnp.float32
    pq_shape = gq.shape
    shape = jax.ShapeDtypeStruct
    small_rows = ROW_OTHER + other.shape[0]
    outs = [shape(pq_shape[4:], f32)] + [shape(s.shape[4:], f32) for s in (parts[2], parts[1], parts[0])]
    outs += [shape((small_rows, 128), f32), shape(out_s.shape, bf), shape(x.shape, bf)]
    dma = pltpu.SemaphoreType.DMA
    scratch = [
        pltpu.VMEM((nrm.shape[0], TILE), bf),
        pltpu.VMEM((4, 3, 512), f32),
        pltpu.VMEM(packed.shape, bf),
        pltpu.VMEM(gctx.shape, bf),
        pltpu.VMEM(gq.shape, bf),
        pltpu.VMEM(nrm.shape, bf),
        pltpu.VMEM(x.shape, bf),
        pltpu.VMEM(gmid.shape, f32),
        pltpu.VMEM(gmid.shape, f32),
        pltpu.VMEM((4, 3, 768), f32),
        pltpu.VMEM(pq_shape, bf),
        pltpu.VMEM(x.shape, bf),
        pltpu.VMEM(x.shape, bf),
        dma((13,)),
    ]
    scratch += [pltpu.VMEM((depth, 2, 2) + s.shape[4:], bf) for s in parts]
    scratch += [dma((depth,))] * 3
    for s in (*(s.shape for s in parts), pq_shape):
        scratch += Scatter.scratch(depth, *s[4:])
    scratch += Exchange.sems() * 2 + Sum.scratch(bits, small_rows)
    return pl.pallas_call(
        functools.partial(back_kernel, depth, bits, group),
        out_shape=outs,
        in_specs=[hbm] * 10 + [vmem] + [pl.BlockSpec(memory_space=pltpu.SMEM)] + [vmem] * 4,
        out_specs=[vmem] * 5 + [hbm] * 2,
        scratch_shapes=scratch,
        compiler_params=pltpu.CompilerParams(
            collective_id=3, has_side_effects=True, vmem_limit_bytes=63 * 2**20
        ),
        name="back",
    )(packed, gctx, gq, nrm, x, gmid, *parts, out_s, gain, lengths, pos_table, jnp.asarray(offset_onehot()), onehot, other)


def finish_kernel(
    q, o, i, u, small, choice,
    gq, go, gi, gu, g_attn, g_ffn, g_table, g_rules, g_dl, g_dr, g_ul, g_ur,
):
    for h in range(3):
        gq[h] = precise(q[: gq.shape[1], :], choice[3 * DH * h : 3 * DH * (h + 1), :], NT)
    go[...] = o[: go.shape[0], :]
    gi[...] = i[: gi.shape[0], :]
    gu[...] = u[: gu.shape[0], :]
    for k in range(D // 128):
        lanes = slice(128 * k, 128 * (k + 1))
        g_attn[:, lanes] = small[ROW_GAIN + k : ROW_GAIN + k + 1, :]
        g_ffn[:, lanes] = small[ROW_OTHER + ROW_FFN + k : ROW_OTHER + ROW_FFN + k + 1, :]
    g_table[...] = small[ROW_TABLE : ROW_TABLE + g_table.shape[0], :NB]
    for i in range(KRON):
        at = ROW_OTHER + ROW_RULES + 4 * i
        g_rules[i] = small[at : at + 4, :KRON]
    for ref, at in ((g_dl, ROW_OTHER + ROW_DL), (g_ur, ROW_OTHER + ROW_UR)):
        ref[:, :128] = small[at : at + 4, :]
        ref[:, 128:] = small[at + 4 : at + 8, : ref.shape[1] - 128]
    for ref, at in ((g_dr, ROW_OTHER + ROW_DR), (g_ul, ROW_OTHER + ROW_UL)):
        ref[...] = small[at : at + 4, :KA]


def finish(q, o, i, u, small, group, shapes):
    vmem = pl.BlockSpec(memory_space=pltpu.VMEM)
    return pl.pallas_call(
        finish_kernel,
        out_shape=[jax.ShapeDtypeStruct(s, jnp.float32) for s in shapes],
        in_specs=[vmem] * 6,
        out_specs=[vmem] * 12,
        name="finish",
    )(q, o, i, u, small, jnp.asarray(column_choice(group)))


def round_up(n, m):
    return -(-n // m) * m


def pad_rows(a, rows):
    return jnp.pad(a, ((0, rows - a.shape[0]), (0, 0)))


HEADS = 12


def local(
    tokens,
    lengths,
    cotangent,
    w_qkv,
    w_o,
    w_in,
    w_out,
    gain_attn,
    gain_ffn,
    pos_table,
    phm_rules,
    down_left,
    down_right,
    up_left,
    up_right,
):
    dp_count, mp_count = lax.axis_size("dp"), lax.axis_size("mp")
    depth = dp_count // 2
    bits = dp_count.bit_length() - 1
    devices = dp_count * mp_count
    member = lax.axis_index("mp")
    tok_rows = tokens.shape[0]
    seg_count = tok_rows // SEG
    o_rows, in_rows, q_rows = w_o.shape[0], w_in.shape[1], w_qkv.shape[0]
    bf = jnp.bfloat16
    group = o_rows if o_rows % 24 == 0 and round_up(o_rows, 16) * 3 == o_rows * 4 else 3 * DH
    rows_of_shards = [round_up(r, 16) for r in (q_rows, o_rows, in_rows, in_rows)]
    tok_in, cot_in = tokens.reshape(seg_count, SEG, D), cotangent.reshape(seg_count, SEG, D)
    merged = depth == 4 and group == o_rows and rows_of_shards[0] == q_rows and rows_of_shards[2] == in_rows
    factors = (phm_rules, down_left, down_right, up_left, up_right)
    gains = (gain_attn.reshape(1, D), gain_ffn.reshape(1, D))
    if merged:
        shards = (w_qkv.transpose(1, 0, 2), w_o, w_in.T, w_out)
        tok_s, gq, normed_attn, packed, result, grad_mid, grad_context, grad_w_o, grad_w_in, grad_w_out, other = front(
            depth, group, tok_in, cot_in, shards, rows_of_shards, gains, lengths, pos_table.T, factors
        )
    else:
        shards = (head_columns(w_qkv.astype(bf), group), w_o.astype(bf), w_in.astype(bf).T, w_out.astype(bf))
        shards = [pad_rows(s, r) for s, r in zip(shards, rows_of_shards)]
        tok_s, cot_s, gq, go, gi, gu = gather_all(depth, tok_in, cot_in, shards)
    tokens_s = tok_s.reshape(tok_rows, D)

    def plain(g, rows):
        return g.reshape(devices, g.shape[-2], D)[:, :rows].reshape(devices * rows, D)

    def slots(g, rows):
        padded = jnp.pad(g.reshape(devices, rows, D), ((0, 0), (0, round_up(rows, 16) - rows), (0, 0)))
        return padded.reshape(depth, 2, 2, 2, padded.shape[1], D)

    if not merged:
        if group == o_rows:
            dense_o = go.reshape(mp_count, CTX_PAD, D)
        else:
            dense_o = plain(go, o_rows).reshape(mp_count, 3 * DH, D)
            dense_o = jnp.pad(dense_o, ((0, 0), (0, CTX_PAD - 3 * DH), (0, 0)))
        qkv_full = gq.reshape(mp_count, dp_count, rows_of_shards[0], QKV_PAD)[:, :, :q_rows]
        qkv_full = qkv_full.reshape(mp_count, D, QKV_PAD)
        live = jnp.concatenate(
            [jnp.arange(length) < own_length(lengths, member, i) for i, (_, length) in enumerate(SPANS)]
        )
        mask = key_mask(live)
        rows = jnp.einsum("bh,br->hr", pos_table, offset_onehot(), precision=FULL_PRECISION).reshape(mp_count, 3, 512)
        normed_attn, packed, context = attention(tokens_s, gains[0], qkv_full, mask, rows, group)
        result, grad_mid, grad_context, grad_w_o, grad_w_in, grad_w_out, other = middle(
            tokens_s,
            context,
            dense_o,
            plain(gi, in_rows),
            plain(gu, in_rows),
            cot_s.reshape(tok_rows, D),
            gains[1],
            lengths,
            factors,
        )
    if group == o_rows:
        part_o = grad_w_o.reshape(depth, 2, 2, 2, round_up(o_rows, 16), D)
    else:
        part_o = slots(grad_w_o.reshape(mp_count, CTX_PAD, D)[:, : 3 * DH].reshape(D, D), o_rows)
    part_in, part_out = slots(grad_w_in, in_rows), slots(grad_w_out, in_rows)
    result = result.reshape(seg_count, SEG, D)
    onehot = jnp.asarray(np.pad(table_onehot(), ((0, 0), (0, 128 - NB))))
    if merged:
        oq, oo, oi, ou, summed, out, gtok = back(
            depth, bits, group, packed, grad_context, gq, normed_attn, tok_s, grad_mid,
            (part_out, part_in, part_o), result, gains[0], lengths, pos_table.T, onehot, other,
        )
    else:
        packed_grads, sums = attention_back(packed, grad_context, mask, rows, group)
        table_grad = jnp.dot(sums.reshape(HEADS, 768), onehot, precision=FULL_PRECISION)
        grad_w_qkv = jnp.einsum("td,mtc->mdc", normed_attn, packed_grads, preferred_element_type=jnp.float32).astype(bf)
        grad_n1 = jnp.einsum("mtc,mdc->td", packed_grads, qkv_full, preferred_element_type=jnp.float32)
        _, norm_back_attn = jax.vjp(normed, tokens_s.astype(jnp.float32), gain_attn)
        grad_x_part, grad_gain_attn = norm_back_attn(grad_n1)
        grad_tokens = (grad_mid + grad_x_part).astype(bf)
        small = jnp.concatenate([
            jnp.pad(grad_gain_attn.reshape(D // 128, 128), ((0, ROW_TABLE - D // 128), (0, 0))),
            jnp.pad(table_grad, ((0, ROW_OTHER - ROW_TABLE - HEADS), (0, 0))),
            other,
        ])
        part_q = grad_w_qkv.reshape(mp_count, dp_count, q_rows, QKV_PAD)
        part_q = jnp.pad(part_q, ((0, 0), (0, 0), (0, rows_of_shards[0] - q_rows), (0, 0)))
        part_q = part_q.reshape(2, 2, depth, 2, rows_of_shards[0], QKV_PAD)
        oq, oo, oi, ou, summed, out, gtok = scatter_all(
            depth, bits, (part_q, part_o, part_in, part_out), small, result, grad_tokens.reshape(seg_count, SEG, D)
        )
    shapes = (
        (3, q_rows, 3 * DH), w_o.shape, w_in.shape[::-1], w_out.shape, (1, D), (1, D), pos_table.shape[::-1],
        phm_rules.shape, down_left.shape, down_right.shape, up_left.shape, up_right.shape,
    )
    g_qkv, g_o, g_in, g_out, g_attn, g_ffn, g_table, *smalls = finish(oq, oo, oi, ou, summed, group, shapes)
    return (
        out.reshape(tok_rows, D),
        gtok.reshape(tok_rows, D),
        g_qkv.transpose(1, 0, 2),
        g_o,
        g_in.T,
        g_out,
        g_attn.reshape(D),
        g_ffn.reshape(D),
        g_table.T,
        *smalls,
    )


def solution(mesh):
    return jax.shard_map(
        local,
        mesh=mesh,
        in_specs=(
            P(("dp", "mp"), None),
            P("dp"),
            P(("dp", "mp"), None),
            P("dp", "mp", None),
            P(("dp", "mp"), None),
            P(None, ("dp", "mp")),
            P(("dp", "mp"), None),
            P(),
            P(),
            P(),
            P(),
            P(),
            P(),
            P(),
            P(),
        ),
        out_specs=(
            P(("dp", "mp"), None),
            P(("dp", "mp"), None),
            P("dp", "mp", None),
            P(("dp", "mp"), None),
            P(None, ("dp", "mp")),
            P(("dp", "mp"), None),
            P(),
            P(),
            P(),
            P(),
            P(),
            P(),
            P(),
            P(),
        ),
        check_vma=False,
    )
```

```python
import functools
import itertools

import jax
import jax.experimental.pallas as pl
import jax.experimental.pallas.tpu as pltpu
import jax.numpy as jnp
import numpy as np
from jax import lax
from jax.sharding import PartitionSpec as P

D = 768
DH = 64
NB = 32
MAXDIST = 128
ADAPT = 48
KRON = 4
LEN_LONG = 512
LEN_MID = 256
LEN_SHORT = 128
SEG = 128


NORM_EPS = 1e-06
FULL_PRECISION = lax.Precision.HIGHEST


def rel_buckets(length):
    offsets = np.arange(-(length - 1), length)
    half_count = NB // 2
    exact_count = half_count // 2
    upward = (offsets > 0).astype(np.int64) * half_count
    distance = np.abs(offsets)
    scaled = (
        np.log(np.maximum(distance, 1) / exact_count)
        / np.log(MAXDIST / exact_count)
        * (half_count - exact_count)
    )
    far_bucket = np.minimum(
        exact_count + np.floor(np.maximum(scaled, 0.0)).astype(np.int64), half_count - 1
    )
    return upward + np.where(distance < exact_count, distance, far_bucket)


def normed(values, gain):
    return values * lax.rsqrt(jnp.mean(values * values, axis=-1, keepdims=True) + NORM_EPS) * gain


MESH = pl.DeviceIdType.MESH


class Place:
    def __init__(self, depth):
        d, m = lax.axis_index("dp"), lax.axis_index("mp")
        self.depth = depth
        self.d, self.m = d, m
        self.z, self.x, self.y, self.c = d // 2, d % 2, m // 2, m % 2
        dx, dy, c = 1 - 2 * self.x, 2 - 4 * self.y, self.c
        self.sib = (d, m + 1 - 2 * c)
        self.right, self.left = (d + 2, m), (d - 2, m)
        self.mp_peer = ((d, m + 1 - 2 * c), (d, m + dy), (d, 3 - m))
        self.xn, self.yn = (d + dx, m), (d, m + dy)
        self.a_nbr = (d + (1 - c) * dx, m + c * dy)
        self.b_nbr = (d + c * dx, m + (1 - c) * dy)
        self.a = self.x + c * (self.y - self.x)
        self.b = self.y + c * (self.x - self.y)

    def by_core(self, run):
        for core in (0, 1):
            pl.when(self.c == core)(functools.partial(run, core))

    def order(self, k):
        n = self.depth
        base = k // 2 if k % 2 == 0 else n - 1 - k // 2
        near = 1 - jnp.minimum(self.z // max(n // 2, 1), 1)
        return base + near * (n - 1 - 2 * base)

    def nearest(self, e):
        n, z = self.depth, self.z
        ahead = 1 - 2 * (z // ((n + 1) // 2))
        short = jnp.minimum(z, n - 1 - z)
        around = (1 - 2 * (e % 2)) * ((e + 1) // 2)
        return z + ahead * jnp.where(e <= 2 * short, around, e - short)

    def flip(self, bit):
        step = 1 << bit
        return (self.d + step * (1 - 2 * ((self.d // step) % 2)), self.m)

    def barrier(self, bits):
        self.greet(bits)
        self.meet(bits)

    def pals(self, bits):
        return [*self.mp_peer, self.xn] + [self.flip(bit) for bit in range(2, bits)]

    def greet(self, bits):
        sem = pltpu.get_barrier_semaphore()

        def greet(dev):
            pl.semaphore_signal(sem, 1, device_id=dev, device_id_type=MESH)

        for dev in self.pals(bits):
            greet(dev)
        pl.when(self.z > 0)(lambda: greet(self.left))
        pl.when(self.z < self.depth - 1)(lambda: greet(self.right))

    def meet(self, bits):
        ends = jnp.minimum(self.z, 1) + jnp.minimum(self.depth - 1 - self.z, 1)
        pl.semaphore_wait(pltpu.get_barrier_semaphore(), len(self.pals(bits)) + ends)


def remote(src, dst, send, recv, dev):
    return pltpu.make_async_remote_copy(
        src_ref=src, dst_ref=dst, send_sem=send, recv_sem=recv, device_id=dev, device_id_type=MESH
    )


def slot_of(buf, by_head, p):
    return buf.at[p.y, p.c, p.z, p.x] if by_head else buf.at[p.z, p.x, p.y, p.c]


def pair_of(buf, by_head, core, b, z):
    if by_head:
        return buf.at[b, 0, z] if core == 0 else buf.at[:, 1, z, b]
    return buf.at[z, :, b, 0] if core == 0 else buf.at[z, b, :, 1]


class Gather:
    def __init__(self, p, by_head, shard, buf, send, recv, own):
        self.p, self.by_head, self.shard, self.buf = p, by_head, shard, buf
        self.send, self.recv, self.own = send, recv, own
        n = p.depth
        self.first = remote(shard, slot_of(buf, by_head, p), send.at[5 * n], recv.at[4 * n], p.a_nbr)
        self.keep = pltpu.make_async_copy(shard, slot_of(buf, by_head, p), own)

    @staticmethod
    def sems(n):
        return [
            pltpu.SemaphoreType.DMA((5 * n + 1,)),
            pltpu.SemaphoreType.DMA((4 * n + 1,)),
            pltpu.SemaphoreType.DMA,
        ]

    def _copy(self, core, b, z, kind):
        p, n = self.p, self.p.depth
        ref = pair_of(self.buf, self.by_head, core, b, z)
        if kind == "right":
            return remote(ref, ref, self.send.at[z], self.recv.at[z], p.right)
        if kind == "left":
            return remote(ref, ref, self.send.at[n + z], self.recv.at[z], p.left)
        return remote(ref, ref, self.send.at[2 * n + z], self.recv.at[n + z], p.b_nbr)

    def _sib(self, core, b, z):
        n = self.p.depth
        ref = pair_of(self.buf, self.by_head, core, b, z)
        return remote(ref, ref, self.send.at[3 * n + b * n + z], self.recv.at[2 * n + b * n + z], self.p.sib)

    def start(self):
        self.keep.start()
        self.first.start()

    def _spread(self, core, z, right, left):
        p = self.p
        if right:
            pl.when(p.z < p.depth - 1)(lambda: self._copy(core, p.b, z, "right").start())
        if left:
            pl.when(p.z > 0)(lambda: self._copy(core, p.b, z, "left").start())
        self._copy(core, p.b, z, "b").start()
        self._sib(core, p.b, z).start()

    def along(self, k):
        p = self.p
        if isinstance(k, int) and k == 0:
            self.keep.wait()
            self.first.wait_recv()
            p.by_core(lambda core: self._spread(core, p.z, True, True))
            return

        def from_left(core):
            self._copy(core, p.b, p.z - k, "right").wait_recv()
            self._spread(core, p.z - k, True, False)

        def from_right(core):
            self._copy(core, p.b, p.z + k, "left").wait_recv()
            self._spread(core, p.z + k, False, True)

        pl.when(p.z - k >= 0)(lambda: p.by_core(from_left))
        pl.when(p.z + k < p.depth)(lambda: p.by_core(from_right))

    def across(self, k):
        p = self.p

        def one(z, core):
            self._copy(core, 1 - p.b, z, "b").wait_recv()
            self._sib(core, 1 - p.b, z).start()

        pl.when(p.z - k >= 0)(lambda: p.by_core(lambda core: one(p.z - k, core)))
        if not (isinstance(k, int) and k == 0):
            pl.when(p.z + k < p.depth)(lambda: p.by_core(lambda core: one(p.z + k, core)))

    def finish_at(self, z):
        def one(core):
            for b in (0, 1):
                self._sib(1 - core, b, z).wait_recv()

        self.p.by_core(one)

    def finish(self):
        each_of(self.p.depth, self.finish_at)

    def drain(self):
        p, n = self.p, self.p.depth
        self.first.wait_send()

        def each(z, carry):
            def one(core):
                pl.when(jnp.logical_and(p.z < n - 1, z <= p.z))(
                    lambda: self._copy(core, p.b, z, "right").wait_send()
                )
                pl.when(jnp.logical_and(p.z > 0, z >= p.z))(
                    lambda: self._copy(core, p.b, z, "left").wait_send()
                )
                self._copy(core, p.b, z, "b").wait_send()
                for b in (0, 1):
                    self._sib(core, b, z).wait_send()

            p.by_core(one)
            return carry

        lax.fori_loop(0, n, each, 0)


class Exchange:
    def __init__(self, p, src, dst, send, recv, own):
        m = p.m
        c, other = m % 2, 1 - m % 2
        self.local = [
            pltpu.make_async_copy(src.at[m], dst.at[m], own.at[0]),
            pltpu.make_async_copy(src.at[4 + c], dst.at[4 + c], own.at[1]),
            pltpu.make_async_copy(src.at[pl.ds(6, 2)], dst.at[pl.ds(6, 2)], own.at[2]),
        ]
        self.out = [
            remote(src.at[dev[1]], dst.at[m], send.at[j], recv.at[j], dev)
            for j, dev in enumerate(p.mp_peer)
        ] + [remote(src.at[4 + other], dst.at[4 + c], send.at[3], recv.at[3], p.sib)]

    @staticmethod
    def sems():
        return [
            pltpu.SemaphoreType.DMA((4,)),
            pltpu.SemaphoreType.DMA((4,)),
            pltpu.SemaphoreType.DMA((3,)),
        ]

    def start(self):
        for copy in self.out + self.local:
            copy.start()

    def finish(self):
        for copy in self.local:
            copy.wait()
        for copy in self.out:
            copy.wait_recv()

    def drain(self):
        for copy in self.out:
            copy.wait_send()


def add_rows(dst, src, rows):
    step = 32 if rows % 32 == 0 else 16

    def one(i, carry):
        at = pl.ds(pl.multiple_of(i * step, step), step)
        total = dst[at, :].astype(jnp.float32) + src[at, :].astype(jnp.float32)
        dst[at, :] = total.astype(dst.dtype)
        return carry

    lax.fori_loop(0, rows // step, one, 0)


class Scatter:
    def __init__(self, p, by_head, part, total, half, quarter, arrive, last, send, recv, mine=None, mine_sem=None, region=None):
        self.p, self.by_head, self.part, self.total = p, by_head, part, total
        self.mine, self.mine_sem, self.region = mine, mine_sem, region
        self.half, self.quarter, self.arrive, self.last = half, quarter, arrive, last
        self.send, self.recv = send, recv
        self.rows = part.shape[-2]

    @staticmethod
    def scratch(n, rows, cols, dtype=jnp.bfloat16):
        return [
            pltpu.VMEM((n, 2, 2, rows, cols), dtype),
            pltpu.VMEM((n, 2, rows, cols), dtype),
            pltpu.VMEM((n + 1, 2, rows, cols), dtype),
            pltpu.VMEM((rows, cols), dtype),
            pltpu.SemaphoreType.DMA((3 * n + 1,)),
            pltpu.SemaphoreType.DMA((3 * n + 2,)),
        ]

    def order(self, k):
        return self.p.order(k)

    def _region(self, core, z):
        if self.region is not None:
            return self.region(core, z)
        return self.part.at[:, core, z] if self.by_head else self.part.at[z, :, :, core]

    def _half_pair(self, core, b, z):
        over_first = (core == 0) != self.by_head
        return self.half.at[z, :, b] if over_first else self.half.at[z, b]

    def _sib(self, core, z):
        return remote(
            self._region(1 - core, z), self.half.at[z], self.send.at[z], self.recv.at[z], self.p.sib
        )

    def _b(self, core, z):
        n, p = self.p.depth, self.p
        return remote(
            self._half_pair(core, 1 - p.b, z), self.quarter.at[z], self.send.at[n + z], self.recv.at[n + z], p.b_nbr
        )

    def _right(self, z):
        n, p = self.p.depth, self.p
        return remote(
            self.quarter.at[z], self.arrive.at[z], self.send.at[2 * n + z], self.recv.at[2 * n + z], p.right
        )

    def _left(self, z, goal):
        n, p = self.p.depth, self.p
        return remote(
            self.quarter.at[z], self.arrive.at[goal], self.send.at[2 * n + z], self.recv.at[2 * n + goal], p.left
        )

    def _a(self):
        n, p = self.p.depth, self.p
        return remote(
            self.quarter.at[p.z, 1 - p.a], self.last, self.send.at[3 * n], self.recv.at[3 * n + 1], p.a_nbr
        )

    def _keep(self, core, z):
        return pltpu.make_async_copy(self._region(core, z), self.mine.at[z], self.mine_sem.at[z])

    def start(self, k):
        z = self.order(k)

        def one(core):
            self._sib(core, z).start()
            if self.mine is not None:
                self._keep(core, z).start()

        self.p.by_core(one)

    def to_half(self, k):
        z = self.order(k)

        def one(core):
            self._sib(core, z).wait_recv()
            region = self._region(core, z)
            if self.mine is not None:
                self._keep(core, z).wait()
                region = self.mine.at[z]
            for i in (0, 1):
                for j in (0, 1):
                    add_rows(self.half.at[z, i, j], region.at[i, j], self.rows)
            self._b(core, z).start()

        self.p.by_core(one)

    def to_quarter(self, k):
        z = self.order(k)

        def one(core):
            self._b(core, z).wait_recv()
            for i in (0, 1):
                add_rows(self.quarter.at[z, i], self._half_pair(core, self.p.b, z).at[i], self.rows)

        self.p.by_core(one)

    def _take(self, z, slot):
        for i in (0, 1):
            add_rows(self.quarter.at[z, i], self.arrive.at[slot, i], self.rows)

    def _send_left(self, z):
        p, n = self.p, self.p.depth
        pl.when(z == p.z - 1)(lambda: self._left(z, n).start())
        pl.when(z < p.z - 1)(lambda: self._left(z, z).start())

    def origin(self, k):
        p, n = self.p, self.p.depth
        z = self.order(k)
        pl.when(jnp.logical_and(p.z == 0, z > p.z))(lambda: self._right(z).start())
        pl.when(jnp.logical_and(p.z == n - 1, z < p.z))(lambda: self._send_left(z))

    def forward(self, k):
        p, n = self.p, self.p.depth
        z = self.order(k)

        def rightward():
            self._right(z).wait_recv()
            self._take(z, z)
            self._right(z).start()

        def leftward():
            self._left(z, z).wait_recv()
            self._take(z, z)
            self._send_left(z)

        pl.when(jnp.logical_and(p.z > 0, z > p.z))(rightward)
        pl.when(jnp.logical_and(p.z < n - 1, z < p.z))(leftward)

    def collect(self):
        p, n = self.p, self.p.depth

        def from_left():
            self._right(p.z).wait_recv()
            self._take(p.z, p.z)

        def from_right():
            self._left(p.z, n).wait_recv()
            self._take(p.z, n)

        pl.when(p.z > 0)(from_left)
        pl.when(p.z < n - 1)(from_right)
        self._a().start()

    def finish(self):
        p = self.p
        self._a().wait_recv()
        self.total[...] = self.quarter[p.z, p.a].astype(jnp.float32) + self.last[...].astype(jnp.float32)

    def drain(self):
        p, n = self.p, self.p.depth
        self._a().wait_send()

        def each(z, carry):
            def one(core):
                self._sib(core, z).wait_send()
                self._b(core, z).wait_send()

            p.by_core(one)
            pl.when(z != p.z)(lambda: self._right(z).wait_send())
            return carry

        lax.fori_loop(0, n, each, 0)

    def steps(self):
        n = self.p.depth
        todo = [lambda: [self.start(k) for k in range(n)]]
        todo += [functools.partial(self.to_half, k) for k in range(n)]
        for k in range(n):
            todo.append(functools.partial(lambda k: (self.to_quarter(k), self.origin(k), self.forward(k)), k))
        return todo


class Sum:
    def __init__(self, p, bits, value, slots, send, recv):
        self.p, self.bits, self.value, self.slots = p, bits, value, slots
        self.send, self.recv = send, recv

    @staticmethod
    def scratch(bits, rows):
        return [
            pltpu.VMEM((2 * (bits + 2), rows, 128), jnp.float32),
            pltpu.SemaphoreType.DMA((bits + 2,)),
            pltpu.SemaphoreType.DMA((bits + 2,)),
        ]

    def _copy(self, s):
        p = self.p
        dev = (p.sib, p.yn, *[p.flip(bit) for bit in range(self.bits)])[s]
        return remote(self.slots.at[2 * s], self.slots.at[2 * s + 1], self.send.at[s], self.recv.at[s], dev)

    def steps(self):
        def begin():
            self.slots[0] = self.value[...]
            self._copy(0).start()

        def one(s):
            self._copy(s).wait_recv()
            total = self.slots[2 * s] + self.slots[2 * s + 1]
            if s == self.bits + 1:
                self.value[...] = total
            else:
                self.slots[2 * s + 2] = total
                self._copy(s + 1).start()

        return [begin] + [functools.partial(one, s) for s in range(self.bits + 2)]

    def drain(self):
        for s in range(self.bits + 2):
            self._copy(s).wait_send()


def in_waves(lists, lag):
    for t in range(max(len(todo) + lag * r for r, todo in enumerate(lists))):
        for r, todo in enumerate(lists):
            if 0 <= t - lag * r < len(todo):
                todo[t - lag * r]()


def gather_kernel(p_depth, tok, cot, wq, wo, wi, wu, tok_s, cot_s, gq, go, gi, gu, *sems):
    p = Place(p_depth)
    n = p_depth
    arrays = []
    for i, (by_head, shard, buf) in enumerate(
        ((True, wq, gq), (False, wo, go), (False, wi, gi), (False, wu, gu))
    ):
        arrays.append(Gather(p, by_head, shard, buf, *sems[3 * i : 3 * i + 3]))
    rows = [Exchange(p, tok, tok_s, *sems[12:15]), Exchange(p, cot, cot_s, *sems[15:18])]
    p.barrier(0)
    for g in arrays:
        g.start()
    rows[0].start()
    if n <= 8:
        for k in range(n):
            for g in arrays:
                g.along(k)
            if k > 0:
                for g in arrays:
                    g.across(k - 1)
            if k == 1:
                rows[1].start()
        for g in arrays:
            g.across(n - 1)
    else:
        for g in arrays:
            g.along(0)
            lax.fori_loop(1, n, lambda k, carry: (g.along(k), carry)[1], 0)
        rows[1].start()
        for g in arrays:
            g.across(0)
            lax.fori_loop(1, n, lambda k, carry: (g.across(k), carry)[1], 0)
    for g in arrays + rows:
        g.finish()
    for g in arrays + rows:
        g.drain()


def gather_all(depth, tok, cot, shards):
    hbm = pl.BlockSpec(memory_space=pl.ANY)
    outs = [jax.ShapeDtypeStruct(tok.shape, tok.dtype)] * 2
    for i, s in enumerate(shards):
        lead = (2, 2, depth, 2) if i == 0 else (depth, 2, 2, 2)
        outs.append(jax.ShapeDtypeStruct(lead + s.shape, s.dtype))
    sems = Gather.sems(depth) * 4 + Exchange.sems() * 2
    return pl.pallas_call(
        functools.partial(gather_kernel, depth),
        out_shape=outs,
        in_specs=[hbm] * 6,
        out_specs=[hbm] * 6,
        scratch_shapes=sems,
        compiler_params=pltpu.CompilerParams(collective_id=0, has_side_effects=True),
        name="gather",
    )(tok, cot, *shards)


def scatter_kernel(depth, bits, pq, po, pi, pu, small, out_s, gtok_s, oq, oo, oi, ou, small_o, out, gtok, *scr):
    p = Place(depth)
    arrays = []
    for i, (by_head, part, total) in enumerate(
        ((False, pu, ou), (False, pi, oi), (False, po, oo), (True, pq, oq))
    ):
        arrays.append(Scatter(p, by_head, part, total, *scr[6 * i : 6 * i + 6]))
    rows = [Exchange(p, out_s, out, *scr[24:27]), Exchange(p, gtok_s, gtok, *scr[27:30])]
    small_o[...] = small[...]
    sums = Sum(p, bits, small_o, *scr[30:33])
    p.barrier(bits)
    rows[0].start()
    in_waves([g.steps() for g in arrays], min(depth, 4))
    rows[1].start()
    close(arrays, sums)
    for r in rows:
        r.finish()
    for g in arrays + rows + [sums]:
        g.drain()


def close(arrays, sums):
    closing = [g.collect for g in arrays] + [g.finish for g in arrays]
    for step in itertools.chain(*itertools.zip_longest(sums.steps(), closing)):
        if step is not None:
            step()


def scatter_all(depth, bits, parts, small, out_s, gtok_s):
    hbm = pl.BlockSpec(memory_space=pl.ANY)
    vmem = pl.BlockSpec(memory_space=pltpu.VMEM)
    outs = [jax.ShapeDtypeStruct(s.shape[4:], jnp.float32) for s in parts]
    outs += [jax.ShapeDtypeStruct(small.shape, jnp.float32)]
    outs += [jax.ShapeDtypeStruct(out_s.shape, out_s.dtype)] * 2
    scr = []
    for s in (parts[3], parts[2], parts[1], parts[0]):
        scr += Scatter.scratch(depth, *s.shape[4:])
    scr += Exchange.sems() * 2 + Sum.scratch(bits, small.shape[0])
    return pl.pallas_call(
        functools.partial(scatter_kernel, depth, bits),
        out_shape=outs,
        in_specs=[vmem] * 5 + [hbm] * 2,
        out_specs=[vmem] * 5 + [hbm] * 2,
        scratch_shapes=scr,
        compiler_params=pltpu.CompilerParams(
            collective_id=1, has_side_effects=True, vmem_limit_bytes=60 * 2**20
        ),
        name="scatter",
    )(*parts, small, out_s, gtok_s)

SPANS = ((0, LEN_LONG), (LEN_LONG, LEN_MID), (LEN_LONG + LEN_MID, LEN_SHORT), (LEN_LONG + LEN_MID + LEN_SHORT, LEN_SHORT))
TILE = 128
QKV_PAD = 640
CTX_PAD = 256
ADAPT_PAD = 128
MASK_LOW = -1e9
NN = (((1,), (0,)), ((), ()))
NT = (((1,), (1,)), ((), ()))
TN = (((0,), (0,)), ((), ()))


def dot(a, b, dims=NN):
    return lax.dot_general(a, b, dims, preferred_element_type=jnp.float32)


def table_onehot():
    buckets = rel_buckets(257)
    offset = np.clip(256 - np.arange(512), -256, 256) + 256
    index = np.concatenate([buckets[offset], np.full(128, NB // 2 - 1), np.full(128, NB - 1)])
    return (index[:, None] == np.arange(NB)[None, :]).astype(np.float32)


def bias_tiles(row):
    spread = pltpu.roll(jnp.broadcast_to(row, (TILE, 512)), 0, 1, stride=1, stride_axis=0)
    far = [jnp.broadcast_to(row[:, at : at + 1], (TILE, TILE)) for at in (511, 0)]
    near = [spread[:, 256 - 128 * delta : 384 - 128 * delta] for delta in (-1, 0, 1)]
    return [far[0], *near, far[1]]


def diagonal_sums(tiles):
    grid = jnp.concatenate([jnp.zeros((TILE, TILE), jnp.float32), tiles[2], tiles[1], tiles[0]], axis=1)
    rows = TILE
    while rows > 8:
        rows //= 2
        grid = grid[:rows] + pltpu.roll(grid[rows:], 512 - rows, 1)
    total = grid[0:1]
    for r in range(1, 8):
        total = total + pltpu.roll(grid[r : r + 1], 512 - r, 1)
    return total


def swap_halves(tile):
    return jnp.concatenate([tile[:, DH:], tile[:, :DH]], axis=1)


def lanes_below(shape, at=DH):
    return lax.broadcasted_iota(jnp.int32, shape, len(shape) - 1) < at


def key_side(qk, mask):
    swapped = swap_halves(qk)
    return jnp.where(lanes_below(qk.shape), swapped, mask), swapped


def query_side(qk):
    lane = lax.broadcasted_iota(jnp.int32, qk.shape, 1)
    return jnp.where(lane < DH, qk, jnp.where(lane == DH, 1.0, 0.0).astype(qk.dtype))


def probabilities(scores, tiles, length, q0=0):
    width = scores.shape[1]
    blocks = []
    for kb in range(length // TILE):
        deltas = [max(-2, min(2, kb - (q0 + qi))) + 2 for qi in range(width // TILE)]
        bias = tiles[deltas[0]] if len(deltas) == 1 else jnp.concatenate([tiles[d] for d in deltas], axis=1)
        blocks.append(scores[kb * TILE : (kb + 1) * TILE] + bias)
    top = blocks[0]
    for block in blocks[1:]:
        top = jnp.maximum(top, block)
    top = jnp.max(top, axis=0, keepdims=True)
    blocks = [jnp.exp(block - top) for block in blocks]
    total = blocks[0]
    for block in blocks[1:]:
        total = total + block
    inverse = 1.0 / jnp.sum(total, axis=0, keepdims=True)
    return [block * inverse for block in blocks]


def join(blocks, axis=0):
    return blocks[0] if len(blocks) == 1 else jnp.concatenate(blocks, axis=axis)


def value_lanes(group):
    stride = group * CTX_PAD // (3 * DH)
    lane = np.arange(CTX_PAD)
    column = lane // stride * group + lane % stride
    return np.where(lane % stride < group, column // DH, -1), column


def head_runs(group):
    heads, _ = value_lanes(group)
    runs = []
    for lane in range(CTX_PAD):
        head = int(heads[lane])
        head = runs[-1][2] if head < 0 else head
        if runs and runs[-1][2] == head:
            runs[-1][1] = lane + 1
        else:
            runs.append([lane, lane + 1, head])
    return runs


def head_lanes(shape, group, head):
    lane = lax.broadcasted_iota(jnp.int32, shape, len(shape) - 1)
    inside = None
    for lo, hi, h in head_runs(group):
        if h == head:
            run = jnp.logical_and(lane >= lo, lane < hi)
            inside = run if inside is None else jnp.logical_or(inside, run)
    return inside


def no_tick(j):
    pass


def no_keep(number, place, h, probs):
    pass


FRONT_SPANS = (SPANS[:1], SPANS[1:])
FRONT_WIDTH = 256


def attend_group(packed, mask_ref, rows, context, group, tick=no_tick, keep=no_keep):
    tiles = [bias_tiles(rows[h : h + 1, :]) for h in range(3)]
    for number, spans in enumerate(FRONT_SPANS):
        units = []
        for offset, length in spans:
            width = min(length, FRONT_WIDTH)
            units += [(offset, length, q0, width) for q0 in range(0, length, width)]
        batches = [[unit] for unit in units] if number == 0 else [units]
        keys = {
            (offset, h): key_side(packed[pl.ds(offset, length), h * TILE : (h + 1) * TILE], mask_ref[pl.ds(offset, length), :])[0]
            for offset, length in spans
            for h in range(3)
        }
        values = {offset: packed[pl.ds(offset, length), 3 * TILE : QKV_PAD].T for offset, length in spans}
        for turn, batch in enumerate(batches):
            work = [(unit, h) for unit in batch for h in range(3)]
            scores = []
            for (offset, length, q0, width), h in work:
                queries = query_side(packed[pl.ds(offset + q0, width), h * TILE : (h + 1) * TILE])
                scores.append(dot(keys[offset, h], queries, NT))
            probs = []
            for ((offset, length, q0, width), h), score in zip(work, scores):
                blocks = probabilities(score, tiles[h], length, q0 // TILE)
                probs.append(join([block.astype(jnp.bfloat16) for block in blocks]))
            for (unit, h), prob in zip(work, probs):
                keep(number, unit, h, prob)
            outs = [dot(values[unit[0]], prob) for (unit, h), prob in zip(work, probs)]
            for i, (offset, length, q0, width) in enumerate(batch):
                own = outs[3 * i : 3 * i + 3]
                whole = jnp.concatenate([own[h][lo:hi] for lo, hi, h in head_runs(group)], axis=0)
                context[pl.ds(offset + q0, width), :] = whole.T.astype(jnp.bfloat16)
            tick((number, turn))


BACK_SPANS = (SPANS[:1], SPANS[1:])
SKEW = (5, 0)


def head_back(packed, recall, grad_context, grad_packed, group, near, far, value_sums, span_of, h):
    offset, length = span_of
    span, at = pl.ds(offset, length), pl.ds(h * TILE, TILE)
    qk = packed[span, at]
    low = lanes_below(qk.shape)
    swapped = swap_halves(qk)
    g_tile = grad_context[span, :]
    g_tile = jnp.where(head_lanes(g_tile.shape, group, h), g_tile, jnp.zeros_like(g_tile))
    scores = recall.scores(qk, span, h)
    g_probs = dot(packed[span, 3 * TILE : QKV_PAD], g_tile, NT)
    yield
    probs = recall.probs(scores, span_of, h)
    yield
    count = length // TILE
    g_blocks = [g_probs[kb * TILE : (kb + 1) * TILE] for kb in range(count)]
    total = probs[0] * g_blocks[0]
    for kb in range(1, count):
        total = total + probs[kb] * g_blocks[kb]
    centre = jnp.sum(total, axis=0, keepdims=True)
    low_probs = join([block.astype(jnp.bfloat16) for block in probs])
    g_scores = [(a * (g - centre)).astype(jnp.bfloat16) for a, g in zip(probs, g_blocks)]
    for kb, block in enumerate(g_scores):
        wide = block.astype(jnp.float32)
        for qi in range(count):
            piece = wide[:, qi * TILE : (qi + 1) * TILE]
            delta = kb - qi
            if abs(delta) <= 1:
                held = near[h][delta + 1]
                near[h][delta + 1] = piece if held is None else held + piece
            else:
                side = 0 if delta < 0 else 1
                far[h][side] = far[h][side] + piece
    yield
    g_scores = join(g_scores)
    g_v = dot(low_probs, g_tile)
    value_sums[offset] = value_sums[offset] + g_v if offset in value_sums else g_v
    grad_keys = dot(g_scores, jnp.where(low, jnp.zeros_like(qk), swapped))
    grad_queries = dot(jnp.where(low, swapped, jnp.zeros_like(qk)).T, g_scores).T
    yield
    grad_packed[span, at] = (grad_queries + grad_keys).astype(jnp.bfloat16)


class Again:
    def __init__(self, mask, rows):
        self.mask = mask
        self.tiles = [bias_tiles(rows[h : h + 1, :]) for h in range(3)]

    def scores(self, qk, span, h):
        return dot(key_side(qk, self.mask[span, :])[0], query_side(qk), NT)

    def probs(self, scores, span_of, h):
        return probabilities(scores, self.tiles[h], span_of[1])


class Kept:
    def __init__(self, kept):
        self.kept = kept

    def scores(self, qk, span, h):
        return None

    def probs(self, scores, span_of, h):
        offset, length = span_of
        pieces = [self.kept[r : r + n, c : c + w] for r, n, c, w in kept_at(offset, length, h)]
        whole = join(pieces, axis=1).astype(jnp.float32)
        return [whole[kb * TILE : (kb + 1) * TILE] for kb in range(length // TILE)]


KEPT_LONG, KEPT_REST = 1024, 384


def kept_at(offset, length, h):
    if length == LEN_LONG:
        if h < 2:
            return [(LEN_LONG * h, LEN_LONG, 0, LEN_LONG)]
        return [(LEN_LONG * k, LEN_LONG, LEN_LONG, LEN_LONG // 2) for k in range(2)]
    if length == LEN_MID:
        return [(KEPT_LONG, LEN_MID, LEN_MID * h, LEN_MID)]
    second = (offset - LEN_LONG - LEN_MID) // LEN_SHORT
    return [(KEPT_LONG + LEN_MID, LEN_SHORT, LEN_SHORT * (3 * second + h), LEN_SHORT)]


def attend_group_back(packed, recall, grad_context, grad_packed, sums, group, tick=no_tick):
    near = [[None] * 3 for _ in range(3)]
    far = [[jnp.zeros((TILE, TILE), jnp.float32)] * 2 for _ in range(3)]
    value_sums = {}

    def heads_of(spans):
        return [
            head_back(packed, recall, grad_context, grad_packed, group, near, far, value_sums, s, h)
            for s in spans
            for h in range(3)
        ]

    def values_of(spans):
        for offset, length in spans:
            grad_packed[pl.ds(offset, length), 3 * TILE : QKV_PAD] = value_sums.pop(offset).astype(jnp.bfloat16)

    for number, spans in enumerate(BACK_SPANS):
        heads = heads_of(spans)
        skew = SKEW[number]
        for t in range(5 + skew * (len(heads) - 1)):
            for i, head in enumerate(heads):
                if 0 <= t - skew * i < 5:
                    next(head, None)
                    if t - skew * i == 4:
                        tick((number, i))
        values_of(spans)
    for h in range(3):
        sums[h : h + 1, :512] = diagonal_sums(near[h])
        for side in range(2):
            sums[h : h + 1, 512 + side * TILE : 640 + side * TILE] = jnp.sum(far[h][side], axis=0, keepdims=True)


def attention_kernel(group, x_ref, gain, w_ref, mask, rows, normed_out, packed, context):
    @pl.when(pl.program_id(0) == 0)
    def _():
        x = x_ref[...].astype(jnp.float32)
        scale = lax.rsqrt(jnp.mean(x * x, axis=-1, keepdims=True) + NORM_EPS)
        normed_out[...] = (x * scale * gain[...]).astype(jnp.bfloat16)

    packed[0] = dot(normed_out[...], w_ref[0]).astype(jnp.bfloat16)
    attend_group(packed.at[0], mask, rows[0], context.at[0], group)


def attention(x, gain, w, mask, rows, group):
    n = x.shape[0]
    bf = jnp.bfloat16
    return pl.pallas_call(
        functools.partial(attention_kernel, group),
        grid=(4,),
        out_shape=[
            jax.ShapeDtypeStruct((n, D), bf),
            jax.ShapeDtypeStruct((4, n, QKV_PAD), bf),
            jax.ShapeDtypeStruct((4, n, CTX_PAD), bf),
        ],
        in_specs=[
            pl.BlockSpec((n, D), lambda i: (0, 0)),
            pl.BlockSpec((1, D), lambda i: (0, 0)),
            pl.BlockSpec((1, D, QKV_PAD), lambda i: (i, 0, 0)),
            pl.BlockSpec((n, TILE), lambda i: (0, 0)),
            pl.BlockSpec((1, 3, 512), lambda i: (i, 0, 0)),
        ],
        out_specs=[
            pl.BlockSpec((n, D), lambda i: (0, 0)),
            pl.BlockSpec((1, n, QKV_PAD), lambda i: (i, 0, 0)),
            pl.BlockSpec((1, n, CTX_PAD), lambda i: (i, 0, 0)),
        ],
        compiler_params=pltpu.CompilerParams(vmem_limit_bytes=56 * 2**20),
        name="attention",
    )(x, gain, w, mask, rows)


def attention_back_kernel(group, packed, grad_context, mask, rows, grad_packed, sums):
    attend_group_back(packed.at[0], Again(mask, rows[0]), grad_context.at[0], grad_packed.at[0], sums.at[0], group)


def attention_back(packed, grad_context, mask, rows, group):
    n = packed.shape[1]
    return pl.pallas_call(
        functools.partial(attention_back_kernel, group),
        grid=(4,),
        out_shape=[
            jax.ShapeDtypeStruct((4, n, QKV_PAD), jnp.bfloat16),
            jax.ShapeDtypeStruct((4, 3, 768), jnp.float32),
        ],
        in_specs=[
            pl.BlockSpec((1, n, QKV_PAD), lambda i: (i, 0, 0)),
            pl.BlockSpec((1, n, CTX_PAD), lambda i: (i, 0, 0)),
            pl.BlockSpec((n, TILE), lambda i: (0, 0)),
            pl.BlockSpec((1, 3, 512), lambda i: (i, 0, 0)),
        ],
        out_specs=[
            pl.BlockSpec((1, n, QKV_PAD), lambda i: (i, 0, 0)),
            pl.BlockSpec((1, 3, 768), lambda i: (i, 0, 0)),
        ],
        compiler_params=pltpu.CompilerParams(vmem_limit_bytes=56 * 2**20),
        name="attention_back",
    )(packed, grad_context, mask, rows)


def head_columns(w, group):
    n = w.shape[0]
    qk = w[:, :, : 2 * DH].reshape(n, 6 * DH)
    v = w[:, :, 2 * DH :].reshape(n, 3 * DH // group, group)
    v = jnp.pad(v, ((0, 0), (0, 0), (0, group // 3))).reshape(n, CTX_PAD)
    return jnp.concatenate([qk, v], axis=1)


def key_mask(live):
    lane = jnp.arange(TILE)[None, :]
    return jnp.where((lane == DH) & ~live[:, None], MASK_LOW, 0.0).astype(jnp.bfloat16)


def precise(a, b, dims=NN):
    return lax.dot_general(a, b, dims, precision=FULL_PRECISION, preferred_element_type=jnp.float32)


def offset_onehot():
    buckets = rel_buckets(257)
    offset = np.clip(256 - np.arange(512), -256, 256) + 256
    return (np.arange(NB)[:, None] == buckets[offset][None, :]).astype(np.float32)


def column_choice(group):
    choice = np.zeros((9 * DH, QKV_PAD), np.float32)
    for h in range(3):
        for k in range(2 * DH):
            choice[3 * DH * h + k, TILE * h + k] = 1
    heads, column = value_lanes(group)
    for lane in range(CTX_PAD):
        if heads[lane] >= 0:
            choice[3 * DH * heads[lane] + 2 * DH + column[lane] % DH, 3 * TILE + lane] = 1
    return choice


def own_length(lengths, member, number):
    at = (member, 4 + member // 2 + 2 * (member % 2), 8 + member, 12 + member)[number]
    return lengths[at]


def fill_mask(mask, lengths, member):
    for number, (offset, length) in enumerate(SPANS):
        row = lax.broadcasted_iota(jnp.int32, (length, TILE), 0)
        lane = lax.broadcasted_iota(jnp.int32, (length, TILE), 1)
        dead = jnp.logical_and(row >= own_length(lengths, member, number), lane == DH)
        mask[offset : offset + length, :] = jnp.where(dead, MASK_LOW, 0.0).astype(jnp.bfloat16)


def fill_rows(rows, pos_table, onehot):
    table = precise(pos_table[...], onehot[...])
    for m in range(4):
        rows[m] = table[3 * m : 3 * m + 3, :]


KA = ADAPT // KRON


def adapter_constants():
    i, b = np.arange(16) // 4, np.arange(16) % 4
    same = (np.arange(4)[:, None] == i[None, :]).astype(np.float32)
    pick = np.zeros((4, 4, 16), np.float32)
    pick[i, b, np.arange(16)] = 1
    fold = np.zeros((ADAPT_PAD, KA), np.float32)
    fold[np.arange(ADAPT), np.arange(ADAPT) % KA] = 1
    agree = np.zeros((ADAPT_PAD, 16), np.float32)
    agree[:ADAPT] = np.arange(ADAPT)[:, None] // KA == b[None, :]
    return same, pick, fold, agree


class Factor:
    def __init__(self, rules, tall, short, consts):
        self.same, _, self.fold, self.agree = consts
        spread = precise(tall, self.same, TN)
        self.tall = jnp.concatenate([spread] * KRON, axis=0)
        rows = spread.shape[0]
        self.rules = jnp.concatenate(
            [jnp.broadcast_to(rules[a : a + 1, :], (rows, 16)) for a in range(KRON)], axis=0
        )
        self.short = precise(self.fold, precise(short, self.same, TN)) * self.agree

    def whole(self):
        return precise(self.rules * self.tall, self.short, NT)

    def back(self, grad):
        wide = precise(grad, self.short)
        rows = wide.shape[0] // KRON
        tall = wide * self.rules
        tall = sum(tall[a * rows : (a + 1) * rows] for a in range(KRON))
        rules = wide * self.tall
        rules = [jnp.sum(rules[a * rows : (a + 1) * rows], axis=0, keepdims=True) for a in range(KRON)]
        short = precise(self.rules * self.tall, grad, TN) * self.agree.T
        short = precise(precise(self.same, short), self.fold)
        return jnp.concatenate(rules, axis=0), precise(self.same, tall, NT), short


def rule_tables(rules, pick):
    return [sum(precise(rules[i], pick[i], dims) for i in range(KRON)) for dims in (NN, TN)]


ROW_GAIN, ROW_TABLE, ROW_OTHER = 0, 8, 24
ROW_FFN, ROW_DL, ROW_UR, ROW_DR, ROW_UL, ROW_RULES, ROW_END = 0, 8, 16, 24, 28, 32, 48


def put_row(ref, at, row):
    for k in range(row.shape[1] // 128):
        ref[at + k : at + k + 1, :] = row[:, 128 * k : 128 * (k + 1)]


FCH = 768
RCH = 256


def gelu_both(v):
    phi = 0.5 + 0.5 * lax.erf(v * np.float32(np.sqrt(0.5)))
    return v * phi, phi + v * (jnp.exp(-0.5 * v * v) * np.float32(1.0 / np.sqrt(2.0 * np.pi)))


def rows_of(i, size=RCH):
    return pl.ds(pl.multiple_of(i * size, size), size)


def each_of(count, body):
    lax.fori_loop(0, count, lambda i, carry: (body(i), carry)[1], 0)


class Layer:
    def __init__(self, **refs):
        self.__dict__.update(refs)
        self.n = self.n2.shape[0]

    def midway(self, i):
        r = rows_of(i)
        total = self.x_rows(i)
        for m in range(4):
            total = total + dot(self.ctx[m, r, :], self.wo(m))
        self.mid[r, :] = total
        scale = lax.rsqrt(jnp.mean(total * total, axis=-1, keepdims=True) + NORM_EPS)
        self.n2[r, :] = (total * scale * self.gain[...]).astype(jnp.bfloat16)

    def forward(self, j):
        f = rows_of(j, self.chunk)
        for half in range(2):
            r = pl.ds(half * (self.n // 2), self.n // 2)
            value, slope = gelu_both(dot(self.n2[r, :], self.wi(j), NT))
            value = value.astype(jnp.bfloat16)
            self.act[r, f] = value
            self.dg[r, f] = slope.astype(jnp.bfloat16)
            self.acc[r, :] += dot(value, self.wu(j))

    def factors(self):
        consts = [c[...] for c in self.consts]
        by_a, by_b = rule_tables(self.rules, consts[1])
        d_left, d_right, u_left, u_right = self.sides
        return (
            Factor(by_a, d_left[...], d_right[...], consts),
            Factor(by_b, u_right[...], u_left[...], consts),
        )

    def prepare(self, member):
        down, up = self.factors()
        self.down[...] = down.whole().astype(jnp.bfloat16)
        self.up[...] = up.whole().astype(jnp.bfloat16)
        for number, (offset, length) in enumerate(SPANS):
            row = lax.broadcasted_iota(jnp.int32, (length, 1), 0)
            alive = row < own_length(self.lengths, member, number)
            self.live[offset : offset + length, :] = jnp.where(alive, 1.0, 0.0)

    def adapter(self, i):
        bf = jnp.bfloat16
        r = rows_of(i)
        ffn = self.acc[r, :]
        low = ffn.astype(bf)
        value, slope = gelu_both(dot(low, self.down[...]))
        value = value.astype(bf)
        self.put_res(i, (self.mid[r, :] + ffn + dot(value, self.up[...], NT)).astype(bf))
        g_out = self.cot_rows(i) * self.live[r, :]
        g_low = g_out.astype(bf)
        self.gout[r, :] = g_low
        g_sq = (dot(g_low, self.up[...]) * slope).astype(bf)
        self.g_up[...] += dot(g_low, value, TN)
        self.g_down[...] += dot(low, g_sq, TN)
        self.gffn[r, :] = (g_out + dot(g_sq, self.down[...], NT)).astype(bf)

    def backward(self, j):
        dg = self.slope(j)
        for half in range(2):
            r = pl.ds(half * (self.n // 2), self.n // 2)
            g = (dot(self.gffn[r, :], self.wu(j), NT) * dg[r, :].astype(jnp.float32)).astype(jnp.bfloat16)
            dg[r, :] = g
            self.acc[r, :] += dot(g, self.wi(j))

    def last(self, i):
        r = rows_of(i)
        total = self.mid[r, :]
        g_n2 = self.acc[r, :]
        scale = lax.rsqrt(jnp.mean(total * total, axis=-1, keepdims=True) + NORM_EPS)
        self.g_gain[...] += jnp.sum(total * scale * g_n2, axis=0, keepdims=True)
        scaled = self.gain[...] * g_n2
        centre = jnp.mean(total * scaled, axis=-1, keepdims=True)
        g_mid = self.gout[r, :].astype(jnp.float32) + scale * scaled - total * (scale * scale * scale * centre)
        self.mid[r, :] = g_mid
        self.glow[r, :] = g_mid.astype(jnp.bfloat16)

    def projection(self, m):
        grad = dot(self.ctx[m], self.glow[...], TN).astype(jnp.bfloat16)
        self.ctx[m] = dot(self.glow[...], self.wo(m), NT).astype(jnp.bfloat16)
        return grad

    def adapter_all(self):
        self.g_down[...] = jnp.zeros_like(self.g_down)
        self.g_up[...] = jnp.zeros_like(self.g_up)
        each_of(self.n // RCH, self.adapter)

    def adapter_grads(self):
        other, pick = self.other, self.consts[1]
        down, up = self.factors()
        g_a, g_dl, g_dr = down.back(self.g_down[...])
        g_b, g_ur, g_ul = up.back(self.g_up[...])
        other[...] = jnp.zeros_like(other)
        for at, tall in ((ROW_DL, g_dl), (ROW_UR, g_ur)):
            other[at : at + 4, :] = tall[:, :128]
            other[at + 4 : at + 8, : tall.shape[1] - 128] = tall[:, 128:]
        for at, short in ((ROW_DR, g_dr), (ROW_UL, g_ul)):
            other[at : at + 4, :KA] = short
        for i in range(KRON):
            at = ROW_RULES + 4 * i
            other[at : at + 4, :KRON] = precise(g_a, pick[i], NT) + precise(pick[i], g_b, NT)


def middle_kernel(
    x_hbm, ctx_hbm, wo_hbm, wi_hbm, wu_hbm, cot_hbm, gain, lengths, rules, d_left, d_right, u_left, u_right,
    same, pick, fold, agree,
    res_hbm, gmid_hbm, gctx_hbm, go_hbm, gi_hbm, gu_hbm, other,
    down, up, g_down, g_up, g_gain, live, x, ctx, wo, wi, wu, cot, mid, n2, act, dg, acc, gffn, glow, sem, sems, out_sems,
):
    gain = gain[...].reshape(1, D)
    loads = [
        pltpu.make_async_copy(src, dst, sems.at[i])
        for i, (src, dst) in enumerate(
            ((x_hbm, x), (ctx_hbm, ctx), (wo_hbm, wo), (wi_hbm, wi), (wu_hbm, wu), (cot_hbm, cot))
        )
    ]
    for load in loads:
        load.start()
    def put_res(i, value):
        x[rows_of(i), :] = value

    layer = Layer(
        x_rows=lambda i: x[rows_of(i), :].astype(jnp.float32), cot_rows=lambda i: cot[rows_of(i), :].astype(jnp.float32),
        wo=lambda m: wo[m], wi=lambda j: wi[rows_of(j, FCH), :], wu=lambda j: wu[rows_of(j, FCH), :],
        chunk=FCH, ctx=ctx, gain=gain, lengths=lengths, rules=rules, sides=(d_left, d_right, u_left, u_right),
        consts=(same, pick, fold, agree), down=down, up=up, g_down=g_down, g_up=g_up, g_gain=g_gain, live=live, mid=mid,
        n2=n2, act=act, dg=dg, acc=acc, gffn=gffn, glow=glow, put_res=put_res, gout=cot, other=other,
        slope=lambda j: dg.at[:, rows_of(j, FCH)],
    )
    layer.prepare(lax.axis_index("mp"))
    for load in loads:
        load.wait()
    each_of(layer.n // RCH, layer.midway)
    acc[...] = jnp.zeros_like(acc)
    count = wi.shape[0] // FCH
    each_of(count, layer.forward)
    layer.adapter_all()
    acc[...] = jnp.zeros_like(acc)
    g_gain[...] = jnp.zeros_like(g_gain)

    def stores(j):
        f = rows_of(j, FCH)
        return [
            pltpu.make_async_copy(src.at[pl.ds(0, FCH), f], dst.at[f], sem.at[k, j])
            for k, (src, dst) in enumerate(((act, gu_hbm), (dg, gi_hbm)))
        ]

    def backward(j):
        f = rows_of(j, FCH)
        layer.backward(j)
        act[:FCH, f] = dot(act[:, f], gffn[...], TN).astype(jnp.bfloat16)
        dg[:FCH, f] = dot(dg[:, f], n2[...], TN).astype(jnp.bfloat16)
        for store in stores(j):
            store.start()

    each_of(count, backward)
    each_of(layer.n // RCH, layer.last)
    for m in range(4):
        gffn[CTX_PAD * m : CTX_PAD * (m + 1), :] = layer.projection(m)
    layer.adapter_grads()
    put_row(other, ROW_FFN, g_gain[...])
    copies = [
        pltpu.make_async_copy(src, dst, out_sems.at[k])
        for k, (src, dst) in enumerate(((x, res_hbm), (mid, gmid_hbm), (gffn, go_hbm), (ctx, gctx_hbm)))
    ]
    for copy in copies:
        copy.start()
    each_of(count, lambda j: [store.wait() for store in stores(j)])
    for copy in copies:
        copy.wait()


def middle(x, ctx, wo, wi, wu, cot, gain, lengths, factors):
    n, ff = x.shape[0], wi.shape[0]
    bf, f32 = jnp.bfloat16, jnp.float32
    hbm = pl.BlockSpec(memory_space=pl.ANY)
    vmem = pl.BlockSpec(memory_space=pltpu.VMEM)
    shape = jax.ShapeDtypeStruct
    return pl.pallas_call(
        middle_kernel,
        out_shape=[
            shape((n, D), bf),
            shape((n, D), f32),
            shape((4, n, CTX_PAD), bf),
            shape((4 * CTX_PAD, D), bf),
            shape((ff, D), bf),
            shape((ff, D), bf),
            shape((ROW_END, 128), f32),
        ],
        in_specs=[hbm] * 6 + [vmem] + [pl.BlockSpec(memory_space=pltpu.SMEM)] + [vmem] * 9,
        out_specs=[hbm] * 6 + [vmem],
        scratch_shapes=[
            pltpu.VMEM((D, ADAPT_PAD), bf),
            pltpu.VMEM((D, ADAPT_PAD), bf),
            pltpu.VMEM((D, ADAPT_PAD), f32),
            pltpu.VMEM((D, ADAPT_PAD), f32),
            pltpu.VMEM((1, D), f32),
            pltpu.VMEM((n, 1), f32),
            pltpu.VMEM((n, D), bf),
            pltpu.VMEM((4, n, CTX_PAD), bf),
            pltpu.VMEM((4, CTX_PAD, D), bf),
            pltpu.VMEM((ff, D), bf),
            pltpu.VMEM((ff, D), bf),
            pltpu.VMEM((n, D), bf),
            pltpu.VMEM((n, D), f32),
            pltpu.VMEM((n, D), bf),
            pltpu.VMEM((n, ff), bf),
            pltpu.VMEM((n, ff), bf),
            pltpu.VMEM((n, D), f32),
            pltpu.VMEM((n, D), bf),
            pltpu.VMEM((n, D), bf),
            pltpu.SemaphoreType.DMA((2, ff // FCH)),
            pltpu.SemaphoreType.DMA((6,)),
            pltpu.SemaphoreType.DMA((4,)),
        ],
        compiler_params=pltpu.CompilerParams(vmem_limit_bytes=63 * 2**20),
        name="middle",
    )(x, ctx, wo, wi, wu, cot, gain, lengths, *factors, *map(jnp.asarray, adapter_constants()))


FRONT = (
    "s:o s:q ex0 a:o0",
    "a:q0 a:q1 s:i a:q2",
    "c:q0 a:o1 c:o0 s:u",
    "a:q3 c:q1 a:o2 a:i0",
    "c:q2 c:o1 c:q3 a:u0",
    "f:q ex1 n A",
    "A A a:o3 a:u1",
    "A a:i1 c:i0 A",
    "A A c:u0 c:o2",
    "A A c:o3 A",
    "f:o a:i2 A A",
    "O c:i1 c:u1 a:u2",
    "F0 a:i3 F1 c:i2",
    "c:u2 a:u3 c:i3 F2",
    "c:u3 F3",
)


def front_order():
    plan, now = {"first": []}, "first"
    pieces = 0
    for step in " ".join(FRONT).split():
        if step == "A":
            now, pieces = ("A", pieces), pieces + 1
        elif step[0] in "OF":
            plan["before", step] = plan.pop("open", [])
            now = "open"
        else:
            plan.setdefault(now, []).append(step)
    return plan


def front_kernel(
    depth, group, tok, cot, w_qkv, w_o, w_in, w_out, choice, gain, gain_ffn, lengths, pos_table, onehot,
    rules, d_left, d_right, u_left, u_right, same, pick, fold, agree,
    tok_s, gq_hbm, normed_hbm, packed_hbm, out, mid_hbm, ctx_hbm, go_hbm, gi_hbm, gu_hbm, dg_hbm, pu_hbm, gffn_hbm, n2_hbm,
    gout_hbm, long_hbm, rest_hbm, other,
    wq, wo, wi, wu, mask, rows, x, y, gq, go, gi, gu, nrm, packed, ctx,
    down, up, g_down, g_up, live, mid, n2, act, dg, acc, gffn, res, sem, out_sems, local, *sems,
):
    p = Place(depth)
    bf = jnp.bfloat16
    p.greet(0)
    gain, gain_ffn = gain[...].reshape(1, D), gain_ffn[...].reshape(1, D)
    per_head = [dot(w_qkv[h].astype(bf), choice[3 * DH * h : 3 * DH * (h + 1), :]) for h in range(3)]
    wq[...] = sum(per_head).astype(bf)
    wo[...] = jnp.zeros_like(wo)
    wo[: w_o.shape[0], :] = w_o[...].astype(bf)
    wi[...] = w_in[...].astype(bf)
    wu[...] = w_out[...].astype(bf)
    arrays = {
        name: Gather(p, name == "q", shard, buf, *sems[3 * i : 3 * i + 3])
        for i, (name, shard, buf) in enumerate((("q", wq, gq), ("o", wo, go), ("i", wi, gi), ("u", wu, gu)))
    }
    first, second = Exchange(p, tok, x, *sems[12:15]), Exchange(p, cot, y, *sems[15:18])
    keep_x = pltpu.make_async_copy(x, tok_s, local.at[0])
    keep_n = pltpu.make_async_copy(nrm, normed_hbm, local.at[1])
    keep_q = pltpu.make_async_copy(gq, gq_hbm, local.at[2])
    quarter = RCH // SEG

    def float_rows(ref):
        return lambda i: ref[pl.ds(quarter * i, quarter)].reshape(RCH, D).astype(jnp.float32)

    def put_res(i, value):
        res[pl.ds(quarter * i, quarter)] = value.reshape(quarter, SEG, D)

    chunk_rows = 8 * wi.shape[0]
    layer = Layer(
        x_rows=float_rows(x), cot_rows=float_rows(y),
        wo=lambda m: go[m].reshape(CTX_PAD, D), wi=lambda j: gi[j].reshape(-1, D), wu=lambda j: gu[j].reshape(-1, D),
        chunk=chunk_rows, ctx=ctx, gain=gain_ffn, lengths=lengths, rules=rules, sides=(d_left, d_right, u_left, u_right),
        consts=(same, pick, fold, agree), down=down, up=up, g_down=g_down, g_up=g_up, live=live, mid=mid, n2=n2, act=act,
        dg=dg, acc=acc, gffn=gffn, put_res=put_res, gout=nrm, other=other,
    )
    third = Exchange(p, res, out, *sems[18:21])

    def norm(i):
        v = x[i].astype(jnp.float32)
        scale = lax.rsqrt(jnp.mean(v * v, axis=-1, keepdims=True) + NORM_EPS)
        nrm[rows_of(i, SEG), :] = (v * scale * gain[...]).astype(bf)

    def norms():
        first.finish()
        keep_x.start()
        each_of(x.shape[0], norm)
        keep_n.start()
        fill_mask(mask, lengths, p.m)
        fill_rows(rows, pos_table, onehot)
        layer.prepare(p.m)
        acc[...] = jnp.zeros_like(acc)

    def step(name):
        kind, rest = name[0], name[2:]
        if name == "n":
            norms()
        elif name in ("ex0", "ex1"):
            (first, second)[int(name[2])].start()
        elif kind == "s":
            arrays[rest].start()
        elif kind == "f":
            arrays[rest].finish()
        elif kind == "a":
            arrays[rest[0]].along(int(rest[1:]))
        elif kind == "c":
            arrays[rest[0]].across(int(rest[1:]))

    def steps(names):
        for name in names:
            step(name)

    plan = front_order()
    p.meet(0)
    steps(plan["first"])
    keep_q.start()

    def piece(m, place):
        at = sum(place) + place[0]
        for loop in range(4):
            names = plan.get(("A", 3 * loop + at))
            if names:
                pl.when(m == loop)(functools.partial(steps, names))

    def keeps(m):
        lanes = rows_of(m, D)
        return [
            pltpu.make_async_copy(packed.at[m], packed_hbm.at[m], local.at[3 + m]),
            pltpu.make_async_copy(act.at[:, lanes], long_hbm.at[m], local.at[7 + m]),
            pltpu.make_async_copy(dg.at[pl.ds(0, KEPT_REST), lanes], rest_hbm.at[m], local.at[11 + m]),
            pltpu.make_async_copy(ctx.at[m], ctx_hbm.at[m], local.at[15 + m]),
        ]

    def keep_probs(m, number, unit, h, probs):
        offset, length, q0, width = unit
        places = kept_at(offset, length, h)
        row, rows_kept, lane, _ = places[min(q0 // width, len(places) - 1)]
        lane = lane + (q0 if len(places) == 1 else 0)
        lanes = pl.ds(pl.multiple_of(D * m + lane, TILE), width)
        if row < KEPT_LONG:
            act[row : row + rows_kept, lanes] = probs
        else:
            dg[row - KEPT_LONG : row - KEPT_LONG + rows_kept, lanes] = probs

    def heads(m):
        w = gq[m // 2, m % 2].reshape(D, QKV_PAD)
        packed[m] = dot(nrm[...], w).astype(bf)
        keeps(m)[0].start()
        attend_group(
            packed.at[m], mask, rows[m], ctx.at[m], group, functools.partial(piece, m), functools.partial(keep_probs, m)
        )
        for copy in keeps(m)[1:]:
            copy.start()

    def stores(z):
        lanes = rows_of(z, chunk_rows)
        return [
            pltpu.make_async_copy(gi.at[z], gi_hbm.at[z], sem.at[0, z]),
            pltpu.make_async_copy(gu.at[z], gu_hbm.at[z], sem.at[1, z]),
            pltpu.make_async_copy(dg.at[:, lanes], dg_hbm.at[z], sem.at[2, z]),
        ]

    def weights(z):
        lanes = rows_of(z, chunk_rows)
        return pltpu.make_async_copy(act.at[pl.ds(0, chunk_rows), lanes], pu_hbm.at[z], sem.at[3, z])

    each_of(4, heads)
    steps(plan[("before", "O")])
    keep_o = pltpu.make_async_copy(go, go_hbm, out_sems.at[0])
    keep_o.start()
    each_of(layer.n // RCH, layer.midway)
    tail = [
        pltpu.make_async_copy(src, dst, out_sems.at[1 + k])
        for k, (src, dst) in enumerate(((mid, mid_hbm), (n2, n2_hbm), (nrm, gout_hbm), (gffn, gffn_hbm)))
    ]
    tail[0].start()
    tail[1].start()
    each_of(4, lambda m: [copy.wait() for copy in keeps(m)])

    def chunk(e):
        for k in range(depth):
            pl.when(e == k)(functools.partial(steps, plan[("before", f"F{k}")]))
        z = p.nearest(e)
        for name in "iu":
            arrays[name].finish_at(z)
        layer.forward(z)
        for copy in stores(z):
            copy.start()

    each_of(depth, chunk)
    second.finish()
    for copy in (keep_x, keep_n, keep_q):
        copy.wait()
    layer.adapter_all()
    third.start()
    tail[2].start()
    tail[3].start()

    def weights_out(k):
        z = p.order(k)
        lanes = rows_of(z, chunk_rows)
        act[:chunk_rows, lanes] = dot(act[:, lanes], gffn[...], TN).astype(bf)
        weights(z).start()

    for k in range(depth):
        weights_out(k)
    layer.adapter_grads()
    for copy in (keep_o, *tail):
        copy.wait()
    each_of(depth, lambda z: [copy.wait() for copy in (*stores(z), weights(z))])
    third.finish()
    for g in (*arrays.values(), first, second, third):
        g.drain()


def front(depth, group, tok, cot, shards, rows_of_shards, gains, lengths, pos_table, factors):
    hbm = pl.BlockSpec(memory_space=pl.ANY)
    vmem = pl.BlockSpec(memory_space=pltpu.VMEM)
    bf, f32 = jnp.bfloat16, jnp.float32
    shape = jax.ShapeDtypeStruct
    n = tok.shape[0] * SEG
    kept = [(rows, QKV_PAD if i == 0 else D) for i, rows in enumerate(rows_of_shards)]
    whole = [((2, 2, depth, 2) if i == 0 else (depth, 2, 2, 2)) + s for i, s in enumerate(kept)]
    ff = 8 * depth * kept[2][0]
    return pl.pallas_call(
        functools.partial(front_kernel, depth, group),
        out_shape=[
            shape(tok.shape, bf),
            shape(whole[0], bf),
            shape((n, D), bf),
            shape((4, n, QKV_PAD), bf),
            shape(tok.shape, bf),
            shape((n, D), f32),
            shape((4, n, CTX_PAD), bf),
            *[shape(s, bf) for s in whole[1:]],
            shape((depth, n, D), bf),
            shape((depth, D, D), bf),
            shape((n, D), bf),
            shape((n, D), bf),
            shape((n, D), bf),
            shape((4, KEPT_LONG, D), bf),
            shape((4, KEPT_REST, D), bf),
            shape((ROW_END, 128), f32),
        ],
        in_specs=[hbm] * 2 + [vmem] * 7 + [pl.BlockSpec(memory_space=pltpu.SMEM)] + [vmem] * 11,
        out_specs=[hbm] * 17 + [vmem],
        scratch_shapes=[pltpu.VMEM(s, bf) for s in kept]
        + [
            pltpu.VMEM((n, TILE), bf),
            pltpu.VMEM((4, 3, 512), f32),
            pltpu.VMEM(tok.shape, bf),
            pltpu.VMEM(tok.shape, bf),
            *[pltpu.VMEM(s, bf) for s in whole],
            pltpu.VMEM((n, D), bf),
            pltpu.VMEM((4, n, QKV_PAD), bf),
            pltpu.VMEM((4, n, CTX_PAD), bf),
            pltpu.VMEM((D, ADAPT_PAD), bf),
            pltpu.VMEM((D, ADAPT_PAD), bf),
            pltpu.VMEM((D, ADAPT_PAD), f32),
            pltpu.VMEM((D, ADAPT_PAD), f32),
            pltpu.VMEM((n, 1), f32),
            pltpu.VMEM((n, D), f32),
            pltpu.VMEM((n, D), bf),
            pltpu.VMEM((n, ff), bf),
            pltpu.VMEM((n, ff), bf),
            pltpu.VMEM((n, D), f32),
            pltpu.VMEM((n, D), bf),
            pltpu.VMEM(tok.shape, bf),
            pltpu.SemaphoreType.DMA((4, depth)),
            pltpu.SemaphoreType.DMA((5,)),
            pltpu.SemaphoreType.DMA((19,)),
        ]
        + Gather.sems(depth) * 4
        + Exchange.sems() * 3,
        compiler_params=pltpu.CompilerParams(
            collective_id=2, has_side_effects=True, vmem_limit_bytes=63 * 2**20
        ),
        name="front",
    )(
        tok, cot, *shards, jnp.asarray(column_choice(group), bf), *gains, lengths, pos_table,
        jnp.asarray(offset_onehot()), *factors, *map(jnp.asarray, adapter_constants()),
    )


BACK = (
    "Su0 K Su3 Hu0",
    "Su2 K K Hu3",
    "Hu2 Si0 Qu0 K",
    "Su1 K Hi0 K",
    "K Qu3 K Qu2",
    "K Hu1 K K",
    "So3 So2 K Fu0",
    "Qi0 So0 K K",
    "Si2 K K Ho0",
    "Hi2 Ho3 K K",
    "Qu1 K K Si1",
    "Si3 K Qo0 K",
    "Ho2 K Fu1 Qo3",
    "So1 K Qi2 Fu2",
    "K Qo2 Hi1 K",
    "K K Hi3 K",
    "K Fi0 K K",
    "K Ho1 K Sq0",
    "Fu3 Fo3 Qi3 Qi1",
    "Hq0 Fo0 Sq3 Sq2",
    "Fo2 N TB Cu",
    "Qo1 Fi3 Fi2 Hq2",
    "Sq1 Qq0 T0 Hq1",
    "Fo1 Eu Hq3 Co",
    "Fi1 Qq2 Fq0 T1",
    "Qq1 T2 x1 Fq2",
    "Ci Qq3 T3 Fq3",
    "Fq1 Eo Cq Ei",
    "Eq T4",
)


def back_order():
    plan, pieces = {}, 0
    for step in " ".join(BACK).split():
        if step in "KN":
            pieces += 1
        else:
            plan.setdefault(pieces, []).append(step)
    return plan


PIECES = 6


def back_kernel(
    depth, bits, group,
    tok_hbm, gq_hbm, nrm_hbm, packed_hbm, mid_hbm, ctx_hbm, go_hbm, gi_hbm, gu_hbm, dg_hbm, gffn_hbm, n2_hbm, gout_hbm,
    long_hbm, rest_hbm, pu, gain, gain_ffn, onehot, other,
    oq, oo, oi, ou, small, gtok,
    wu, wi, dg, acc, mid, gffn, nrm, gout, x, ctx, go, kept, g_gain, sums_s, mine_u, sem_u, local, chunk_sem, gq_sem, *scr,
):
    p = Place(depth)
    n = depth
    bf = jnp.bfloat16
    gain, gain_ffn = gain[...].reshape(1, D), gain_ffn[...].reshape(1, D)
    width = pl.ds(0, QKV_PAD)
    arrays = {
        "u": Scatter(p, False, pu, ou, *scr[0:6], mine_u, sem_u),
        "i": Scatter(p, False, wi, oi, *scr[6:12]),
        "o": Scatter(p, False, go, oo, *scr[12:18]),
        "q": Scatter(
            p, True, wu, oq, *scr[18:24],
            region=lambda core, z: wu.at[:, core, z // 2, z % 2, :, :, width],
        ),
    }
    row_g = Exchange(p, x, gtok, *scr[24:27])
    total = Sum(p, bits, small, *scr[27:30])
    layer = Layer(
        wo=lambda m: go[m].reshape(CTX_PAD, D), wi=lambda z: wi[z].reshape(-1, D),
        wu=lambda z: wu[z // 2, z % 2].reshape(-1, D), slope=lambda z: dg.at[z], ctx=ctx, gain=gain_ffn, g_gain=g_gain,
        mid=mid, n2=nrm, acc=acc, gffn=gffn, glow=gffn, gout=gout,
    )

    def load(src, dst, k):
        return pltpu.make_async_copy(src, dst, local.at[k])

    early = [
        load(src, dst, k)
        for k, (src, dst) in enumerate(
            ((gffn_hbm, gffn), (n2_hbm, nrm), (mid_hbm, mid), (gout_hbm, gout), (ctx_hbm, ctx), (go_hbm, go), (tok_hbm, x))
        )
    ]

    def chunk_in(k):
        z = p.order(k)
        pairs = ((dg_hbm.at[z], dg.at[z]), (gu_hbm.at[z], wu.at[z // 2, z % 2]), (gi_hbm.at[z], wi.at[z]))
        return [pltpu.make_async_copy(src, dst, chunk_sem.at[j, k]) for j, (src, dst) in enumerate(pairs)]

    def packed_in(m):
        return load(packed_hbm.at[m], dg.at[m, :, width], 8 + m)

    def gq_in(m, z):
        y, c = m // 2, m % 2
        return pltpu.make_async_copy(
            gq_hbm.at[y, c, z], wu.at[y, c, z // 2, z % 2, :, :, width], gq_sem.at[m, z]
        )

    def kept_in(m):
        slot = m % 2
        return [
            load(long_hbm.at[m], kept.at[slot, pl.ds(0, KEPT_LONG)], 12 + slot),
            load(rest_hbm.at[m], kept.at[slot, pl.ds(KEPT_LONG, KEPT_REST)], 14 + slot),
        ]

    todo = total.steps()

    def steps(names):
        for name in names:
            if name == "x1":
                row_g.start()
            elif name[0] == "T":
                todo.pop(0)()
            else:
                array = arrays[name[1]]
                if name[0] in "CE":
                    (array.collect if name[0] == "C" else array.finish)()
                else:
                    k = int(name[2:])
                    {"S": array.start, "H": array.to_half, "Q": array.to_quarter, "F": array.forward}[name[0]](k)
                    if name[0] == "Q":
                        array.origin(k)

    plan = back_order()

    def place(k):
        steps(plan.pop(k, ()))

    p.greet(bits)
    early[0].start()
    for k in range(n):
        for copy in chunk_in(k):
            copy.start()
        if k == 0:
            early[1].start()
    for copy in (*early[2:], *kept_in(0)):
        copy.start()
    small[...] = jnp.zeros_like(small)
    small[ROW_OTHER:, :] = other[...]
    acc[...] = jnp.zeros_like(acc)
    g_gain[...] = jnp.zeros_like(g_gain)
    p.meet(bits)
    place(0)
    early[0].wait()
    for k in range(n):
        z = p.order(k)
        for copy in chunk_in(k):
            copy.wait()
        layer.backward(z)
        place(2 * k + 1)
        if k == 0:
            early[1].wait()
        wi[z] = dot(dg[z], nrm[...], TN).astype(bf).reshape(wi.shape[1:])
        place(2 * k + 2)
    for m in range(4):
        packed_in(m).start()
        for z in range(n):
            gq_in(m, z).start()
    renew = load(nrm_hbm, nrm, 7)
    renew.start()
    for copy in early[2:]:
        copy.wait()
    each_of(layer.n // RCH, layer.last)
    place(2 * n + 1)

    def project(m):
        go[m] = layer.projection(m).reshape(go.shape[1:])

    each_of(4, project)
    acc[...] = jnp.zeros_like(acc)
    place(2 * n + 2)
    renew.wait()
    for m in range(4):
        packed_in(m).wait()
        for z in range(n):
            gq_in(m, z).wait()

    def piece(m, j):
        for loop in range(4):
            names = plan.get(2 * n + 2 + PIECES * loop + j + 1)
            if names:
                pl.when(m == loop)(functools.partial(steps, names))

    def tick(m, at):
        number, head = at
        if number == 0:
            piece(m, head)
        elif head == 8:
            piece(m, 3)

    def heads(m):
        slot, y, c = m % 2, m // 2, m % 2
        for copy in kept_in(m):
            copy.wait()

        def ahead():
            for copy in kept_in(m + 1):
                copy.start()

        pl.when(m < 3)(ahead)
        packed = dg.at[m, :, width]
        attend_group_back(packed, Kept(kept.at[slot]), ctx.at[m], packed, sums_s.at[m], group, functools.partial(tick, m))
        whole = (Ellipsis, slice(0, QKV_PAD))
        acc[...] += dot(packed[...], wu[y, c][whole].reshape(D, QKV_PAD), NT)
        piece(m, 4)
        wu[y, c, :, :, :, :, 0:QKV_PAD] = dot(nrm[...], packed[...], TN).astype(bf).reshape(*wu.shape[2:6], QKV_PAD)
        piece(m, 5)

    each_of(4, heads)
    small[ROW_TABLE : ROW_TABLE + 16, :] = jnp.zeros((16, 128), jnp.float32)
    for m in range(4):
        small[ROW_TABLE + 3 * m : ROW_TABLE + 3 * m + 3, :] = precise(sums_s[m], onehot[...])
    put_row(small, ROW_OTHER + ROW_FFN, g_gain[...])

    def last(s, g_gain):
        r = rows_of(s, SEG)
        v = x[s].astype(jnp.float32)
        g_n1 = acc[r, :]
        scale = lax.rsqrt(jnp.mean(v * v, axis=-1, keepdims=True) + NORM_EPS)
        scaled = gain * g_n1
        centre = jnp.mean(v * scaled, axis=-1, keepdims=True)
        x[s] = (mid[r, :] + scale * scaled - v * (scale * scale * scale * centre)).astype(bf)
        return g_gain + jnp.sum(v * scale * g_n1, axis=0, keepdims=True)

    put_row(small, ROW_GAIN, lax.fori_loop(0, x.shape[0], last, jnp.zeros((1, D), jnp.float32)))
    place(2 * n + 2 + 4 * PIECES + 1)
    row_g.finish()
    for g in (*arrays.values(), row_g, total):
        g.drain()


def back(depth, bits, group, kept, ffn, pu, gains, onehot, other):
    hbm = pl.BlockSpec(memory_space=pl.ANY)
    vmem = pl.BlockSpec(memory_space=pltpu.VMEM)
    bf, f32 = jnp.bfloat16, jnp.float32
    shape = jax.ShapeDtypeStruct
    tok, gq = kept[:2]
    mid, ctx, go, gi = ffn[:4]
    n = mid.shape[0]
    small_rows = ROW_OTHER + other.shape[0]
    outs = [shape(s.shape[4:], f32) for s in (gq, go, gi, gi)]
    outs += [shape((small_rows, 128), f32), shape(tok.shape, bf)]
    dma = pltpu.SemaphoreType.DMA
    scratch = [
        pltpu.VMEM((2, 2, 2, 2, 2, *gi.shape[4:]), bf),
        pltpu.VMEM(gi.shape, bf),
        pltpu.VMEM((depth, n, D), bf),
        pltpu.VMEM((n, D), f32),
        pltpu.VMEM((n, D), f32),
        pltpu.VMEM((n, D), bf),
        pltpu.VMEM((n, D), bf),
        pltpu.VMEM((n, D), bf),
        pltpu.VMEM(tok.shape, bf),
        pltpu.VMEM(ctx.shape, bf),
        pltpu.VMEM(go.shape, bf),
        pltpu.VMEM((2, KEPT_LONG + KEPT_REST, D), bf),
        pltpu.VMEM((1, D), f32),
        pltpu.VMEM((4, 3, 768), f32),
        pltpu.VMEM((depth, 2, 2) + gi.shape[4:], bf),
        dma((depth,)),
        dma((16,)),
        dma((3, depth)),
        dma((4, depth)),
    ]
    for s in (gi, gi, go, gq):
        scratch += Scatter.scratch(depth, *s.shape[4:])
    scratch += Exchange.sems() + Sum.scratch(bits, small_rows)
    return pl.pallas_call(
        functools.partial(back_kernel, depth, bits, group),
        out_shape=outs,
        in_specs=[hbm] * 16 + [vmem] * 4,
        out_specs=[vmem] * 5 + [hbm],
        scratch_shapes=scratch,
        compiler_params=pltpu.CompilerParams(
            collective_id=3, has_side_effects=True, vmem_limit_bytes=63 * 2**20
        ),
        name="back",
    )(*kept, *ffn, pu.reshape(gi.shape), *gains, onehot, other)


def finish_kernel(
    q, o, i, u, small, choice,
    gq, go, gi, gu, g_attn, g_ffn, g_table, g_rules, g_dl, g_dr, g_ul, g_ur,
):
    left = q[: gq.shape[1], :]
    parts = []
    for _ in range(3):
        parts.append(left.astype(jnp.bfloat16))
        left = left - parts[-1].astype(jnp.float32)
    for h in range(3):
        chosen = choice[3 * DH * h : 3 * DH * (h + 1), :]
        gq[h] = sum(dot(part, chosen, NT) for part in parts)
    go[...] = o[: go.shape[0], :]
    gi[...] = i[: gi.shape[0], :]
    gu[...] = u[: gu.shape[0], :]
    for k in range(D // 128):
        lanes = slice(128 * k, 128 * (k + 1))
        g_attn[lanes] = small[ROW_GAIN + k, :]
        g_ffn[lanes] = small[ROW_OTHER + ROW_FFN + k, :]
    g_table[...] = small[ROW_TABLE : ROW_TABLE + g_table.shape[0], :NB]
    for i in range(KRON):
        at = ROW_OTHER + ROW_RULES + 4 * i
        g_rules[i] = small[at : at + 4, :KRON]
    for ref, at in ((g_dl, ROW_OTHER + ROW_DL), (g_ur, ROW_OTHER + ROW_UR)):
        ref[:, :128] = small[at : at + 4, :]
        ref[:, 128:] = small[at + 4 : at + 8, : ref.shape[1] - 128]
    for ref, at in ((g_dr, ROW_OTHER + ROW_DR), (g_ul, ROW_OTHER + ROW_UL)):
        ref[...] = small[at : at + 4, :KA]


def finish(q, o, i, u, small, group, shapes):
    vmem = pl.BlockSpec(memory_space=pltpu.VMEM)
    return pl.pallas_call(
        finish_kernel,
        out_shape=[jax.ShapeDtypeStruct(s, jnp.float32) for s in shapes],
        in_specs=[vmem] * 6,
        out_specs=[vmem] * 12,
        name="finish",
    )(q, o, i, u, small, jnp.asarray(column_choice(group), jnp.bfloat16))


def round_up(n, m):
    return -(-n // m) * m


def pad_rows(a, rows):
    return jnp.pad(a, ((0, rows - a.shape[0]), (0, 0)))


HEADS = 12


def local(
    tokens,
    lengths,
    cotangent,
    w_qkv,
    w_o,
    w_in,
    w_out,
    gain_attn,
    gain_ffn,
    pos_table,
    phm_rules,
    down_left,
    down_right,
    up_left,
    up_right,
):
    dp_count, mp_count = lax.axis_size("dp"), lax.axis_size("mp")
    depth = dp_count // 2
    bits = dp_count.bit_length() - 1
    devices = dp_count * mp_count
    member = lax.axis_index("mp")
    tok_rows = tokens.shape[0]
    seg_count = tok_rows // SEG
    o_rows, in_rows, q_rows = w_o.shape[0], w_in.shape[1], w_qkv.shape[0]
    bf = jnp.bfloat16
    group = o_rows if o_rows % 24 == 0 and round_up(o_rows, 16) * 3 == o_rows * 4 else 3 * DH
    rows_of_shards = [round_up(r, 16) for r in (q_rows, o_rows, in_rows, in_rows)]
    tok_in, cot_in = tokens.reshape(seg_count, SEG, D), cotangent.reshape(seg_count, SEG, D)
    merged = depth == 4 and group == o_rows and rows_of_shards[0] == q_rows and rows_of_shards[2] == in_rows
    factors = (phm_rules, down_left, down_right, up_left, up_right)
    gains = (gain_attn, gain_ffn)
    if merged:
        shards = (w_qkv.transpose(1, 0, 2), w_o, w_in.T, w_out)
        *kept, out, mid, ctx, go, gi, gu, dg, pu, gffn, n2, gout, long, rest, other = front(
            depth, group, tok_in, cot_in, shards, rows_of_shards, gains, lengths, pos_table.T, factors
        )
    else:
        shards = (head_columns(w_qkv.astype(bf), group), w_o.astype(bf), w_in.astype(bf).T, w_out.astype(bf))
        shards = [pad_rows(s, r) for s, r in zip(shards, rows_of_shards)]
        tok_s, cot_s, gq, go, gi, gu = gather_all(depth, tok_in, cot_in, shards)
    def plain(g, rows):
        return g.reshape(devices, g.shape[-2], D)[:, :rows].reshape(devices * rows, D)

    def slots(g, rows):
        padded = jnp.pad(g.reshape(devices, rows, D), ((0, 0), (0, round_up(rows, 16) - rows), (0, 0)))
        return padded.reshape(depth, 2, 2, 2, padded.shape[1], D)

    if not merged:
        tokens_s = tok_s.reshape(tok_rows, D)
        if group == o_rows:
            dense_o = go.reshape(mp_count, CTX_PAD, D)
        else:
            dense_o = plain(go, o_rows).reshape(mp_count, 3 * DH, D)
            dense_o = jnp.pad(dense_o, ((0, 0), (0, CTX_PAD - 3 * DH), (0, 0)))
        qkv_full = gq.reshape(mp_count, dp_count, rows_of_shards[0], QKV_PAD)[:, :, :q_rows]
        qkv_full = qkv_full.reshape(mp_count, D, QKV_PAD)
        live = jnp.concatenate(
            [jnp.arange(length) < own_length(lengths, member, i) for i, (_, length) in enumerate(SPANS)]
        )
        mask = key_mask(live)
        rows = jnp.einsum("bh,br->hr", pos_table, offset_onehot(), precision=FULL_PRECISION).reshape(mp_count, 3, 512)
        normed_attn, packed, context = attention(tokens_s, gains[0].reshape(1, D), qkv_full, mask, rows, group)
        result, grad_mid, grad_context, grad_w_o, grad_w_in, grad_w_out, other = middle(
            tokens_s,
            context,
            dense_o,
            plain(gi, in_rows),
            plain(gu, in_rows),
            cot_s.reshape(tok_rows, D),
            gains[1],
            lengths,
            factors,
        )
    onehot = jnp.asarray(np.pad(table_onehot(), ((0, 0), (0, 128 - NB))))
    if merged:
        oq, oo, oi, ou, summed, gtok = back(
            depth, bits, group, kept, (mid, ctx, go, gi, gu, dg, gffn, n2, gout, long, rest), pu, gains, onehot, other
        )
    else:
        if group == o_rows:
            part_o = grad_w_o.reshape(depth, 2, 2, 2, round_up(o_rows, 16), D)
        else:
            part_o = slots(grad_w_o.reshape(mp_count, CTX_PAD, D)[:, : 3 * DH].reshape(D, D), o_rows)
        result = result.reshape(seg_count, SEG, D)
        packed_grads, sums = attention_back(packed, grad_context, mask, rows, group)
        table_grad = jnp.dot(sums.reshape(HEADS, 768), onehot, precision=FULL_PRECISION)
        grad_w_qkv = jnp.einsum("td,mtc->mdc", normed_attn, packed_grads, preferred_element_type=jnp.float32).astype(bf)
        grad_n1 = jnp.einsum("mtc,mdc->td", packed_grads, qkv_full, preferred_element_type=jnp.float32)
        _, norm_back_attn = jax.vjp(normed, tokens_s.astype(jnp.float32), gain_attn)
        grad_x_part, grad_gain_attn = norm_back_attn(grad_n1)
        grad_tokens = (grad_mid + grad_x_part).astype(bf)
        small = jnp.concatenate([
            jnp.pad(grad_gain_attn.reshape(D // 128, 128), ((0, ROW_TABLE - D // 128), (0, 0))),
            jnp.pad(table_grad, ((0, ROW_OTHER - ROW_TABLE - HEADS), (0, 0))),
            other,
        ])
        part_q = grad_w_qkv.reshape(mp_count, dp_count, q_rows, QKV_PAD)
        part_q = jnp.pad(part_q, ((0, 0), (0, 0), (0, rows_of_shards[0] - q_rows), (0, 0)))
        part_q = part_q.reshape(2, 2, depth, 2, rows_of_shards[0], QKV_PAD)
        oq, oo, oi, ou, summed, out, gtok = scatter_all(
            depth, bits, (part_q, part_o, slots(grad_w_in, in_rows), slots(grad_w_out, in_rows)), small, result, grad_tokens.reshape(seg_count, SEG, D)
        )
    shapes = (
        (3, q_rows, 3 * DH), w_o.shape, w_in.shape[::-1], w_out.shape, (D,), (D,), pos_table.shape[::-1],
        phm_rules.shape, down_left.shape, down_right.shape, up_left.shape, up_right.shape,
    )
    g_qkv, g_o, g_in, g_out, g_attn, g_ffn, g_table, *smalls = finish(oq, oo, oi, ou, summed, group, shapes)
    return (
        out.reshape(tok_rows, D),
        gtok.reshape(tok_rows, D),
        g_qkv.transpose(1, 0, 2),
        g_o,
        g_in.T,
        g_out,
        g_attn,
        g_ffn,
        g_table.T,
        *smalls,
    )


def solution(mesh):
    return jax.shard_map(
        local,
        mesh=mesh,
        in_specs=(
            P(("dp", "mp"), None),
            P("dp"),
            P(("dp", "mp"), None),
            P("dp", "mp", None),
            P(("dp", "mp"), None),
            P(None, ("dp", "mp")),
            P(("dp", "mp"), None),
            P(),
            P(),
            P(),
            P(),
            P(),
            P(),
            P(),
            P(),
        ),
        out_specs=(
            P(("dp", "mp"), None),
            P(("dp", "mp"), None),
            P("dp", "mp", None),
            P(("dp", "mp"), None),
            P(None, ("dp", "mp")),
            P(("dp", "mp"), None),
            P(),
            P(),
            P(),
            P(),
            P(),
            P(),
            P(),
            P(),
        ),
        check_vma=False,
    )
```

```python
import functools
import itertools

import jax
import jax.experimental.pallas as pl
import jax.experimental.pallas.tpu as pltpu
import jax.numpy as jnp
import numpy as np
from jax import lax
from jax.sharding import PartitionSpec as P

D = 768
DH = 64
NB = 32
MAXDIST = 128
ADAPT = 48
KRON = 4
LEN_LONG = 512
LEN_MID = 256
LEN_SHORT = 128
SEG = 128


NORM_EPS = 1e-06
FULL_PRECISION = lax.Precision.HIGHEST


def rel_buckets(length):
    offsets = np.arange(-(length - 1), length)
    half_count = NB // 2
    exact_count = half_count // 2
    upward = (offsets > 0).astype(np.int64) * half_count
    distance = np.abs(offsets)
    scaled = (
        np.log(np.maximum(distance, 1) / exact_count)
        / np.log(MAXDIST / exact_count)
        * (half_count - exact_count)
    )
    far_bucket = np.minimum(
        exact_count + np.floor(np.maximum(scaled, 0.0)).astype(np.int64), half_count - 1
    )
    return upward + np.where(distance < exact_count, distance, far_bucket)


def normed(values, gain):
    return values * lax.rsqrt(jnp.mean(values * values, axis=-1, keepdims=True) + NORM_EPS) * gain


MESH = pl.DeviceIdType.MESH


class Place:
    def __init__(self, depth):
        d, m = lax.axis_index("dp"), lax.axis_index("mp")
        self.depth = depth
        self.d, self.m = d, m
        self.z, self.x, self.y, self.c = d // 2, d % 2, m // 2, m % 2
        dx, dy, c = 1 - 2 * self.x, 2 - 4 * self.y, self.c
        self.sib = (d, m + 1 - 2 * c)
        self.right, self.left = (d + 2, m), (d - 2, m)
        self.mp_peer = ((d, m + 1 - 2 * c), (d, m + dy), (d, 3 - m))
        self.xn, self.yn = (d + dx, m), (d, m + dy)
        self.a_nbr = (d + (1 - c) * dx, m + c * dy)
        self.b_nbr = (d + c * dx, m + (1 - c) * dy)
        self.a = self.x + c * (self.y - self.x)
        self.b = self.y + c * (self.x - self.y)

    def by_core(self, run):
        for core in (0, 1):
            pl.when(self.c == core)(functools.partial(run, core))

    def order(self, k):
        n = self.depth
        base = k // 2 if k % 2 == 0 else n - 1 - k // 2
        near = 1 - jnp.minimum(self.z // max(n // 2, 1), 1)
        return base + near * (n - 1 - 2 * base)

    def nearest(self, e):
        n, z = self.depth, self.z
        ahead = 1 - 2 * (z // ((n + 1) // 2))
        short = jnp.minimum(z, n - 1 - z)
        around = (1 - 2 * (e % 2)) * ((e + 1) // 2)
        return z + ahead * jnp.where(e <= 2 * short, around, e - short)

    def flip(self, bit):
        step = 1 << bit
        return (self.d + step * (1 - 2 * ((self.d // step) % 2)), self.m)

    def barrier(self, bits):
        self.greet(bits)
        self.meet(bits)

    def pals(self, bits):
        return [*self.mp_peer, self.xn] + [self.flip(bit) for bit in range(2, bits)]

    def greet(self, bits):
        sem = pltpu.get_barrier_semaphore()

        def greet(dev):
            pl.semaphore_signal(sem, 1, device_id=dev, device_id_type=MESH)

        for dev in self.pals(bits):
            greet(dev)
        pl.when(self.z > 0)(lambda: greet(self.left))
        pl.when(self.z < self.depth - 1)(lambda: greet(self.right))

    def meet(self, bits):
        ends = jnp.minimum(self.z, 1) + jnp.minimum(self.depth - 1 - self.z, 1)
        pl.semaphore_wait(pltpu.get_barrier_semaphore(), len(self.pals(bits)) + ends)


def remote(src, dst, send, recv, dev):
    return pltpu.make_async_remote_copy(
        src_ref=src, dst_ref=dst, send_sem=send, recv_sem=recv, device_id=dev, device_id_type=MESH
    )


def slot_of(buf, by_head, p):
    return buf.at[p.y, p.c, p.z, p.x] if by_head else buf.at[p.z, p.x, p.y, p.c]


def pair_of(buf, by_head, core, b, z):
    if by_head:
        return buf.at[b, 0, z] if core == 0 else buf.at[:, 1, z, b]
    return buf.at[z, :, b, 0] if core == 0 else buf.at[z, b, :, 1]


class Gather:
    def __init__(self, p, by_head, shard, buf, send, recv, own):
        self.p, self.by_head, self.shard, self.buf = p, by_head, shard, buf
        self.send, self.recv, self.own = send, recv, own
        n = p.depth
        self.first = remote(shard, slot_of(buf, by_head, p), send.at[5 * n], recv.at[4 * n], p.a_nbr)
        self.keep = pltpu.make_async_copy(shard, slot_of(buf, by_head, p), own)

    @staticmethod
    def sems(n):
        return [
            pltpu.SemaphoreType.DMA((5 * n + 1,)),
            pltpu.SemaphoreType.DMA((4 * n + 1,)),
            pltpu.SemaphoreType.DMA,
        ]

    def _copy(self, core, b, z, kind):
        p, n = self.p, self.p.depth
        ref = pair_of(self.buf, self.by_head, core, b, z)
        if kind == "right":
            return remote(ref, ref, self.send.at[z], self.recv.at[z], p.right)
        if kind == "left":
            return remote(ref, ref, self.send.at[n + z], self.recv.at[z], p.left)
        return remote(ref, ref, self.send.at[2 * n + z], self.recv.at[n + z], p.b_nbr)

    def _sib(self, core, b, z):
        n = self.p.depth
        ref = pair_of(self.buf, self.by_head, core, b, z)
        return remote(ref, ref, self.send.at[3 * n + b * n + z], self.recv.at[2 * n + b * n + z], self.p.sib)

    def start(self):
        self.keep.start()
        self.first.start()

    def _spread(self, core, z, right, left):
        p = self.p
        if right:
            pl.when(p.z < p.depth - 1)(lambda: self._copy(core, p.b, z, "right").start())
        if left:
            pl.when(p.z > 0)(lambda: self._copy(core, p.b, z, "left").start())
        self._copy(core, p.b, z, "b").start()
        self._sib(core, p.b, z).start()

    def along(self, k):
        p = self.p
        if isinstance(k, int) and k == 0:
            self.keep.wait()
            self.first.wait_recv()
            p.by_core(lambda core: self._spread(core, p.z, True, True))
            return

        def from_left(core):
            self._copy(core, p.b, p.z - k, "right").wait_recv()
            self._spread(core, p.z - k, True, False)

        def from_right(core):
            self._copy(core, p.b, p.z + k, "left").wait_recv()
            self._spread(core, p.z + k, False, True)

        pl.when(p.z - k >= 0)(lambda: p.by_core(from_left))
        pl.when(p.z + k < p.depth)(lambda: p.by_core(from_right))

    def across(self, k):
        p = self.p

        def one(z, core):
            self._copy(core, 1 - p.b, z, "b").wait_recv()
            self._sib(core, 1 - p.b, z).start()

        pl.when(p.z - k >= 0)(lambda: p.by_core(lambda core: one(p.z - k, core)))
        if not (isinstance(k, int) and k == 0):
            pl.when(p.z + k < p.depth)(lambda: p.by_core(lambda core: one(p.z + k, core)))

    def finish_at(self, z):
        def one(core):
            for b in (0, 1):
                self._sib(1 - core, b, z).wait_recv()

        self.p.by_core(one)

    def finish(self):
        each_of(self.p.depth, self.finish_at)

    def drain(self):
        p, n = self.p, self.p.depth
        self.first.wait_send()

        def each(z, carry):
            def one(core):
                pl.when(jnp.logical_and(p.z < n - 1, z <= p.z))(
                    lambda: self._copy(core, p.b, z, "right").wait_send()
                )
                pl.when(jnp.logical_and(p.z > 0, z >= p.z))(
                    lambda: self._copy(core, p.b, z, "left").wait_send()
                )
                self._copy(core, p.b, z, "b").wait_send()
                for b in (0, 1):
                    self._sib(core, b, z).wait_send()

            p.by_core(one)
            return carry

        lax.fori_loop(0, n, each, 0)


class Exchange:
    def __init__(self, p, src, dst, send, recv, own):
        m = p.m
        c, other = m % 2, 1 - m % 2
        self.local = [
            pltpu.make_async_copy(src.at[m], dst.at[m], own.at[0]),
            pltpu.make_async_copy(src.at[4 + c], dst.at[4 + c], own.at[1]),
            pltpu.make_async_copy(src.at[pl.ds(6, 2)], dst.at[pl.ds(6, 2)], own.at[2]),
        ]
        self.out = [
            remote(src.at[dev[1]], dst.at[m], send.at[j], recv.at[j], dev)
            for j, dev in enumerate(p.mp_peer)
        ] + [remote(src.at[4 + other], dst.at[4 + c], send.at[3], recv.at[3], p.sib)]

    @staticmethod
    def sems():
        return [
            pltpu.SemaphoreType.DMA((4,)),
            pltpu.SemaphoreType.DMA((4,)),
            pltpu.SemaphoreType.DMA((3,)),
        ]

    def start(self):
        for copy in self.out + self.local:
            copy.start()

    def finish(self):
        for copy in self.local:
            copy.wait()
        for copy in self.out:
            copy.wait_recv()

    def drain(self):
        for copy in self.out:
            copy.wait_send()


def add_rows(dst, src, rows):
    step = 32 if rows % 32 == 0 else 16

    def one(i, carry):
        at = pl.ds(pl.multiple_of(i * step, step), step)
        total = dst[at, :].astype(jnp.float32) + src[at, :].astype(jnp.float32)
        dst[at, :] = total.astype(dst.dtype)
        return carry

    lax.fori_loop(0, rows // step, one, 0)


class Scatter:
    def __init__(self, p, by_head, part, total, half, quarter, arrive, last, send, recv, mine=None, mine_sem=None, region=None):
        self.p, self.by_head, self.part, self.total = p, by_head, part, total
        self.mine, self.mine_sem, self.region = mine, mine_sem, region
        self.half, self.quarter, self.arrive, self.last = half, quarter, arrive, last
        self.send, self.recv = send, recv
        self.rows = part.shape[-2]

    @staticmethod
    def scratch(n, rows, cols, dtype=jnp.bfloat16):
        return [
            pltpu.VMEM((n, 2, 2, rows, cols), dtype),
            pltpu.VMEM((n, 2, rows, cols), dtype),
            pltpu.VMEM((n + 1, 2, rows, cols), dtype),
            pltpu.VMEM((rows, cols), dtype),
            pltpu.SemaphoreType.DMA((3 * n + 1,)),
            pltpu.SemaphoreType.DMA((3 * n + 2,)),
        ]

    def order(self, k):
        return self.p.order(k)

    def _region(self, core, z):
        if self.region is not None:
            return self.region(core, z)
        return self.part.at[:, core, z] if self.by_head else self.part.at[z, :, :, core]

    def _half_pair(self, core, b, z):
        over_first = (core == 0) != self.by_head
        return self.half.at[z, :, b] if over_first else self.half.at[z, b]

    def _sib(self, core, z):
        return remote(
            self._region(1 - core, z), self.half.at[z], self.send.at[z], self.recv.at[z], self.p.sib
        )

    def _b(self, core, z):
        n, p = self.p.depth, self.p
        return remote(
            self._half_pair(core, 1 - p.b, z), self.quarter.at[z], self.send.at[n + z], self.recv.at[n + z], p.b_nbr
        )

    def _right(self, z):
        n, p = self.p.depth, self.p
        return remote(
            self.quarter.at[z], self.arrive.at[z], self.send.at[2 * n + z], self.recv.at[2 * n + z], p.right
        )

    def _left(self, z, goal):
        n, p = self.p.depth, self.p
        return remote(
            self.quarter.at[z], self.arrive.at[goal], self.send.at[2 * n + z], self.recv.at[2 * n + goal], p.left
        )

    def _a(self):
        n, p = self.p.depth, self.p
        return remote(
            self.quarter.at[p.z, 1 - p.a], self.last, self.send.at[3 * n], self.recv.at[3 * n + 1], p.a_nbr
        )

    def _keep(self, core, z):
        return pltpu.make_async_copy(self._region(core, z), self.mine.at[z], self.mine_sem.at[z])

    def start(self, k):
        z = self.order(k)

        def one(core):
            self._sib(core, z).start()
            if self.mine is not None:
                self._keep(core, z).start()

        self.p.by_core(one)

    def to_half(self, k):
        z = self.order(k)

        def one(core):
            self._sib(core, z).wait_recv()
            region = self._region(core, z)
            if self.mine is not None:
                self._keep(core, z).wait()
                region = self.mine.at[z]
            for i in (0, 1):
                for j in (0, 1):
                    add_rows(self.half.at[z, i, j], region.at[i, j], self.rows)
            self._b(core, z).start()

        self.p.by_core(one)

    def to_quarter(self, k):
        z = self.order(k)

        def one(core):
            self._b(core, z).wait_recv()
            for i in (0, 1):
                add_rows(self.quarter.at[z, i], self._half_pair(core, self.p.b, z).at[i], self.rows)

        self.p.by_core(one)

    def _take(self, z, slot):
        for i in (0, 1):
            add_rows(self.quarter.at[z, i], self.arrive.at[slot, i], self.rows)

    def _send_left(self, z):
        p, n = self.p, self.p.depth
        pl.when(z == p.z - 1)(lambda: self._left(z, n).start())
        pl.when(z < p.z - 1)(lambda: self._left(z, z).start())

    def origin(self, k):
        p, n = self.p, self.p.depth
        z = self.order(k)
        pl.when(jnp.logical_and(p.z == 0, z > p.z))(lambda: self._right(z).start())
        pl.when(jnp.logical_and(p.z == n - 1, z < p.z))(lambda: self._send_left(z))

    def forward(self, k):
        p, n = self.p, self.p.depth
        z = self.order(k)

        def rightward():
            self._right(z).wait_recv()
            self._take(z, z)
            self._right(z).start()

        def leftward():
            self._left(z, z).wait_recv()
            self._take(z, z)
            self._send_left(z)

        pl.when(jnp.logical_and(p.z > 0, z > p.z))(rightward)
        pl.when(jnp.logical_and(p.z < n - 1, z < p.z))(leftward)

    def collect(self):
        p, n = self.p, self.p.depth

        def from_left():
            self._right(p.z).wait_recv()
            self._take(p.z, p.z)

        def from_right():
            self._left(p.z, n).wait_recv()
            self._take(p.z, n)

        pl.when(p.z > 0)(from_left)
        pl.when(p.z < n - 1)(from_right)
        self._a().start()

    def finish(self):
        p = self.p
        self._a().wait_recv()
        self.total[...] = self.quarter[p.z, p.a].astype(jnp.float32) + self.last[...].astype(jnp.float32)

    def drain(self):
        p, n = self.p, self.p.depth
        self._a().wait_send()

        def each(z, carry):
            def one(core):
                self._sib(core, z).wait_send()
                self._b(core, z).wait_send()

            p.by_core(one)
            pl.when(z != p.z)(lambda: self._right(z).wait_send())
            return carry

        lax.fori_loop(0, n, each, 0)

    def steps(self):
        n = self.p.depth
        todo = [lambda: [self.start(k) for k in range(n)]]
        todo += [functools.partial(self.to_half, k) for k in range(n)]
        for k in range(n):
            todo.append(functools.partial(lambda k: (self.to_quarter(k), self.origin(k), self.forward(k)), k))
        return todo


class Sum:
    def __init__(self, p, bits, value, slots, send, recv):
        self.p, self.bits, self.value, self.slots = p, bits, value, slots
        self.send, self.recv = send, recv

    @staticmethod
    def scratch(bits, rows):
        return [
            pltpu.VMEM((2 * (bits + 2), rows, 128), jnp.float32),
            pltpu.SemaphoreType.DMA((bits + 2,)),
            pltpu.SemaphoreType.DMA((bits + 2,)),
        ]

    def _copy(self, s):
        p = self.p
        dev = (p.sib, p.yn, *[p.flip(bit) for bit in range(self.bits)])[s]
        return remote(self.slots.at[2 * s], self.slots.at[2 * s + 1], self.send.at[s], self.recv.at[s], dev)

    def steps(self):
        def begin():
            self.slots[0] = self.value[...]
            self._copy(0).start()

        def one(s):
            self._copy(s).wait_recv()
            total = self.slots[2 * s] + self.slots[2 * s + 1]
            if s == self.bits + 1:
                self.value[...] = total
            else:
                self.slots[2 * s + 2] = total
                self._copy(s + 1).start()

        return [begin] + [functools.partial(one, s) for s in range(self.bits + 2)]

    def drain(self):
        for s in range(self.bits + 2):
            self._copy(s).wait_send()


def in_waves(lists, lag):
    for t in range(max(len(todo) + lag * r for r, todo in enumerate(lists))):
        for r, todo in enumerate(lists):
            if 0 <= t - lag * r < len(todo):
                todo[t - lag * r]()


def gather_kernel(p_depth, tok, cot, wq, wo, wi, wu, tok_s, cot_s, gq, go, gi, gu, *sems):
    p = Place(p_depth)
    n = p_depth
    arrays = []
    for i, (by_head, shard, buf) in enumerate(
        ((True, wq, gq), (False, wo, go), (False, wi, gi), (False, wu, gu))
    ):
        arrays.append(Gather(p, by_head, shard, buf, *sems[3 * i : 3 * i + 3]))
    rows = [Exchange(p, tok, tok_s, *sems[12:15]), Exchange(p, cot, cot_s, *sems[15:18])]
    p.barrier(0)
    for g in arrays:
        g.start()
    rows[0].start()
    if n <= 8:
        for k in range(n):
            for g in arrays:
                g.along(k)
            if k > 0:
                for g in arrays:
                    g.across(k - 1)
            if k == 1:
                rows[1].start()
        for g in arrays:
            g.across(n - 1)
    else:
        for g in arrays:
            g.along(0)
            lax.fori_loop(1, n, lambda k, carry: (g.along(k), carry)[1], 0)
        rows[1].start()
        for g in arrays:
            g.across(0)
            lax.fori_loop(1, n, lambda k, carry: (g.across(k), carry)[1], 0)
    for g in arrays + rows:
        g.finish()
    for g in arrays + rows:
        g.drain()


def gather_all(depth, tok, cot, shards):
    hbm = pl.BlockSpec(memory_space=pl.ANY)
    outs = [jax.ShapeDtypeStruct(tok.shape, tok.dtype)] * 2
    for i, s in enumerate(shards):
        lead = (2, 2, depth, 2) if i == 0 else (depth, 2, 2, 2)
        outs.append(jax.ShapeDtypeStruct(lead + s.shape, s.dtype))
    sems = Gather.sems(depth) * 4 + Exchange.sems() * 2
    return pl.pallas_call(
        functools.partial(gather_kernel, depth),
        out_shape=outs,
        in_specs=[hbm] * 6,
        out_specs=[hbm] * 6,
        scratch_shapes=sems,
        compiler_params=pltpu.CompilerParams(collective_id=0, has_side_effects=True),
        name="gather",
    )(tok, cot, *shards)


def scatter_kernel(depth, bits, pq, po, pi, pu, small, out_s, gtok_s, oq, oo, oi, ou, small_o, out, gtok, *scr):
    p = Place(depth)
    arrays = []
    for i, (by_head, part, total) in enumerate(
        ((False, pu, ou), (False, pi, oi), (False, po, oo), (True, pq, oq))
    ):
        arrays.append(Scatter(p, by_head, part, total, *scr[6 * i : 6 * i + 6]))
    rows = [Exchange(p, out_s, out, *scr[24:27]), Exchange(p, gtok_s, gtok, *scr[27:30])]
    small_o[...] = small[...]
    sums = Sum(p, bits, small_o, *scr[30:33])
    p.barrier(bits)
    rows[0].start()
    in_waves([g.steps() for g in arrays], min(depth, 4))
    rows[1].start()
    close(arrays, sums)
    for r in rows:
        r.finish()
    for g in arrays + rows + [sums]:
        g.drain()


def close(arrays, sums):
    closing = [g.collect for g in arrays] + [g.finish for g in arrays]
    for step in itertools.chain(*itertools.zip_longest(sums.steps(), closing)):
        if step is not None:
            step()


def scatter_all(depth, bits, parts, small, out_s, gtok_s):
    hbm = pl.BlockSpec(memory_space=pl.ANY)
    vmem = pl.BlockSpec(memory_space=pltpu.VMEM)
    outs = [jax.ShapeDtypeStruct(s.shape[4:], jnp.float32) for s in parts]
    outs += [jax.ShapeDtypeStruct(small.shape, jnp.float32)]
    outs += [jax.ShapeDtypeStruct(out_s.shape, out_s.dtype)] * 2
    scr = []
    for s in (parts[3], parts[2], parts[1], parts[0]):
        scr += Scatter.scratch(depth, *s.shape[4:])
    scr += Exchange.sems() * 2 + Sum.scratch(bits, small.shape[0])
    return pl.pallas_call(
        functools.partial(scatter_kernel, depth, bits),
        out_shape=outs,
        in_specs=[vmem] * 5 + [hbm] * 2,
        out_specs=[vmem] * 5 + [hbm] * 2,
        scratch_shapes=scr,
        compiler_params=pltpu.CompilerParams(
            collective_id=1, has_side_effects=True, vmem_limit_bytes=60 * 2**20
        ),
        name="scatter",
    )(*parts, small, out_s, gtok_s)

SPANS = ((0, LEN_LONG), (LEN_LONG, LEN_MID), (LEN_LONG + LEN_MID, LEN_SHORT), (LEN_LONG + LEN_MID + LEN_SHORT, LEN_SHORT))
TILE = 128
QKV_PAD = 640
CTX_PAD = 256
ADAPT_PAD = 128
MASK_LOW = -1e9
NN = (((1,), (0,)), ((), ()))
NT = (((1,), (1,)), ((), ()))
TN = (((0,), (0,)), ((), ()))


def dot(a, b, dims=NN):
    return lax.dot_general(a, b, dims, preferred_element_type=jnp.float32)


def table_onehot():
    buckets = rel_buckets(257)
    offset = np.clip(256 - np.arange(512), -256, 256) + 256
    index = np.concatenate([buckets[offset], np.full(128, NB // 2 - 1), np.full(128, NB - 1)])
    return (index[:, None] == np.arange(NB)[None, :]).astype(np.float32)


def bias_tiles(row):
    spread = pltpu.roll(jnp.broadcast_to(row, (TILE, 512)), 0, 1, stride=1, stride_axis=0)
    far = [jnp.broadcast_to(row[:, at : at + 1], (TILE, TILE)) for at in (511, 0)]
    near = [spread[:, 256 - 128 * delta : 384 - 128 * delta] for delta in (-1, 0, 1)]
    return [far[0], *near, far[1]]


def diagonal_sums(tiles):
    grid = jnp.concatenate([jnp.zeros((TILE, TILE), jnp.float32), tiles[2], tiles[1], tiles[0]], axis=1)
    rows = TILE
    while rows > 8:
        rows //= 2
        grid = grid[:rows] + pltpu.roll(grid[rows:], 512 - rows, 1)
    total = grid[0:1]
    for r in range(1, 8):
        total = total + pltpu.roll(grid[r : r + 1], 512 - r, 1)
    return total


def swap_halves(tile):
    return jnp.concatenate([tile[:, DH:], tile[:, :DH]], axis=1)


def lanes_below(shape, at=DH):
    return lax.broadcasted_iota(jnp.int32, shape, len(shape) - 1) < at


def key_side(qk, mask):
    swapped = swap_halves(qk)
    return jnp.where(lanes_below(qk.shape), swapped, mask), swapped


def query_side(qk):
    lane = lax.broadcasted_iota(jnp.int32, qk.shape, 1)
    return jnp.where(lane < DH, qk, jnp.where(lane == DH, 1.0, 0.0).astype(qk.dtype))


def probabilities(scores, tiles, length, q0=0):
    width = scores.shape[1]
    blocks = []
    for kb in range(length // TILE):
        deltas = [max(-2, min(2, kb - (q0 + qi))) + 2 for qi in range(width // TILE)]
        bias = tiles[deltas[0]] if len(deltas) == 1 else jnp.concatenate([tiles[d] for d in deltas], axis=1)
        blocks.append(scores[kb * TILE : (kb + 1) * TILE] + bias)
    top = blocks[0]
    for block in blocks[1:]:
        top = jnp.maximum(top, block)
    top = jnp.max(top, axis=0, keepdims=True)
    blocks = [jnp.exp(block - top) for block in blocks]
    total = blocks[0]
    for block in blocks[1:]:
        total = total + block
    inverse = 1.0 / jnp.sum(total, axis=0, keepdims=True)
    return [block * inverse for block in blocks]


def join(blocks, axis=0):
    return blocks[0] if len(blocks) == 1 else jnp.concatenate(blocks, axis=axis)


def value_lanes(group):
    stride = group * CTX_PAD // (3 * DH)
    lane = np.arange(CTX_PAD)
    column = lane // stride * group + lane % stride
    return np.where(lane % stride < group, column // DH, -1), column


def head_runs(group):
    heads, _ = value_lanes(group)
    runs = []
    for lane in range(CTX_PAD):
        head = int(heads[lane])
        head = runs[-1][2] if head < 0 else head
        if runs and runs[-1][2] == head:
            runs[-1][1] = lane + 1
        else:
            runs.append([lane, lane + 1, head])
    return runs


def head_lanes(shape, group, head):
    lane = lax.broadcasted_iota(jnp.int32, shape, len(shape) - 1)
    inside = None
    for lo, hi, h in head_runs(group):
        if h == head:
            run = jnp.logical_and(lane >= lo, lane < hi)
            inside = run if inside is None else jnp.logical_or(inside, run)
    return inside


def no_tick(j):
    pass


def no_keep(number, place, h, probs):
    pass


FRONT_SPANS = (SPANS[:1], SPANS[1:])
FRONT_WIDTH = 256


def attend_group(packed, mask_ref, rows, context, group, tick=no_tick, keep=no_keep):
    tiles = [bias_tiles(rows[h : h + 1, :]) for h in range(3)]
    for number, spans in enumerate(FRONT_SPANS):
        units = []
        for offset, length in spans:
            width = min(length, FRONT_WIDTH)
            units += [(offset, length, q0, width) for q0 in range(0, length, width)]
        batches = [[unit] for unit in units] if number == 0 else [units]
        keys = {
            (offset, h): key_side(packed[pl.ds(offset, length), h * TILE : (h + 1) * TILE], mask_ref[pl.ds(offset, length), :])[0]
            for offset, length in spans
            for h in range(3)
        }
        values = {offset: packed[pl.ds(offset, length), 3 * TILE : QKV_PAD].T for offset, length in spans}
        for turn, batch in enumerate(batches):
            work = [(unit, h) for unit in batch for h in range(3)]
            scores = []
            for (offset, length, q0, width), h in work:
                queries = query_side(packed[pl.ds(offset + q0, width), h * TILE : (h + 1) * TILE])
                scores.append(dot(keys[offset, h], queries, NT))
            probs = []
            for ((offset, length, q0, width), h), score in zip(work, scores):
                blocks = probabilities(score, tiles[h], length, q0 // TILE)
                probs.append(join([block.astype(jnp.bfloat16) for block in blocks]))
            for (unit, h), prob in zip(work, probs):
                keep(number, unit, h, prob)
            outs = [dot(values[unit[0]], prob) for (unit, h), prob in zip(work, probs)]
            for i, (offset, length, q0, width) in enumerate(batch):
                own = outs[3 * i : 3 * i + 3]
                whole = jnp.concatenate([own[h][lo:hi] for lo, hi, h in head_runs(group)], axis=0)
                context[pl.ds(offset + q0, width), :] = whole.T.astype(jnp.bfloat16)
            tick((number, turn))


BACK_SPANS = (SPANS[:1], SPANS[1:])
SKEW = (5, 0)


def head_back(packed, recall, grad_context, grad_packed, group, near, far, value_sums, span_of, h):
    offset, length = span_of
    span, at = pl.ds(offset, length), pl.ds(h * TILE, TILE)
    qk = packed[span, at]
    low = lanes_below(qk.shape)
    swapped = swap_halves(qk)
    g_tile = grad_context[span, :]
    g_tile = jnp.where(head_lanes(g_tile.shape, group, h), g_tile, jnp.zeros_like(g_tile))
    scores = recall.scores(qk, span, h)
    g_probs = dot(packed[span, 3 * TILE : QKV_PAD], g_tile, NT)
    yield
    probs = recall.probs(scores, span_of, h)
    yield
    count = length // TILE
    g_blocks = [g_probs[kb * TILE : (kb + 1) * TILE] for kb in range(count)]
    total = probs[0] * g_blocks[0]
    for kb in range(1, count):
        total = total + probs[kb] * g_blocks[kb]
    centre = jnp.sum(total, axis=0, keepdims=True)
    low_probs = join([block.astype(jnp.bfloat16) for block in probs])
    g_scores = [(a * (g - centre)).astype(jnp.bfloat16) for a, g in zip(probs, g_blocks)]
    for kb, block in enumerate(g_scores):
        wide = block.astype(jnp.float32)
        for qi in range(count):
            piece = wide[:, qi * TILE : (qi + 1) * TILE]
            delta = kb - qi
            if abs(delta) <= 1:
                held = near[h][delta + 1]
                near[h][delta + 1] = piece if held is None else held + piece
            else:
                side = 0 if delta < 0 else 1
                far[h][side] = far[h][side] + piece
    yield
    g_scores = join(g_scores)
    g_v = dot(low_probs, g_tile)
    value_sums[offset] = value_sums[offset] + g_v if offset in value_sums else g_v
    grad_keys = dot(g_scores, jnp.where(low, jnp.zeros_like(qk), swapped))
    grad_queries = dot(jnp.where(low, swapped, jnp.zeros_like(qk)).T, g_scores).T
    yield
    grad_packed[span, at] = (grad_queries + grad_keys).astype(jnp.bfloat16)


class Again:
    def __init__(self, mask, rows):
        self.mask = mask
        self.tiles = [bias_tiles(rows[h : h + 1, :]) for h in range(3)]

    def scores(self, qk, span, h):
        return dot(key_side(qk, self.mask[span, :])[0], query_side(qk), NT)

    def probs(self, scores, span_of, h):
        return probabilities(scores, self.tiles[h], span_of[1])


class Kept:
    def __init__(self, kept):
        self.kept = kept

    def scores(self, qk, span, h):
        return None

    def probs(self, scores, span_of, h):
        offset, length = span_of
        pieces = [self.kept[r : r + n, c : c + w] for r, n, c, w in kept_at(offset, length, h)]
        whole = join(pieces, axis=1).astype(jnp.float32)
        return [whole[kb * TILE : (kb + 1) * TILE] for kb in range(length // TILE)]


KEPT_LONG, KEPT_REST = 1024, 384


def kept_at(offset, length, h):
    if length == LEN_LONG:
        if h < 2:
            return [(LEN_LONG * h, LEN_LONG, 0, LEN_LONG)]
        return [(LEN_LONG * k, LEN_LONG, LEN_LONG, LEN_LONG // 2) for k in range(2)]
    if length == LEN_MID:
        return [(KEPT_LONG, LEN_MID, LEN_MID * h, LEN_MID)]
    second = (offset - LEN_LONG - LEN_MID) // LEN_SHORT
    return [(KEPT_LONG + LEN_MID, LEN_SHORT, LEN_SHORT * (3 * second + h), LEN_SHORT)]


def attend_group_back(packed, recall, grad_context, grad_packed, sums, group, tick=no_tick):
    near = [[None] * 3 for _ in range(3)]
    far = [[jnp.zeros((TILE, TILE), jnp.float32)] * 2 for _ in range(3)]
    value_sums = {}

    def heads_of(spans):
        return [
            head_back(packed, recall, grad_context, grad_packed, group, near, far, value_sums, s, h)
            for s in spans
            for h in range(3)
        ]

    def values_of(spans):
        for offset, length in spans:
            grad_packed[pl.ds(offset, length), 3 * TILE : QKV_PAD] = value_sums.pop(offset).astype(jnp.bfloat16)

    for number, spans in enumerate(BACK_SPANS):
        heads = heads_of(spans)
        skew = SKEW[number]
        for t in range(5 + skew * (len(heads) - 1)):
            for i, head in enumerate(heads):
                if 0 <= t - skew * i < 5:
                    next(head, None)
                    if t - skew * i == 4:
                        tick((number, i))
        values_of(spans)
    for h in range(3):
        sums[h : h + 1, :512] = diagonal_sums(near[h])
        for side in range(2):
            sums[h : h + 1, 512 + side * TILE : 640 + side * TILE] = jnp.sum(far[h][side], axis=0, keepdims=True)


def attention_kernel(group, x_ref, gain, w_ref, mask, rows, normed_out, packed, context):
    @pl.when(pl.program_id(0) == 0)
    def _():
        x = x_ref[...].astype(jnp.float32)
        scale = lax.rsqrt(jnp.mean(x * x, axis=-1, keepdims=True) + NORM_EPS)
        normed_out[...] = (x * scale * gain[...]).astype(jnp.bfloat16)

    packed[0] = dot(normed_out[...], w_ref[0]).astype(jnp.bfloat16)
    attend_group(packed.at[0], mask, rows[0], context.at[0], group)


def attention(x, gain, w, mask, rows, group):
    n = x.shape[0]
    bf = jnp.bfloat16
    return pl.pallas_call(
        functools.partial(attention_kernel, group),
        grid=(4,),
        out_shape=[
            jax.ShapeDtypeStruct((n, D), bf),
            jax.ShapeDtypeStruct((4, n, QKV_PAD), bf),
            jax.ShapeDtypeStruct((4, n, CTX_PAD), bf),
        ],
        in_specs=[
            pl.BlockSpec((n, D), lambda i: (0, 0)),
            pl.BlockSpec((1, D), lambda i: (0, 0)),
            pl.BlockSpec((1, D, QKV_PAD), lambda i: (i, 0, 0)),
            pl.BlockSpec((n, TILE), lambda i: (0, 0)),
            pl.BlockSpec((1, 3, 512), lambda i: (i, 0, 0)),
        ],
        out_specs=[
            pl.BlockSpec((n, D), lambda i: (0, 0)),
            pl.BlockSpec((1, n, QKV_PAD), lambda i: (i, 0, 0)),
            pl.BlockSpec((1, n, CTX_PAD), lambda i: (i, 0, 0)),
        ],
        compiler_params=pltpu.CompilerParams(vmem_limit_bytes=56 * 2**20),
        name="attention",
    )(x, gain, w, mask, rows)


def attention_back_kernel(group, packed, grad_context, mask, rows, grad_packed, sums):
    attend_group_back(packed.at[0], Again(mask, rows[0]), grad_context.at[0], grad_packed.at[0], sums.at[0], group)


def attention_back(packed, grad_context, mask, rows, group):
    n = packed.shape[1]
    return pl.pallas_call(
        functools.partial(attention_back_kernel, group),
        grid=(4,),
        out_shape=[
            jax.ShapeDtypeStruct((4, n, QKV_PAD), jnp.bfloat16),
            jax.ShapeDtypeStruct((4, 3, 768), jnp.float32),
        ],
        in_specs=[
            pl.BlockSpec((1, n, QKV_PAD), lambda i: (i, 0, 0)),
            pl.BlockSpec((1, n, CTX_PAD), lambda i: (i, 0, 0)),
            pl.BlockSpec((n, TILE), lambda i: (0, 0)),
            pl.BlockSpec((1, 3, 512), lambda i: (i, 0, 0)),
        ],
        out_specs=[
            pl.BlockSpec((1, n, QKV_PAD), lambda i: (i, 0, 0)),
            pl.BlockSpec((1, 3, 768), lambda i: (i, 0, 0)),
        ],
        compiler_params=pltpu.CompilerParams(vmem_limit_bytes=56 * 2**20),
        name="attention_back",
    )(packed, grad_context, mask, rows)


def head_columns(w, group):
    n = w.shape[0]
    qk = w[:, :, : 2 * DH].reshape(n, 6 * DH)
    v = w[:, :, 2 * DH :].reshape(n, 3 * DH // group, group)
    v = jnp.pad(v, ((0, 0), (0, 0), (0, group // 3))).reshape(n, CTX_PAD)
    return jnp.concatenate([qk, v], axis=1)


def key_mask(live):
    lane = jnp.arange(TILE)[None, :]
    return jnp.where((lane == DH) & ~live[:, None], MASK_LOW, 0.0).astype(jnp.bfloat16)


def precise(a, b, dims=NN):
    return lax.dot_general(a, b, dims, precision=FULL_PRECISION, preferred_element_type=jnp.float32)


def offset_onehot():
    buckets = rel_buckets(257)
    offset = np.clip(256 - np.arange(512), -256, 256) + 256
    return (np.arange(NB)[:, None] == buckets[offset][None, :]).astype(np.float32)


def column_choice(group):
    choice = np.zeros((9 * DH, QKV_PAD), np.float32)
    for h in range(3):
        for k in range(2 * DH):
            choice[3 * DH * h + k, TILE * h + k] = 1
    heads, column = value_lanes(group)
    for lane in range(CTX_PAD):
        if heads[lane] >= 0:
            choice[3 * DH * heads[lane] + 2 * DH + column[lane] % DH, 3 * TILE + lane] = 1
    return choice


def own_length(lengths, member, number):
    at = (member, 4 + member // 2 + 2 * (member % 2), 8 + member, 12 + member)[number]
    return lengths[at]


def fill_mask(mask, lengths, member):
    for number, (offset, length) in enumerate(SPANS):
        row = lax.broadcasted_iota(jnp.int32, (length, TILE), 0)
        lane = lax.broadcasted_iota(jnp.int32, (length, TILE), 1)
        dead = jnp.logical_and(row >= own_length(lengths, member, number), lane == DH)
        mask[offset : offset + length, :] = jnp.where(dead, MASK_LOW, 0.0).astype(jnp.bfloat16)


def fill_rows(rows, pos_table, onehot):
    table = precise(pos_table[...], onehot[...])
    for m in range(4):
        rows[m] = table[3 * m : 3 * m + 3, :]


KA = ADAPT // KRON


def adapter_constants():
    i, b = np.arange(16) // 4, np.arange(16) % 4
    same = (np.arange(4)[:, None] == i[None, :]).astype(np.float32)
    pick = np.zeros((4, 4, 16), np.float32)
    pick[i, b, np.arange(16)] = 1
    fold = np.zeros((ADAPT_PAD, KA), np.float32)
    fold[np.arange(ADAPT), np.arange(ADAPT) % KA] = 1
    agree = np.zeros((ADAPT_PAD, 16), np.float32)
    agree[:ADAPT] = np.arange(ADAPT)[:, None] // KA == b[None, :]
    return same, pick, fold, agree


class Factor:
    def __init__(self, rules, tall, short, consts):
        self.same, _, self.fold, self.agree = consts
        spread = precise(tall, self.same, TN)
        self.tall = jnp.concatenate([spread] * KRON, axis=0)
        rows = spread.shape[0]
        self.rules = jnp.concatenate(
            [jnp.broadcast_to(rules[a : a + 1, :], (rows, 16)) for a in range(KRON)], axis=0
        )
        self.short = precise(self.fold, precise(short, self.same, TN)) * self.agree

    def whole(self):
        return precise(self.rules * self.tall, self.short, NT)

    def back(self, grad):
        wide = precise(grad, self.short)
        rows = wide.shape[0] // KRON
        tall = wide * self.rules
        tall = sum(tall[a * rows : (a + 1) * rows] for a in range(KRON))
        rules = wide * self.tall
        rules = [jnp.sum(rules[a * rows : (a + 1) * rows], axis=0, keepdims=True) for a in range(KRON)]
        short = precise(self.rules * self.tall, grad, TN) * self.agree.T
        short = precise(precise(self.same, short), self.fold)
        return jnp.concatenate(rules, axis=0), precise(self.same, tall, NT), short


def rule_tables(rules, pick):
    return [sum(precise(rules[i], pick[i], dims) for i in range(KRON)) for dims in (NN, TN)]


ROW_GAIN, ROW_TABLE, ROW_OTHER = 0, 8, 24
ROW_FFN, ROW_DL, ROW_UR, ROW_DR, ROW_UL, ROW_RULES, ROW_END = 0, 8, 16, 24, 28, 32, 48


def put_row(ref, at, row):
    for k in range(row.shape[1] // 128):
        ref[at + k : at + k + 1, :] = row[:, 128 * k : 128 * (k + 1)]


FCH = 768
RCH = 256


def gelu_both(v):
    phi = 0.5 + 0.5 * lax.erf(v * np.float32(np.sqrt(0.5)))
    return v * phi, phi + v * (jnp.exp(-0.5 * v * v) * np.float32(1.0 / np.sqrt(2.0 * np.pi)))


def rows_of(i, size=RCH):
    return pl.ds(pl.multiple_of(i * size, size), size)


def each_of(count, body):
    lax.fori_loop(0, count, lambda i, carry: (body(i), carry)[1], 0)


class Layer:
    def __init__(self, **refs):
        self.__dict__.update(refs)
        self.n = self.n2.shape[0]

    def midway(self, i):
        r = rows_of(i)
        total = self.x_rows(i)
        for m in range(4):
            total = total + dot(self.ctx[m, r, :], self.wo(m))
        self.mid[r, :] = total
        scale = lax.rsqrt(jnp.mean(total * total, axis=-1, keepdims=True) + NORM_EPS)
        self.n2[r, :] = (total * scale * self.gain[...]).astype(jnp.bfloat16)

    def forward(self, j):
        f = rows_of(j, self.chunk)
        for half in range(2):
            r = pl.ds(half * (self.n // 2), self.n // 2)
            value, slope = gelu_both(dot(self.n2[r, :], self.wi(j), NT))
            value = value.astype(jnp.bfloat16)
            self.act[r, f] = value
            self.dg[r, f] = slope.astype(jnp.bfloat16)
            self.acc[r, :] += dot(value, self.wu(j))

    def factors(self):
        consts = [c[...] for c in self.consts]
        by_a, by_b = rule_tables(self.rules, consts[1])
        d_left, d_right, u_left, u_right = self.sides
        return (
            Factor(by_a, d_left[...], d_right[...], consts),
            Factor(by_b, u_right[...], u_left[...], consts),
        )

    def prepare(self, member):
        down, up = self.factors()
        self.down[...] = down.whole().astype(jnp.bfloat16)
        self.up[...] = up.whole().astype(jnp.bfloat16)
        for number, (offset, length) in enumerate(SPANS):
            row = lax.broadcasted_iota(jnp.int32, (length, 1), 0)
            alive = row < own_length(self.lengths, member, number)
            self.live[offset : offset + length, :] = jnp.where(alive, 1.0, 0.0)

    def adapter(self, i):
        bf = jnp.bfloat16
        r = rows_of(i)
        ffn = self.acc[r, :]
        low = ffn.astype(bf)
        value, slope = gelu_both(dot(low, self.down[...]))
        value = value.astype(bf)
        self.put_res(i, (self.mid[r, :] + ffn + dot(value, self.up[...], NT)).astype(bf))
        g_out = self.cot_rows(i) * self.live[r, :]
        g_low = g_out.astype(bf)
        self.gout[r, :] = g_low
        g_sq = (dot(g_low, self.up[...]) * slope).astype(bf)
        self.g_up[...] += dot(g_low, value, TN)
        self.g_down[...] += dot(low, g_sq, TN)
        self.gffn[r, :] = (g_out + dot(g_sq, self.down[...], NT)).astype(bf)

    def backward(self, j):
        dg = self.slope(j)
        for half in range(2):
            r = pl.ds(half * (self.n // 2), self.n // 2)
            g = (dot(self.gffn[r, :], self.wu(j), NT) * dg[r, :].astype(jnp.float32)).astype(jnp.bfloat16)
            dg[r, :] = g
            self.acc[r, :] += dot(g, self.wi(j))

    def last(self, i):
        r = rows_of(i)
        total = self.mid[r, :]
        g_n2 = self.acc[r, :]
        scale = lax.rsqrt(jnp.mean(total * total, axis=-1, keepdims=True) + NORM_EPS)
        self.g_gain[...] += jnp.sum(total * scale * g_n2, axis=0, keepdims=True)
        scaled = self.gain[...] * g_n2
        centre = jnp.mean(total * scaled, axis=-1, keepdims=True)
        g_mid = self.gout[r, :].astype(jnp.float32) + scale * scaled - total * (scale * scale * scale * centre)
        self.mid[r, :] = g_mid
        self.glow[r, :] = g_mid.astype(jnp.bfloat16)

    def projection(self, m):
        grad = dot(self.ctx[m], self.glow[...], TN).astype(jnp.bfloat16)
        self.ctx[m] = dot(self.glow[...], self.wo(m), NT).astype(jnp.bfloat16)
        return grad

    def adapter_all(self):
        self.g_down[...] = jnp.zeros_like(self.g_down)
        self.g_up[...] = jnp.zeros_like(self.g_up)
        each_of(self.n // RCH, self.adapter)

    def adapter_grads(self):
        other, pick = self.other, self.consts[1]
        down, up = self.factors()
        g_a, g_dl, g_dr = down.back(self.g_down[...])
        g_b, g_ur, g_ul = up.back(self.g_up[...])
        other[...] = jnp.zeros_like(other)
        for at, tall in ((ROW_DL, g_dl), (ROW_UR, g_ur)):
            other[at : at + 4, :] = tall[:, :128]
            other[at + 4 : at + 8, : tall.shape[1] - 128] = tall[:, 128:]
        for at, short in ((ROW_DR, g_dr), (ROW_UL, g_ul)):
            other[at : at + 4, :KA] = short
        for i in range(KRON):
            at = ROW_RULES + 4 * i
            other[at : at + 4, :KRON] = precise(g_a, pick[i], NT) + precise(pick[i], g_b, NT)


def middle_kernel(
    x_hbm, ctx_hbm, wo_hbm, wi_hbm, wu_hbm, cot_hbm, gain, lengths, rules, d_left, d_right, u_left, u_right,
    same, pick, fold, agree,
    res_hbm, gmid_hbm, gctx_hbm, go_hbm, gi_hbm, gu_hbm, other,
    down, up, g_down, g_up, g_gain, live, x, ctx, wo, wi, wu, cot, mid, n2, act, dg, acc, gffn, glow, sem, sems, out_sems,
):
    gain = gain[...].reshape(1, D)
    loads = [
        pltpu.make_async_copy(src, dst, sems.at[i])
        for i, (src, dst) in enumerate(
            ((x_hbm, x), (ctx_hbm, ctx), (wo_hbm, wo), (wi_hbm, wi), (wu_hbm, wu), (cot_hbm, cot))
        )
    ]
    for load in loads:
        load.start()
    def put_res(i, value):
        x[rows_of(i), :] = value

    layer = Layer(
        x_rows=lambda i: x[rows_of(i), :].astype(jnp.float32), cot_rows=lambda i: cot[rows_of(i), :].astype(jnp.float32),
        wo=lambda m: wo[m], wi=lambda j: wi[rows_of(j, FCH), :], wu=lambda j: wu[rows_of(j, FCH), :],
        chunk=FCH, ctx=ctx, gain=gain, lengths=lengths, rules=rules, sides=(d_left, d_right, u_left, u_right),
        consts=(same, pick, fold, agree), down=down, up=up, g_down=g_down, g_up=g_up, g_gain=g_gain, live=live, mid=mid,
        n2=n2, act=act, dg=dg, acc=acc, gffn=gffn, glow=glow, put_res=put_res, gout=cot, other=other,
        slope=lambda j: dg.at[:, rows_of(j, FCH)],
    )
    layer.prepare(lax.axis_index("mp"))
    for load in loads:
        load.wait()
    each_of(layer.n // RCH, layer.midway)
    acc[...] = jnp.zeros_like(acc)
    count = wi.shape[0] // FCH
    each_of(count, layer.forward)
    layer.adapter_all()
    acc[...] = jnp.zeros_like(acc)
    g_gain[...] = jnp.zeros_like(g_gain)

    def stores(j):
        f = rows_of(j, FCH)
        return [
            pltpu.make_async_copy(src.at[pl.ds(0, FCH), f], dst.at[f], sem.at[k, j])
            for k, (src, dst) in enumerate(((act, gu_hbm), (dg, gi_hbm)))
        ]

    def backward(j):
        f = rows_of(j, FCH)
        layer.backward(j)
        act[:FCH, f] = dot(act[:, f], gffn[...], TN).astype(jnp.bfloat16)
        dg[:FCH, f] = dot(dg[:, f], n2[...], TN).astype(jnp.bfloat16)
        for store in stores(j):
            store.start()

    each_of(count, backward)
    each_of(layer.n // RCH, layer.last)
    for m in range(4):
        gffn[CTX_PAD * m : CTX_PAD * (m + 1), :] = layer.projection(m)
    layer.adapter_grads()
    put_row(other, ROW_FFN, g_gain[...])
    copies = [
        pltpu.make_async_copy(src, dst, out_sems.at[k])
        for k, (src, dst) in enumerate(((x, res_hbm), (mid, gmid_hbm), (gffn, go_hbm), (ctx, gctx_hbm)))
    ]
    for copy in copies:
        copy.start()
    each_of(count, lambda j: [store.wait() for store in stores(j)])
    for copy in copies:
        copy.wait()


def middle(x, ctx, wo, wi, wu, cot, gain, lengths, factors):
    n, ff = x.shape[0], wi.shape[0]
    bf, f32 = jnp.bfloat16, jnp.float32
    hbm = pl.BlockSpec(memory_space=pl.ANY)
    vmem = pl.BlockSpec(memory_space=pltpu.VMEM)
    shape = jax.ShapeDtypeStruct
    return pl.pallas_call(
        middle_kernel,
        out_shape=[
            shape((n, D), bf),
            shape((n, D), f32),
            shape((4, n, CTX_PAD), bf),
            shape((4 * CTX_PAD, D), bf),
            shape((ff, D), bf),
            shape((ff, D), bf),
            shape((ROW_END, 128), f32),
        ],
        in_specs=[hbm] * 6 + [vmem] + [pl.BlockSpec(memory_space=pltpu.SMEM)] + [vmem] * 9,
        out_specs=[hbm] * 6 + [vmem],
        scratch_shapes=[
            pltpu.VMEM((D, ADAPT_PAD), bf),
            pltpu.VMEM((D, ADAPT_PAD), bf),
            pltpu.VMEM((D, ADAPT_PAD), f32),
            pltpu.VMEM((D, ADAPT_PAD), f32),
            pltpu.VMEM((1, D), f32),
            pltpu.VMEM((n, 1), f32),
            pltpu.VMEM((n, D), bf),
            pltpu.VMEM((4, n, CTX_PAD), bf),
            pltpu.VMEM((4, CTX_PAD, D), bf),
            pltpu.VMEM((ff, D), bf),
            pltpu.VMEM((ff, D), bf),
            pltpu.VMEM((n, D), bf),
            pltpu.VMEM((n, D), f32),
            pltpu.VMEM((n, D), bf),
            pltpu.VMEM((n, ff), bf),
            pltpu.VMEM((n, ff), bf),
            pltpu.VMEM((n, D), f32),
            pltpu.VMEM((n, D), bf),
            pltpu.VMEM((n, D), bf),
            pltpu.SemaphoreType.DMA((2, ff // FCH)),
            pltpu.SemaphoreType.DMA((6,)),
            pltpu.SemaphoreType.DMA((4,)),
        ],
        compiler_params=pltpu.CompilerParams(vmem_limit_bytes=63 * 2**20),
        name="middle",
    )(x, ctx, wo, wi, wu, cot, gain, lengths, *factors, *map(jnp.asarray, adapter_constants()))


FRONT = (
    "s:o s:q ex0 a:o0",
    "s:i a:q0 a:q1 a:q2",
    "c:q0 a:o1 c:q1 a:i0",
    "c:o0 a:q3 s:u n",
    "c:q2 a:o2 ex1 c:q3",
    "f:q a:u0 A A",
    "A c:o1 A a:i1",
    "a:o3 c:i0 A c:o2",
    "a:u1 A A A",
    "A A a:i2 c:o3",
    "A c:u0 A c:i1",
    "f:o O c:u1 a:u2",
    "c:i2 F0 a:i3 F1",
    "c:u2 a:u3 c:i3 F2",
    "c:u3 F3",
)


def front_order():
    plan, now = {"first": []}, "first"
    pieces = 0
    for step in " ".join(FRONT).split():
        if step == "A":
            now, pieces = ("A", pieces), pieces + 1
        elif step[0] in "OF":
            plan["before", step] = plan.pop("open", [])
            now = "open"
        else:
            plan.setdefault(now, []).append(step)
    return plan


def front_kernel(
    depth, group, tok, cot, w_qkv, w_o, w_in, w_out, choice, gain, gain_ffn, lengths, pos_table, onehot,
    rules, d_left, d_right, u_left, u_right, same, pick, fold, agree,
    tok_s, gq_hbm, normed_hbm, packed_hbm, out, mid_hbm, ctx_hbm, go_hbm, gi_hbm, gu_hbm, dg_hbm, pu_hbm, gffn_hbm, n2_hbm,
    gout_hbm, long_hbm, rest_hbm, other,
    wq, wo, wi, wu, mask, rows, x, y, gq, go, gi, gu, nrm, packed, ctx,
    down, up, g_down, g_up, live, mid, n2, act, dg, acc, gffn, res, sem, out_sems, local, *sems,
):
    p = Place(depth)
    bf = jnp.bfloat16
    p.greet(0)
    gain, gain_ffn = gain[...].reshape(1, D), gain_ffn[...].reshape(1, D)
    per_head = [dot(w_qkv[h].astype(bf), choice[3 * DH * h : 3 * DH * (h + 1), :]) for h in range(3)]
    wq[...] = sum(per_head).astype(bf)
    wo[...] = jnp.zeros_like(wo)
    wo[: w_o.shape[0], :] = w_o[...].astype(bf)
    wi[...] = w_in[...].astype(bf)
    wu[...] = w_out[...].astype(bf)
    arrays = {
        name: Gather(p, name == "q", shard, buf, *sems[3 * i : 3 * i + 3])
        for i, (name, shard, buf) in enumerate((("q", wq, gq), ("o", wo, go), ("i", wi, gi), ("u", wu, gu)))
    }
    first, second = Exchange(p, tok, x, *sems[12:15]), Exchange(p, cot, y, *sems[15:18])
    keep_x = pltpu.make_async_copy(x, tok_s, local.at[0])
    keep_n = pltpu.make_async_copy(nrm, normed_hbm, local.at[1])
    keep_q = pltpu.make_async_copy(gq, gq_hbm, local.at[2])
    quarter = RCH // SEG

    def float_rows(ref):
        return lambda i: ref[pl.ds(quarter * i, quarter)].reshape(RCH, D).astype(jnp.float32)

    def put_res(i, value):
        res[pl.ds(quarter * i, quarter)] = value.reshape(quarter, SEG, D)

    chunk_rows = 8 * wi.shape[0]
    layer = Layer(
        x_rows=float_rows(x), cot_rows=float_rows(y),
        wo=lambda m: go[m].reshape(CTX_PAD, D), wi=lambda j: gi[j].reshape(-1, D), wu=lambda j: gu[j].reshape(-1, D),
        chunk=chunk_rows, ctx=ctx, gain=gain_ffn, lengths=lengths, rules=rules, sides=(d_left, d_right, u_left, u_right),
        consts=(same, pick, fold, agree), down=down, up=up, g_down=g_down, g_up=g_up, live=live, mid=mid, n2=n2, act=act,
        dg=dg, acc=acc, gffn=gffn, put_res=put_res, gout=nrm, other=other,
    )
    third = Exchange(p, res, out, *sems[18:21])

    def norm(i):
        v = x[i].astype(jnp.float32)
        scale = lax.rsqrt(jnp.mean(v * v, axis=-1, keepdims=True) + NORM_EPS)
        nrm[rows_of(i, SEG), :] = (v * scale * gain[...]).astype(bf)

    def norms():
        first.finish()
        keep_x.start()
        each_of(x.shape[0], norm)
        keep_n.start()
        fill_mask(mask, lengths, p.m)
        fill_rows(rows, pos_table, onehot)
        layer.prepare(p.m)
        acc[...] = jnp.zeros_like(acc)

    def step(name):
        kind, rest = name[0], name[2:]
        if name == "n":
            norms()
        elif name in ("ex0", "ex1"):
            (first, second)[int(name[2])].start()
        elif kind == "s":
            arrays[rest].start()
        elif kind == "f":
            arrays[rest].finish()
        elif kind == "a":
            arrays[rest[0]].along(int(rest[1:]))
        elif kind == "c":
            arrays[rest[0]].across(int(rest[1:]))

    def steps(names):
        for name in names:
            step(name)

    plan = front_order()
    p.meet(0)
    steps(plan["first"])
    keep_q.start()

    def piece(m, place):
        at = sum(place) + place[0]
        for loop in range(4):
            names = plan.get(("A", 3 * loop + at))
            if names:
                pl.when(m == loop)(functools.partial(steps, names))

    def keeps(m):
        lanes = rows_of(m, D)
        return [
            pltpu.make_async_copy(packed.at[m], packed_hbm.at[m], local.at[3 + m]),
            pltpu.make_async_copy(act.at[:, lanes], long_hbm.at[m], local.at[7 + m]),
            pltpu.make_async_copy(dg.at[pl.ds(0, KEPT_REST), lanes], rest_hbm.at[m], local.at[11 + m]),
            pltpu.make_async_copy(ctx.at[m], ctx_hbm.at[m], local.at[15 + m]),
        ]

    def keep_probs(m, number, unit, h, probs):
        offset, length, q0, width = unit
        places = kept_at(offset, length, h)
        row, rows_kept, lane, _ = places[min(q0 // width, len(places) - 1)]
        lane = lane + (q0 if len(places) == 1 else 0)
        lanes = pl.ds(pl.multiple_of(D * m + lane, TILE), width)
        if row < KEPT_LONG:
            act[row : row + rows_kept, lanes] = probs
        else:
            dg[row - KEPT_LONG : row - KEPT_LONG + rows_kept, lanes] = probs

    def heads(m):
        w = gq[m // 2, m % 2].reshape(D, QKV_PAD)
        packed[m] = dot(nrm[...], w).astype(bf)
        keeps(m)[0].start()
        attend_group(
            packed.at[m], mask, rows[m], ctx.at[m], group, functools.partial(piece, m), functools.partial(keep_probs, m)
        )
        for copy in keeps(m)[1:]:
            copy.start()

    def stores(z):
        lanes = rows_of(z, chunk_rows)
        return [
            pltpu.make_async_copy(gi.at[z], gi_hbm.at[z], sem.at[0, z]),
            pltpu.make_async_copy(gu.at[z], gu_hbm.at[z], sem.at[1, z]),
            pltpu.make_async_copy(dg.at[:, lanes], dg_hbm.at[z], sem.at[2, z]),
        ]

    def weights(z):
        lanes = rows_of(z, chunk_rows)
        return pltpu.make_async_copy(act.at[pl.ds(0, chunk_rows), lanes], pu_hbm.at[z], sem.at[3, z])

    each_of(4, heads)
    steps(plan[("before", "O")])
    keep_o = pltpu.make_async_copy(go, go_hbm, out_sems.at[0])
    keep_o.start()
    each_of(layer.n // RCH, layer.midway)
    tail = [
        pltpu.make_async_copy(src, dst, out_sems.at[1 + k])
        for k, (src, dst) in enumerate(((mid, mid_hbm), (n2, n2_hbm), (nrm, gout_hbm), (gffn, gffn_hbm)))
    ]
    tail[0].start()
    tail[1].start()
    each_of(4, lambda m: [copy.wait() for copy in keeps(m)])

    def chunk(e):
        for k in range(depth):
            pl.when(e == k)(functools.partial(steps, plan[("before", f"F{k}")]))
        z = p.nearest(e)
        for name in "iu":
            arrays[name].finish_at(z)
        layer.forward(z)
        for copy in stores(z):
            copy.start()

    each_of(depth, chunk)
    second.finish()
    for copy in (keep_x, keep_n, keep_q):
        copy.wait()
    layer.adapter_all()
    third.start()
    tail[2].start()
    tail[3].start()

    def weights_out(k):
        z = p.order(k)
        lanes = rows_of(z, chunk_rows)
        act[:chunk_rows, lanes] = dot(act[:, lanes], gffn[...], TN).astype(bf)
        weights(z).start()

    for k in range(depth):
        weights_out(k)
    layer.adapter_grads()
    for copy in (keep_o, *tail):
        copy.wait()
    each_of(depth, lambda z: [copy.wait() for copy in (*stores(z), weights(z))])
    third.finish()
    for g in (*arrays.values(), first, second, third):
        g.drain()


def front(depth, group, tok, cot, shards, rows_of_shards, gains, lengths, pos_table, factors):
    hbm = pl.BlockSpec(memory_space=pl.ANY)
    vmem = pl.BlockSpec(memory_space=pltpu.VMEM)
    bf, f32 = jnp.bfloat16, jnp.float32
    shape = jax.ShapeDtypeStruct
    n = tok.shape[0] * SEG
    kept = [(rows, QKV_PAD if i == 0 else D) for i, rows in enumerate(rows_of_shards)]
    whole = [((2, 2, depth, 2) if i == 0 else (depth, 2, 2, 2)) + s for i, s in enumerate(kept)]
    ff = 8 * depth * kept[2][0]
    return pl.pallas_call(
        functools.partial(front_kernel, depth, group),
        out_shape=[
            shape(tok.shape, bf),
            shape(whole[0], bf),
            shape((n, D), bf),
            shape((4, n, QKV_PAD), bf),
            shape(tok.shape, bf),
            shape((n, D), f32),
            shape((4, n, CTX_PAD), bf),
            *[shape(s, bf) for s in whole[1:]],
            shape((depth, n, D), bf),
            shape((depth, D, D), bf),
            shape((n, D), bf),
            shape((n, D), bf),
            shape((n, D), bf),
            shape((4, KEPT_LONG, D), bf),
            shape((4, KEPT_REST, D), bf),
            shape((ROW_END, 128), f32),
        ],
        in_specs=[hbm] * 2 + [vmem] * 7 + [pl.BlockSpec(memory_space=pltpu.SMEM)] + [vmem] * 11,
        out_specs=[hbm] * 17 + [vmem],
        scratch_shapes=[pltpu.VMEM(s, bf) for s in kept]
        + [
            pltpu.VMEM((n, TILE), bf),
            pltpu.VMEM((4, 3, 512), f32),
            pltpu.VMEM(tok.shape, bf),
            pltpu.VMEM(tok.shape, bf),
            *[pltpu.VMEM(s, bf) for s in whole],
            pltpu.VMEM((n, D), bf),
            pltpu.VMEM((4, n, QKV_PAD), bf),
            pltpu.VMEM((4, n, CTX_PAD), bf),
            pltpu.VMEM((D, ADAPT_PAD), bf),
            pltpu.VMEM((D, ADAPT_PAD), bf),
            pltpu.VMEM((D, ADAPT_PAD), f32),
            pltpu.VMEM((D, ADAPT_PAD), f32),
            pltpu.VMEM((n, 1), f32),
            pltpu.VMEM((n, D), f32),
            pltpu.VMEM((n, D), bf),
            pltpu.VMEM((n, ff), bf),
            pltpu.VMEM((n, ff), bf),
            pltpu.VMEM((n, D), f32),
            pltpu.VMEM((n, D), bf),
            pltpu.VMEM(tok.shape, bf),
            pltpu.SemaphoreType.DMA((4, depth)),
            pltpu.SemaphoreType.DMA((5,)),
            pltpu.SemaphoreType.DMA((19,)),
        ]
        + Gather.sems(depth) * 4
        + Exchange.sems() * 3,
        compiler_params=pltpu.CompilerParams(
            collective_id=2, has_side_effects=True, vmem_limit_bytes=63 * 2**20
        ),
        name="front",
    )(
        tok, cot, *shards, jnp.asarray(column_choice(group), bf), *gains, lengths, pos_table,
        jnp.asarray(offset_onehot()), *factors, *map(jnp.asarray, adapter_constants()),
    )


BACK = (
    "Su2 Su0 Su3 Su1",
    "K K K Hu0",
    "K K Si0 Hu2",
    "K Si2 Hu3 Qu0",
    "K K K Si3",
    "Qu2 K So0 K",
    "So2 Si1 Hi0 K",
    "Qu3 K K Ho0",
    "K Fu3 Hi2 So3",
    "K K K K",
    "Hu1 Qo0 K Fu2",
    "K Ho2 Qi0 K",
    "K Ho3 Fu0 K",
    "K Hi3 K Qi2",
    "Hi1 Qu1 K So1",
    "K K Qo3 Fi0",
    "K K K Fo0",
    "Ho1 K Fu1 Qo2",
    "K Fo3 Qi3 Sq0",
    "N Fi3 Sq2 TB",
    "Hq0 Fi2 Sq3 T0",
    "Qi1 Qo1 Fi1 Hq2",
    "Fo1 Hq3 Qq0 Sq1",
    "Fo2 Cu Hq1 Qq2",
    "Fq0 T1 T2 Ci",
    "Eu x1 Qq3 Qq1",
    "Fq2 Fq1 Co Fq3",
    "Ei Cq T3 Eo",
    "Eq T4",
)


def back_order():
    plan, pieces = {}, 0
    for step in " ".join(BACK).split():
        if step in "KN":
            pieces += 1
        else:
            plan.setdefault(pieces, []).append(step)
    return plan


PIECES = 6


def back_kernel(
    depth, bits, group,
    tok_hbm, gq_hbm, nrm_hbm, packed_hbm, mid_hbm, ctx_hbm, go_hbm, gi_hbm, gu_hbm, dg_hbm, gffn_hbm, n2_hbm, gout_hbm,
    long_hbm, rest_hbm, pu, gain, gain_ffn, onehot, other,
    oq, oo, oi, ou, small, gtok,
    wu, wi, dg, acc, mid, gffn, nrm, gout, x, ctx, go, kept, g_gain, sums_s, mine_u, sem_u, local, chunk_sem, gq_sem, *scr,
):
    p = Place(depth)
    n = depth
    bf = jnp.bfloat16
    gain, gain_ffn = gain[...].reshape(1, D), gain_ffn[...].reshape(1, D)
    width = pl.ds(0, QKV_PAD)
    arrays = {
        "u": Scatter(p, False, pu, ou, *scr[0:6], mine_u, sem_u),
        "i": Scatter(p, False, wi, oi, *scr[6:12]),
        "o": Scatter(p, False, go, oo, *scr[12:18]),
        "q": Scatter(
            p, True, wu, oq, *scr[18:24],
            region=lambda core, z: wu.at[:, core, z // 2, z % 2, :, :, width],
        ),
    }
    row_g = Exchange(p, x, gtok, *scr[24:27])
    total = Sum(p, bits, small, *scr[27:30])
    layer = Layer(
        wo=lambda m: go[m].reshape(CTX_PAD, D), wi=lambda z: wi[z].reshape(-1, D),
        wu=lambda z: wu[z // 2, z % 2].reshape(-1, D), slope=lambda z: dg.at[z], ctx=ctx, gain=gain_ffn, g_gain=g_gain,
        mid=mid, n2=nrm, acc=acc, gffn=gffn, glow=gffn, gout=gout,
    )

    def load(src, dst, k):
        return pltpu.make_async_copy(src, dst, local.at[k])

    early = [
        load(src, dst, k)
        for k, (src, dst) in enumerate(
            ((gffn_hbm, gffn), (n2_hbm, nrm), (mid_hbm, mid), (gout_hbm, gout), (ctx_hbm, ctx), (go_hbm, go), (tok_hbm, x))
        )
    ]

    def chunk_in(k):
        z = p.order(k)
        pairs = ((dg_hbm.at[z], dg.at[z]), (gu_hbm.at[z], wu.at[z // 2, z % 2]), (gi_hbm.at[z], wi.at[z]))
        return [pltpu.make_async_copy(src, dst, chunk_sem.at[j, k]) for j, (src, dst) in enumerate(pairs)]

    def packed_in(m):
        return load(packed_hbm.at[m], dg.at[m, :, width], 8 + m)

    def gq_in(m, z):
        y, c = m // 2, m % 2
        return pltpu.make_async_copy(
            gq_hbm.at[y, c, z], wu.at[y, c, z // 2, z % 2, :, :, width], gq_sem.at[m, z]
        )

    def kept_in(m):
        slot = m % 2
        return [
            load(long_hbm.at[m], kept.at[slot, pl.ds(0, KEPT_LONG)], 12 + slot),
            load(rest_hbm.at[m], kept.at[slot, pl.ds(KEPT_LONG, KEPT_REST)], 14 + slot),
        ]

    todo = total.steps()

    def steps(names):
        for name in names:
            if name == "x1":
                row_g.start()
            elif name[0] == "T":
                todo.pop(0)()
            else:
                array = arrays[name[1]]
                if name[0] in "CE":
                    (array.collect if name[0] == "C" else array.finish)()
                else:
                    k = int(name[2:])
                    {"S": array.start, "H": array.to_half, "Q": array.to_quarter, "F": array.forward}[name[0]](k)
                    if name[0] == "Q":
                        array.origin(k)

    plan = back_order()

    def place(k):
        steps(plan.pop(k, ()))

    ahead_of = {1: chunk_in(2), 2: early[2:3], 3: chunk_in(3), 4: early[3:4], 5: early[4:6], 6: kept_in(0), 7: early[6:]}

    def load_ahead(k):
        for copy in ahead_of.get(k, ()):
            copy.start()

    p.greet(bits)
    for copy in (early[0], *chunk_in(0), early[1]):
        copy.start()
    small[...] = jnp.zeros_like(small)
    small[ROW_OTHER:, :] = other[...]
    acc[...] = jnp.zeros_like(acc)
    g_gain[...] = jnp.zeros_like(g_gain)
    p.meet(bits)
    place(0)
    for copy in chunk_in(1):
        copy.start()
    early[0].wait()
    for k in range(n):
        z = p.order(k)
        for copy in chunk_in(k):
            copy.wait()
        load_ahead(2 * k + 1)
        layer.backward(z)
        place(2 * k + 1)
        load_ahead(2 * k + 2)
        if k == 0:
            early[1].wait()
        wi[z] = dot(dg[z], nrm[...], TN).astype(bf).reshape(wi.shape[1:])
        place(2 * k + 2)
    for m in range(4):
        packed_in(m).start()
        for z in range(n):
            gq_in(m, z).start()
    renew = load(nrm_hbm, nrm, 7)
    renew.start()
    for copy in early[2:]:
        copy.wait()
    each_of(layer.n // RCH, layer.last)
    place(2 * n + 1)

    def project(m):
        go[m] = layer.projection(m).reshape(go.shape[1:])

    each_of(4, project)
    acc[...] = jnp.zeros_like(acc)
    place(2 * n + 2)
    renew.wait()
    for m in range(4):
        packed_in(m).wait()
        for z in range(n):
            gq_in(m, z).wait()

    def piece(m, j):
        for loop in range(4):
            names = plan.get(2 * n + 2 + PIECES * loop + j + 1)
            if names:
                pl.when(m == loop)(functools.partial(steps, names))

    def tick(m, at):
        number, head = at
        if number == 0:
            piece(m, head)
        elif head == 8:
            piece(m, 3)

    def heads(m):
        slot, y, c = m % 2, m // 2, m % 2
        for copy in kept_in(m):
            copy.wait()

        def ahead():
            for copy in kept_in(m + 1):
                copy.start()

        pl.when(m < 3)(ahead)
        packed = dg.at[m, :, width]
        attend_group_back(packed, Kept(kept.at[slot]), ctx.at[m], packed, sums_s.at[m], group, functools.partial(tick, m))
        whole = (Ellipsis, slice(0, QKV_PAD))
        acc[...] += dot(packed[...], wu[y, c][whole].reshape(D, QKV_PAD), NT)
        piece(m, 4)
        wu[y, c, :, :, :, :, 0:QKV_PAD] = dot(nrm[...], packed[...], TN).astype(bf).reshape(*wu.shape[2:6], QKV_PAD)
        piece(m, 5)

    each_of(4, heads)
    small[ROW_TABLE : ROW_TABLE + 16, :] = jnp.zeros((16, 128), jnp.float32)
    for m in range(4):
        small[ROW_TABLE + 3 * m : ROW_TABLE + 3 * m + 3, :] = precise(sums_s[m], onehot[...])
    put_row(small, ROW_OTHER + ROW_FFN, g_gain[...])

    def last(s, g_gain):
        r = rows_of(s, SEG)
        v = x[s].astype(jnp.float32)
        g_n1 = acc[r, :]
        scale = lax.rsqrt(jnp.mean(v * v, axis=-1, keepdims=True) + NORM_EPS)
        scaled = gain * g_n1
        centre = jnp.mean(v * scaled, axis=-1, keepdims=True)
        x[s] = (mid[r, :] + scale * scaled - v * (scale * scale * scale * centre)).astype(bf)
        return g_gain + jnp.sum(v * scale * g_n1, axis=0, keepdims=True)

    put_row(small, ROW_GAIN, lax.fori_loop(0, x.shape[0], last, jnp.zeros((1, D), jnp.float32)))
    place(2 * n + 2 + 4 * PIECES + 1)
    row_g.finish()
    for g in (*arrays.values(), row_g, total):
        g.drain()


def back(depth, bits, group, kept, ffn, pu, gains, onehot, other):
    hbm = pl.BlockSpec(memory_space=pl.ANY)
    vmem = pl.BlockSpec(memory_space=pltpu.VMEM)
    bf, f32 = jnp.bfloat16, jnp.float32
    shape = jax.ShapeDtypeStruct
    tok, gq = kept[:2]
    mid, ctx, go, gi = ffn[:4]
    n = mid.shape[0]
    small_rows = ROW_OTHER + other.shape[0]
    outs = [shape(s.shape[4:], f32) for s in (gq, go, gi, gi)]
    outs += [shape((small_rows, 128), f32), shape(tok.shape, bf)]
    dma = pltpu.SemaphoreType.DMA
    scratch = [
        pltpu.VMEM((2, 2, 2, 2, 2, *gi.shape[4:]), bf),
        pltpu.VMEM(gi.shape, bf),
        pltpu.VMEM((depth, n, D), bf),
        pltpu.VMEM((n, D), f32),
        pltpu.VMEM((n, D), f32),
        pltpu.VMEM((n, D), bf),
        pltpu.VMEM((n, D), bf),
        pltpu.VMEM((n, D), bf),
        pltpu.VMEM(tok.shape, bf),
        pltpu.VMEM(ctx.shape, bf),
        pltpu.VMEM(go.shape, bf),
        pltpu.VMEM((2, KEPT_LONG + KEPT_REST, D), bf),
        pltpu.VMEM((1, D), f32),
        pltpu.VMEM((4, 3, 768), f32),
        pltpu.VMEM((depth, 2, 2) + gi.shape[4:], bf),
        dma((depth,)),
        dma((16,)),
        dma((3, depth)),
        dma((4, depth)),
    ]
    for s in (gi, gi, go, gq):
        scratch += Scatter.scratch(depth, *s.shape[4:])
    scratch += Exchange.sems() + Sum.scratch(bits, small_rows)
    return pl.pallas_call(
        functools.partial(back_kernel, depth, bits, group),
        out_shape=outs,
        in_specs=[hbm] * 16 + [vmem] * 4,
        out_specs=[vmem] * 5 + [hbm],
        scratch_shapes=scratch,
        compiler_params=pltpu.CompilerParams(
            collective_id=3, has_side_effects=True, vmem_limit_bytes=63 * 2**20
        ),
        name="back",
    )(*kept, *ffn, pu.reshape(gi.shape), *gains, onehot, other)


def finish_kernel(
    q, o, i, u, small, choice,
    gq, go, gi, gu, g_attn, g_ffn, g_table, g_rules, g_dl, g_dr, g_ul, g_ur,
):
    left = q[: gq.shape[1], :]
    parts = []
    for _ in range(3):
        parts.append(left.astype(jnp.bfloat16))
        left = left - parts[-1].astype(jnp.float32)
    for h in range(3):
        chosen = choice[3 * DH * h : 3 * DH * (h + 1), :]
        gq[h] = sum(dot(part, chosen, NT) for part in parts)
    go[...] = o[: go.shape[0], :]
    gi[...] = i[: gi.shape[0], :]
    gu[...] = u[: gu.shape[0], :]
    for k in range(D // 128):
        lanes = slice(128 * k, 128 * (k + 1))
        g_attn[lanes] = small[ROW_GAIN + k, :]
        g_ffn[lanes] = small[ROW_OTHER + ROW_FFN + k, :]
    g_table[...] = small[ROW_TABLE : ROW_TABLE + g_table.shape[0], :NB]
    for i in range(KRON):
        at = ROW_OTHER + ROW_RULES + 4 * i
        g_rules[i] = small[at : at + 4, :KRON]
    for ref, at in ((g_dl, ROW_OTHER + ROW_DL), (g_ur, ROW_OTHER + ROW_UR)):
        ref[:, :128] = small[at : at + 4, :]
        ref[:, 128:] = small[at + 4 : at + 8, : ref.shape[1] - 128]
    for ref, at in ((g_dr, ROW_OTHER + ROW_DR), (g_ul, ROW_OTHER + ROW_UL)):
        ref[...] = small[at : at + 4, :KA]


def finish(q, o, i, u, small, group, shapes):
    vmem = pl.BlockSpec(memory_space=pltpu.VMEM)
    return pl.pallas_call(
        finish_kernel,
        out_shape=[jax.ShapeDtypeStruct(s, jnp.float32) for s in shapes],
        in_specs=[vmem] * 6,
        out_specs=[vmem] * 12,
        name="finish",
    )(q, o, i, u, small, jnp.asarray(column_choice(group), jnp.bfloat16))


def round_up(n, m):
    return -(-n // m) * m


def pad_rows(a, rows):
    return jnp.pad(a, ((0, rows - a.shape[0]), (0, 0)))


HEADS = 12


def local(
    tokens,
    lengths,
    cotangent,
    w_qkv,
    w_o,
    w_in,
    w_out,
    gain_attn,
    gain_ffn,
    pos_table,
    phm_rules,
    down_left,
    down_right,
    up_left,
    up_right,
):
    dp_count, mp_count = lax.axis_size("dp"), lax.axis_size("mp")
    depth = dp_count // 2
    bits = dp_count.bit_length() - 1
    devices = dp_count * mp_count
    member = lax.axis_index("mp")
    tok_rows = tokens.shape[0]
    seg_count = tok_rows // SEG
    o_rows, in_rows, q_rows = w_o.shape[0], w_in.shape[1], w_qkv.shape[0]
    bf = jnp.bfloat16
    group = o_rows if o_rows % 24 == 0 and round_up(o_rows, 16) * 3 == o_rows * 4 else 3 * DH
    rows_of_shards = [round_up(r, 16) for r in (q_rows, o_rows, in_rows, in_rows)]
    tok_in, cot_in = tokens.reshape(seg_count, SEG, D), cotangent.reshape(seg_count, SEG, D)
    merged = depth == 4 and group == o_rows and rows_of_shards[0] == q_rows and rows_of_shards[2] == in_rows
    factors = (phm_rules, down_left, down_right, up_left, up_right)
    gains = (gain_attn, gain_ffn)
    if merged:
        shards = (w_qkv.transpose(1, 0, 2), w_o, w_in.T, w_out)
        *kept, out, mid, ctx, go, gi, gu, dg, pu, gffn, n2, gout, long, rest, other = front(
            depth, group, tok_in, cot_in, shards, rows_of_shards, gains, lengths, pos_table.T, factors
        )
    else:
        shards = (head_columns(w_qkv.astype(bf), group), w_o.astype(bf), w_in.astype(bf).T, w_out.astype(bf))
        shards = [pad_rows(s, r) for s, r in zip(shards, rows_of_shards)]
        tok_s, cot_s, gq, go, gi, gu = gather_all(depth, tok_in, cot_in, shards)
    def plain(g, rows):
        return g.reshape(devices, g.shape[-2], D)[:, :rows].reshape(devices * rows, D)

    def slots(g, rows):
        padded = jnp.pad(g.reshape(devices, rows, D), ((0, 0), (0, round_up(rows, 16) - rows), (0, 0)))
        return padded.reshape(depth, 2, 2, 2, padded.shape[1], D)

    if not merged:
        tokens_s = tok_s.reshape(tok_rows, D)
        if group == o_rows:
            dense_o = go.reshape(mp_count, CTX_PAD, D)
        else:
            dense_o = plain(go, o_rows).reshape(mp_count, 3 * DH, D)
            dense_o = jnp.pad(dense_o, ((0, 0), (0, CTX_PAD - 3 * DH), (0, 0)))
        qkv_full = gq.reshape(mp_count, dp_count, rows_of_shards[0], QKV_PAD)[:, :, :q_rows]
        qkv_full = qkv_full.reshape(mp_count, D, QKV_PAD)
        live = jnp.concatenate(
            [jnp.arange(length) < own_length(lengths, member, i) for i, (_, length) in enumerate(SPANS)]
        )
        mask = key_mask(live)
        rows = jnp.einsum("bh,br->hr", pos_table, offset_onehot(), precision=FULL_PRECISION).reshape(mp_count, 3, 512)
        normed_attn, packed, context = attention(tokens_s, gains[0].reshape(1, D), qkv_full, mask, rows, group)
        result, grad_mid, grad_context, grad_w_o, grad_w_in, grad_w_out, other = middle(
            tokens_s,
            context,
            dense_o,
            plain(gi, in_rows),
            plain(gu, in_rows),
            cot_s.reshape(tok_rows, D),
            gains[1],
            lengths,
            factors,
        )
    onehot = jnp.asarray(np.pad(table_onehot(), ((0, 0), (0, 128 - NB))))
    if merged:
        oq, oo, oi, ou, summed, gtok = back(
            depth, bits, group, kept, (mid, ctx, go, gi, gu, dg, gffn, n2, gout, long, rest), pu, gains, onehot, other
        )
    else:
        if group == o_rows:
            part_o = grad_w_o.reshape(depth, 2, 2, 2, round_up(o_rows, 16), D)
        else:
            part_o = slots(grad_w_o.reshape(mp_count, CTX_PAD, D)[:, : 3 * DH].reshape(D, D), o_rows)
        result = result.reshape(seg_count, SEG, D)
        packed_grads, sums = attention_back(packed, grad_context, mask, rows, group)
        table_grad = jnp.dot(sums.reshape(HEADS, 768), onehot, precision=FULL_PRECISION)
        grad_w_qkv = jnp.einsum("td,mtc->mdc", normed_attn, packed_grads, preferred_element_type=jnp.float32).astype(bf)
        grad_n1 = jnp.einsum("mtc,mdc->td", packed_grads, qkv_full, preferred_element_type=jnp.float32)
        _, norm_back_attn = jax.vjp(normed, tokens_s.astype(jnp.float32), gain_attn)
        grad_x_part, grad_gain_attn = norm_back_attn(grad_n1)
        grad_tokens = (grad_mid + grad_x_part).astype(bf)
        small = jnp.concatenate([
            jnp.pad(grad_gain_attn.reshape(D // 128, 128), ((0, ROW_TABLE - D // 128), (0, 0))),
            jnp.pad(table_grad, ((0, ROW_OTHER - ROW_TABLE - HEADS), (0, 0))),
            other,
        ])
        part_q = grad_w_qkv.reshape(mp_count, dp_count, q_rows, QKV_PAD)
        part_q = jnp.pad(part_q, ((0, 0), (0, 0), (0, rows_of_shards[0] - q_rows), (0, 0)))
        part_q = part_q.reshape(2, 2, depth, 2, rows_of_shards[0], QKV_PAD)
        oq, oo, oi, ou, summed, out, gtok = scatter_all(
            depth, bits, (part_q, part_o, slots(grad_w_in, in_rows), slots(grad_w_out, in_rows)), small, result, grad_tokens.reshape(seg_count, SEG, D)
        )
    shapes = (
        (3, q_rows, 3 * DH), w_o.shape, w_in.shape[::-1], w_out.shape, (D,), (D,), pos_table.shape[::-1],
        phm_rules.shape, down_left.shape, down_right.shape, up_left.shape, up_right.shape,
    )
    g_qkv, g_o, g_in, g_out, g_attn, g_ffn, g_table, *smalls = finish(oq, oo, oi, ou, summed, group, shapes)
    return (
        out.reshape(tok_rows, D),
        gtok.reshape(tok_rows, D),
        g_qkv.transpose(1, 0, 2),
        g_o,
        g_in.T,
        g_out,
        g_attn,
        g_ffn,
        g_table.T,
        *smalls,
    )


def solution(mesh):
    return jax.shard_map(
        local,
        mesh=mesh,
        in_specs=(
            P(("dp", "mp"), None),
            P("dp"),
            P(("dp", "mp"), None),
            P("dp", "mp", None),
            P(("dp", "mp"), None),
            P(None, ("dp", "mp")),
            P(("dp", "mp"), None),
            P(),
            P(),
            P(),
            P(),
            P(),
            P(),
            P(),
            P(),
        ),
        out_specs=(
            P(("dp", "mp"), None),
            P(("dp", "mp"), None),
            P("dp", "mp", None),
            P(("dp", "mp"), None),
            P(None, ("dp", "mp")),
            P(("dp", "mp"), None),
            P(),
            P(),
            P(),
            P(),
            P(),
            P(),
            P(),
            P(),
        ),
        check_vma=False,
    )
```

```python
import functools
import itertools

import jax
import jax.experimental.pallas as pl
import jax.experimental.pallas.tpu as pltpu
import jax.numpy as jnp
import numpy as np
from jax import lax
from jax.sharding import PartitionSpec as P

D = 768
DH = 64
NB = 32
MAXDIST = 128
ADAPT = 48
KRON = 4
LEN_LONG = 512
LEN_MID = 256
LEN_SHORT = 128
SEG = 128


NORM_EPS = 1e-06
FULL_PRECISION = lax.Precision.HIGHEST


def rel_buckets(length):
    offsets = np.arange(-(length - 1), length)
    half_count = NB // 2
    exact_count = half_count // 2
    upward = (offsets > 0).astype(np.int64) * half_count
    distance = np.abs(offsets)
    scaled = (
        np.log(np.maximum(distance, 1) / exact_count)
        / np.log(MAXDIST / exact_count)
        * (half_count - exact_count)
    )
    far_bucket = np.minimum(
        exact_count + np.floor(np.maximum(scaled, 0.0)).astype(np.int64), half_count - 1
    )
    return upward + np.where(distance < exact_count, distance, far_bucket)


def normed(values, gain):
    return values * lax.rsqrt(jnp.mean(values * values, axis=-1, keepdims=True) + NORM_EPS) * gain


MESH = pl.DeviceIdType.MESH


class Place:
    def __init__(self, depth):
        d, m = lax.axis_index("dp"), lax.axis_index("mp")
        self.depth = depth
        self.d, self.m = d, m
        self.z, self.x, self.y, self.c = d // 2, d % 2, m // 2, m % 2
        dx, dy, c = 1 - 2 * self.x, 2 - 4 * self.y, self.c
        self.sib = (d, m + 1 - 2 * c)
        self.right, self.left = (d + 2, m), (d - 2, m)
        self.mp_peer = ((d, m + 1 - 2 * c), (d, m + dy), (d, 3 - m))
        self.xn, self.yn = (d + dx, m), (d, m + dy)
        self.a_nbr = (d + (1 - c) * dx, m + c * dy)
        self.b_nbr = (d + c * dx, m + (1 - c) * dy)
        self.a = self.x + c * (self.y - self.x)
        self.b = self.y + c * (self.x - self.y)

    def by_core(self, run):
        for core in (0, 1):
            pl.when(self.c == core)(functools.partial(run, core))

    def order(self, k):
        n = self.depth
        base = k // 2 if k % 2 == 0 else n - 1 - k // 2
        near = 1 - jnp.minimum(self.z // max(n // 2, 1), 1)
        return base + near * (n - 1 - 2 * base)

    def nearest(self, e):
        n, z = self.depth, self.z
        ahead = 1 - 2 * (z // ((n + 1) // 2))
        short = jnp.minimum(z, n - 1 - z)
        around = (1 - 2 * (e % 2)) * ((e + 1) // 2)
        return z + ahead * jnp.where(e <= 2 * short, around, e - short)

    def flip(self, bit):
        step = 1 << bit
        return (self.d + step * (1 - 2 * ((self.d // step) % 2)), self.m)

    def barrier(self, bits):
        self.greet(bits)
        self.meet(bits)

    def pals(self, bits):
        return [*self.mp_peer, self.xn] + [self.flip(bit) for bit in range(2, bits)]

    def greet(self, bits):
        sem = pltpu.get_barrier_semaphore()

        def greet(dev):
            pl.semaphore_signal(sem, 1, device_id=dev, device_id_type=MESH)

        for dev in self.pals(bits):
            greet(dev)
        pl.when(self.z > 0)(lambda: greet(self.left))
        pl.when(self.z < self.depth - 1)(lambda: greet(self.right))

    def meet(self, bits):
        ends = jnp.minimum(self.z, 1) + jnp.minimum(self.depth - 1 - self.z, 1)
        pl.semaphore_wait(pltpu.get_barrier_semaphore(), len(self.pals(bits)) + ends)


def remote(src, dst, send, recv, dev):
    return pltpu.make_async_remote_copy(
        src_ref=src, dst_ref=dst, send_sem=send, recv_sem=recv, device_id=dev, device_id_type=MESH
    )


def slot_of(buf, by_head, p):
    return buf.at[p.y, p.c, p.z, p.x] if by_head else buf.at[p.z, p.x, p.y, p.c]


def pair_of(buf, by_head, core, b, z):
    if by_head:
        return buf.at[b, 0, z] if core == 0 else buf.at[:, 1, z, b]
    return buf.at[z, :, b, 0] if core == 0 else buf.at[z, b, :, 1]


class Gather:
    def __init__(self, p, by_head, shard, buf, send, recv, own):
        self.p, self.by_head, self.shard, self.buf = p, by_head, shard, buf
        self.send, self.recv, self.own = send, recv, own
        n = p.depth
        self.first = remote(shard, slot_of(buf, by_head, p), send.at[5 * n], recv.at[4 * n], p.a_nbr)
        self.keep = pltpu.make_async_copy(shard, slot_of(buf, by_head, p), own)

    @staticmethod
    def sems(n):
        return [
            pltpu.SemaphoreType.DMA((5 * n + 1,)),
            pltpu.SemaphoreType.DMA((4 * n + 1,)),
            pltpu.SemaphoreType.DMA,
        ]

    def _copy(self, core, b, z, kind):
        p, n = self.p, self.p.depth
        ref = pair_of(self.buf, self.by_head, core, b, z)
        if kind == "right":
            return remote(ref, ref, self.send.at[z], self.recv.at[z], p.right)
        if kind == "left":
            return remote(ref, ref, self.send.at[n + z], self.recv.at[z], p.left)
        return remote(ref, ref, self.send.at[2 * n + z], self.recv.at[n + z], p.b_nbr)

    def _sib(self, core, b, z):
        n = self.p.depth
        ref = pair_of(self.buf, self.by_head, core, b, z)
        return remote(ref, ref, self.send.at[3 * n + b * n + z], self.recv.at[2 * n + b * n + z], self.p.sib)

    def start(self):
        self.keep.start()
        self.first.start()

    def _spread(self, core, z, right, left):
        p = self.p
        if right:
            pl.when(p.z < p.depth - 1)(lambda: self._copy(core, p.b, z, "right").start())
        if left:
            pl.when(p.z > 0)(lambda: self._copy(core, p.b, z, "left").start())
        self._copy(core, p.b, z, "b").start()
        self._sib(core, p.b, z).start()

    def along(self, k):
        p = self.p
        if isinstance(k, int) and k == 0:
            self.keep.wait()
            self.first.wait_recv()
            p.by_core(lambda core: self._spread(core, p.z, True, True))
            return

        def from_left(core):
            self._copy(core, p.b, p.z - k, "right").wait_recv()
            self._spread(core, p.z - k, True, False)

        def from_right(core):
            self._copy(core, p.b, p.z + k, "left").wait_recv()
            self._spread(core, p.z + k, False, True)

        pl.when(p.z - k >= 0)(lambda: p.by_core(from_left))
        pl.when(p.z + k < p.depth)(lambda: p.by_core(from_right))

    def across(self, k):
        p = self.p

        def one(z, core):
            self._copy(core, 1 - p.b, z, "b").wait_recv()
            self._sib(core, 1 - p.b, z).start()

        pl.when(p.z - k >= 0)(lambda: p.by_core(lambda core: one(p.z - k, core)))
        if not (isinstance(k, int) and k == 0):
            pl.when(p.z + k < p.depth)(lambda: p.by_core(lambda core: one(p.z + k, core)))

    def finish_at(self, z):
        def one(core):
            for b in (0, 1):
                self._sib(1 - core, b, z).wait_recv()

        self.p.by_core(one)

    def finish(self):
        each_of(self.p.depth, self.finish_at)

    def drain(self):
        p, n = self.p, self.p.depth
        self.first.wait_send()

        def each(z, carry):
            def one(core):
                pl.when(jnp.logical_and(p.z < n - 1, z <= p.z))(
                    lambda: self._copy(core, p.b, z, "right").wait_send()
                )
                pl.when(jnp.logical_and(p.z > 0, z >= p.z))(
                    lambda: self._copy(core, p.b, z, "left").wait_send()
                )
                self._copy(core, p.b, z, "b").wait_send()
                for b in (0, 1):
                    self._sib(core, b, z).wait_send()

            p.by_core(one)
            return carry

        lax.fori_loop(0, n, each, 0)


class Exchange:
    def __init__(self, p, src, dst, send, recv, own):
        m = p.m
        c, other = m % 2, 1 - m % 2
        self.local = [
            pltpu.make_async_copy(src.at[m], dst.at[m], own.at[0]),
            pltpu.make_async_copy(src.at[4 + c], dst.at[4 + c], own.at[1]),
            pltpu.make_async_copy(src.at[pl.ds(6, 2)], dst.at[pl.ds(6, 2)], own.at[2]),
        ]
        self.out = [
            remote(src.at[dev[1]], dst.at[m], send.at[j], recv.at[j], dev)
            for j, dev in enumerate(p.mp_peer)
        ] + [remote(src.at[4 + other], dst.at[4 + c], send.at[3], recv.at[3], p.sib)]

    @staticmethod
    def sems():
        return [
            pltpu.SemaphoreType.DMA((4,)),
            pltpu.SemaphoreType.DMA((4,)),
            pltpu.SemaphoreType.DMA((3,)),
        ]

    def start(self):
        for copy in self.out + self.local:
            copy.start()

    def finish(self):
        for copy in self.local:
            copy.wait()
        for copy in self.out:
            copy.wait_recv()

    def drain(self):
        for copy in self.out:
            copy.wait_send()


def add_rows(dst, src, rows):
    step = 32 if rows % 32 == 0 else 16

    def one(i, carry):
        at = pl.ds(pl.multiple_of(i * step, step), step)
        total = dst[at, :].astype(jnp.float32) + src[at, :].astype(jnp.float32)
        dst[at, :] = total.astype(dst.dtype)
        return carry

    lax.fori_loop(0, rows // step, one, 0)


class Scatter:
    def __init__(self, p, by_head, part, total, half, quarter, arrive, last, send, recv, mine=None, mine_sem=None, region=None):
        self.p, self.by_head, self.part, self.total = p, by_head, part, total
        self.mine, self.mine_sem, self.region = mine, mine_sem, region
        self.half, self.quarter, self.arrive, self.last = half, quarter, arrive, last
        self.send, self.recv = send, recv
        self.rows = part.shape[-2]

    @staticmethod
    def scratch(n, rows, cols, dtype=jnp.bfloat16):
        return [
            pltpu.VMEM((n, 2, 2, rows, cols), dtype),
            pltpu.VMEM((n, 2, rows, cols), dtype),
            pltpu.VMEM((n + 1, 2, rows, cols), dtype),
            pltpu.VMEM((rows, cols), dtype),
            pltpu.SemaphoreType.DMA((3 * n + 1,)),
            pltpu.SemaphoreType.DMA((3 * n + 2,)),
        ]

    def order(self, k):
        return self.p.order(k)

    def _region(self, core, z):
        if self.region is not None:
            return self.region(core, z)
        return self.part.at[:, core, z] if self.by_head else self.part.at[z, :, :, core]

    def _half_pair(self, core, b, z):
        over_first = (core == 0) != self.by_head
        return self.half.at[z, :, b] if over_first else self.half.at[z, b]

    def _sib(self, core, z):
        return remote(
            self._region(1 - core, z), self.half.at[z], self.send.at[z], self.recv.at[z], self.p.sib
        )

    def _b(self, core, z):
        n, p = self.p.depth, self.p
        return remote(
            self._half_pair(core, 1 - p.b, z), self.quarter.at[z], self.send.at[n + z], self.recv.at[n + z], p.b_nbr
        )

    def _right(self, z):
        n, p = self.p.depth, self.p
        return remote(
            self.quarter.at[z], self.arrive.at[z], self.send.at[2 * n + z], self.recv.at[2 * n + z], p.right
        )

    def _left(self, z, goal):
        n, p = self.p.depth, self.p
        return remote(
            self.quarter.at[z], self.arrive.at[goal], self.send.at[2 * n + z], self.recv.at[2 * n + goal], p.left
        )

    def _a(self):
        n, p = self.p.depth, self.p
        return remote(
            self.quarter.at[p.z, 1 - p.a], self.last, self.send.at[3 * n], self.recv.at[3 * n + 1], p.a_nbr
        )

    def _keep(self, core, z):
        return pltpu.make_async_copy(self._region(core, z), self.mine.at[z], self.mine_sem.at[z])

    def start(self, k):
        z = self.order(k)

        def one(core):
            self._sib(core, z).start()
            if self.mine is not None:
                self._keep(core, z).start()

        self.p.by_core(one)

    def to_half(self, k):
        z = self.order(k)

        def one(core):
            self._sib(core, z).wait_recv()
            region = self._region(core, z)
            if self.mine is not None:
                self._keep(core, z).wait()
                region = self.mine.at[z]
            for i in (0, 1):
                for j in (0, 1):
                    add_rows(self.half.at[z, i, j], region.at[i, j], self.rows)
            self._b(core, z).start()

        self.p.by_core(one)

    def to_quarter(self, k):
        z = self.order(k)

        def one(core):
            self._b(core, z).wait_recv()
            for i in (0, 1):
                add_rows(self.quarter.at[z, i], self._half_pair(core, self.p.b, z).at[i], self.rows)

        self.p.by_core(one)

    def _take(self, z, slot):
        for i in (0, 1):
            add_rows(self.quarter.at[z, i], self.arrive.at[slot, i], self.rows)

    def _send_left(self, z):
        p, n = self.p, self.p.depth
        pl.when(z == p.z - 1)(lambda: self._left(z, n).start())
        pl.when(z < p.z - 1)(lambda: self._left(z, z).start())

    def origin(self, k):
        p, n = self.p, self.p.depth
        z = self.order(k)
        pl.when(jnp.logical_and(p.z == 0, z > p.z))(lambda: self._right(z).start())
        pl.when(jnp.logical_and(p.z == n - 1, z < p.z))(lambda: self._send_left(z))

    def forward(self, k):
        p, n = self.p, self.p.depth
        z = self.order(k)

        def rightward():
            self._right(z).wait_recv()
            self._take(z, z)
            self._right(z).start()

        def leftward():
            self._left(z, z).wait_recv()
            self._take(z, z)
            self._send_left(z)

        pl.when(jnp.logical_and(p.z > 0, z > p.z))(rightward)
        pl.when(jnp.logical_and(p.z < n - 1, z < p.z))(leftward)

    def collect(self):
        p, n = self.p, self.p.depth

        def from_left():
            self._right(p.z).wait_recv()
            self._take(p.z, p.z)

        def from_right():
            self._left(p.z, n).wait_recv()
            self._take(p.z, n)

        pl.when(p.z > 0)(from_left)
        pl.when(p.z < n - 1)(from_right)
        self._a().start()

    def finish(self):
        p = self.p
        self._a().wait_recv()
        self.total[...] = self.quarter[p.z, p.a].astype(jnp.float32) + self.last[...].astype(jnp.float32)

    def drain(self):
        p, n = self.p, self.p.depth
        self._a().wait_send()

        def each(z, carry):
            def one(core):
                self._sib(core, z).wait_send()
                self._b(core, z).wait_send()

            p.by_core(one)
            pl.when(z != p.z)(lambda: self._right(z).wait_send())
            return carry

        lax.fori_loop(0, n, each, 0)

    def steps(self):
        n = self.p.depth
        todo = [lambda: [self.start(k) for k in range(n)]]
        todo += [functools.partial(self.to_half, k) for k in range(n)]
        for k in range(n):
            todo.append(functools.partial(lambda k: (self.to_quarter(k), self.origin(k), self.forward(k)), k))
        return todo


class Sum:
    def __init__(self, p, bits, value, slots, send, recv):
        self.p, self.bits, self.value, self.slots = p, bits, value, slots
        self.send, self.recv = send, recv

    @staticmethod
    def scratch(bits, rows):
        return [
            pltpu.VMEM((2 * (bits + 2), rows, 128), jnp.float32),
            pltpu.SemaphoreType.DMA((bits + 2,)),
            pltpu.SemaphoreType.DMA((bits + 2,)),
        ]

    def _copy(self, s):
        p = self.p
        dev = (p.sib, p.yn, *[p.flip(bit) for bit in range(self.bits)])[s]
        return remote(self.slots.at[2 * s], self.slots.at[2 * s + 1], self.send.at[s], self.recv.at[s], dev)

    def steps(self):
        def begin():
            self.slots[0] = self.value[...]
            self._copy(0).start()

        def one(s):
            self._copy(s).wait_recv()
            total = self.slots[2 * s] + self.slots[2 * s + 1]
            if s == self.bits + 1:
                self.value[...] = total
            else:
                self.slots[2 * s + 2] = total
                self._copy(s + 1).start()

        return [begin] + [functools.partial(one, s) for s in range(self.bits + 2)]

    def drain(self):
        for s in range(self.bits + 2):
            self._copy(s).wait_send()


def in_waves(lists, lag):
    for t in range(max(len(todo) + lag * r for r, todo in enumerate(lists))):
        for r, todo in enumerate(lists):
            if 0 <= t - lag * r < len(todo):
                todo[t - lag * r]()


def gather_kernel(p_depth, tok, cot, wq, wo, wi, wu, tok_s, cot_s, gq, go, gi, gu, *sems):
    p = Place(p_depth)
    n = p_depth
    arrays = []
    for i, (by_head, shard, buf) in enumerate(
        ((True, wq, gq), (False, wo, go), (False, wi, gi), (False, wu, gu))
    ):
        arrays.append(Gather(p, by_head, shard, buf, *sems[3 * i : 3 * i + 3]))
    rows = [Exchange(p, tok, tok_s, *sems[12:15]), Exchange(p, cot, cot_s, *sems[15:18])]
    p.barrier(0)
    for g in arrays:
        g.start()
    rows[0].start()
    if n <= 8:
        for k in range(n):
            for g in arrays:
                g.along(k)
            if k > 0:
                for g in arrays:
                    g.across(k - 1)
            if k == 1:
                rows[1].start()
        for g in arrays:
            g.across(n - 1)
    else:
        for g in arrays:
            g.along(0)
            lax.fori_loop(1, n, lambda k, carry: (g.along(k), carry)[1], 0)
        rows[1].start()
        for g in arrays:
            g.across(0)
            lax.fori_loop(1, n, lambda k, carry: (g.across(k), carry)[1], 0)
    for g in arrays + rows:
        g.finish()
    for g in arrays + rows:
        g.drain()


def gather_all(depth, tok, cot, shards):
    hbm = pl.BlockSpec(memory_space=pl.ANY)
    outs = [jax.ShapeDtypeStruct(tok.shape, tok.dtype)] * 2
    for i, s in enumerate(shards):
        lead = (2, 2, depth, 2) if i == 0 else (depth, 2, 2, 2)
        outs.append(jax.ShapeDtypeStruct(lead + s.shape, s.dtype))
    sems = Gather.sems(depth) * 4 + Exchange.sems() * 2
    return pl.pallas_call(
        functools.partial(gather_kernel, depth),
        out_shape=outs,
        in_specs=[hbm] * 6,
        out_specs=[hbm] * 6,
        scratch_shapes=sems,
        compiler_params=pltpu.CompilerParams(collective_id=0, has_side_effects=True),
        name="gather",
    )(tok, cot, *shards)


def scatter_kernel(depth, bits, pq, po, pi, pu, small, out_s, gtok_s, oq, oo, oi, ou, small_o, out, gtok, *scr):
    p = Place(depth)
    arrays = []
    for i, (by_head, part, total) in enumerate(
        ((False, pu, ou), (False, pi, oi), (False, po, oo), (True, pq, oq))
    ):
        arrays.append(Scatter(p, by_head, part, total, *scr[6 * i : 6 * i + 6]))
    rows = [Exchange(p, out_s, out, *scr[24:27]), Exchange(p, gtok_s, gtok, *scr[27:30])]
    small_o[...] = small[...]
    sums = Sum(p, bits, small_o, *scr[30:33])
    p.barrier(bits)
    rows[0].start()
    in_waves([g.steps() for g in arrays], min(depth, 4))
    rows[1].start()
    close(arrays, sums)
    for r in rows:
        r.finish()
    for g in arrays + rows + [sums]:
        g.drain()


def close(arrays, sums):
    closing = [g.collect for g in arrays] + [g.finish for g in arrays]
    for step in itertools.chain(*itertools.zip_longest(sums.steps(), closing)):
        if step is not None:
            step()


def scatter_all(depth, bits, parts, small, out_s, gtok_s):
    hbm = pl.BlockSpec(memory_space=pl.ANY)
    vmem = pl.BlockSpec(memory_space=pltpu.VMEM)
    outs = [jax.ShapeDtypeStruct(s.shape[4:], jnp.float32) for s in parts]
    outs += [jax.ShapeDtypeStruct(small.shape, jnp.float32)]
    outs += [jax.ShapeDtypeStruct(out_s.shape, out_s.dtype)] * 2
    scr = []
    for s in (parts[3], parts[2], parts[1], parts[0]):
        scr += Scatter.scratch(depth, *s.shape[4:])
    scr += Exchange.sems() * 2 + Sum.scratch(bits, small.shape[0])
    return pl.pallas_call(
        functools.partial(scatter_kernel, depth, bits),
        out_shape=outs,
        in_specs=[vmem] * 5 + [hbm] * 2,
        out_specs=[vmem] * 5 + [hbm] * 2,
        scratch_shapes=scr,
        compiler_params=pltpu.CompilerParams(
            collective_id=1, has_side_effects=True, vmem_limit_bytes=60 * 2**20
        ),
        name="scatter",
    )(*parts, small, out_s, gtok_s)

SPANS = ((0, LEN_LONG), (LEN_LONG, LEN_MID), (LEN_LONG + LEN_MID, LEN_SHORT), (LEN_LONG + LEN_MID + LEN_SHORT, LEN_SHORT))
TILE = 128
QKV_PAD = 640
CTX_PAD = 256
ADAPT_PAD = 128
MASK_LOW = -1e9
NN = (((1,), (0,)), ((), ()))
NT = (((1,), (1,)), ((), ()))
TN = (((0,), (0,)), ((), ()))


def dot(a, b, dims=NN):
    return lax.dot_general(a, b, dims, preferred_element_type=jnp.float32)


def table_onehot():
    buckets = rel_buckets(257)
    offset = np.clip(256 - np.arange(512), -256, 256) + 256
    index = np.concatenate([buckets[offset], np.full(128, NB // 2 - 1), np.full(128, NB - 1)])
    return (index[:, None] == np.arange(NB)[None, :]).astype(np.float32)


def bias_tiles(row):
    spread = pltpu.roll(jnp.broadcast_to(row, (TILE, 512)), 0, 1, stride=1, stride_axis=0)
    far = [jnp.broadcast_to(row[:, at : at + 1], (TILE, TILE)) for at in (511, 0)]
    near = [spread[:, 256 - 128 * delta : 384 - 128 * delta] for delta in (-1, 0, 1)]
    return [far[0], *near, far[1]]


def diagonal_sums(tiles):
    grid = jnp.concatenate([jnp.zeros((TILE, TILE), jnp.float32), tiles[2], tiles[1], tiles[0]], axis=1)
    rows = TILE
    while rows > 8:
        rows //= 2
        grid = grid[:rows] + pltpu.roll(grid[rows:], 512 - rows, 1)
    total = grid[0:1]
    for r in range(1, 8):
        total = total + pltpu.roll(grid[r : r + 1], 512 - r, 1)
    return total


def swap_halves(tile):
    return jnp.concatenate([tile[:, DH:], tile[:, :DH]], axis=1)


def lanes_below(shape, at=DH):
    return lax.broadcasted_iota(jnp.int32, shape, len(shape) - 1) < at


def key_side(qk, mask):
    swapped = swap_halves(qk)
    return jnp.where(lanes_below(qk.shape), swapped, mask), swapped


def query_side(qk):
    lane = lax.broadcasted_iota(jnp.int32, qk.shape, 1)
    return jnp.where(lane < DH, qk, jnp.where(lane == DH, 1.0, 0.0).astype(qk.dtype))


def probabilities(scores, tiles, length, q0=0):
    width = scores.shape[1]
    blocks = []
    for kb in range(length // TILE):
        deltas = [max(-2, min(2, kb - (q0 + qi))) + 2 for qi in range(width // TILE)]
        bias = tiles[deltas[0]] if len(deltas) == 1 else jnp.concatenate([tiles[d] for d in deltas], axis=1)
        blocks.append(scores[kb * TILE : (kb + 1) * TILE] + bias)
    top = blocks[0]
    for block in blocks[1:]:
        top = jnp.maximum(top, block)
    top = jnp.max(top, axis=0, keepdims=True)
    blocks = [jnp.exp(block - top) for block in blocks]
    total = blocks[0]
    for block in blocks[1:]:
        total = total + block
    inverse = 1.0 / jnp.sum(total, axis=0, keepdims=True)
    return [block * inverse for block in blocks]


def join(blocks, axis=0):
    return blocks[0] if len(blocks) == 1 else jnp.concatenate(blocks, axis=axis)


def value_lanes(group):
    stride = group * CTX_PAD // (3 * DH)
    lane = np.arange(CTX_PAD)
    column = lane // stride * group + lane % stride
    return np.where(lane % stride < group, column // DH, -1), column


def head_runs(group):
    heads, _ = value_lanes(group)
    runs = []
    for lane in range(CTX_PAD):
        head = int(heads[lane])
        head = runs[-1][2] if head < 0 else head
        if runs and runs[-1][2] == head:
            runs[-1][1] = lane + 1
        else:
            runs.append([lane, lane + 1, head])
    return runs


def head_lanes(shape, group, head):
    lane = lax.broadcasted_iota(jnp.int32, shape, len(shape) - 1)
    inside = None
    for lo, hi, h in head_runs(group):
        if h == head:
            run = jnp.logical_and(lane >= lo, lane < hi)
            inside = run if inside is None else jnp.logical_or(inside, run)
    return inside


def no_tick(j):
    pass


def no_keep(number, place, h, probs):
    pass


FRONT_SPANS = (SPANS[:1], SPANS[1:])
FRONT_WIDTH = 256


def attend_group(packed, mask_ref, rows, context, group, tick=no_tick, keep=no_keep):
    tiles = [bias_tiles(rows[h : h + 1, :]) for h in range(3)]
    for number, spans in enumerate(FRONT_SPANS):
        units = []
        for offset, length in spans:
            width = min(length, FRONT_WIDTH)
            units += [(offset, length, q0, width) for q0 in range(0, length, width)]
        batches = [[unit] for unit in units] if number == 0 else [units]
        keys = {
            (offset, h): key_side(packed[pl.ds(offset, length), h * TILE : (h + 1) * TILE], mask_ref[pl.ds(offset, length), :])[0]
            for offset, length in spans
            for h in range(3)
        }
        values = {offset: packed[pl.ds(offset, length), 3 * TILE : QKV_PAD].T for offset, length in spans}
        for turn, batch in enumerate(batches):
            work = [(unit, h) for unit in batch for h in range(3)]
            scores = []
            for (offset, length, q0, width), h in work:
                queries = query_side(packed[pl.ds(offset + q0, width), h * TILE : (h + 1) * TILE])
                scores.append(dot(keys[offset, h], queries, NT))
            probs = []
            for ((offset, length, q0, width), h), score in zip(work, scores):
                blocks = probabilities(score, tiles[h], length, q0 // TILE)
                probs.append(join([block.astype(jnp.bfloat16) for block in blocks]))
            for (unit, h), prob in zip(work, probs):
                keep(number, unit, h, prob)
            outs = [dot(values[unit[0]], prob) for (unit, h), prob in zip(work, probs)]
            for i, (offset, length, q0, width) in enumerate(batch):
                own = outs[3 * i : 3 * i + 3]
                whole = jnp.concatenate([own[h][lo:hi] for lo, hi, h in head_runs(group)], axis=0)
                context[pl.ds(offset + q0, width), :] = whole.T.astype(jnp.bfloat16)
            tick((number, turn))


BACK_SPANS = (SPANS[:1], SPANS[1:])
SKEW = (5, 0)


def head_back(packed, recall, grad_context, grad_packed, group, near, far, value_sums, span_of, h):
    offset, length = span_of
    span, at = pl.ds(offset, length), pl.ds(h * TILE, TILE)
    qk = packed[span, at]
    low = lanes_below(qk.shape)
    swapped = swap_halves(qk)
    g_tile = grad_context[span, :]
    g_tile = jnp.where(head_lanes(g_tile.shape, group, h), g_tile, jnp.zeros_like(g_tile))
    scores = recall.scores(qk, span, h)
    g_probs = dot(packed[span, 3 * TILE : QKV_PAD], g_tile, NT)
    yield
    probs = recall.probs(scores, span_of, h)
    yield
    count = length // TILE
    g_blocks = [g_probs[kb * TILE : (kb + 1) * TILE] for kb in range(count)]
    total = probs[0] * g_blocks[0]
    for kb in range(1, count):
        total = total + probs[kb] * g_blocks[kb]
    centre = jnp.sum(total, axis=0, keepdims=True)
    low_probs = join([block.astype(jnp.bfloat16) for block in probs])
    g_scores = [(a * (g - centre)).astype(jnp.bfloat16) for a, g in zip(probs, g_blocks)]
    for kb, block in enumerate(g_scores):
        wide = block.astype(jnp.float32)
        for qi in range(count):
            piece = wide[:, qi * TILE : (qi + 1) * TILE]
            delta = kb - qi
            if abs(delta) <= 1:
                held = near[h][delta + 1]
                near[h][delta + 1] = piece if held is None else held + piece
            else:
                side = 0 if delta < 0 else 1
                far[h][side] = far[h][side] + piece
    yield
    g_scores = join(g_scores)
    g_v = dot(low_probs, g_tile)
    value_sums[offset] = value_sums[offset] + g_v if offset in value_sums else g_v
    grad_keys = dot(g_scores, jnp.where(low, jnp.zeros_like(qk), swapped))
    grad_queries = dot(jnp.where(low, swapped, jnp.zeros_like(qk)).T, g_scores).T
    yield
    grad_packed[span, at] = (grad_queries + grad_keys).astype(jnp.bfloat16)


class Again:
    def __init__(self, mask, rows):
        self.mask = mask
        self.tiles = [bias_tiles(rows[h : h + 1, :]) for h in range(3)]

    def scores(self, qk, span, h):
        return dot(key_side(qk, self.mask[span, :])[0], query_side(qk), NT)

    def probs(self, scores, span_of, h):
        return probabilities(scores, self.tiles[h], span_of[1])


class Kept:
    def __init__(self, kept):
        self.kept = kept

    def scores(self, qk, span, h):
        return None

    def probs(self, scores, span_of, h):
        offset, length = span_of
        pieces = [self.kept[r : r + n, c : c + w] for r, n, c, w in kept_at(offset, length, h)]
        whole = join(pieces, axis=1).astype(jnp.float32)
        return [whole[kb * TILE : (kb + 1) * TILE] for kb in range(length // TILE)]


KEPT_LONG, KEPT_REST = 1024, 384


def kept_at(offset, length, h):
    if length == LEN_LONG:
        if h < 2:
            return [(LEN_LONG * h, LEN_LONG, 0, LEN_LONG)]
        return [(LEN_LONG * k, LEN_LONG, LEN_LONG, LEN_LONG // 2) for k in range(2)]
    if length == LEN_MID:
        return [(KEPT_LONG, LEN_MID, LEN_MID * h, LEN_MID)]
    second = (offset - LEN_LONG - LEN_MID) // LEN_SHORT
    return [(KEPT_LONG + LEN_MID, LEN_SHORT, LEN_SHORT * (3 * second + h), LEN_SHORT)]


def attend_group_back(packed, recall, grad_context, grad_packed, sums, group, tick=no_tick):
    near = [[None] * 3 for _ in range(3)]
    far = [[jnp.zeros((TILE, TILE), jnp.float32)] * 2 for _ in range(3)]
    value_sums = {}

    def heads_of(spans):
        return [
            head_back(packed, recall, grad_context, grad_packed, group, near, far, value_sums, s, h)
            for s in spans
            for h in range(3)
        ]

    def values_of(spans):
        for offset, length in spans:
            grad_packed[pl.ds(offset, length), 3 * TILE : QKV_PAD] = value_sums.pop(offset).astype(jnp.bfloat16)

    for number, spans in enumerate(BACK_SPANS):
        heads = heads_of(spans)
        skew = SKEW[number]
        for t in range(5 + skew * (len(heads) - 1)):
            for i, head in enumerate(heads):
                if 0 <= t - skew * i < 5:
                    next(head, None)
                    if t - skew * i == 4:
                        tick((number, i))
        values_of(spans)
    for h in range(3):
        sums[h : h + 1, :512] = diagonal_sums(near[h])
        for side in range(2):
            sums[h : h + 1, 512 + side * TILE : 640 + side * TILE] = jnp.sum(far[h][side], axis=0, keepdims=True)


def attention_kernel(group, x_ref, gain, w_ref, mask, rows, normed_out, packed, context):
    @pl.when(pl.program_id(0) == 0)
    def _():
        x = x_ref[...].astype(jnp.float32)
        scale = lax.rsqrt(jnp.mean(x * x, axis=-1, keepdims=True) + NORM_EPS)
        normed_out[...] = (x * scale * gain[...]).astype(jnp.bfloat16)

    packed[0] = dot(normed_out[...], w_ref[0]).astype(jnp.bfloat16)
    attend_group(packed.at[0], mask, rows[0], context.at[0], group)


def attention(x, gain, w, mask, rows, group):
    n = x.shape[0]
    bf = jnp.bfloat16
    return pl.pallas_call(
        functools.partial(attention_kernel, group),
        grid=(4,),
        out_shape=[
            jax.ShapeDtypeStruct((n, D), bf),
            jax.ShapeDtypeStruct((4, n, QKV_PAD), bf),
            jax.ShapeDtypeStruct((4, n, CTX_PAD), bf),
        ],
        in_specs=[
            pl.BlockSpec((n, D), lambda i: (0, 0)),
            pl.BlockSpec((1, D), lambda i: (0, 0)),
            pl.BlockSpec((1, D, QKV_PAD), lambda i: (i, 0, 0)),
            pl.BlockSpec((n, TILE), lambda i: (0, 0)),
            pl.BlockSpec((1, 3, 512), lambda i: (i, 0, 0)),
        ],
        out_specs=[
            pl.BlockSpec((n, D), lambda i: (0, 0)),
            pl.BlockSpec((1, n, QKV_PAD), lambda i: (i, 0, 0)),
            pl.BlockSpec((1, n, CTX_PAD), lambda i: (i, 0, 0)),
        ],
        compiler_params=pltpu.CompilerParams(vmem_limit_bytes=56 * 2**20),
        name="attention",
    )(x, gain, w, mask, rows)


def attention_back_kernel(group, packed, grad_context, mask, rows, grad_packed, sums):
    attend_group_back(packed.at[0], Again(mask, rows[0]), grad_context.at[0], grad_packed.at[0], sums.at[0], group)


def attention_back(packed, grad_context, mask, rows, group):
    n = packed.shape[1]
    return pl.pallas_call(
        functools.partial(attention_back_kernel, group),
        grid=(4,),
        out_shape=[
            jax.ShapeDtypeStruct((4, n, QKV_PAD), jnp.bfloat16),
            jax.ShapeDtypeStruct((4, 3, 768), jnp.float32),
        ],
        in_specs=[
            pl.BlockSpec((1, n, QKV_PAD), lambda i: (i, 0, 0)),
            pl.BlockSpec((1, n, CTX_PAD), lambda i: (i, 0, 0)),
            pl.BlockSpec((n, TILE), lambda i: (0, 0)),
            pl.BlockSpec((1, 3, 512), lambda i: (i, 0, 0)),
        ],
        out_specs=[
            pl.BlockSpec((1, n, QKV_PAD), lambda i: (i, 0, 0)),
            pl.BlockSpec((1, 3, 768), lambda i: (i, 0, 0)),
        ],
        compiler_params=pltpu.CompilerParams(vmem_limit_bytes=56 * 2**20),
        name="attention_back",
    )(packed, grad_context, mask, rows)


def head_columns(w, group):
    n = w.shape[0]
    qk = w[:, :, : 2 * DH].reshape(n, 6 * DH)
    v = w[:, :, 2 * DH :].reshape(n, 3 * DH // group, group)
    v = jnp.pad(v, ((0, 0), (0, 0), (0, group // 3))).reshape(n, CTX_PAD)
    return jnp.concatenate([qk, v], axis=1)


def key_mask(live):
    lane = jnp.arange(TILE)[None, :]
    return jnp.where((lane == DH) & ~live[:, None], MASK_LOW, 0.0).astype(jnp.bfloat16)


def precise(a, b, dims=NN):
    return lax.dot_general(a, b, dims, precision=FULL_PRECISION, preferred_element_type=jnp.float32)


def offset_onehot():
    buckets = rel_buckets(257)
    offset = np.clip(256 - np.arange(512), -256, 256) + 256
    return (np.arange(NB)[:, None] == buckets[offset][None, :]).astype(np.float32)


def value_choice(group):
    choice = np.zeros((3 * DH, CTX_PAD), np.float32)
    heads, column = value_lanes(group)
    lanes = np.flatnonzero(heads >= 0)
    choice[column[lanes], lanes] = 1
    return choice


def own_length(lengths, member, number):
    at = (member, 4 + member // 2 + 2 * (member % 2), 8 + member, 12 + member)[number]
    return lengths[at]


def fill_mask(mask, lengths, member):
    for number, (offset, length) in enumerate(SPANS):
        row = lax.broadcasted_iota(jnp.int32, (length, TILE), 0)
        lane = lax.broadcasted_iota(jnp.int32, (length, TILE), 1)
        dead = jnp.logical_and(row >= own_length(lengths, member, number), lane == DH)
        mask[offset : offset + length, :] = jnp.where(dead, MASK_LOW, 0.0).astype(jnp.bfloat16)


def fill_rows(rows, pos_table, onehot):
    table = precise(pos_table[...], onehot[...])
    for m in range(4):
        rows[m] = table[3 * m : 3 * m + 3, :]


KA = ADAPT // KRON


def adapter_constants():
    i, b = np.arange(16) // 4, np.arange(16) % 4
    same = (np.arange(4)[:, None] == i[None, :]).astype(np.float32)
    pick = np.zeros((4, 4, 16), np.float32)
    pick[i, b, np.arange(16)] = 1
    fold = np.zeros((ADAPT_PAD, KA), np.float32)
    fold[np.arange(ADAPT), np.arange(ADAPT) % KA] = 1
    agree = np.zeros((ADAPT_PAD, 16), np.float32)
    agree[:ADAPT] = np.arange(ADAPT)[:, None] // KA == b[None, :]
    return same, pick, fold, agree


class Factor:
    def __init__(self, rules, tall, short, consts):
        self.same, _, self.fold, self.agree = consts
        spread = precise(tall, self.same, TN)
        self.tall = jnp.concatenate([spread] * KRON, axis=0)
        rows = spread.shape[0]
        self.rules = jnp.concatenate(
            [jnp.broadcast_to(rules[a : a + 1, :], (rows, 16)) for a in range(KRON)], axis=0
        )
        self.short = precise(self.fold, precise(short, self.same, TN)) * self.agree

    def whole(self):
        return precise(self.rules * self.tall, self.short, NT)

    def back(self, grad):
        wide = precise(grad, self.short)
        rows = wide.shape[0] // KRON
        tall = wide * self.rules
        tall = sum(tall[a * rows : (a + 1) * rows] for a in range(KRON))
        rules = wide * self.tall
        rules = [jnp.sum(rules[a * rows : (a + 1) * rows], axis=0, keepdims=True) for a in range(KRON)]
        short = precise(self.rules * self.tall, grad, TN) * self.agree.T
        short = precise(precise(self.same, short), self.fold)
        return jnp.concatenate(rules, axis=0), precise(self.same, tall, NT), short


def rule_tables(rules, pick):
    return [sum(precise(rules[i], pick[i], dims) for i in range(KRON)) for dims in (NN, TN)]


ROW_GAIN, ROW_TABLE, ROW_OTHER = 0, 8, 24
ROW_FFN, ROW_DL, ROW_UR, ROW_DR, ROW_UL, ROW_RULES, ROW_END = 0, 8, 16, 24, 28, 32, 48


def put_row(ref, at, row):
    for k in range(row.shape[1] // 128):
        ref[at + k : at + k + 1, :] = row[:, 128 * k : 128 * (k + 1)]


FCH = 768
RCH = 256


def gelu_both(v):
    phi = 0.5 + 0.5 * lax.erf(v * np.float32(np.sqrt(0.5)))
    return v * phi, phi + v * (jnp.exp(-0.5 * v * v) * np.float32(1.0 / np.sqrt(2.0 * np.pi)))


def rows_of(i, size=RCH):
    return pl.ds(pl.multiple_of(i * size, size), size)


def each_of(count, body):
    lax.fori_loop(0, count, lambda i, carry: (body(i), carry)[1], 0)


class Layer:
    def __init__(self, **refs):
        self.__dict__.update(refs)
        self.n = self.n2.shape[0]

    def midway(self, i):
        r = rows_of(i)
        total = self.x_rows(i)
        for m in range(4):
            total = total + dot(self.ctx[m, r, :], self.wo(m))
        self.mid[r, :] = total
        scale = lax.rsqrt(jnp.mean(total * total, axis=-1, keepdims=True) + NORM_EPS)
        self.n2[r, :] = (total * scale * self.gain[...]).astype(jnp.bfloat16)

    def forward(self, j):
        f = rows_of(j, self.chunk)
        for half in range(2):
            r = pl.ds(half * (self.n // 2), self.n // 2)
            value, slope = gelu_both(dot(self.n2[r, :], self.wi(j), NT))
            value = value.astype(jnp.bfloat16)
            self.act[r, f] = value
            self.dg[r, f] = slope.astype(jnp.bfloat16)
            self.acc[r, :] += dot(value, self.wu(j))

    def factors(self):
        consts = [c[...] for c in self.consts]
        by_a, by_b = rule_tables(self.rules, consts[1])
        d_left, d_right, u_left, u_right = self.sides
        return (
            Factor(by_a, d_left[...], d_right[...], consts),
            Factor(by_b, u_right[...], u_left[...], consts),
        )

    def prepare(self, member):
        down, up = self.factors()
        self.down[...] = down.whole().astype(jnp.bfloat16)
        self.up[...] = up.whole().astype(jnp.bfloat16)
        for number, (offset, length) in enumerate(SPANS):
            row = lax.broadcasted_iota(jnp.int32, (length, 1), 0)
            alive = row < own_length(self.lengths, member, number)
            self.live[offset : offset + length, :] = jnp.where(alive, 1.0, 0.0)

    def adapter(self, i):
        bf = jnp.bfloat16
        r = rows_of(i)
        ffn = self.acc[r, :]
        low = ffn.astype(bf)
        value, slope = gelu_both(dot(low, self.down[...]))
        value = value.astype(bf)
        self.put_res(i, (self.mid[r, :] + ffn + dot(value, self.up[...], NT)).astype(bf))
        g_out = self.cot_rows(i) * self.live[r, :]
        g_low = g_out.astype(bf)
        self.gout[r, :] = g_low
        g_sq = (dot(g_low, self.up[...]) * slope).astype(bf)
        self.g_up[...] += dot(g_low, value, TN)
        self.g_down[...] += dot(low, g_sq, TN)
        self.gffn[r, :] = (g_out + dot(g_sq, self.down[...], NT)).astype(bf)

    def backward(self, j):
        dg = self.slope(j)
        for half in range(2):
            r = pl.ds(half * (self.n // 2), self.n // 2)
            g = (dot(self.gffn[r, :], self.wu(j), NT) * dg[r, :].astype(jnp.float32)).astype(jnp.bfloat16)
            dg[r, :] = g
            self.acc[r, :] += dot(g, self.wi(j))

    def last(self, i):
        r = rows_of(i)
        total = self.mid[r, :]
        g_n2 = self.acc[r, :]
        scale = lax.rsqrt(jnp.mean(total * total, axis=-1, keepdims=True) + NORM_EPS)
        self.g_gain[...] += jnp.sum(total * scale * g_n2, axis=0, keepdims=True)
        scaled = self.gain[...] * g_n2
        centre = jnp.mean(total * scaled, axis=-1, keepdims=True)
        g_mid = self.gout[r, :].astype(jnp.float32) + scale * scaled - total * (scale * scale * scale * centre)
        self.mid[r, :] = g_mid
        self.glow[r, :] = g_mid.astype(jnp.bfloat16)

    def projection(self, m):
        grad = dot(self.ctx[m], self.glow[...], TN).astype(jnp.bfloat16)
        self.ctx[m] = dot(self.glow[...], self.wo(m), NT).astype(jnp.bfloat16)
        return grad

    def adapter_all(self):
        self.g_down[...] = jnp.zeros_like(self.g_down)
        self.g_up[...] = jnp.zeros_like(self.g_up)
        each_of(self.n // RCH, self.adapter)

    def adapter_grads(self):
        other, pick = self.other, self.consts[1]
        down, up = self.factors()
        g_a, g_dl, g_dr = down.back(self.g_down[...])
        g_b, g_ur, g_ul = up.back(self.g_up[...])
        other[...] = jnp.zeros_like(other)
        for at, tall in ((ROW_DL, g_dl), (ROW_UR, g_ur)):
            other[at : at + 4, :] = tall[:, :128]
            other[at + 4 : at + 8, : tall.shape[1] - 128] = tall[:, 128:]
        for at, short in ((ROW_DR, g_dr), (ROW_UL, g_ul)):
            other[at : at + 4, :KA] = short
        for i in range(KRON):
            at = ROW_RULES + 4 * i
            other[at : at + 4, :KRON] = precise(g_a, pick[i], NT) + precise(pick[i], g_b, NT)


def middle_kernel(
    x_hbm, ctx_hbm, wo_hbm, wi_hbm, wu_hbm, cot_hbm, gain, lengths, rules, d_left, d_right, u_left, u_right,
    same, pick, fold, agree,
    res_hbm, gmid_hbm, gctx_hbm, go_hbm, gi_hbm, gu_hbm, other,
    down, up, g_down, g_up, g_gain, live, x, ctx, wo, wi, wu, cot, mid, n2, act, dg, acc, gffn, glow, sem, sems, out_sems,
):
    gain = gain[...].reshape(1, D)
    loads = [
        pltpu.make_async_copy(src, dst, sems.at[i])
        for i, (src, dst) in enumerate(
            ((x_hbm, x), (ctx_hbm, ctx), (wo_hbm, wo), (wi_hbm, wi), (wu_hbm, wu), (cot_hbm, cot))
        )
    ]
    for load in loads:
        load.start()
    def put_res(i, value):
        x[rows_of(i), :] = value

    layer = Layer(
        x_rows=lambda i: x[rows_of(i), :].astype(jnp.float32), cot_rows=lambda i: cot[rows_of(i), :].astype(jnp.float32),
        wo=lambda m: wo[m], wi=lambda j: wi[rows_of(j, FCH), :], wu=lambda j: wu[rows_of(j, FCH), :],
        chunk=FCH, ctx=ctx, gain=gain, lengths=lengths, rules=rules, sides=(d_left, d_right, u_left, u_right),
        consts=(same, pick, fold, agree), down=down, up=up, g_down=g_down, g_up=g_up, g_gain=g_gain, live=live, mid=mid,
        n2=n2, act=act, dg=dg, acc=acc, gffn=gffn, glow=glow, put_res=put_res, gout=cot, other=other,
        slope=lambda j: dg.at[:, rows_of(j, FCH)],
    )
    layer.prepare(lax.axis_index("mp"))
    for load in loads:
        load.wait()
    each_of(layer.n // RCH, layer.midway)
    acc[...] = jnp.zeros_like(acc)
    count = wi.shape[0] // FCH
    each_of(count, layer.forward)
    layer.adapter_all()
    acc[...] = jnp.zeros_like(acc)
    g_gain[...] = jnp.zeros_like(g_gain)

    def stores(j):
        f = rows_of(j, FCH)
        return [
            pltpu.make_async_copy(src.at[pl.ds(0, FCH), f], dst.at[f], sem.at[k, j])
            for k, (src, dst) in enumerate(((act, gu_hbm), (dg, gi_hbm)))
        ]

    def backward(j):
        f = rows_of(j, FCH)
        layer.backward(j)
        act[:FCH, f] = dot(act[:, f], gffn[...], TN).astype(jnp.bfloat16)
        dg[:FCH, f] = dot(dg[:, f], n2[...], TN).astype(jnp.bfloat16)
        for store in stores(j):
            store.start()

    each_of(count, backward)
    each_of(layer.n // RCH, layer.last)
    for m in range(4):
        gffn[CTX_PAD * m : CTX_PAD * (m + 1), :] = layer.projection(m)
    layer.adapter_grads()
    put_row(other, ROW_FFN, g_gain[...])
    copies = [
        pltpu.make_async_copy(src, dst, out_sems.at[k])
        for k, (src, dst) in enumerate(((x, res_hbm), (mid, gmid_hbm), (gffn, go_hbm), (ctx, gctx_hbm)))
    ]
    for copy in copies:
        copy.start()
    each_of(count, lambda j: [store.wait() for store in stores(j)])
    for copy in copies:
        copy.wait()


def middle(x, ctx, wo, wi, wu, cot, gain, lengths, factors):
    n, ff = x.shape[0], wi.shape[0]
    bf, f32 = jnp.bfloat16, jnp.float32
    hbm = pl.BlockSpec(memory_space=pl.ANY)
    vmem = pl.BlockSpec(memory_space=pltpu.VMEM)
    shape = jax.ShapeDtypeStruct
    return pl.pallas_call(
        middle_kernel,
        out_shape=[
            shape((n, D), bf),
            shape((n, D), f32),
            shape((4, n, CTX_PAD), bf),
            shape((4 * CTX_PAD, D), bf),
            shape((ff, D), bf),
            shape((ff, D), bf),
            shape((ROW_END, 128), f32),
        ],
        in_specs=[hbm] * 6 + [vmem] + [pl.BlockSpec(memory_space=pltpu.SMEM)] + [vmem] * 9,
        out_specs=[hbm] * 6 + [vmem],
        scratch_shapes=[
            pltpu.VMEM((D, ADAPT_PAD), bf),
            pltpu.VMEM((D, ADAPT_PAD), bf),
            pltpu.VMEM((D, ADAPT_PAD), f32),
            pltpu.VMEM((D, ADAPT_PAD), f32),
            pltpu.VMEM((1, D), f32),
            pltpu.VMEM((n, 1), f32),
            pltpu.VMEM((n, D), bf),
            pltpu.VMEM((4, n, CTX_PAD), bf),
            pltpu.VMEM((4, CTX_PAD, D), bf),
            pltpu.VMEM((ff, D), bf),
            pltpu.VMEM((ff, D), bf),
            pltpu.VMEM((n, D), bf),
            pltpu.VMEM((n, D), f32),
            pltpu.VMEM((n, D), bf),
            pltpu.VMEM((n, ff), bf),
            pltpu.VMEM((n, ff), bf),
            pltpu.VMEM((n, D), f32),
            pltpu.VMEM((n, D), bf),
            pltpu.VMEM((n, D), bf),
            pltpu.SemaphoreType.DMA((2, ff // FCH)),
            pltpu.SemaphoreType.DMA((6,)),
            pltpu.SemaphoreType.DMA((4,)),
        ],
        compiler_params=pltpu.CompilerParams(vmem_limit_bytes=63 * 2**20),
        name="middle",
    )(x, ctx, wo, wi, wu, cot, gain, lengths, *factors, *map(jnp.asarray, adapter_constants()))


FRONT = (
    "s:o s:q ex0 a:o0",
    "s:i a:q0 a:q1 a:q2",
    "c:q0 a:o1 c:q1 a:i0",
    "c:o0 a:q3 s:u n",
    "c:q2 a:o2 ex1 c:q3",
    "f:q a:u0 A A",
    "A c:o1 A a:i1",
    "a:o3 c:i0 A c:o2",
    "a:u1 A A A",
    "A A a:i2 c:o3",
    "A c:u0 A c:i1",
    "f:o O c:u1 a:u2",
    "c:i2 F0 a:i3 F1",
    "c:u2 a:u3 c:i3 F2",
    "c:u3 F3",
)


def front_order():
    plan, now = {"first": []}, "first"
    pieces = 0
    for step in " ".join(FRONT).split():
        if step == "A":
            now, pieces = ("A", pieces), pieces + 1
        elif step[0] in "OF":
            plan["before", step] = plan.pop("open", [])
            now = "open"
        else:
            plan.setdefault(now, []).append(step)
    return plan


def front_kernel(
    depth, group, tok, cot, w_qkv, w_o, w_in, w_out, choice, gain, gain_ffn, lengths, pos_table, onehot,
    rules, d_left, d_right, u_left, u_right, same, pick, fold, agree,
    tok_s, gq_hbm, normed_hbm, packed_hbm, out, mid_hbm, ctx_hbm, go_hbm, gi_hbm, gu_hbm, dg_hbm, pu_hbm, gffn_hbm, n2_hbm,
    gout_hbm, long_hbm, rest_hbm, other,
    wq, wo, wi, wu, mask, rows, x, y, gq, go, gi, gu, nrm, packed, ctx,
    down, up, g_down, g_up, live, mid, n2, act, dg, acc, gffn, res, sem, out_sems, local, *sems,
):
    p = Place(depth)
    bf = jnp.bfloat16
    p.greet(0)
    gain, gain_ffn = gain[...].reshape(1, D), gain_ffn[...].reshape(1, D)
    for h in range(3):
        wq[:, TILE * h : TILE * (h + 1)] = w_qkv[h, :, :TILE].astype(bf)
    values = [dot(w_qkv[h, :, TILE:].astype(bf), choice[DH * h : DH * (h + 1), :]) for h in range(3)]
    wq[:, 3 * TILE :] = sum(values).astype(bf)
    wo[...] = jnp.zeros_like(wo)
    wo[: w_o.shape[0], :] = w_o[...].astype(bf)
    wi[...] = w_in[...].astype(bf)
    wu[...] = w_out[...].astype(bf)
    arrays = {
        name: Gather(p, name == "q", shard, buf, *sems[3 * i : 3 * i + 3])
        for i, (name, shard, buf) in enumerate((("q", wq, gq), ("o", wo, go), ("i", wi, gi), ("u", wu, gu)))
    }
    first, second = Exchange(p, tok, x, *sems[12:15]), Exchange(p, cot, y, *sems[15:18])
    keep_x = pltpu.make_async_copy(x, tok_s, local.at[0])
    keep_n = pltpu.make_async_copy(nrm, normed_hbm, local.at[1])
    keep_q = pltpu.make_async_copy(gq, gq_hbm, local.at[2])
    quarter = RCH // SEG

    def float_rows(ref):
        return lambda i: ref[pl.ds(quarter * i, quarter)].reshape(RCH, D).astype(jnp.float32)

    def put_res(i, value):
        res[pl.ds(quarter * i, quarter)] = value.reshape(quarter, SEG, D)

    chunk_rows = 8 * wi.shape[0]
    layer = Layer(
        x_rows=float_rows(x), cot_rows=float_rows(y),
        wo=lambda m: go[m].reshape(CTX_PAD, D), wi=lambda j: gi[j].reshape(-1, D), wu=lambda j: gu[j].reshape(-1, D),
        chunk=chunk_rows, ctx=ctx, gain=gain_ffn, lengths=lengths, rules=rules, sides=(d_left, d_right, u_left, u_right),
        consts=(same, pick, fold, agree), down=down, up=up, g_down=g_down, g_up=g_up, live=live, mid=mid, n2=n2, act=act,
        dg=dg, acc=acc, gffn=gffn, put_res=put_res, gout=nrm, other=other,
    )
    third = Exchange(p, res, out, *sems[18:21])

    def norm(i):
        v = x[i].astype(jnp.float32)
        scale = lax.rsqrt(jnp.mean(v * v, axis=-1, keepdims=True) + NORM_EPS)
        nrm[rows_of(i, SEG), :] = (v * scale * gain[...]).astype(bf)

    def norms():
        first.finish()
        keep_x.start()
        each_of(x.shape[0], norm)
        keep_n.start()
        fill_mask(mask, lengths, p.m)
        fill_rows(rows, pos_table, onehot)
        layer.prepare(p.m)
        acc[...] = jnp.zeros_like(acc)

    def step(name):
        kind, rest = name[0], name[2:]
        if name == "n":
            norms()
        elif name in ("ex0", "ex1"):
            (first, second)[int(name[2])].start()
        elif kind == "s":
            arrays[rest].start()
        elif kind == "f":
            arrays[rest].finish()
        elif kind == "a":
            arrays[rest[0]].along(int(rest[1:]))
        elif kind == "c":
            arrays[rest[0]].across(int(rest[1:]))

    def steps(names):
        for name in names:
            step(name)

    plan = front_order()
    p.meet(0)
    steps(plan["first"])
    keep_q.start()

    def piece(m, place):
        at = sum(place) + place[0]
        for loop in range(4):
            names = plan.get(("A", 3 * loop + at))
            if names:
                pl.when(m == loop)(functools.partial(steps, names))

    def keeps(m):
        lanes = rows_of(m, D)
        return [
            pltpu.make_async_copy(packed.at[m], packed_hbm.at[m], local.at[3 + m]),
            pltpu.make_async_copy(act.at[:, lanes], long_hbm.at[m], local.at[7 + m]),
            pltpu.make_async_copy(dg.at[pl.ds(0, KEPT_REST), lanes], rest_hbm.at[m], local.at[11 + m]),
            pltpu.make_async_copy(ctx.at[m], ctx_hbm.at[m], local.at[15 + m]),
        ]

    def keep_probs(m, number, unit, h, probs):
        offset, length, q0, width = unit
        places = kept_at(offset, length, h)
        row, rows_kept, lane, _ = places[min(q0 // width, len(places) - 1)]
        lane = lane + (q0 if len(places) == 1 else 0)
        lanes = pl.ds(pl.multiple_of(D * m + lane, TILE), width)
        if row < KEPT_LONG:
            act[row : row + rows_kept, lanes] = probs
        else:
            dg[row - KEPT_LONG : row - KEPT_LONG + rows_kept, lanes] = probs

    def heads(m):
        w = gq[m // 2, m % 2].reshape(D, QKV_PAD)
        packed[m] = dot(nrm[...], w).astype(bf)
        keeps(m)[0].start()
        attend_group(
            packed.at[m], mask, rows[m], ctx.at[m], group, functools.partial(piece, m), functools.partial(keep_probs, m)
        )
        for copy in keeps(m)[1:]:
            copy.start()

    def stores(z):
        lanes = rows_of(z, chunk_rows)
        return [
            pltpu.make_async_copy(gi.at[z], gi_hbm.at[z], sem.at[0, z]),
            pltpu.make_async_copy(gu.at[z], gu_hbm.at[z], sem.at[1, z]),
            pltpu.make_async_copy(dg.at[:, lanes], dg_hbm.at[z], sem.at[2, z]),
        ]

    def weights(z):
        lanes = rows_of(z, chunk_rows)
        return pltpu.make_async_copy(act.at[pl.ds(0, chunk_rows), lanes], pu_hbm.at[z], sem.at[3, z])

    each_of(4, heads)
    steps(plan[("before", "O")])
    keep_o = pltpu.make_async_copy(go, go_hbm, out_sems.at[0])
    keep_o.start()
    each_of(layer.n // RCH, layer.midway)
    tail = [
        pltpu.make_async_copy(src, dst, out_sems.at[1 + k])
        for k, (src, dst) in enumerate(((mid, mid_hbm), (n2, n2_hbm), (nrm, gout_hbm), (gffn, gffn_hbm)))
    ]
    tail[0].start()
    tail[1].start()
    each_of(4, lambda m: [copy.wait() for copy in keeps(m)])

    def chunk(e):
        for k in range(depth):
            pl.when(e == k)(functools.partial(steps, plan[("before", f"F{k}")]))
        z = p.nearest(e)
        for name in "iu":
            arrays[name].finish_at(z)
        layer.forward(z)
        for copy in stores(z):
            copy.start()

    each_of(depth, chunk)
    second.finish()
    for copy in (keep_x, keep_n, keep_q):
        copy.wait()
    layer.adapter_all()
    third.start()
    tail[2].start()
    tail[3].start()

    def weights_out(k):
        z = p.order(k)
        lanes = rows_of(z, chunk_rows)
        act[:chunk_rows, lanes] = dot(act[:, lanes], gffn[...], TN).astype(bf)
        weights(z).start()

    for k in range(depth):
        weights_out(k)
    layer.adapter_grads()
    for copy in (keep_o, *tail):
        copy.wait()
    each_of(depth, lambda z: [copy.wait() for copy in (*stores(z), weights(z))])
    third.finish()
    for g in (*arrays.values(), first, second, third):
        g.drain()


def front(depth, group, tok, cot, shards, rows_of_shards, gains, lengths, pos_table, factors):
    hbm = pl.BlockSpec(memory_space=pl.ANY)
    vmem = pl.BlockSpec(memory_space=pltpu.VMEM)
    bf, f32 = jnp.bfloat16, jnp.float32
    shape = jax.ShapeDtypeStruct
    n = tok.shape[0] * SEG
    kept = [(rows, QKV_PAD if i == 0 else D) for i, rows in enumerate(rows_of_shards)]
    whole = [((2, 2, depth, 2) if i == 0 else (depth, 2, 2, 2)) + s for i, s in enumerate(kept)]
    ff = 8 * depth * kept[2][0]
    return pl.pallas_call(
        functools.partial(front_kernel, depth, group),
        out_shape=[
            shape(tok.shape, bf),
            shape(whole[0], bf),
            shape((n, D), bf),
            shape((4, n, QKV_PAD), bf),
            shape(tok.shape, bf),
            shape((n, D), f32),
            shape((4, n, CTX_PAD), bf),
            *[shape(s, bf) for s in whole[1:]],
            shape((depth, n, D), bf),
            shape((depth, D, D), bf),
            shape((n, D), bf),
            shape((n, D), bf),
            shape((n, D), bf),
            shape((4, KEPT_LONG, D), bf),
            shape((4, KEPT_REST, D), bf),
            shape((ROW_END, 128), f32),
        ],
        in_specs=[hbm] * 2 + [vmem] * 7 + [pl.BlockSpec(memory_space=pltpu.SMEM)] + [vmem] * 11,
        out_specs=[hbm] * 17 + [vmem],
        scratch_shapes=[pltpu.VMEM(s, bf) for s in kept]
        + [
            pltpu.VMEM((n, TILE), bf),
            pltpu.VMEM((4, 3, 512), f32),
            pltpu.VMEM(tok.shape, bf),
            pltpu.VMEM(tok.shape, bf),
            *[pltpu.VMEM(s, bf) for s in whole],
            pltpu.VMEM((n, D), bf),
            pltpu.VMEM((4, n, QKV_PAD), bf),
            pltpu.VMEM((4, n, CTX_PAD), bf),
            pltpu.VMEM((D, ADAPT_PAD), bf),
            pltpu.VMEM((D, ADAPT_PAD), bf),
            pltpu.VMEM((D, ADAPT_PAD), f32),
            pltpu.VMEM((D, ADAPT_PAD), f32),
            pltpu.VMEM((n, 1), f32),
            pltpu.VMEM((n, D), f32),
            pltpu.VMEM((n, D), bf),
            pltpu.VMEM((n, ff), bf),
            pltpu.VMEM((n, ff), bf),
            pltpu.VMEM((n, D), f32),
            pltpu.VMEM((n, D), bf),
            pltpu.VMEM(tok.shape, bf),
            pltpu.SemaphoreType.DMA((4, depth)),
            pltpu.SemaphoreType.DMA((5,)),
            pltpu.SemaphoreType.DMA((19,)),
        ]
        + Gather.sems(depth) * 4
        + Exchange.sems() * 3,
        compiler_params=pltpu.CompilerParams(
            collective_id=2, has_side_effects=True, vmem_limit_bytes=63 * 2**20
        ),
        name="front",
    )(
        tok, cot, *shards, jnp.asarray(value_choice(group), bf), *gains, lengths, pos_table,
        jnp.asarray(offset_onehot()), *factors, *map(jnp.asarray, adapter_constants()),
    )


BACK = (
    "Su0 Su2 K Su3",
    "K Hu0 Si0 K",
    "Hu2 K Hu3 K",
    "K Qu0 Su1 K",
    "Si2 Qu2 K K",
    "Hi0 K So0 So1",
    "K So2 Si1 K",
    "Qu3 K K K",
    "Hu1 So3 K K",
    "Si3 Ho2 K K",
    "Fu0 Qi0 Ho0 Hi1",
    "K K Hi2 K",
    "Qo2 K K K",
    "K Qu1 K Fu2",
    "Qo0 K K Qi2",
    "Hi3 K Fu1 Fi0",
    "K K K K",
    "Sq0 Qi3 Fi3 Sq2",
    "Sq3 Ho1 Ho3 Fo0",
    "Hq0 Qi1 N Fu3",
    "Qo3 Fi2 Qo1 TB",
    "Sq1 Fo2 Hq2 Cu",
    "Qq0 Fo1 T0 Hq1",
    "Eu Hq3 Fi1 Fo3",
    "T1 Co Qq2 Qq1",
    "x1 Fq0 T2 Qq3",
    "Eo Ci Fq2 Fq3",
    "Fq1 Ei Cq T3",
    "T4 Eq",
)


def back_order():
    plan, pieces = {}, 0
    for step in " ".join(BACK).split():
        if step in "KN":
            pieces += 1
        else:
            plan.setdefault(pieces, []).append(step)
    return plan


PIECES = 6


def back_kernel(
    depth, bits, group,
    tok_hbm, gq_hbm, nrm_hbm, packed_hbm, mid_hbm, ctx_hbm, go_hbm, gi_hbm, gu_hbm, dg_hbm, gffn_hbm, n2_hbm, gout_hbm,
    long_hbm, rest_hbm, pu, gain, gain_ffn, onehot, other,
    oq, oo, oi, ou, small, gtok,
    wu, wi, dg, acc, mid, gffn, nrm, gout, x, ctx, go, kept, g_gain, sums_s, mine_u, sem_u, local, chunk_sem, gq_sem, *scr,
):
    p = Place(depth)
    n = depth
    bf = jnp.bfloat16
    gain, gain_ffn = gain[...].reshape(1, D), gain_ffn[...].reshape(1, D)
    width = pl.ds(0, QKV_PAD)
    arrays = {
        "u": Scatter(p, False, pu, ou, *scr[0:6], mine_u, sem_u),
        "i": Scatter(p, False, wi, oi, *scr[6:12]),
        "o": Scatter(p, False, go, oo, *scr[12:18]),
        "q": Scatter(
            p, True, wu, oq, *scr[18:24],
            region=lambda core, z: wu.at[:, core, z // 2, z % 2, :, :, width],
        ),
    }
    row_g = Exchange(p, x, gtok, *scr[24:27])
    total = Sum(p, bits, small, *scr[27:30])
    layer = Layer(
        wo=lambda m: go[m].reshape(CTX_PAD, D), wi=lambda z: wi[z].reshape(-1, D),
        wu=lambda z: wu[z // 2, z % 2].reshape(-1, D), slope=lambda z: dg.at[z], ctx=ctx, gain=gain_ffn, g_gain=g_gain,
        mid=mid, n2=nrm, acc=acc, gffn=gffn, glow=gffn, gout=gout,
    )

    def load(src, dst, k):
        return pltpu.make_async_copy(src, dst, local.at[k])

    early = [
        load(src, dst, k)
        for k, (src, dst) in enumerate(
            ((gffn_hbm, gffn), (n2_hbm, nrm), (mid_hbm, mid), (gout_hbm, gout), (ctx_hbm, ctx), (go_hbm, go), (tok_hbm, x))
        )
    ]

    def chunk_in(k):
        z = p.order(k)
        pairs = ((dg_hbm.at[z], dg.at[z]), (gu_hbm.at[z], wu.at[z // 2, z % 2]), (gi_hbm.at[z], wi.at[z]))
        return [pltpu.make_async_copy(src, dst, chunk_sem.at[j, k]) for j, (src, dst) in enumerate(pairs)]

    def packed_in(m):
        return load(packed_hbm.at[m], dg.at[m, :, width], 8 + m)

    def gq_in(m, z):
        y, c = m // 2, m % 2
        return pltpu.make_async_copy(
            gq_hbm.at[y, c, z], wu.at[y, c, z // 2, z % 2, :, :, width], gq_sem.at[m, z]
        )

    def kept_in(m):
        slot = m % 2
        return [
            load(long_hbm.at[m], kept.at[slot, pl.ds(0, KEPT_LONG)], 12 + slot),
            load(rest_hbm.at[m], kept.at[slot, pl.ds(KEPT_LONG, KEPT_REST)], 14 + slot),
        ]

    todo = total.steps()

    def steps(names):
        for name in names:
            if name == "x1":
                row_g.start()
            elif name[0] == "T":
                todo.pop(0)()
            else:
                array = arrays[name[1]]
                if name[0] in "CE":
                    (array.collect if name[0] == "C" else array.finish)()
                else:
                    k = int(name[2:])
                    {"S": array.start, "H": array.to_half, "Q": array.to_quarter, "F": array.forward}[name[0]](k)
                    if name[0] == "Q":
                        array.origin(k)

    plan = back_order()

    def place(k):
        steps(plan.pop(k, ()))

    ahead_of = {1: chunk_in(2), 2: early[2:3], 3: chunk_in(3), 4: early[3:4], 5: early[4:6], 6: kept_in(0), 7: early[6:]}

    def load_ahead(k):
        for copy in ahead_of.get(k, ()):
            copy.start()

    p.greet(bits)
    for copy in (early[0], *chunk_in(0), early[1]):
        copy.start()
    small[...] = jnp.zeros_like(small)
    small[ROW_OTHER:, :] = other[...]
    acc[...] = jnp.zeros_like(acc)
    g_gain[...] = jnp.zeros_like(g_gain)
    p.meet(bits)
    place(0)
    for copy in chunk_in(1):
        copy.start()
    early[0].wait()
    for k in range(n):
        z = p.order(k)
        for copy in chunk_in(k):
            copy.wait()
        load_ahead(2 * k + 1)
        layer.backward(z)
        place(2 * k + 1)
        load_ahead(2 * k + 2)
        if k == 0:
            early[1].wait()
        wi[z] = dot(dg[z], nrm[...], TN).astype(bf).reshape(wi.shape[1:])
        place(2 * k + 2)
    for m in range(4):
        packed_in(m).start()
        for z in range(n):
            gq_in(m, z).start()
    renew = load(nrm_hbm, nrm, 7)
    renew.start()
    for copy in early[2:]:
        copy.wait()
    each_of(layer.n // RCH, layer.last)
    place(2 * n + 1)

    def project(m):
        go[m] = layer.projection(m).reshape(go.shape[1:])

    each_of(4, project)
    acc[...] = jnp.zeros_like(acc)
    place(2 * n + 2)
    renew.wait()
    for m in range(4):
        packed_in(m).wait()
        for z in range(n):
            gq_in(m, z).wait()

    def piece(m, j):
        for loop in range(4):
            names = plan.get(2 * n + 2 + PIECES * loop + j + 1)
            if names:
                pl.when(m == loop)(functools.partial(steps, names))

    def tick(m, at):
        number, head = at
        if number == 0:
            piece(m, head)
        elif head == 8:
            piece(m, 3)

    def heads(m):
        slot, y, c = m % 2, m // 2, m % 2
        for copy in kept_in(m):
            copy.wait()

        def ahead():
            for copy in kept_in(m + 1):
                copy.start()

        pl.when(m < 3)(ahead)
        packed = dg.at[m, :, width]
        attend_group_back(packed, Kept(kept.at[slot]), ctx.at[m], packed, sums_s.at[m], group, functools.partial(tick, m))
        whole = (Ellipsis, slice(0, QKV_PAD))
        acc[...] += dot(packed[...], wu[y, c][whole].reshape(D, QKV_PAD), NT)
        piece(m, 4)
        wu[y, c, :, :, :, :, 0:QKV_PAD] = dot(nrm[...], packed[...], TN).astype(bf).reshape(*wu.shape[2:6], QKV_PAD)
        piece(m, 5)

    each_of(4, heads)
    small[ROW_TABLE : ROW_TABLE + 16, :] = jnp.zeros((16, 128), jnp.float32)
    for m in range(4):
        small[ROW_TABLE + 3 * m : ROW_TABLE + 3 * m + 3, :] = precise(sums_s[m], onehot[...])
    put_row(small, ROW_OTHER + ROW_FFN, g_gain[...])

    def last(s, g_gain):
        r = rows_of(s, SEG)
        v = x[s].astype(jnp.float32)
        g_n1 = acc[r, :]
        scale = lax.rsqrt(jnp.mean(v * v, axis=-1, keepdims=True) + NORM_EPS)
        scaled = gain * g_n1
        centre = jnp.mean(v * scaled, axis=-1, keepdims=True)
        x[s] = (mid[r, :] + scale * scaled - v * (scale * scale * scale * centre)).astype(bf)
        return g_gain + jnp.sum(v * scale * g_n1, axis=0, keepdims=True)

    put_row(small, ROW_GAIN, lax.fori_loop(0, x.shape[0], last, jnp.zeros((1, D), jnp.float32)))
    place(2 * n + 2 + 4 * PIECES + 1)
    row_g.finish()
    for g in (*arrays.values(), row_g, total):
        g.drain()


def back(depth, bits, group, kept, ffn, pu, gains, onehot, other):
    hbm = pl.BlockSpec(memory_space=pl.ANY)
    vmem = pl.BlockSpec(memory_space=pltpu.VMEM)
    bf, f32 = jnp.bfloat16, jnp.float32
    shape = jax.ShapeDtypeStruct
    tok, gq = kept[:2]
    mid, ctx, go, gi = ffn[:4]
    n = mid.shape[0]
    small_rows = ROW_OTHER + other.shape[0]
    outs = [shape(s.shape[4:], f32) for s in (gq, go, gi, gi)]
    outs += [shape((small_rows, 128), f32), shape(tok.shape, bf)]
    dma = pltpu.SemaphoreType.DMA
    scratch = [
        pltpu.VMEM((2, 2, 2, 2, 2, *gi.shape[4:]), bf),
        pltpu.VMEM(gi.shape, bf),
        pltpu.VMEM((depth, n, D), bf),
        pltpu.VMEM((n, D), f32),
        pltpu.VMEM((n, D), f32),
        pltpu.VMEM((n, D), bf),
        pltpu.VMEM((n, D), bf),
        pltpu.VMEM((n, D), bf),
        pltpu.VMEM(tok.shape, bf),
        pltpu.VMEM(ctx.shape, bf),
        pltpu.VMEM(go.shape, bf),
        pltpu.VMEM((2, KEPT_LONG + KEPT_REST, D), bf),
        pltpu.VMEM((1, D), f32),
        pltpu.VMEM((4, 3, 768), f32),
        pltpu.VMEM((depth, 2, 2) + gi.shape[4:], bf),
        dma((depth,)),
        dma((16,)),
        dma((3, depth)),
        dma((4, depth)),
    ]
    for s in (gi, gi, go, gq):
        scratch += Scatter.scratch(depth, *s.shape[4:])
    scratch += Exchange.sems() + Sum.scratch(bits, small_rows)
    return pl.pallas_call(
        functools.partial(back_kernel, depth, bits, group),
        out_shape=outs,
        in_specs=[hbm] * 16 + [vmem] * 4,
        out_specs=[vmem] * 5 + [hbm],
        scratch_shapes=scratch,
        compiler_params=pltpu.CompilerParams(
            collective_id=3, has_side_effects=True, vmem_limit_bytes=63 * 2**20
        ),
        name="back",
    )(*kept, *ffn, pu.reshape(gi.shape), *gains, onehot, other)


def finish_kernel(
    q, o, i, u, small, choice, out_hbm, gtok_hbm,
    gq, go, gi, gu, g_attn, g_ffn, g_table, g_rules, g_dl, g_dr, g_ul, g_ur, out, gtok, held, sems,
):
    rows_in = [pltpu.make_async_copy(src, held.at[k], sems.at[k]) for k, src in enumerate((out_hbm, gtok_hbm))]
    rows_out = [pltpu.make_async_copy(held.at[k], dst, sems.at[2 + k]) for k, dst in enumerate((out, gtok))]
    for copy in rows_in:
        copy.start()
    left = q[: gq.shape[1], 3 * TILE :]
    parts = []
    for _ in range(3):
        parts.append(left.astype(jnp.bfloat16))
        left = left - parts[-1].astype(jnp.float32)
    for h in range(3):
        gq[h, :, :TILE] = q[: gq.shape[1], TILE * h : TILE * (h + 1)]
        chosen = choice[DH * h : DH * (h + 1), :]
        gq[h, :, TILE:] = sum(dot(part, chosen, NT) for part in parts)
    for copy_in, copy_out in zip(rows_in, rows_out):
        copy_in.wait()
        copy_out.start()
    go[...] = o[: go.shape[0], :]
    gi[...] = i[: gi.shape[0], :]
    gu[...] = u[: gu.shape[0], :]
    for k in range(D // 128):
        lanes = slice(128 * k, 128 * (k + 1))
        g_attn[lanes] = small[ROW_GAIN + k, :]
        g_ffn[lanes] = small[ROW_OTHER + ROW_FFN + k, :]
    g_table[...] = small[ROW_TABLE : ROW_TABLE + g_table.shape[0], :NB]
    for i in range(KRON):
        at = ROW_OTHER + ROW_RULES + 4 * i
        g_rules[i] = small[at : at + 4, :KRON]
    for ref, at in ((g_dl, ROW_OTHER + ROW_DL), (g_ur, ROW_OTHER + ROW_UR)):
        ref[:, :128] = small[at : at + 4, :]
        ref[:, 128:] = small[at + 4 : at + 8, : ref.shape[1] - 128]
    for ref, at in ((g_dr, ROW_OTHER + ROW_DR), (g_ul, ROW_OTHER + ROW_UL)):
        ref[...] = small[at : at + 4, :KA]
    for copy in rows_out:
        copy.wait()


def finish(q, o, i, u, small, out, gtok, group, shapes):
    vmem = pl.BlockSpec(memory_space=pltpu.VMEM)
    hbm = pl.BlockSpec(memory_space=pl.ANY)
    return pl.pallas_call(
        finish_kernel,
        out_shape=[jax.ShapeDtypeStruct(s, jnp.float32) for s in shapes]
        + [jax.ShapeDtypeStruct(a.shape, a.dtype) for a in (out, gtok)],
        in_specs=[vmem] * 6 + [hbm] * 2,
        out_specs=[vmem] * 12 + [hbm] * 2,
        scratch_shapes=[pltpu.VMEM((2, *out.shape), out.dtype), pltpu.SemaphoreType.DMA((4,))],
        compiler_params=pltpu.CompilerParams(vmem_limit_bytes=60 * 2**20),
        name="finish",
    )(q, o, i, u, small, jnp.asarray(value_choice(group), jnp.bfloat16), out, gtok)


def round_up(n, m):
    return -(-n // m) * m


def pad_rows(a, rows):
    return jnp.pad(a, ((0, rows - a.shape[0]), (0, 0)))


HEADS = 12


def local(
    tokens,
    lengths,
    cotangent,
    w_qkv,
    w_o,
    w_in,
    w_out,
    gain_attn,
    gain_ffn,
    pos_table,
    phm_rules,
    down_left,
    down_right,
    up_left,
    up_right,
):
    dp_count, mp_count = lax.axis_size("dp"), lax.axis_size("mp")
    depth = dp_count // 2
    bits = dp_count.bit_length() - 1
    devices = dp_count * mp_count
    member = lax.axis_index("mp")
    tok_rows = tokens.shape[0]
    seg_count = tok_rows // SEG
    o_rows, in_rows, q_rows = w_o.shape[0], w_in.shape[1], w_qkv.shape[0]
    bf = jnp.bfloat16
    group = o_rows if o_rows % 24 == 0 and round_up(o_rows, 16) * 3 == o_rows * 4 else 3 * DH
    rows_of_shards = [round_up(r, 16) for r in (q_rows, o_rows, in_rows, in_rows)]
    tok_in, cot_in = tokens.reshape(seg_count, SEG, D), cotangent.reshape(seg_count, SEG, D)
    merged = depth == 4 and group == o_rows and rows_of_shards[0] == q_rows and rows_of_shards[2] == in_rows
    factors = (phm_rules, down_left, down_right, up_left, up_right)
    gains = (gain_attn, gain_ffn)
    if merged:
        shards = (w_qkv.transpose(1, 0, 2), w_o, w_in.T, w_out)
        *kept, out, mid, ctx, go, gi, gu, dg, pu, gffn, n2, gout, long, rest, other = front(
            depth, group, tok_in, cot_in, shards, rows_of_shards, gains, lengths, pos_table.T, factors
        )
    else:
        shards = (head_columns(w_qkv.astype(bf), group), w_o.astype(bf), w_in.astype(bf).T, w_out.astype(bf))
        shards = [pad_rows(s, r) for s, r in zip(shards, rows_of_shards)]
        tok_s, cot_s, gq, go, gi, gu = gather_all(depth, tok_in, cot_in, shards)
    def plain(g, rows):
        return g.reshape(devices, g.shape[-2], D)[:, :rows].reshape(devices * rows, D)

    def slots(g, rows):
        padded = jnp.pad(g.reshape(devices, rows, D), ((0, 0), (0, round_up(rows, 16) - rows), (0, 0)))
        return padded.reshape(depth, 2, 2, 2, padded.shape[1], D)

    if not merged:
        tokens_s = tok_s.reshape(tok_rows, D)
        if group == o_rows:
            dense_o = go.reshape(mp_count, CTX_PAD, D)
        else:
            dense_o = plain(go, o_rows).reshape(mp_count, 3 * DH, D)
            dense_o = jnp.pad(dense_o, ((0, 0), (0, CTX_PAD - 3 * DH), (0, 0)))
        qkv_full = gq.reshape(mp_count, dp_count, rows_of_shards[0], QKV_PAD)[:, :, :q_rows]
        qkv_full = qkv_full.reshape(mp_count, D, QKV_PAD)
        live = jnp.concatenate(
            [jnp.arange(length) < own_length(lengths, member, i) for i, (_, length) in enumerate(SPANS)]
        )
        mask = key_mask(live)
        rows = jnp.einsum("bh,br->hr", pos_table, offset_onehot(), precision=FULL_PRECISION).reshape(mp_count, 3, 512)
        normed_attn, packed, context = attention(tokens_s, gains[0].reshape(1, D), qkv_full, mask, rows, group)
        result, grad_mid, grad_context, grad_w_o, grad_w_in, grad_w_out, other = middle(
            tokens_s,
            context,
            dense_o,
            plain(gi, in_rows),
            plain(gu, in_rows),
            cot_s.reshape(tok_rows, D),
            gains[1],
            lengths,
            factors,
        )
    onehot = jnp.asarray(np.pad(table_onehot(), ((0, 0), (0, 128 - NB))))
    if merged:
        oq, oo, oi, ou, summed, gtok = back(
            depth, bits, group, kept, (mid, ctx, go, gi, gu, dg, gffn, n2, gout, long, rest), pu, gains, onehot, other
        )
    else:
        if group == o_rows:
            part_o = grad_w_o.reshape(depth, 2, 2, 2, round_up(o_rows, 16), D)
        else:
            part_o = slots(grad_w_o.reshape(mp_count, CTX_PAD, D)[:, : 3 * DH].reshape(D, D), o_rows)
        result = result.reshape(seg_count, SEG, D)
        packed_grads, sums = attention_back(packed, grad_context, mask, rows, group)
        table_grad = jnp.dot(sums.reshape(HEADS, 768), onehot, precision=FULL_PRECISION)
        grad_w_qkv = jnp.einsum("td,mtc->mdc", normed_attn, packed_grads, preferred_element_type=jnp.float32).astype(bf)
        grad_n1 = jnp.einsum("mtc,mdc->td", packed_grads, qkv_full, preferred_element_type=jnp.float32)
        _, norm_back_attn = jax.vjp(normed, tokens_s.astype(jnp.float32), gain_attn)
        grad_x_part, grad_gain_attn = norm_back_attn(grad_n1)
        grad_tokens = (grad_mid + grad_x_part).astype(bf)
        small = jnp.concatenate([
            jnp.pad(grad_gain_attn.reshape(D // 128, 128), ((0, ROW_TABLE - D // 128), (0, 0))),
            jnp.pad(table_grad, ((0, ROW_OTHER - ROW_TABLE - HEADS), (0, 0))),
            other,
        ])
        part_q = grad_w_qkv.reshape(mp_count, dp_count, q_rows, QKV_PAD)
        part_q = jnp.pad(part_q, ((0, 0), (0, 0), (0, rows_of_shards[0] - q_rows), (0, 0)))
        part_q = part_q.reshape(2, 2, depth, 2, rows_of_shards[0], QKV_PAD)
        oq, oo, oi, ou, summed, out, gtok = scatter_all(
            depth, bits, (part_q, part_o, slots(grad_w_in, in_rows), slots(grad_w_out, in_rows)), small, result, grad_tokens.reshape(seg_count, SEG, D)
        )
    shapes = (
        (3, q_rows, 3 * DH), w_o.shape, w_in.shape[::-1], w_out.shape, (D,), (D,), pos_table.shape[::-1],
        phm_rules.shape, down_left.shape, down_right.shape, up_left.shape, up_right.shape,
    )
    g_qkv, g_o, g_in, g_out, g_attn, g_ffn, g_table, *smalls, out, gtok = finish(
        oq, oo, oi, ou, summed, out, gtok, group, shapes
    )
    return (
        out.reshape(tok_rows, D),
        gtok.reshape(tok_rows, D),
        g_qkv.transpose(1, 0, 2),
        g_o,
        g_in.T,
        g_out,
        g_attn,
        g_ffn,
        g_table.T,
        *smalls,
    )


def solution(mesh):
    return jax.shard_map(
        local,
        mesh=mesh,
        in_specs=(
            P(("dp", "mp"), None),
            P("dp"),
            P(("dp", "mp"), None),
            P("dp", "mp", None),
            P(("dp", "mp"), None),
            P(None, ("dp", "mp")),
            P(("dp", "mp"), None),
            P(),
            P(),
            P(),
            P(),
            P(),
            P(),
            P(),
            P(),
        ),
        out_specs=(
            P(("dp", "mp"), None),
            P(("dp", "mp"), None),
            P("dp", "mp", None),
            P(("dp", "mp"), None),
            P(None, ("dp", "mp")),
            P(("dp", "mp"), None),
            P(),
            P(),
            P(),
            P(),
            P(),
            P(),
            P(),
            P(),
        ),
        check_vma=False,
    )
```

```python
import functools
import itertools

import jax
import jax.experimental.pallas as pl
import jax.experimental.pallas.tpu as pltpu
import jax.numpy as jnp
import numpy as np
from jax import lax
from jax.sharding import PartitionSpec as P

D = 768
DH = 64
NB = 32
MAXDIST = 128
ADAPT = 48
KRON = 4
LEN_LONG = 512
LEN_MID = 256
LEN_SHORT = 128
SEG = 128


NORM_EPS = 1e-06
FULL_PRECISION = lax.Precision.HIGHEST


def rel_buckets(length):
    offsets = np.arange(-(length - 1), length)
    half_count = NB // 2
    exact_count = half_count // 2
    upward = (offsets > 0).astype(np.int64) * half_count
    distance = np.abs(offsets)
    scaled = (
        np.log(np.maximum(distance, 1) / exact_count)
        / np.log(MAXDIST / exact_count)
        * (half_count - exact_count)
    )
    far_bucket = np.minimum(
        exact_count + np.floor(np.maximum(scaled, 0.0)).astype(np.int64), half_count - 1
    )
    return upward + np.where(distance < exact_count, distance, far_bucket)


def normed(values, gain):
    return values * lax.rsqrt(jnp.mean(values * values, axis=-1, keepdims=True) + NORM_EPS) * gain


MESH = pl.DeviceIdType.MESH


class Place:
    def __init__(self, depth):
        d, m = lax.axis_index("dp"), lax.axis_index("mp")
        self.depth = depth
        self.d, self.m = d, m
        self.z, self.x, self.y, self.c = d // 2, d % 2, m // 2, m % 2
        dx, dy, c = 1 - 2 * self.x, 2 - 4 * self.y, self.c
        self.sib = (d, m + 1 - 2 * c)
        self.right, self.left = (d + 2, m), (d - 2, m)
        self.mp_peer = ((d, m + 1 - 2 * c), (d, m + dy), (d, 3 - m))
        self.xn, self.yn = (d + dx, m), (d, m + dy)
        self.a_nbr = (d + (1 - c) * dx, m + c * dy)
        self.b_nbr = (d + c * dx, m + (1 - c) * dy)
        self.a = self.x + c * (self.y - self.x)
        self.b = self.y + c * (self.x - self.y)

    def by_core(self, run):
        for core in (0, 1):
            pl.when(self.c == core)(functools.partial(run, core))

    def order(self, k):
        n = self.depth
        base = k // 2 if k % 2 == 0 else n - 1 - k // 2
        near = 1 - jnp.minimum(self.z // max(n // 2, 1), 1)
        return base + near * (n - 1 - 2 * base)

    def nearest(self, e):
        n, z = self.depth, self.z
        ahead = 1 - 2 * (z // ((n + 1) // 2))
        short = jnp.minimum(z, n - 1 - z)
        around = (1 - 2 * (e % 2)) * ((e + 1) // 2)
        return z + ahead * jnp.where(e <= 2 * short, around, e - short)

    def flip(self, bit):
        step = 1 << bit
        return (self.d + step * (1 - 2 * ((self.d // step) % 2)), self.m)

    def barrier(self, bits):
        self.greet(bits)
        self.meet(bits)

    def pals(self, bits):
        return [*self.mp_peer, self.xn] + [self.flip(bit) for bit in range(2, bits)]

    def greet(self, bits):
        sem = pltpu.get_barrier_semaphore()

        def greet(dev):
            pl.semaphore_signal(sem, 1, device_id=dev, device_id_type=MESH)

        for dev in self.pals(bits):
            greet(dev)
        pl.when(self.z > 0)(lambda: greet(self.left))
        pl.when(self.z < self.depth - 1)(lambda: greet(self.right))

    def meet(self, bits):
        ends = jnp.minimum(self.z, 1) + jnp.minimum(self.depth - 1 - self.z, 1)
        pl.semaphore_wait(pltpu.get_barrier_semaphore(), len(self.pals(bits)) + ends)


def remote(src, dst, send, recv, dev):
    return pltpu.make_async_remote_copy(
        src_ref=src, dst_ref=dst, send_sem=send, recv_sem=recv, device_id=dev, device_id_type=MESH
    )


def slot_of(buf, by_head, p):
    return buf.at[p.y, p.c, p.z, p.x] if by_head else buf.at[p.z, p.x, p.y, p.c]


def pair_of(buf, by_head, core, b, z):
    if by_head:
        return buf.at[b, 0, z] if core == 0 else buf.at[:, 1, z, b]
    return buf.at[z, :, b, 0] if core == 0 else buf.at[z, b, :, 1]


class Gather:
    def __init__(self, p, by_head, shard, buf, send, recv, own):
        self.p, self.by_head, self.shard, self.buf = p, by_head, shard, buf
        self.send, self.recv, self.own = send, recv, own
        n = p.depth
        self.first = remote(shard, slot_of(buf, by_head, p), send.at[5 * n], recv.at[4 * n], p.a_nbr)
        self.keep = pltpu.make_async_copy(shard, slot_of(buf, by_head, p), own)

    @staticmethod
    def sems(n):
        return [
            pltpu.SemaphoreType.DMA((5 * n + 1,)),
            pltpu.SemaphoreType.DMA((4 * n + 1,)),
            pltpu.SemaphoreType.DMA,
        ]

    def _copy(self, core, b, z, kind):
        p, n = self.p, self.p.depth
        ref = pair_of(self.buf, self.by_head, core, b, z)
        if kind == "right":
            return remote(ref, ref, self.send.at[z], self.recv.at[z], p.right)
        if kind == "left":
            return remote(ref, ref, self.send.at[n + z], self.recv.at[z], p.left)
        return remote(ref, ref, self.send.at[2 * n + z], self.recv.at[n + z], p.b_nbr)

    def _sib(self, core, b, z):
        n = self.p.depth
        ref = pair_of(self.buf, self.by_head, core, b, z)
        return remote(ref, ref, self.send.at[3 * n + b * n + z], self.recv.at[2 * n + b * n + z], self.p.sib)

    def start(self):
        self.keep.start()
        self.first.start()

    def _spread(self, core, z, right, left):
        p = self.p
        if right:
            pl.when(p.z < p.depth - 1)(lambda: self._copy(core, p.b, z, "right").start())
        if left:
            pl.when(p.z > 0)(lambda: self._copy(core, p.b, z, "left").start())
        self._copy(core, p.b, z, "b").start()
        self._sib(core, p.b, z).start()

    def along(self, k):
        p = self.p
        if isinstance(k, int) and k == 0:
            self.keep.wait()
            self.first.wait_recv()
            p.by_core(lambda core: self._spread(core, p.z, True, True))
            return

        def from_left(core):
            self._copy(core, p.b, p.z - k, "right").wait_recv()
            self._spread(core, p.z - k, True, False)

        def from_right(core):
            self._copy(core, p.b, p.z + k, "left").wait_recv()
            self._spread(core, p.z + k, False, True)

        pl.when(p.z - k >= 0)(lambda: p.by_core(from_left))
        pl.when(p.z + k < p.depth)(lambda: p.by_core(from_right))

    def across(self, k):
        p = self.p

        def one(z, core):
            self._copy(core, 1 - p.b, z, "b").wait_recv()
            self._sib(core, 1 - p.b, z).start()

        pl.when(p.z - k >= 0)(lambda: p.by_core(lambda core: one(p.z - k, core)))
        if not (isinstance(k, int) and k == 0):
            pl.when(p.z + k < p.depth)(lambda: p.by_core(lambda core: one(p.z + k, core)))

    def finish_at(self, z):
        def one(core):
            for b in (0, 1):
                self._sib(1 - core, b, z).wait_recv()

        self.p.by_core(one)

    def finish(self):
        each_of(self.p.depth, self.finish_at)

    def drain(self):
        p, n = self.p, self.p.depth
        self.first.wait_send()

        def each(z, carry):
            def one(core):
                pl.when(jnp.logical_and(p.z < n - 1, z <= p.z))(
                    lambda: self._copy(core, p.b, z, "right").wait_send()
                )
                pl.when(jnp.logical_and(p.z > 0, z >= p.z))(
                    lambda: self._copy(core, p.b, z, "left").wait_send()
                )
                self._copy(core, p.b, z, "b").wait_send()
                for b in (0, 1):
                    self._sib(core, b, z).wait_send()

            p.by_core(one)
            return carry

        lax.fori_loop(0, n, each, 0)


class Exchange:
    def __init__(self, p, src, dst, send, recv, own):
        m = p.m
        c, other = m % 2, 1 - m % 2
        self.local = [
            pltpu.make_async_copy(src.at[m], dst.at[m], own.at[0]),
            pltpu.make_async_copy(src.at[4 + c], dst.at[4 + c], own.at[1]),
            pltpu.make_async_copy(src.at[pl.ds(6, 2)], dst.at[pl.ds(6, 2)], own.at[2]),
        ]
        self.out = [
            remote(src.at[dev[1]], dst.at[m], send.at[j], recv.at[j], dev)
            for j, dev in enumerate(p.mp_peer)
        ] + [remote(src.at[4 + other], dst.at[4 + c], send.at[3], recv.at[3], p.sib)]

    @staticmethod
    def sems():
        return [
            pltpu.SemaphoreType.DMA((4,)),
            pltpu.SemaphoreType.DMA((4,)),
            pltpu.SemaphoreType.DMA((3,)),
        ]

    def start(self):
        for copy in self.out + self.local:
            copy.start()

    def finish(self):
        for copy in self.local:
            copy.wait()
        for copy in self.out:
            copy.wait_recv()

    def drain(self):
        for copy in self.out:
            copy.wait_send()


def add_rows(dst, src, rows):
    step = 32 if rows % 32 == 0 else 16

    def one(i, carry):
        at = pl.ds(pl.multiple_of(i * step, step), step)
        total = dst[at, :].astype(jnp.float32) + src[at, :].astype(jnp.float32)
        dst[at, :] = total.astype(dst.dtype)
        return carry

    lax.fori_loop(0, rows // step, one, 0)


class Scatter:
    def __init__(self, p, by_head, part, total, half, quarter, arrive, last, send, recv, mine=None, mine_sem=None, region=None):
        self.p, self.by_head, self.part, self.total = p, by_head, part, total
        self.mine, self.mine_sem, self.region = mine, mine_sem, region
        self.half, self.quarter, self.arrive, self.last = half, quarter, arrive, last
        self.send, self.recv = send, recv
        self.rows = part.shape[-2]

    @staticmethod
    def scratch(n, rows, cols, dtype=jnp.bfloat16):
        return [
            pltpu.VMEM((n, 2, 2, rows, cols), dtype),
            pltpu.VMEM((n, 2, rows, cols), dtype),
            pltpu.VMEM((n + 1, 2, rows, cols), dtype),
            pltpu.VMEM((rows, cols), dtype),
            pltpu.SemaphoreType.DMA((3 * n + 1,)),
            pltpu.SemaphoreType.DMA((3 * n + 2,)),
        ]

    def order(self, k):
        return self.p.order(k)

    def _region(self, core, z):
        if self.region is not None:
            return self.region(core, z)
        return self.part.at[:, core, z] if self.by_head else self.part.at[z, :, :, core]

    def _half_pair(self, core, b, z):
        over_first = (core == 0) != self.by_head
        return self.half.at[z, :, b] if over_first else self.half.at[z, b]

    def _sib(self, core, z):
        return remote(
            self._region(1 - core, z), self.half.at[z], self.send.at[z], self.recv.at[z], self.p.sib
        )

    def _b(self, core, z):
        n, p = self.p.depth, self.p
        return remote(
            self._half_pair(core, 1 - p.b, z), self.quarter.at[z], self.send.at[n + z], self.recv.at[n + z], p.b_nbr
        )

    def _right(self, z):
        n, p = self.p.depth, self.p
        return remote(
            self.quarter.at[z], self.arrive.at[z], self.send.at[2 * n + z], self.recv.at[2 * n + z], p.right
        )

    def _left(self, z, goal):
        n, p = self.p.depth, self.p
        return remote(
            self.quarter.at[z], self.arrive.at[goal], self.send.at[2 * n + z], self.recv.at[2 * n + goal], p.left
        )

    def _a(self):
        n, p = self.p.depth, self.p
        return remote(
            self.quarter.at[p.z, 1 - p.a], self.last, self.send.at[3 * n], self.recv.at[3 * n + 1], p.a_nbr
        )

    def _keep(self, core, z):
        return pltpu.make_async_copy(self._region(core, z), self.mine.at[z], self.mine_sem.at[z])

    def start(self, k):
        z = self.order(k)

        def one(core):
            self._sib(core, z).start()
            if self.mine is not None:
                self._keep(core, z).start()

        self.p.by_core(one)

    def to_half(self, k):
        z = self.order(k)

        def one(core):
            self._sib(core, z).wait_recv()
            region = self._region(core, z)
            if self.mine is not None:
                self._keep(core, z).wait()
                region = self.mine.at[z]
            for i in (0, 1):
                for j in (0, 1):
                    add_rows(self.half.at[z, i, j], region.at[i, j], self.rows)
            self._b(core, z).start()

        self.p.by_core(one)

    def to_quarter(self, k):
        z = self.order(k)

        def one(core):
            self._b(core, z).wait_recv()
            for i in (0, 1):
                add_rows(self.quarter.at[z, i], self._half_pair(core, self.p.b, z).at[i], self.rows)

        self.p.by_core(one)

    def _take(self, z, slot):
        for i in (0, 1):
            add_rows(self.quarter.at[z, i], self.arrive.at[slot, i], self.rows)

    def _send_left(self, z):
        p, n = self.p, self.p.depth
        pl.when(z == p.z - 1)(lambda: self._left(z, n).start())
        pl.when(z < p.z - 1)(lambda: self._left(z, z).start())

    def origin(self, k):
        p, n = self.p, self.p.depth
        z = self.order(k)
        pl.when(jnp.logical_and(p.z == 0, z > p.z))(lambda: self._right(z).start())
        pl.when(jnp.logical_and(p.z == n - 1, z < p.z))(lambda: self._send_left(z))

    def forward(self, k):
        p, n = self.p, self.p.depth
        z = self.order(k)

        def rightward():
            self._right(z).wait_recv()
            self._take(z, z)
            self._right(z).start()

        def leftward():
            self._left(z, z).wait_recv()
            self._take(z, z)
            self._send_left(z)

        pl.when(jnp.logical_and(p.z > 0, z > p.z))(rightward)
        pl.when(jnp.logical_and(p.z < n - 1, z < p.z))(leftward)

    def collect(self):
        p, n = self.p, self.p.depth

        def from_left():
            self._right(p.z).wait_recv()
            self._take(p.z, p.z)

        def from_right():
            self._left(p.z, n).wait_recv()
            self._take(p.z, n)

        pl.when(p.z > 0)(from_left)
        pl.when(p.z < n - 1)(from_right)
        self._a().start()

    def finish(self):
        p = self.p
        self._a().wait_recv()
        self.total[...] = self.quarter[p.z, p.a].astype(jnp.float32) + self.last[...].astype(jnp.float32)

    def drain(self):
        p, n = self.p, self.p.depth
        self._a().wait_send()

        def each(z, carry):
            def one(core):
                self._sib(core, z).wait_send()
                self._b(core, z).wait_send()

            p.by_core(one)
            pl.when(z != p.z)(lambda: self._right(z).wait_send())
            return carry

        lax.fori_loop(0, n, each, 0)

    def steps(self):
        n = self.p.depth
        todo = [lambda: [self.start(k) for k in range(n)]]
        todo += [functools.partial(self.to_half, k) for k in range(n)]
        for k in range(n):
            todo.append(functools.partial(lambda k: (self.to_quarter(k), self.origin(k), self.forward(k)), k))
        return todo


class Sum:
    def __init__(self, p, bits, value, slots, send, recv):
        self.p, self.bits, self.value, self.slots = p, bits, value, slots
        self.send, self.recv = send, recv

    @staticmethod
    def scratch(bits, rows):
        return [
            pltpu.VMEM((2 * (bits + 2), rows, 128), jnp.float32),
            pltpu.SemaphoreType.DMA((bits + 2,)),
            pltpu.SemaphoreType.DMA((bits + 2,)),
        ]

    def _copy(self, s):
        p = self.p
        dev = (p.sib, p.yn, *[p.flip(bit) for bit in range(self.bits)])[s]
        return remote(self.slots.at[2 * s], self.slots.at[2 * s + 1], self.send.at[s], self.recv.at[s], dev)

    def steps(self):
        def begin():
            self.slots[0] = self.value[...]
            self._copy(0).start()

        def one(s):
            self._copy(s).wait_recv()
            total = self.slots[2 * s] + self.slots[2 * s + 1]
            if s == self.bits + 1:
                self.value[...] = total
            else:
                self.slots[2 * s + 2] = total
                self._copy(s + 1).start()

        return [begin] + [functools.partial(one, s) for s in range(self.bits + 2)]

    def drain(self):
        for s in range(self.bits + 2):
            self._copy(s).wait_send()


def in_waves(lists, lag):
    for t in range(max(len(todo) + lag * r for r, todo in enumerate(lists))):
        for r, todo in enumerate(lists):
            if 0 <= t - lag * r < len(todo):
                todo[t - lag * r]()


def gather_kernel(p_depth, tok, cot, wq, wo, wi, wu, tok_s, cot_s, gq, go, gi, gu, *sems):
    p = Place(p_depth)
    n = p_depth
    arrays = []
    for i, (by_head, shard, buf) in enumerate(
        ((True, wq, gq), (False, wo, go), (False, wi, gi), (False, wu, gu))
    ):
        arrays.append(Gather(p, by_head, shard, buf, *sems[3 * i : 3 * i + 3]))
    rows = [Exchange(p, tok, tok_s, *sems[12:15]), Exchange(p, cot, cot_s, *sems[15:18])]
    p.barrier(0)
    for g in arrays:
        g.start()
    rows[0].start()
    if n <= 8:
        for k in range(n):
            for g in arrays:
                g.along(k)
            if k > 0:
                for g in arrays:
                    g.across(k - 1)
            if k == 1:
                rows[1].start()
        for g in arrays:
            g.across(n - 1)
    else:
        for g in arrays:
            g.along(0)
            lax.fori_loop(1, n, lambda k, carry: (g.along(k), carry)[1], 0)
        rows[1].start()
        for g in arrays:
            g.across(0)
            lax.fori_loop(1, n, lambda k, carry: (g.across(k), carry)[1], 0)
    for g in arrays + rows:
        g.finish()
    for g in arrays + rows:
        g.drain()


def gather_all(depth, tok, cot, shards):
    hbm = pl.BlockSpec(memory_space=pl.ANY)
    outs = [jax.ShapeDtypeStruct(tok.shape, tok.dtype)] * 2
    for i, s in enumerate(shards):
        lead = (2, 2, depth, 2) if i == 0 else (depth, 2, 2, 2)
        outs.append(jax.ShapeDtypeStruct(lead + s.shape, s.dtype))
    sems = Gather.sems(depth) * 4 + Exchange.sems() * 2
    return pl.pallas_call(
        functools.partial(gather_kernel, depth),
        out_shape=outs,
        in_specs=[hbm] * 6,
        out_specs=[hbm] * 6,
        scratch_shapes=sems,
        compiler_params=pltpu.CompilerParams(collective_id=0, has_side_effects=True),
        name="gather",
    )(tok, cot, *shards)


def scatter_kernel(depth, bits, pq, po, pi, pu, small, out_s, gtok_s, oq, oo, oi, ou, small_o, out, gtok, *scr):
    p = Place(depth)
    arrays = []
    for i, (by_head, part, total) in enumerate(
        ((False, pu, ou), (False, pi, oi), (False, po, oo), (True, pq, oq))
    ):
        arrays.append(Scatter(p, by_head, part, total, *scr[6 * i : 6 * i + 6]))
    rows = [Exchange(p, out_s, out, *scr[24:27]), Exchange(p, gtok_s, gtok, *scr[27:30])]
    small_o[...] = small[...]
    sums = Sum(p, bits, small_o, *scr[30:33])
    p.barrier(bits)
    rows[0].start()
    in_waves([g.steps() for g in arrays], min(depth, 4))
    rows[1].start()
    close(arrays, sums)
    for r in rows:
        r.finish()
    for g in arrays + rows + [sums]:
        g.drain()


def close(arrays, sums):
    closing = [g.collect for g in arrays] + [g.finish for g in arrays]
    for step in itertools.chain(*itertools.zip_longest(sums.steps(), closing)):
        if step is not None:
            step()


def scatter_all(depth, bits, parts, small, out_s, gtok_s):
    hbm = pl.BlockSpec(memory_space=pl.ANY)
    vmem = pl.BlockSpec(memory_space=pltpu.VMEM)
    outs = [jax.ShapeDtypeStruct(s.shape[4:], jnp.float32) for s in parts]
    outs += [jax.ShapeDtypeStruct(small.shape, jnp.float32)]
    outs += [jax.ShapeDtypeStruct(out_s.shape, out_s.dtype)] * 2
    scr = []
    for s in (parts[3], parts[2], parts[1], parts[0]):
        scr += Scatter.scratch(depth, *s.shape[4:])
    scr += Exchange.sems() * 2 + Sum.scratch(bits, small.shape[0])
    return pl.pallas_call(
        functools.partial(scatter_kernel, depth, bits),
        out_shape=outs,
        in_specs=[vmem] * 5 + [hbm] * 2,
        out_specs=[vmem] * 5 + [hbm] * 2,
        scratch_shapes=scr,
        compiler_params=pltpu.CompilerParams(
            collective_id=1, has_side_effects=True, vmem_limit_bytes=60 * 2**20
        ),
        name="scatter",
    )(*parts, small, out_s, gtok_s)

SPANS = ((0, LEN_LONG), (LEN_LONG, LEN_MID), (LEN_LONG + LEN_MID, LEN_SHORT), (LEN_LONG + LEN_MID + LEN_SHORT, LEN_SHORT))
TILE = 128
QKV_PAD = 640
CTX_PAD = 256
ADAPT_PAD = 128
MASK_LOW = -1e9
NN = (((1,), (0,)), ((), ()))
NT = (((1,), (1,)), ((), ()))
TN = (((0,), (0,)), ((), ()))


def dot(a, b, dims=NN):
    return lax.dot_general(a, b, dims, preferred_element_type=jnp.float32)


def table_onehot():
    buckets = rel_buckets(257)
    offset = np.clip(256 - np.arange(512), -256, 256) + 256
    index = np.concatenate([buckets[offset], np.full(128, NB // 2 - 1), np.full(128, NB - 1)])
    return (index[:, None] == np.arange(NB)[None, :]).astype(np.float32)


def bias_tiles(row):
    spread = pltpu.roll(jnp.broadcast_to(row, (TILE, 512)), 0, 1, stride=1, stride_axis=0)
    far = [jnp.broadcast_to(row[:, at : at + 1], (TILE, TILE)) for at in (511, 0)]
    near = [spread[:, 256 - 128 * delta : 384 - 128 * delta] for delta in (-1, 0, 1)]
    return [far[0], *near, far[1]]


def diagonal_sums(tiles):
    grid = jnp.concatenate([jnp.zeros((TILE, TILE), jnp.float32), tiles[2], tiles[1], tiles[0]], axis=1)
    rows = TILE
    while rows > 8:
        rows //= 2
        grid = grid[:rows] + pltpu.roll(grid[rows:], 512 - rows, 1)
    total = grid[0:1]
    for r in range(1, 8):
        total = total + pltpu.roll(grid[r : r + 1], 512 - r, 1)
    return total


def swap_halves(tile):
    return jnp.concatenate([tile[:, DH:], tile[:, :DH]], axis=1)


def lanes_below(shape, at=DH):
    return lax.broadcasted_iota(jnp.int32, shape, len(shape) - 1) < at


def key_side(qk, mask):
    swapped = swap_halves(qk)
    return jnp.where(lanes_below(qk.shape), swapped, mask), swapped


def query_side(qk):
    lane = lax.broadcasted_iota(jnp.int32, qk.shape, 1)
    return jnp.where(lane < DH, qk, jnp.where(lane == DH, 1.0, 0.0).astype(qk.dtype))


def probabilities(scores, tiles, length, q0=0):
    width = scores.shape[1]
    blocks = []
    for kb in range(length // TILE):
        deltas = [max(-2, min(2, kb - (q0 + qi))) + 2 for qi in range(width // TILE)]
        bias = tiles[deltas[0]] if len(deltas) == 1 else jnp.concatenate([tiles[d] for d in deltas], axis=1)
        blocks.append(scores[kb * TILE : (kb + 1) * TILE] + bias)
    top = blocks[0]
    for block in blocks[1:]:
        top = jnp.maximum(top, block)
    top = jnp.max(top, axis=0, keepdims=True)
    blocks = [jnp.exp(block - top) for block in blocks]
    total = blocks[0]
    for block in blocks[1:]:
        total = total + block
    inverse = 1.0 / jnp.sum(total, axis=0, keepdims=True)
    return [block * inverse for block in blocks]


def join(blocks, axis=0):
    return blocks[0] if len(blocks) == 1 else jnp.concatenate(blocks, axis=axis)


def value_lanes(group):
    stride = group * CTX_PAD // (3 * DH)
    lane = np.arange(CTX_PAD)
    column = lane // stride * group + lane % stride
    return np.where(lane % stride < group, column // DH, -1), column


def head_runs(group):
    heads, _ = value_lanes(group)
    runs = []
    for lane in range(CTX_PAD):
        head = int(heads[lane])
        head = runs[-1][2] if head < 0 else head
        if runs and runs[-1][2] == head:
            runs[-1][1] = lane + 1
        else:
            runs.append([lane, lane + 1, head])
    return runs


def head_lanes(shape, group, head):
    lane = lax.broadcasted_iota(jnp.int32, shape, len(shape) - 1)
    inside = None
    for lo, hi, h in head_runs(group):
        if h == head:
            run = jnp.logical_and(lane >= lo, lane < hi)
            inside = run if inside is None else jnp.logical_or(inside, run)
    return inside


def no_tick(j):
    pass


def no_keep(number, place, h, probs):
    pass


FRONT_SPANS = (SPANS[:1], SPANS[1:])
FRONT_WIDTH = 256


def attend_group(packed, mask_ref, rows, context, group, tick=no_tick, keep=no_keep):
    tiles = [bias_tiles(rows[h : h + 1, :]) for h in range(3)]
    for number, spans in enumerate(FRONT_SPANS):
        units = []
        for offset, length in spans:
            width = min(length, FRONT_WIDTH)
            units += [(offset, length, q0, width) for q0 in range(0, length, width)]
        batches = [[unit] for unit in units] if number == 0 else [units]
        keys = {
            (offset, h): key_side(packed[pl.ds(offset, length), h * TILE : (h + 1) * TILE], mask_ref[pl.ds(offset, length), :])[0]
            for offset, length in spans
            for h in range(3)
        }
        values = {offset: packed[pl.ds(offset, length), 3 * TILE : QKV_PAD].T for offset, length in spans}
        for turn, batch in enumerate(batches):
            work = [(unit, h) for unit in batch for h in range(3)]
            scores = []
            for (offset, length, q0, width), h in work:
                queries = query_side(packed[pl.ds(offset + q0, width), h * TILE : (h + 1) * TILE])
                scores.append(dot(keys[offset, h], queries, NT))
            probs = []
            for ((offset, length, q0, width), h), score in zip(work, scores):
                blocks = probabilities(score, tiles[h], length, q0 // TILE)
                probs.append(join([block.astype(jnp.bfloat16) for block in blocks]))
            for (unit, h), prob in zip(work, probs):
                keep(number, unit, h, prob)
            outs = [dot(values[unit[0]], prob) for (unit, h), prob in zip(work, probs)]
            for i, (offset, length, q0, width) in enumerate(batch):
                own = outs[3 * i : 3 * i + 3]
                whole = jnp.concatenate([own[h][lo:hi] for lo, hi, h in head_runs(group)], axis=0)
                context[pl.ds(offset + q0, width), :] = whole.T.astype(jnp.bfloat16)
            tick((number, turn))


BACK_SPANS = (SPANS[:1], SPANS[1:])
SKEW = (5, 0)


def head_back(packed, recall, grad_context, grad_packed, group, near, far, value_sums, span_of, h):
    offset, length = span_of
    span, at = pl.ds(offset, length), pl.ds(h * TILE, TILE)
    qk = packed[span, at]
    low = lanes_below(qk.shape)
    swapped = swap_halves(qk)
    g_tile = grad_context[span, :]
    g_tile = jnp.where(head_lanes(g_tile.shape, group, h), g_tile, jnp.zeros_like(g_tile))
    scores = recall.scores(qk, span, h)
    g_probs = dot(packed[span, 3 * TILE : QKV_PAD], g_tile, NT)
    yield
    probs = recall.probs(scores, span_of, h)
    yield
    count = length // TILE
    g_blocks = [g_probs[kb * TILE : (kb + 1) * TILE] for kb in range(count)]
    total = probs[0] * g_blocks[0]
    for kb in range(1, count):
        total = total + probs[kb] * g_blocks[kb]
    centre = jnp.sum(total, axis=0, keepdims=True)
    low_probs = join([block.astype(jnp.bfloat16) for block in probs])
    g_scores = [(a * (g - centre)).astype(jnp.bfloat16) for a, g in zip(probs, g_blocks)]
    for kb, block in enumerate(g_scores):
        wide = block.astype(jnp.float32)
        for qi in range(count):
            piece = wide[:, qi * TILE : (qi + 1) * TILE]
            delta = kb - qi
            if abs(delta) <= 1:
                held = near[h][delta + 1]
                near[h][delta + 1] = piece if held is None else held + piece
            else:
                side = 0 if delta < 0 else 1
                far[h][side] = far[h][side] + piece
    yield
    g_scores = join(g_scores)
    g_v = dot(low_probs, g_tile)
    value_sums[offset] = value_sums[offset] + g_v if offset in value_sums else g_v
    grad_keys = dot(g_scores, jnp.where(low, jnp.zeros_like(qk), swapped))
    grad_queries = dot(jnp.where(low, swapped, jnp.zeros_like(qk)).T, g_scores).T
    yield
    grad_packed[span, at] = (grad_queries + grad_keys).astype(jnp.bfloat16)


class Again:
    def __init__(self, mask, rows):
        self.mask = mask
        self.tiles = [bias_tiles(rows[h : h + 1, :]) for h in range(3)]

    def scores(self, qk, span, h):
        return dot(key_side(qk, self.mask[span, :])[0], query_side(qk), NT)

    def probs(self, scores, span_of, h):
        return probabilities(scores, self.tiles[h], span_of[1])


class Kept:
    def __init__(self, kept):
        self.kept = kept

    def scores(self, qk, span, h):
        return None

    def probs(self, scores, span_of, h):
        offset, length = span_of
        pieces = [self.kept[r : r + n, c : c + w] for r, n, c, w in kept_at(offset, length, h)]
        whole = join(pieces, axis=1).astype(jnp.float32)
        return [whole[kb * TILE : (kb + 1) * TILE] for kb in range(length // TILE)]


KEPT_LONG, KEPT_REST = 1024, 384


def kept_at(offset, length, h):
    if length == LEN_LONG:
        if h < 2:
            return [(LEN_LONG * h, LEN_LONG, 0, LEN_LONG)]
        return [(LEN_LONG * k, LEN_LONG, LEN_LONG, LEN_LONG // 2) for k in range(2)]
    if length == LEN_MID:
        return [(KEPT_LONG, LEN_MID, LEN_MID * h, LEN_MID)]
    second = (offset - LEN_LONG - LEN_MID) // LEN_SHORT
    return [(KEPT_LONG + LEN_MID, LEN_SHORT, LEN_SHORT * (3 * second + h), LEN_SHORT)]


def attend_group_back(packed, recall, grad_context, grad_packed, sums, group, tick=no_tick):
    near = [[None] * 3 for _ in range(3)]
    far = [[jnp.zeros((TILE, TILE), jnp.float32)] * 2 for _ in range(3)]
    value_sums = {}

    def heads_of(spans):
        return [
            head_back(packed, recall, grad_context, grad_packed, group, near, far, value_sums, s, h)
            for s in spans
            for h in range(3)
        ]

    def values_of(spans):
        for offset, length in spans:
            grad_packed[pl.ds(offset, length), 3 * TILE : QKV_PAD] = value_sums.pop(offset).astype(jnp.bfloat16)

    for number, spans in enumerate(BACK_SPANS):
        heads = heads_of(spans)
        skew = SKEW[number]
        for t in range(5 + skew * (len(heads) - 1)):
            for i, head in enumerate(heads):
                if 0 <= t - skew * i < 5:
                    next(head, None)
                    if t - skew * i == 4:
                        tick((number, i))
        values_of(spans)
    for h in range(3):
        sums[h : h + 1, :512] = diagonal_sums(near[h])
        for side in range(2):
            sums[h : h + 1, 512 + side * TILE : 640 + side * TILE] = jnp.sum(far[h][side], axis=0, keepdims=True)


def attention_kernel(group, x_ref, gain, w_ref, mask, rows, normed_out, packed, context):
    @pl.when(pl.program_id(0) == 0)
    def _():
        x = x_ref[...].astype(jnp.float32)
        scale = lax.rsqrt(jnp.mean(x * x, axis=-1, keepdims=True) + NORM_EPS)
        normed_out[...] = (x * scale * gain[...]).astype(jnp.bfloat16)

    packed[0] = dot(normed_out[...], w_ref[0]).astype(jnp.bfloat16)
    attend_group(packed.at[0], mask, rows[0], context.at[0], group)


def attention(x, gain, w, mask, rows, group):
    n = x.shape[0]
    bf = jnp.bfloat16
    return pl.pallas_call(
        functools.partial(attention_kernel, group),
        grid=(4,),
        out_shape=[
            jax.ShapeDtypeStruct((n, D), bf),
            jax.ShapeDtypeStruct((4, n, QKV_PAD), bf),
            jax.ShapeDtypeStruct((4, n, CTX_PAD), bf),
        ],
        in_specs=[
            pl.BlockSpec((n, D), lambda i: (0, 0)),
            pl.BlockSpec((1, D), lambda i: (0, 0)),
            pl.BlockSpec((1, D, QKV_PAD), lambda i: (i, 0, 0)),
            pl.BlockSpec((n, TILE), lambda i: (0, 0)),
            pl.BlockSpec((1, 3, 512), lambda i: (i, 0, 0)),
        ],
        out_specs=[
            pl.BlockSpec((n, D), lambda i: (0, 0)),
            pl.BlockSpec((1, n, QKV_PAD), lambda i: (i, 0, 0)),
            pl.BlockSpec((1, n, CTX_PAD), lambda i: (i, 0, 0)),
        ],
        compiler_params=pltpu.CompilerParams(vmem_limit_bytes=56 * 2**20),
        name="attention",
    )(x, gain, w, mask, rows)


def attention_back_kernel(group, packed, grad_context, mask, rows, grad_packed, sums):
    attend_group_back(packed.at[0], Again(mask, rows[0]), grad_context.at[0], grad_packed.at[0], sums.at[0], group)


def attention_back(packed, grad_context, mask, rows, group):
    n = packed.shape[1]
    return pl.pallas_call(
        functools.partial(attention_back_kernel, group),
        grid=(4,),
        out_shape=[
            jax.ShapeDtypeStruct((4, n, QKV_PAD), jnp.bfloat16),
            jax.ShapeDtypeStruct((4, 3, 768), jnp.float32),
        ],
        in_specs=[
            pl.BlockSpec((1, n, QKV_PAD), lambda i: (i, 0, 0)),
            pl.BlockSpec((1, n, CTX_PAD), lambda i: (i, 0, 0)),
            pl.BlockSpec((n, TILE), lambda i: (0, 0)),
            pl.BlockSpec((1, 3, 512), lambda i: (i, 0, 0)),
        ],
        out_specs=[
            pl.BlockSpec((1, n, QKV_PAD), lambda i: (i, 0, 0)),
            pl.BlockSpec((1, 3, 768), lambda i: (i, 0, 0)),
        ],
        compiler_params=pltpu.CompilerParams(vmem_limit_bytes=56 * 2**20),
        name="attention_back",
    )(packed, grad_context, mask, rows)


def head_columns(w, group):
    n = w.shape[0]
    qk = w[:, :, : 2 * DH].reshape(n, 6 * DH)
    v = w[:, :, 2 * DH :].reshape(n, 3 * DH // group, group)
    v = jnp.pad(v, ((0, 0), (0, 0), (0, group // 3))).reshape(n, CTX_PAD)
    return jnp.concatenate([qk, v], axis=1)


def key_mask(live):
    lane = jnp.arange(TILE)[None, :]
    return jnp.where((lane == DH) & ~live[:, None], MASK_LOW, 0.0).astype(jnp.bfloat16)


def precise(a, b, dims=NN):
    return lax.dot_general(a, b, dims, precision=FULL_PRECISION, preferred_element_type=jnp.float32)


def offset_onehot():
    buckets = rel_buckets(257)
    offset = np.clip(256 - np.arange(512), -256, 256) + 256
    return (np.arange(NB)[:, None] == buckets[offset][None, :]).astype(np.float32)


def value_choice(group):
    choice = np.zeros((3 * DH, CTX_PAD), np.float32)
    heads, column = value_lanes(group)
    lanes = np.flatnonzero(heads >= 0)
    choice[column[lanes], lanes] = 1
    return choice


def own_length(lengths, member, number):
    at = (member, 4 + member // 2 + 2 * (member % 2), 8 + member, 12 + member)[number]
    return lengths[at]


def fill_mask(mask, lengths, member):
    for number, (offset, length) in enumerate(SPANS):
        row = lax.broadcasted_iota(jnp.int32, (length, TILE), 0)
        lane = lax.broadcasted_iota(jnp.int32, (length, TILE), 1)
        dead = jnp.logical_and(row >= own_length(lengths, member, number), lane == DH)
        mask[offset : offset + length, :] = jnp.where(dead, MASK_LOW, 0.0).astype(jnp.bfloat16)


def fill_rows(rows, pos_table, onehot):
    table = precise(pos_table[...], onehot[...])
    for m in range(4):
        rows[m] = table[3 * m : 3 * m + 3, :]


KA = ADAPT // KRON


def adapter_constants():
    i, b = np.arange(16) // 4, np.arange(16) % 4
    same = (np.arange(4)[:, None] == i[None, :]).astype(np.float32)
    pick = np.zeros((4, 4, 16), np.float32)
    pick[i, b, np.arange(16)] = 1
    fold = np.zeros((ADAPT_PAD, KA), np.float32)
    fold[np.arange(ADAPT), np.arange(ADAPT) % KA] = 1
    agree = np.zeros((ADAPT_PAD, 16), np.float32)
    agree[:ADAPT] = np.arange(ADAPT)[:, None] // KA == b[None, :]
    return same, pick, fold, agree


class Factor:
    def __init__(self, rules, tall, short, consts):
        self.same, _, self.fold, self.agree = consts
        spread = precise(tall, self.same, TN)
        self.tall = jnp.concatenate([spread] * KRON, axis=0)
        rows = spread.shape[0]
        self.rules = jnp.concatenate(
            [jnp.broadcast_to(rules[a : a + 1, :], (rows, 16)) for a in range(KRON)], axis=0
        )
        self.short = precise(self.fold, precise(short, self.same, TN)) * self.agree

    def whole(self):
        return precise(self.rules * self.tall, self.short, NT)

    def back(self, grad):
        wide = precise(grad, self.short)
        rows = wide.shape[0] // KRON
        tall = wide * self.rules
        tall = sum(tall[a * rows : (a + 1) * rows] for a in range(KRON))
        rules = wide * self.tall
        rules = [jnp.sum(rules[a * rows : (a + 1) * rows], axis=0, keepdims=True) for a in range(KRON)]
        short = precise(self.rules * self.tall, grad, TN) * self.agree.T
        short = precise(precise(self.same, short), self.fold)
        return jnp.concatenate(rules, axis=0), precise(self.same, tall, NT), short


def rule_tables(rules, pick):
    return [sum(precise(rules[i], pick[i], dims) for i in range(KRON)) for dims in (NN, TN)]


ROW_GAIN, ROW_TABLE, ROW_OTHER = 0, 8, 24
ROW_FFN, ROW_DL, ROW_UR, ROW_DR, ROW_UL, ROW_RULES, ROW_END = 0, 8, 16, 24, 28, 32, 48


def put_row(ref, at, row):
    for k in range(row.shape[1] // 128):
        ref[at + k : at + k + 1, :] = row[:, 128 * k : 128 * (k + 1)]


FCH = 768
RCH = 256


def gelu_both(v):
    phi = 0.5 + 0.5 * lax.erf(v * np.float32(np.sqrt(0.5)))
    return v * phi, phi + v * (jnp.exp(-0.5 * v * v) * np.float32(1.0 / np.sqrt(2.0 * np.pi)))


def rows_of(i, size=RCH):
    return pl.ds(pl.multiple_of(i * size, size), size)


def each_of(count, body):
    lax.fori_loop(0, count, lambda i, carry: (body(i), carry)[1], 0)


class Layer:
    def __init__(self, **refs):
        self.__dict__.update(refs)
        self.n = self.n2.shape[0]

    def midway(self, i):
        r = rows_of(i)
        total = self.x_rows(i)
        for m in range(4):
            total = total + dot(self.ctx[m, r, :], self.wo(m))
        self.mid[r, :] = total
        scale = lax.rsqrt(jnp.mean(total * total, axis=-1, keepdims=True) + NORM_EPS)
        self.n2[r, :] = (total * scale * self.gain[...]).astype(jnp.bfloat16)

    def forward(self, j):
        f = rows_of(j, self.chunk)
        for half in range(2):
            r = pl.ds(half * (self.n // 2), self.n // 2)
            value, slope = gelu_both(dot(self.n2[r, :], self.wi(j), NT))
            value = value.astype(jnp.bfloat16)
            self.act[r, f] = value
            self.dg[r, f] = slope.astype(jnp.bfloat16)
            self.acc[r, :] += dot(value, self.wu(j))

    def factors(self):
        consts = [c[...] for c in self.consts]
        by_a, by_b = rule_tables(self.rules, consts[1])
        d_left, d_right, u_left, u_right = self.sides
        return (
            Factor(by_a, d_left[...], d_right[...], consts),
            Factor(by_b, u_right[...], u_left[...], consts),
        )

    def prepare(self, member):
        down, up = self.factors()
        self.down[...] = down.whole().astype(jnp.bfloat16)
        self.up[...] = up.whole().astype(jnp.bfloat16)
        for number, (offset, length) in enumerate(SPANS):
            row = lax.broadcasted_iota(jnp.int32, (length, 1), 0)
            alive = row < own_length(self.lengths, member, number)
            self.live[offset : offset + length, :] = jnp.where(alive, 1.0, 0.0)

    def adapter(self, i):
        bf = jnp.bfloat16
        r = rows_of(i)
        ffn = self.acc[r, :]
        low = ffn.astype(bf)
        value, slope = gelu_both(dot(low, self.down[...]))
        value = value.astype(bf)
        self.put_res(i, (self.mid[r, :] + ffn + dot(value, self.up[...], NT)).astype(bf))
        g_out = self.cot_rows(i) * self.live[r, :]
        g_low = g_out.astype(bf)
        self.gout[r, :] = g_low
        g_sq = (dot(g_low, self.up[...]) * slope).astype(bf)
        self.g_up[...] += dot(g_low, value, TN)
        self.g_down[...] += dot(low, g_sq, TN)
        self.gffn[r, :] = (g_out + dot(g_sq, self.down[...], NT)).astype(bf)

    def backward(self, j):
        dg = self.slope(j)
        for half in range(2):
            r = pl.ds(half * (self.n // 2), self.n // 2)
            g = (dot(self.gffn[r, :], self.wu(j), NT) * dg[r, :].astype(jnp.float32)).astype(jnp.bfloat16)
            dg[r, :] = g
            self.acc[r, :] += dot(g, self.wi(j))

    def last(self, i):
        r = rows_of(i)
        total = self.mid[r, :]
        g_n2 = self.acc[r, :]
        scale = lax.rsqrt(jnp.mean(total * total, axis=-1, keepdims=True) + NORM_EPS)
        self.g_gain[...] += jnp.sum(total * scale * g_n2, axis=0, keepdims=True)
        scaled = self.gain[...] * g_n2
        centre = jnp.mean(total * scaled, axis=-1, keepdims=True)
        g_mid = self.gout[r, :].astype(jnp.float32) + scale * scaled - total * (scale * scale * scale * centre)
        self.mid[r, :] = g_mid
        self.glow[r, :] = g_mid.astype(jnp.bfloat16)

    def projection(self, m):
        grad = dot(self.ctx[m], self.glow[...], TN).astype(jnp.bfloat16)
        self.ctx[m] = dot(self.glow[...], self.wo(m), NT).astype(jnp.bfloat16)
        return grad

    def adapter_all(self):
        self.g_down[...] = jnp.zeros_like(self.g_down)
        self.g_up[...] = jnp.zeros_like(self.g_up)
        each_of(self.n // RCH, self.adapter)

    def adapter_grads(self):
        other, pick = self.other, self.consts[1]
        down, up = self.factors()
        g_a, g_dl, g_dr = down.back(self.g_down[...])
        g_b, g_ur, g_ul = up.back(self.g_up[...])
        other[...] = jnp.zeros_like(other)
        for at, tall in ((ROW_DL, g_dl), (ROW_UR, g_ur)):
            other[at : at + 4, :] = tall[:, :128]
            other[at + 4 : at + 8, : tall.shape[1] - 128] = tall[:, 128:]
        for at, short in ((ROW_DR, g_dr), (ROW_UL, g_ul)):
            other[at : at + 4, :KA] = short
        for i in range(KRON):
            at = ROW_RULES + 4 * i
            other[at : at + 4, :KRON] = precise(g_a, pick[i], NT) + precise(pick[i], g_b, NT)


def middle_kernel(
    x_hbm, ctx_hbm, wo_hbm, wi_hbm, wu_hbm, cot_hbm, gain, lengths, rules, d_left, d_right, u_left, u_right,
    same, pick, fold, agree,
    res_hbm, gmid_hbm, gctx_hbm, go_hbm, gi_hbm, gu_hbm, other,
    down, up, g_down, g_up, g_gain, live, x, ctx, wo, wi, wu, cot, mid, n2, act, dg, acc, gffn, glow, sem, sems, out_sems,
):
    gain = gain[...].reshape(1, D)
    loads = [
        pltpu.make_async_copy(src, dst, sems.at[i])
        for i, (src, dst) in enumerate(
            ((x_hbm, x), (ctx_hbm, ctx), (wo_hbm, wo), (wi_hbm, wi), (wu_hbm, wu), (cot_hbm, cot))
        )
    ]
    for load in loads:
        load.start()
    def put_res(i, value):
        x[rows_of(i), :] = value

    layer = Layer(
        x_rows=lambda i: x[rows_of(i), :].astype(jnp.float32), cot_rows=lambda i: cot[rows_of(i), :].astype(jnp.float32),
        wo=lambda m: wo[m], wi=lambda j: wi[rows_of(j, FCH), :], wu=lambda j: wu[rows_of(j, FCH), :],
        chunk=FCH, ctx=ctx, gain=gain, lengths=lengths, rules=rules, sides=(d_left, d_right, u_left, u_right),
        consts=(same, pick, fold, agree), down=down, up=up, g_down=g_down, g_up=g_up, g_gain=g_gain, live=live, mid=mid,
        n2=n2, act=act, dg=dg, acc=acc, gffn=gffn, glow=glow, put_res=put_res, gout=cot, other=other,
        slope=lambda j: dg.at[:, rows_of(j, FCH)],
    )
    layer.prepare(lax.axis_index("mp"))
    for load in loads:
        load.wait()
    each_of(layer.n // RCH, layer.midway)
    acc[...] = jnp.zeros_like(acc)
    count = wi.shape[0] // FCH
    each_of(count, layer.forward)
    layer.adapter_all()
    acc[...] = jnp.zeros_like(acc)
    g_gain[...] = jnp.zeros_like(g_gain)

    def stores(j):
        f = rows_of(j, FCH)
        return [
            pltpu.make_async_copy(src.at[pl.ds(0, FCH), f], dst.at[f], sem.at[k, j])
            for k, (src, dst) in enumerate(((act, gu_hbm), (dg, gi_hbm)))
        ]

    def backward(j):
        f = rows_of(j, FCH)
        layer.backward(j)
        act[:FCH, f] = dot(act[:, f], gffn[...], TN).astype(jnp.bfloat16)
        dg[:FCH, f] = dot(dg[:, f], n2[...], TN).astype(jnp.bfloat16)
        for store in stores(j):
            store.start()

    each_of(count, backward)
    each_of(layer.n // RCH, layer.last)
    for m in range(4):
        gffn[CTX_PAD * m : CTX_PAD * (m + 1), :] = layer.projection(m)
    layer.adapter_grads()
    put_row(other, ROW_FFN, g_gain[...])
    copies = [
        pltpu.make_async_copy(src, dst, out_sems.at[k])
        for k, (src, dst) in enumerate(((x, res_hbm), (mid, gmid_hbm), (gffn, go_hbm), (ctx, gctx_hbm)))
    ]
    for copy in copies:
        copy.start()
    each_of(count, lambda j: [store.wait() for store in stores(j)])
    for copy in copies:
        copy.wait()


def middle(x, ctx, wo, wi, wu, cot, gain, lengths, factors):
    n, ff = x.shape[0], wi.shape[0]
    bf, f32 = jnp.bfloat16, jnp.float32
    hbm = pl.BlockSpec(memory_space=pl.ANY)
    vmem = pl.BlockSpec(memory_space=pltpu.VMEM)
    shape = jax.ShapeDtypeStruct
    return pl.pallas_call(
        middle_kernel,
        out_shape=[
            shape((n, D), bf),
            shape((n, D), f32),
            shape((4, n, CTX_PAD), bf),
            shape((4 * CTX_PAD, D), bf),
            shape((ff, D), bf),
            shape((ff, D), bf),
            shape((ROW_END, 128), f32),
        ],
        in_specs=[hbm] * 6 + [vmem] + [pl.BlockSpec(memory_space=pltpu.SMEM)] + [vmem] * 9,
        out_specs=[hbm] * 6 + [vmem],
        scratch_shapes=[
            pltpu.VMEM((D, ADAPT_PAD), bf),
            pltpu.VMEM((D, ADAPT_PAD), bf),
            pltpu.VMEM((D, ADAPT_PAD), f32),
            pltpu.VMEM((D, ADAPT_PAD), f32),
            pltpu.VMEM((1, D), f32),
            pltpu.VMEM((n, 1), f32),
            pltpu.VMEM((n, D), bf),
            pltpu.VMEM((4, n, CTX_PAD), bf),
            pltpu.VMEM((4, CTX_PAD, D), bf),
            pltpu.VMEM((ff, D), bf),
            pltpu.VMEM((ff, D), bf),
            pltpu.VMEM((n, D), bf),
            pltpu.VMEM((n, D), f32),
            pltpu.VMEM((n, D), bf),
            pltpu.VMEM((n, ff), bf),
            pltpu.VMEM((n, ff), bf),
            pltpu.VMEM((n, D), f32),
            pltpu.VMEM((n, D), bf),
            pltpu.VMEM((n, D), bf),
            pltpu.SemaphoreType.DMA((2, ff // FCH)),
            pltpu.SemaphoreType.DMA((6,)),
            pltpu.SemaphoreType.DMA((4,)),
        ],
        compiler_params=pltpu.CompilerParams(vmem_limit_bytes=63 * 2**20),
        name="middle",
    )(x, ctx, wo, wi, wu, cot, gain, lengths, *factors, *map(jnp.asarray, adapter_constants()))


FRONT = (
    "s:o s:q ex0 a:o0",
    "s:i a:q0 a:q1 a:q2",
    "c:q0 a:o1 c:q1 a:i0",
    "c:o0 a:q3 s:u n",
    "c:q2 a:o2 ex1 c:q3",
    "f:q a:u0 A A",
    "A c:o1 A a:i1",
    "a:o3 c:i0 A c:o2",
    "a:u1 A A A",
    "A A a:i2 c:o3",
    "A c:u0 A c:i1",
    "f:o O c:u1 a:u2",
    "c:i2 F0 a:i3 F1",
    "c:u2 a:u3 c:i3 F2",
    "c:u3 F3",
)


def front_order():
    plan, now = {"first": []}, "first"
    pieces = 0
    for step in " ".join(FRONT).split():
        if step == "A":
            now, pieces = ("A", pieces), pieces + 1
        elif step[0] in "OF":
            plan["before", step] = plan.pop("open", [])
            now = "open"
        else:
            plan.setdefault(now, []).append(step)
    return plan


def front_kernel(
    depth, group, tok, cot, w_qkv, w_o, w_in, w_out, choice, gain, gain_ffn, lengths, pos_table, onehot,
    rules, d_left, d_right, u_left, u_right, same, pick, fold, agree,
    tok_s, gq_hbm, normed_hbm, packed_hbm, out, mid_hbm, ctx_hbm, go_hbm, gi_hbm, gu_hbm, dg_hbm, pu_hbm, gffn_hbm, n2_hbm,
    gout_hbm, long_hbm, rest_hbm, other,
    wq, wo, wi, wu, mask, rows, x, y, gq, go, gi, gu, nrm, packed, ctx,
    down, up, g_down, g_up, live, mid, n2, act, dg, acc, gffn, res, sem, out_sems, local, *sems,
):
    p = Place(depth)
    bf = jnp.bfloat16
    p.greet(0)
    gain, gain_ffn = gain[...].reshape(1, D), gain_ffn[...].reshape(1, D)
    for h in range(3):
        wq[:, TILE * h : TILE * (h + 1)] = w_qkv[h, :, :TILE].astype(bf)
    values = [dot(w_qkv[h, :, TILE:].astype(bf), choice[DH * h : DH * (h + 1), :]) for h in range(3)]
    wq[:, 3 * TILE :] = sum(values).astype(bf)
    wo[...] = jnp.zeros_like(wo)
    wo[: w_o.shape[0], :] = w_o[...].astype(bf)
    wi[...] = w_in[...].astype(bf)
    wu[...] = w_out[...].astype(bf)
    arrays = {
        name: Gather(p, name == "q", shard, buf, *sems[3 * i : 3 * i + 3])
        for i, (name, shard, buf) in enumerate((("q", wq, gq), ("o", wo, go), ("i", wi, gi), ("u", wu, gu)))
    }
    first, second = Exchange(p, tok, x, *sems[12:15]), Exchange(p, cot, y, *sems[15:18])
    keep_x = pltpu.make_async_copy(x, tok_s, local.at[0])
    keep_n = pltpu.make_async_copy(nrm, normed_hbm, local.at[1])
    keep_q = pltpu.make_async_copy(gq, gq_hbm, local.at[2])
    quarter = RCH // SEG

    def float_rows(ref):
        return lambda i: ref[pl.ds(quarter * i, quarter)].reshape(RCH, D).astype(jnp.float32)

    def put_res(i, value):
        res[pl.ds(quarter * i, quarter)] = value.reshape(quarter, SEG, D)

    chunk_rows = 8 * wi.shape[0]
    layer = Layer(
        x_rows=float_rows(x), cot_rows=float_rows(y),
        wo=lambda m: go[m].reshape(CTX_PAD, D), wi=lambda j: gi[j].reshape(-1, D), wu=lambda j: gu[j].reshape(-1, D),
        chunk=chunk_rows, ctx=ctx, gain=gain_ffn, lengths=lengths, rules=rules, sides=(d_left, d_right, u_left, u_right),
        consts=(same, pick, fold, agree), down=down, up=up, g_down=g_down, g_up=g_up, live=live, mid=mid, n2=n2, act=act,
        dg=dg, acc=acc, gffn=gffn, put_res=put_res, gout=nrm, other=other,
    )
    third = Exchange(p, res, out, *sems[18:21])

    def norm(i):
        v = x[i].astype(jnp.float32)
        scale = lax.rsqrt(jnp.mean(v * v, axis=-1, keepdims=True) + NORM_EPS)
        nrm[rows_of(i, SEG), :] = (v * scale * gain[...]).astype(bf)

    def norms():
        first.finish()
        keep_x.start()
        each_of(x.shape[0], norm)
        keep_n.start()
        fill_mask(mask, lengths, p.m)
        fill_rows(rows, pos_table, onehot)
        layer.prepare(p.m)
        acc[...] = jnp.zeros_like(acc)

    def step(name):
        kind, rest = name[0], name[2:]
        if name == "n":
            norms()
        elif name in ("ex0", "ex1"):
            (first, second)[int(name[2])].start()
        elif kind == "s":
            arrays[rest].start()
        elif kind == "f":
            arrays[rest].finish()
        elif kind == "a":
            arrays[rest[0]].along(int(rest[1:]))
        elif kind == "c":
            arrays[rest[0]].across(int(rest[1:]))

    def steps(names):
        for name in names:
            step(name)

    plan = front_order()
    p.meet(0)
    steps(plan["first"])
    keep_q.start()

    def piece(m, place):
        at = sum(place) + place[0]
        for loop in range(4):
            names = plan.get(("A", 3 * loop + at))
            if names:
                pl.when(m == loop)(functools.partial(steps, names))

    def keeps(m):
        lanes = rows_of(m, D)
        return [
            pltpu.make_async_copy(packed.at[m], packed_hbm.at[m], local.at[3 + m]),
            pltpu.make_async_copy(act.at[:, lanes], long_hbm.at[m], local.at[7 + m]),
            pltpu.make_async_copy(dg.at[pl.ds(0, KEPT_REST), lanes], rest_hbm.at[m], local.at[11 + m]),
            pltpu.make_async_copy(ctx.at[m], ctx_hbm.at[m], local.at[15 + m]),
        ]

    def keep_probs(m, number, unit, h, probs):
        offset, length, q0, width = unit
        places = kept_at(offset, length, h)
        row, rows_kept, lane, _ = places[min(q0 // width, len(places) - 1)]
        lane = lane + (q0 if len(places) == 1 else 0)
        lanes = pl.ds(pl.multiple_of(D * m + lane, TILE), width)
        if row < KEPT_LONG:
            act[row : row + rows_kept, lanes] = probs
        else:
            dg[row - KEPT_LONG : row - KEPT_LONG + rows_kept, lanes] = probs

    def heads(m):
        w = gq[m // 2, m % 2].reshape(D, QKV_PAD)
        packed[m] = dot(nrm[...], w).astype(bf)
        keeps(m)[0].start()
        attend_group(
            packed.at[m], mask, rows[m], ctx.at[m], group, functools.partial(piece, m), functools.partial(keep_probs, m)
        )
        for copy in keeps(m)[1:]:
            copy.start()

    def stores(z):
        lanes = rows_of(z, chunk_rows)
        return [
            pltpu.make_async_copy(gi.at[z], gi_hbm.at[z], sem.at[0, z]),
            pltpu.make_async_copy(gu.at[z], gu_hbm.at[z], sem.at[1, z]),
            pltpu.make_async_copy(dg.at[:, lanes], dg_hbm.at[z], sem.at[2, z]),
        ]

    def weights(z):
        lanes = rows_of(z, chunk_rows)
        return pltpu.make_async_copy(act.at[pl.ds(0, chunk_rows), lanes], pu_hbm.at[z], sem.at[3, z])

    each_of(4, heads)
    steps(plan[("before", "O")])
    keep_o = pltpu.make_async_copy(go, go_hbm, out_sems.at[0])
    keep_o.start()
    each_of(layer.n // RCH, layer.midway)
    tail = [
        pltpu.make_async_copy(src, dst, out_sems.at[1 + k])
        for k, (src, dst) in enumerate(((mid, mid_hbm), (n2, n2_hbm), (nrm, gout_hbm), (gffn, gffn_hbm)))
    ]
    tail[0].start()
    tail[1].start()
    each_of(4, lambda m: [copy.wait() for copy in keeps(m)])

    def chunk(e):
        for k in range(depth):
            pl.when(e == k)(functools.partial(steps, plan[("before", f"F{k}")]))
        z = p.nearest(e)
        for name in "iu":
            arrays[name].finish_at(z)
        layer.forward(z)
        for copy in stores(z):
            copy.start()

    each_of(depth, chunk)
    second.finish()
    for copy in (keep_x, keep_n, keep_q):
        copy.wait()
    layer.adapter_all()
    third.start()
    tail[2].start()
    tail[3].start()

    def weights_out(k):
        z = p.order(k)
        lanes = rows_of(z, chunk_rows)
        act[:chunk_rows, lanes] = dot(act[:, lanes], gffn[...], TN).astype(bf)
        weights(z).start()

    for k in range(depth):
        weights_out(k)
    layer.adapter_grads()
    for copy in (keep_o, *tail):
        copy.wait()
    each_of(depth, lambda z: [copy.wait() for copy in (*stores(z), weights(z))])
    third.finish()
    for g in (*arrays.values(), first, second, third):
        g.drain()


def front(depth, group, tok, cot, shards, rows_of_shards, gains, lengths, pos_table, factors):
    hbm = pl.BlockSpec(memory_space=pl.ANY)
    vmem = pl.BlockSpec(memory_space=pltpu.VMEM)
    bf, f32 = jnp.bfloat16, jnp.float32
    shape = jax.ShapeDtypeStruct
    n = tok.shape[0] * SEG
    kept = [(rows, QKV_PAD if i == 0 else D) for i, rows in enumerate(rows_of_shards)]
    whole = [((2, 2, depth, 2) if i == 0 else (depth, 2, 2, 2)) + s for i, s in enumerate(kept)]
    ff = 8 * depth * kept[2][0]
    return pl.pallas_call(
        functools.partial(front_kernel, depth, group),
        out_shape=[
            shape(tok.shape, bf),
            shape(whole[0], bf),
            shape((n, D), bf),
            shape((4, n, QKV_PAD), bf),
            shape(tok.shape, bf),
            shape((n, D), f32),
            shape((4, n, CTX_PAD), bf),
            *[shape(s, bf) for s in whole[1:]],
            shape((depth, n, D), bf),
            shape((depth, D, D), bf),
            shape((n, D), bf),
            shape((n, D), bf),
            shape((n, D), bf),
            shape((4, KEPT_LONG, D), bf),
            shape((4, KEPT_REST, D), bf),
            shape((ROW_END, 128), f32),
        ],
        in_specs=[hbm] * 2 + [vmem] * 7 + [pl.BlockSpec(memory_space=pltpu.SMEM)] + [vmem] * 11,
        out_specs=[hbm] * 17 + [vmem],
        scratch_shapes=[pltpu.VMEM(s, bf) for s in kept]
        + [
            pltpu.VMEM((n, TILE), bf),
            pltpu.VMEM((4, 3, 512), f32),
            pltpu.VMEM(tok.shape, bf),
            pltpu.VMEM(tok.shape, bf),
            *[pltpu.VMEM(s, bf) for s in whole],
            pltpu.VMEM((n, D), bf),
            pltpu.VMEM((4, n, QKV_PAD), bf),
            pltpu.VMEM((4, n, CTX_PAD), bf),
            pltpu.VMEM((D, ADAPT_PAD), bf),
            pltpu.VMEM((D, ADAPT_PAD), bf),
            pltpu.VMEM((D, ADAPT_PAD), f32),
            pltpu.VMEM((D, ADAPT_PAD), f32),
            pltpu.VMEM((n, 1), f32),
            pltpu.VMEM((n, D), f32),
            pltpu.VMEM((n, D), bf),
            pltpu.VMEM((n, ff), bf),
            pltpu.VMEM((n, ff), bf),
            pltpu.VMEM((n, D), f32),
            pltpu.VMEM((n, D), bf),
            pltpu.VMEM(tok.shape, bf),
            pltpu.SemaphoreType.DMA((4, depth)),
            pltpu.SemaphoreType.DMA((5,)),
            pltpu.SemaphoreType.DMA((19,)),
        ]
        + Gather.sems(depth) * 4
        + Exchange.sems() * 3,
        compiler_params=pltpu.CompilerParams(
            collective_id=2, has_side_effects=True, vmem_limit_bytes=63 * 2**20
        ),
        name="front",
    )(
        tok, cot, *shards, jnp.asarray(value_choice(group), bf), *gains, lengths, pos_table,
        jnp.asarray(offset_onehot()), *factors, *map(jnp.asarray, adapter_constants()),
    )


BACK = (
    "Su2 Su0 K Su3",
    "K Hu0 K Hu2",
    "K K Hu3 Si0",
    "Su1 K Qu0 K",
    "Qu2 K K Si2",
    "Hi0 K So3 So0",
    "So2 K Hu1 K",
    "Qu3 K K Ho2",
    "K Ho3 Qi0 Si3",
    "Ho0 Fu0 K K",
    "K K Qu1 Si1",
    "Qo2 K Hi2 K",
    "K K Qo0 K",
    "K K Fu2 Hi1",
    "Fu1 K K Qi2",
    "K Hi3 K So1",
    "K K Fi0 K",
    "K Sq0 Qi3 Sq2",
    "Sq3 Fo0 Ho1 Hq0",
    "Qo3 Fi2 N Fu3",
    "Fo2 Hq2 TB Fi3",
    "Cu Qi1 Qo1 Sq1",
    "Fo3 Qq0 Fo1 T0",
    "Hq1 Eu Hq3 Fi1",
    "T1 Co Qq2 Qq1",
    "Fq0 Eo x1 T2",
    "Fq2 Fq1 Qq3 Ci",
    "T3 Fq3 Cq T4",
    "Ei Eq",
)


def back_order():
    plan, pieces = {}, 0
    for step in " ".join(BACK).split():
        if step in "KN":
            pieces += 1
        else:
            plan.setdefault(pieces, []).append(step)
    return plan


PIECES = 6


def back_kernel(
    depth, bits, group,
    tok_hbm, gq_hbm, nrm_hbm, packed_hbm, mid_hbm, ctx_hbm, go_hbm, gi_hbm, gu_hbm, dg_hbm, gffn_hbm, n2_hbm, gout_hbm,
    long_hbm, rest_hbm, pu, gain, gain_ffn, onehot, other,
    oq, oo, oi, ou, small, gtok,
    wu, wi, dg, acc, mid, gffn, nrm, gout, x, ctx, go, kept, g_gain, sums_s, mine_u, sem_u, local, chunk_sem, gq_sem, *scr,
):
    p = Place(depth)
    n = depth
    bf = jnp.bfloat16
    gain, gain_ffn = gain[...].reshape(1, D), gain_ffn[...].reshape(1, D)
    width = pl.ds(0, QKV_PAD)
    arrays = {
        "u": Scatter(p, False, pu, ou, *scr[0:6], mine_u, sem_u),
        "i": Scatter(p, False, wi, oi, *scr[6:12]),
        "o": Scatter(p, False, go, oo, *scr[12:18]),
        "q": Scatter(
            p, True, wu, oq, *scr[18:24],
            region=lambda core, z: wu.at[:, core, z // 2, z % 2, :, :, width],
        ),
    }
    row_g = Exchange(p, x, gtok, *scr[24:27])
    total = Sum(p, bits, small, *scr[27:30])
    layer = Layer(
        wo=lambda m: go[m].reshape(CTX_PAD, D), wi=lambda z: wi[z].reshape(-1, D),
        wu=lambda z: wu[z // 2, z % 2].reshape(-1, D), slope=lambda z: dg.at[z], ctx=ctx, gain=gain_ffn, g_gain=g_gain,
        mid=mid, n2=nrm, acc=acc, gffn=gffn, glow=gffn, gout=gout,
    )

    def load(src, dst, k):
        return pltpu.make_async_copy(src, dst, local.at[k])

    early = [
        load(src, dst, k)
        for k, (src, dst) in enumerate(
            ((gffn_hbm, gffn), (n2_hbm, nrm), (mid_hbm, mid), (gout_hbm, gout), (ctx_hbm, ctx), (go_hbm, go), (tok_hbm, x))
        )
    ]

    def chunk_in(k):
        z = p.order(k)
        pairs = ((dg_hbm.at[z], dg.at[z]), (gu_hbm.at[z], wu.at[z // 2, z % 2]), (gi_hbm.at[z], wi.at[z]))
        return [pltpu.make_async_copy(src, dst, chunk_sem.at[j, k]) for j, (src, dst) in enumerate(pairs)]

    def packed_in(m):
        return load(packed_hbm.at[m], dg.at[m, :, width], 8 + m)

    def gq_in(m, z):
        y, c = m // 2, m % 2
        return pltpu.make_async_copy(
            gq_hbm.at[y, c, z], wu.at[y, c, z // 2, z % 2, :, :, width], gq_sem.at[m, z]
        )

    def kept_in(m):
        slot = m % 2
        return [
            load(long_hbm.at[m], kept.at[slot, pl.ds(0, KEPT_LONG)], 12 + slot),
            load(rest_hbm.at[m], kept.at[slot, pl.ds(KEPT_LONG, KEPT_REST)], 14 + slot),
        ]

    todo = total.steps()

    def steps(names):
        for name in names:
            if name == "x1":
                row_g.start()
            elif name[0] == "T":
                todo.pop(0)()
            else:
                array = arrays[name[1]]
                if name[0] in "CE":
                    (array.collect if name[0] == "C" else array.finish)()
                else:
                    k = int(name[2:])
                    {"S": array.start, "H": array.to_half, "Q": array.to_quarter, "F": array.forward}[name[0]](k)
                    if name[0] == "Q":
                        array.origin(k)

    plan = back_order()

    def place(k):
        steps(plan.pop(k, ()))

    ahead_of = {1: chunk_in(2), 2: early[2:3], 3: chunk_in(3), 4: early[3:4], 5: early[4:6], 6: kept_in(0), 7: early[6:]}

    def load_ahead(k):
        for copy in ahead_of.get(k, ()):
            copy.start()

    p.greet(bits)
    for copy in (early[0], *chunk_in(0), early[1]):
        copy.start()
    small[...] = jnp.zeros_like(small)
    small[ROW_OTHER:, :] = other[...]
    acc[...] = jnp.zeros_like(acc)
    g_gain[...] = jnp.zeros_like(g_gain)
    p.meet(bits)
    place(0)
    for copy in chunk_in(1):
        copy.start()
    early[0].wait()
    for k in range(n):
        z = p.order(k)
        for copy in chunk_in(k):
            copy.wait()
        load_ahead(2 * k + 1)
        layer.backward(z)
        place(2 * k + 1)
        load_ahead(2 * k + 2)
        if k == 0:
            early[1].wait()
        wi[z] = dot(dg[z], nrm[...], TN).astype(bf).reshape(wi.shape[1:])
        place(2 * k + 2)
    for m in range(4):
        packed_in(m).start()
        for z in range(n):
            gq_in(m, z).start()
    renew = load(nrm_hbm, nrm, 7)
    renew.start()
    for copy in early[2:]:
        copy.wait()
    each_of(layer.n // RCH, layer.last)
    place(2 * n + 1)

    def project(m):
        go[m] = layer.projection(m).reshape(go.shape[1:])

    each_of(4, project)
    acc[...] = jnp.zeros_like(acc)
    place(2 * n + 2)
    renew.wait()
    for m in range(4):
        packed_in(m).wait()
        for z in range(n):
            gq_in(m, z).wait()

    def piece(m, j):
        for loop in range(4):
            names = plan.get(2 * n + 2 + PIECES * loop + j + 1)
            if names:
                pl.when(m == loop)(functools.partial(steps, names))

    def tick(m, at):
        number, head = at
        if number == 0:
            piece(m, head)
        elif head == 8:
            piece(m, 3)

    def heads(m):
        slot, y, c = m % 2, m // 2, m % 2
        for copy in kept_in(m):
            copy.wait()

        def ahead():
            for copy in kept_in(m + 1):
                copy.start()

        pl.when(m < 3)(ahead)
        packed = dg.at[m, :, width]
        attend_group_back(packed, Kept(kept.at[slot]), ctx.at[m], packed, sums_s.at[m], group, functools.partial(tick, m))
        whole = (Ellipsis, slice(0, QKV_PAD))
        acc[...] += dot(packed[...], wu[y, c][whole].reshape(D, QKV_PAD), NT)
        piece(m, 4)
        wu[y, c, :, :, :, :, 0:QKV_PAD] = dot(nrm[...], packed[...], TN).astype(bf).reshape(*wu.shape[2:6], QKV_PAD)
        piece(m, 5)

    each_of(4, heads)
    small[ROW_TABLE : ROW_TABLE + 16, :] = jnp.zeros((16, 128), jnp.float32)
    for m in range(4):
        small[ROW_TABLE + 3 * m : ROW_TABLE + 3 * m + 3, :] = precise(sums_s[m], onehot[...])
    put_row(small, ROW_OTHER + ROW_FFN, g_gain[...])

    def last(s, g_gain):
        r = rows_of(s, SEG)
        v = x[s].astype(jnp.float32)
        g_n1 = acc[r, :]
        scale = lax.rsqrt(jnp.mean(v * v, axis=-1, keepdims=True) + NORM_EPS)
        scaled = gain * g_n1
        centre = jnp.mean(v * scaled, axis=-1, keepdims=True)
        x[s] = (mid[r, :] + scale * scaled - v * (scale * scale * scale * centre)).astype(bf)
        return g_gain + jnp.sum(v * scale * g_n1, axis=0, keepdims=True)

    put_row(small, ROW_GAIN, lax.fori_loop(0, x.shape[0], last, jnp.zeros((1, D), jnp.float32)))
    place(2 * n + 2 + 4 * PIECES + 1)
    row_g.finish()
    for g in (*arrays.values(), row_g, total):
        g.drain()


def back(depth, bits, group, kept, ffn, pu, gains, onehot, other):
    hbm = pl.BlockSpec(memory_space=pl.ANY)
    vmem = pl.BlockSpec(memory_space=pltpu.VMEM)
    bf, f32 = jnp.bfloat16, jnp.float32
    shape = jax.ShapeDtypeStruct
    tok, gq = kept[:2]
    mid, ctx, go, gi = ffn[:4]
    n = mid.shape[0]
    small_rows = ROW_OTHER + other.shape[0]
    outs = [shape(s.shape[4:], f32) for s in (gq, go, gi, gi)]
    outs += [shape((small_rows, 128), f32), shape(tok.shape, bf)]
    dma = pltpu.SemaphoreType.DMA
    scratch = [
        pltpu.VMEM((2, 2, 2, 2, 2, *gi.shape[4:]), bf),
        pltpu.VMEM(gi.shape, bf),
        pltpu.VMEM((depth, n, D), bf),
        pltpu.VMEM((n, D), f32),
        pltpu.VMEM((n, D), f32),
        pltpu.VMEM((n, D), bf),
        pltpu.VMEM((n, D), bf),
        pltpu.VMEM((n, D), bf),
        pltpu.VMEM(tok.shape, bf),
        pltpu.VMEM(ctx.shape, bf),
        pltpu.VMEM(go.shape, bf),
        pltpu.VMEM((2, KEPT_LONG + KEPT_REST, D), bf),
        pltpu.VMEM((1, D), f32),
        pltpu.VMEM((4, 3, 768), f32),
        pltpu.VMEM((depth, 2, 2) + gi.shape[4:], bf),
        dma((depth,)),
        dma((16,)),
        dma((3, depth)),
        dma((4, depth)),
    ]
    for s in (gi, gi, go, gq):
        scratch += Scatter.scratch(depth, *s.shape[4:])
    scratch += Exchange.sems() + Sum.scratch(bits, small_rows)
    return pl.pallas_call(
        functools.partial(back_kernel, depth, bits, group),
        out_shape=outs,
        in_specs=[hbm] * 16 + [vmem] * 4,
        out_specs=[vmem] * 5 + [hbm],
        scratch_shapes=scratch,
        compiler_params=pltpu.CompilerParams(
            collective_id=3, has_side_effects=True, vmem_limit_bytes=63 * 2**20
        ),
        name="back",
    )(*kept, *ffn, pu.reshape(gi.shape), *gains, onehot, other)


def finish_kernel(
    q, o, i, u, small, choice, out_hbm, gtok_hbm,
    gq, go, gi, gu, g_attn, g_ffn, g_table, g_rules, g_dl, g_dr, g_ul, g_ur, out, gtok, held, sems,
):
    rows_in = [pltpu.make_async_copy(src, held.at[k], sems.at[k]) for k, src in enumerate((out_hbm, gtok_hbm))]
    rows_out = [pltpu.make_async_copy(held.at[k], dst, sems.at[2 + k]) for k, dst in enumerate((out, gtok))]
    for copy in rows_in:
        copy.start()
    left = q[: gq.shape[1], 3 * TILE :]
    parts = []
    for _ in range(3):
        parts.append(left.astype(jnp.bfloat16))
        left = left - parts[-1].astype(jnp.float32)
    for h in range(3):
        gq[h, :, :TILE] = q[: gq.shape[1], TILE * h : TILE * (h + 1)]
        chosen = choice[DH * h : DH * (h + 1), :]
        gq[h, :, TILE:] = sum(dot(part, chosen, NT) for part in parts)
    for copy_in, copy_out in zip(rows_in, rows_out):
        copy_in.wait()
        copy_out.start()
    go[...] = o[: go.shape[0], :]
    gi[...] = i[: gi.shape[0], :]
    gu[...] = u[: gu.shape[0], :]
    for k in range(D // 128):
        lanes = slice(128 * k, 128 * (k + 1))
        g_attn[lanes] = small[ROW_GAIN + k, :]
        g_ffn[lanes] = small[ROW_OTHER + ROW_FFN + k, :]
    g_table[...] = small[ROW_TABLE : ROW_TABLE + g_table.shape[0], :NB]
    for i in range(KRON):
        at = ROW_OTHER + ROW_RULES + 4 * i
        g_rules[i] = small[at : at + 4, :KRON]
    for ref, at in ((g_dl, ROW_OTHER + ROW_DL), (g_ur, ROW_OTHER + ROW_UR)):
        ref[:, :128] = small[at : at + 4, :]
        ref[:, 128:] = small[at + 4 : at + 8, : ref.shape[1] - 128]
    for ref, at in ((g_dr, ROW_OTHER + ROW_DR), (g_ul, ROW_OTHER + ROW_UL)):
        ref[...] = small[at : at + 4, :KA]
    for copy in rows_out:
        copy.wait()


def finish(q, o, i, u, small, out, gtok, group, shapes):
    vmem = pl.BlockSpec(memory_space=pltpu.VMEM)
    hbm = pl.BlockSpec(memory_space=pl.ANY)
    return pl.pallas_call(
        finish_kernel,
        out_shape=[jax.ShapeDtypeStruct(s, jnp.float32) for s in shapes]
        + [jax.ShapeDtypeStruct(a.shape, a.dtype) for a in (out, gtok)],
        in_specs=[vmem] * 6 + [hbm] * 2,
        out_specs=[vmem] * 12 + [hbm] * 2,
        scratch_shapes=[pltpu.VMEM((2, *out.shape), out.dtype), pltpu.SemaphoreType.DMA((4,))],
        compiler_params=pltpu.CompilerParams(vmem_limit_bytes=60 * 2**20),
        name="finish",
    )(q, o, i, u, small, jnp.asarray(value_choice(group), jnp.bfloat16), out, gtok)


def round_up(n, m):
    return -(-n // m) * m


def pad_rows(a, rows):
    return jnp.pad(a, ((0, rows - a.shape[0]), (0, 0)))


HEADS = 12


def local(
    tokens,
    lengths,
    cotangent,
    w_qkv,
    w_o,
    w_in,
    w_out,
    gain_attn,
    gain_ffn,
    pos_table,
    phm_rules,
    down_left,
    down_right,
    up_left,
    up_right,
):
    dp_count, mp_count = lax.axis_size("dp"), lax.axis_size("mp")
    depth = dp_count // 2
    bits = dp_count.bit_length() - 1
    devices = dp_count * mp_count
    member = lax.axis_index("mp")
    tok_rows = tokens.shape[0]
    seg_count = tok_rows // SEG
    o_rows, in_rows, q_rows = w_o.shape[0], w_in.shape[1], w_qkv.shape[0]
    bf = jnp.bfloat16
    group = o_rows if o_rows % 24 == 0 and round_up(o_rows, 16) * 3 == o_rows * 4 else 3 * DH
    rows_of_shards = [round_up(r, 16) for r in (q_rows, o_rows, in_rows, in_rows)]
    tok_in, cot_in = tokens.reshape(seg_count, SEG, D), cotangent.reshape(seg_count, SEG, D)
    merged = depth == 4 and group == o_rows and rows_of_shards[0] == q_rows and rows_of_shards[2] == in_rows
    factors = (phm_rules, down_left, down_right, up_left, up_right)
    gains = (gain_attn, gain_ffn)
    if merged:
        shards = (w_qkv.transpose(1, 0, 2), w_o, w_in.T, w_out)
        *kept, out, mid, ctx, go, gi, gu, dg, pu, gffn, n2, gout, long, rest, other = front(
            depth, group, tok_in, cot_in, shards, rows_of_shards, gains, lengths, pos_table.T, factors
        )
    else:
        shards = (head_columns(w_qkv.astype(bf), group), w_o.astype(bf), w_in.astype(bf).T, w_out.astype(bf))
        shards = [pad_rows(s, r) for s, r in zip(shards, rows_of_shards)]
        tok_s, cot_s, gq, go, gi, gu = gather_all(depth, tok_in, cot_in, shards)
    def plain(g, rows):
        return g.reshape(devices, g.shape[-2], D)[:, :rows].reshape(devices * rows, D)

    def slots(g, rows):
        padded = jnp.pad(g.reshape(devices, rows, D), ((0, 0), (0, round_up(rows, 16) - rows), (0, 0)))
        return padded.reshape(depth, 2, 2, 2, padded.shape[1], D)

    if not merged:
        tokens_s = tok_s.reshape(tok_rows, D)
        if group == o_rows:
            dense_o = go.reshape(mp_count, CTX_PAD, D)
        else:
            dense_o = plain(go, o_rows).reshape(mp_count, 3 * DH, D)
            dense_o = jnp.pad(dense_o, ((0, 0), (0, CTX_PAD - 3 * DH), (0, 0)))
        qkv_full = gq.reshape(mp_count, dp_count, rows_of_shards[0], QKV_PAD)[:, :, :q_rows]
        qkv_full = qkv_full.reshape(mp_count, D, QKV_PAD)
        live = jnp.concatenate(
            [jnp.arange(length) < own_length(lengths, member, i) for i, (_, length) in enumerate(SPANS)]
        )
        mask = key_mask(live)
        rows = jnp.einsum("bh,br->hr", pos_table, offset_onehot(), precision=FULL_PRECISION).reshape(mp_count, 3, 512)
        normed_attn, packed, context = attention(tokens_s, gains[0].reshape(1, D), qkv_full, mask, rows, group)
        result, grad_mid, grad_context, grad_w_o, grad_w_in, grad_w_out, other = middle(
            tokens_s,
            context,
            dense_o,
            plain(gi, in_rows),
            plain(gu, in_rows),
            cot_s.reshape(tok_rows, D),
            gains[1],
            lengths,
            factors,
        )
    onehot = jnp.asarray(np.pad(table_onehot(), ((0, 0), (0, 128 - NB))))
    if merged:
        oq, oo, oi, ou, summed, gtok = back(
            depth, bits, group, kept, (mid, ctx, go, gi, gu, dg, gffn, n2, gout, long, rest), pu, gains, onehot, other
        )
    else:
        if group == o_rows:
            part_o = grad_w_o.reshape(depth, 2, 2, 2, round_up(o_rows, 16), D)
        else:
            part_o = slots(grad_w_o.reshape(mp_count, CTX_PAD, D)[:, : 3 * DH].reshape(D, D), o_rows)
        result = result.reshape(seg_count, SEG, D)
        packed_grads, sums = attention_back(packed, grad_context, mask, rows, group)
        table_grad = jnp.dot(sums.reshape(HEADS, 768), onehot, precision=FULL_PRECISION)
        grad_w_qkv = jnp.einsum("td,mtc->mdc", normed_attn, packed_grads, preferred_element_type=jnp.float32).astype(bf)
        grad_n1 = jnp.einsum("mtc,mdc->td", packed_grads, qkv_full, preferred_element_type=jnp.float32)
        _, norm_back_attn = jax.vjp(normed, tokens_s.astype(jnp.float32), gain_attn)
        grad_x_part, grad_gain_attn = norm_back_attn(grad_n1)
        grad_tokens = (grad_mid + grad_x_part).astype(bf)
        small = jnp.concatenate([
            jnp.pad(grad_gain_attn.reshape(D // 128, 128), ((0, ROW_TABLE - D // 128), (0, 0))),
            jnp.pad(table_grad, ((0, ROW_OTHER - ROW_TABLE - HEADS), (0, 0))),
            other,
        ])
        part_q = grad_w_qkv.reshape(mp_count, dp_count, q_rows, QKV_PAD)
        part_q = jnp.pad(part_q, ((0, 0), (0, 0), (0, rows_of_shards[0] - q_rows), (0, 0)))
        part_q = part_q.reshape(2, 2, depth, 2, rows_of_shards[0], QKV_PAD)
        oq, oo, oi, ou, summed, out, gtok = scatter_all(
            depth, bits, (part_q, part_o, slots(grad_w_in, in_rows), slots(grad_w_out, in_rows)), small, result, grad_tokens.reshape(seg_count, SEG, D)
        )
    shapes = (
        (3, q_rows, 3 * DH), w_o.shape, w_in.shape[::-1], w_out.shape, (D,), (D,), pos_table.shape[::-1],
        phm_rules.shape, down_left.shape, down_right.shape, up_left.shape, up_right.shape,
    )
    g_qkv, g_o, g_in, g_out, g_attn, g_ffn, g_table, *smalls, out, gtok = finish(
        oq, oo, oi, ou, summed, out, gtok, group, shapes
    )
    return (
        out.reshape(tok_rows, D),
        gtok.reshape(tok_rows, D),
        g_qkv.transpose(1, 0, 2),
        g_o,
        g_in.T,
        g_out,
        g_attn,
        g_ffn,
        g_table.T,
        *smalls,
    )


def solution(mesh):
    return jax.shard_map(
        local,
        mesh=mesh,
        in_specs=(
            P(("dp", "mp"), None),
            P("dp"),
            P(("dp", "mp"), None),
            P("dp", "mp", None),
            P(("dp", "mp"), None),
            P(None, ("dp", "mp")),
            P(("dp", "mp"), None),
            P(),
            P(),
            P(),
            P(),
            P(),
            P(),
            P(),
            P(),
        ),
        out_specs=(
            P(("dp", "mp"), None),
            P(("dp", "mp"), None),
            P("dp", "mp", None),
            P(("dp", "mp"), None),
            P(None, ("dp", "mp")),
            P(("dp", "mp"), None),
            P(),
            P(),
            P(),
            P(),
            P(),
            P(),
            P(),
            P(),
        ),
        check_vma=False,
    )
```
